32 devices in a mesh: rows: 16 (over z, x, core), seq: 2 (over y).
Axes of the slice: x: 2, y: 2, z: 4, core: 2. Of those that a mesh axis runs over, the one named last changes fastest.
Arguments:
- target_states: bfloat16 [16, 1024, 512], P('rows', 'seq'), may hold values from -6 to 6
- source_states: bfloat16 [16, 336, 512], P('rows', 'seq'), may hold values from -6 to 6
- target_segments: int32 [16, 1024], P('rows'), may hold values from 0 to 8, as said below
- source_segments: int32 [16, 336], P('rows'), may hold values from 0 to 9, as said below
- output_grad: bfloat16 [16, 1024, 512], P('rows', 'seq'), may hold values from -6 to 6
- self_project: bfloat16 [512, 1536], P(('rows', 'seq')), may hold values from -0.25 to 0.25
- self_output: bfloat16 [512, 512], P(('rows', 'seq')), may hold values from -1 to 1
- cross_query: bfloat16 [512, 512], P(('rows', 'seq')), may hold values from -0.25 to 0.25
- cross_keyval: bfloat16 [512, 1024], P(('rows', 'seq')), may hold values from -0.25 to 0.25
- cross_output: bfloat16 [512, 512], P(('rows', 'seq')), may hold values from -1 to 1
- hidden_up: bfloat16 [512, 2048], P(('rows', 'seq')), may hold values from -0.25 to 0.25
- hidden_bias: bfloat16 [2048], P(('rows', 'seq')), may hold values from -3 to 3
- hidden_down: bfloat16 [2048, 512], P(('rows', 'seq')), may hold values from -0.25 to 0.25
- output_bias: bfloat16 [512], P(('rows', 'seq')), may hold values from -3 to 3
- first_gain: bfloat16 [512], P(('rows', 'seq')), may hold values from 0.25 to 1.75
- first_shift: bfloat16 [512], P(('rows', 'seq')), may hold values from -3 to 3
- second_gain: bfloat16 [512], P(('rows', 'seq')), may hold values from 0.25 to 1.75
- second_shift: bfloat16 [512], P(('rows', 'seq')), may hold values from -3 to 3
- third_gain: bfloat16 [512], P(('rows', 'seq')), may hold values from 0.25 to 1.75
- third_shift: bfloat16 [512], P(('rows', 'seq')), may hold values from -3 to 3
Outputs:
- layer_output: bfloat16 [16, 1024, 512], P('rows', 'seq')
- grad_target: float32 [16, 1024, 512], P('rows', 'seq')
- grad_source: float32 [16, 336, 512], P('rows', 'seq')
- grad_self_project: float32 [512, 1536], P(('rows', 'seq'))
- grad_self_output: float32 [512, 512], P(('rows', 'seq'))
- grad_cross_query: float32 [512, 512], P(('rows', 'seq'))
- grad_cross_keyval: float32 [512, 1024], P(('rows', 'seq'))
- grad_cross_output: float32 [512, 512], P(('rows', 'seq'))
- grad_hidden_up: float32 [512, 2048], P(('rows', 'seq'))
- grad_hidden_bias: float32 [2048], P(('rows', 'seq'))
- grad_hidden_down: float32 [2048, 512], P(('rows', 'seq'))
- grad_output_bias: float32 [512], P(('rows', 'seq'))
- grad_first_gain: float32 [512], P(('rows', 'seq'))
- grad_first_shift: float32 [512], P(('rows', 'seq'))
- grad_second_gain: float32 [512], P(('rows', 'seq'))
- grad_second_shift: float32 [512], P(('rows', 'seq'))
- grad_third_gain: float32 [512], P(('rows', 'seq'))
- grad_third_shift: float32 [512], P(('rows', 'seq'))
The draws below stay inside these ranges and needn't reach their ends.
Inputs may be any that keep to these rules, and one draw needn't show every extreme that they name: `target_segments`: in each row the numbers 0 to 8 rise along the positions, each used. Sentences 0 to 3 and 5 to 8 each hold 64 to 127 positions; sentence 4 begins within the first 512 positions and ends within the last 512. `source_segments`: in each row the numbers 0 to 9 rise along the positions, each used; each sentence's source positions are roughly in proportion to its target positions, and 9 marks padding at the end of the row.
All inputs are finite; a program needn't handle non-finite values.
Results may differ from the reference program's by a relative error of at most 0.024.
Values may be sent and summed in bfloat16 or wider, within the bound.
No kernel may reach another device: no remote copies, remote signals or barrier semaphores. Data moves between devices by JAX's collectives and lax.ppermute only.
A program may use at most 256 MiB of HBM per device.

```python
import jax
import jax.numpy as jnp
from jax import lax

D = 512
HEADS = 8
HD = 64
FF = 2048
POS_DEV = 512
ROWS = 16
LENGTH = 1024
SOURCE = 336


def sentence_cuts(key):
    lengths = jax.random.randint(jax.random.fold_in(key, 5), (ROWS, 8), POS_DEV // 8, POS_DEV // 4)
    head_cuts = jnp.cumsum(lengths[:, :4], 1)
    tail_total = jnp.sum(lengths[:, 4:], 1, keepdims=True)
    middle_end = LENGTH - tail_total
    tail_steps = jnp.concatenate([jnp.zeros((ROWS, 1), jnp.int32), jnp.cumsum(lengths[:, 4:7], 1)], 1)
    return jnp.concatenate([head_cuts, middle_end + tail_steps], 1).astype(jnp.int32)


def draw_target_segments(key, part):
    cuts = sentence_cuts(key)
    positions = jnp.arange(LENGTH, dtype=jnp.int32)
    return jnp.sum((positions[None, :, None] >= cuts[:, None, :]).astype(jnp.int32), 2).astype(jnp.int32)


def draw_source_segments(key, part):
    cuts = sentence_cuts(key)
    key = jax.random.fold_in(key, 23)
    padding = jax.random.randint(key, (ROWS, 1), 1, SOURCE // 16 + 2)
    usable = SOURCE - padding - 9
    steps = jnp.arange(1, 9, dtype=jnp.int32)[None, :]
    source_cuts = cuts * usable // LENGTH + steps
    source_cuts = jnp.concatenate([source_cuts, SOURCE - padding], 1).astype(jnp.int32)
    positions = jnp.arange(SOURCE, dtype=jnp.int32)
    return jnp.sum((positions[None, :, None] >= source_cuts[:, None, :]).astype(jnp.int32), 2).astype(jnp.int32)


def levels(own_key, extent, shards, smallest, top_value):
    def one(position, shards_of):
        heights = jax.random.uniform(jax.random.fold_in(jax.random.fold_in(own_key, 6), position), (shards_of,), jnp.float32, smallest / len(shards), top_value / len(shards))
        return jnp.repeat(jnp.exp(heights), extent[position] // shards_of).reshape((-1,) + (1,) * (len(extent) - position - 1))

    loudness = one(*shards[0])
    for cut in shards[1:]:
        loudness = loudness * one(*cut)
    return loudness


def noise(own_key, extent, spread, bound, pieces=(), kind=jnp.bfloat16):
    drawn = spread * jax.random.normal(own_key, extent, jnp.float32)
    if pieces:
        drawn = drawn * levels(own_key, extent, pieces, -0.22, 0.18)
    return jnp.clip(drawn, -bound, bound).astype(kind)


def setup_inputs(seed: int = 0) -> dict:
    key_list = jax.random.split(jax.random.key(seed), 21)
    return {
        "target_states": noise(key_list[0], (ROWS, LENGTH, D), 1.0, 6.0, ((0, 16), (1, 2))),
        "source_states": noise(key_list[1], (ROWS, SOURCE, D), 1.0, 6.0, ((0, 16), (1, 2))),
        "target_segments": draw_target_segments(jax.random.fold_in(key_list[20], 71), 0),
        "source_segments": draw_source_segments(jax.random.fold_in(key_list[20], 71), 0),
        "output_grad": noise(key_list[4], (ROWS, LENGTH, D), 1.0, 6.0, ((0, 16), (1, 2))),
        "self_project": noise(key_list[5], (D, 3 * D), D ** -0.5, 0.25, ((0, 32),)),
        "self_output": noise(key_list[6], (D, D), (D // 16) ** -0.5, 1.0, ((0, 32),)),
        "cross_query": noise(key_list[7], (D, D), D ** -0.5, 0.25, ((0, 32),)),
        "cross_keyval": noise(key_list[8], (D, 2 * D), D ** -0.5, 0.25, ((0, 32),)),
        "cross_output": noise(key_list[9], (D, D), (D // 16) ** -0.5, 1.0, ((0, 32),)),
        "hidden_up": noise(key_list[10], (D, FF), D ** -0.5, 0.25, ((0, 32),)),
        "hidden_bias": noise(key_list[11], (FF,), 0.5, 3.0, ((0, 32),)),
        "hidden_down": noise(key_list[12], (FF, D), (FF // 4) ** -0.5, 0.25, ((0, 32),)),
        "output_bias": noise(key_list[13], (D,), 0.5, 3.0, ((0, 32),)),
        "first_gain": jnp.clip(1.0 + 0.15 * jax.random.normal(key_list[14], (D,), jnp.float32), 0.25, 1.75).astype(jnp.bfloat16),
        "first_shift": noise(key_list[15], (D,), 0.5, 3.0, ((0, 32),)),
        "second_gain": jnp.clip(1.0 + 0.15 * jax.random.normal(key_list[16], (D,), jnp.float32), 0.25, 1.75).astype(jnp.bfloat16),
        "second_shift": noise(key_list[17], (D,), 0.5, 3.0, ((0, 32),)),
        "third_gain": jnp.clip(1.0 + 0.15 * jax.random.normal(key_list[18], (D,), jnp.float32), 0.25, 1.75).astype(jnp.bfloat16),
        "third_shift": noise(key_list[19], (D,), 0.5, 3.0, ((0, 32),)),
    }


@jax.custom_vjp
def low(v):
    return lax.optimization_barrier(v.astype(jnp.bfloat16)).astype(jnp.float32)

@jax.custom_vjp
def low_back(v):
    return v

def low_keep(v):
    return (low(v), None)

def low_pass(kept, grad):
    return (grad,)

def back_keep(v):
    return (v, None)

def back_low(kept, grad):
    return (low(grad),)
low.defvjp(low_keep, low_pass)
low_back.defvjp(back_keep, back_low)
highest = lax.Precision.HIGHEST

def layer_norm(value, gain, shift):
    row_mean = lax.optimization_barrier(jnp.mean(value, -1, keepdims=True))
    centered = value - row_mean
    variance = lax.optimization_barrier(jnp.mean(centered * centered, -1, keepdims=True))
    return centered * lax.rsqrt(variance + 1e-05) * gain + shift

def matmul(left, right):
    return jnp.dot(left, right, precision=highest)

def attention(queries, key_rows, value_rows, query_seg, key_seg):
    row_count = queries.shape[0]
    block_count = row_count // POS_DEV
    query_heads = queries.reshape(block_count, POS_DEV, HEADS, HD)
    seg_blocks = query_seg.reshape(block_count, POS_DEV)
    key_heads = key_rows.reshape(key_rows.shape[0], HEADS, HD)
    value_heads = value_rows.reshape(value_rows.shape[0], HEADS, HD)

    def one_block(inputs_now):
        block_query, block_seg = inputs_now
        raw_scores = jnp.einsum('qhd,khd->hqk', block_query, key_heads, precision=highest) * HD ** (-0.5)
        same_seg = (block_seg[:, None] == key_seg[None, :])[None]
        scores = jnp.where(same_seg, low_back(raw_scores), -1000000000.0)
        weights = low(jax.nn.softmax(scores, axis=-1))
        return jnp.einsum('hqk,khd->qhd', weights, value_heads, precision=highest)
    mixed = lax.map(jax.checkpoint(one_block), (query_heads, seg_blocks))
    return mixed.reshape(row_count, HEADS * HD)

def forward_row(states, source, params, target_seg, source_seg):
    self_project, self_output, cross_query, cross_keyval, cross_output, hidden_up, hidden_bias, hidden_down, output_bias, first_gain, first_shift, second_gain, second_shift, third_gain, third_shift = params
    model_width = states.shape[1]
    lowered_one = low(layer_norm(states, first_gain, first_shift))
    projected = low(low_back(matmul(lowered_one, self_project)))
    self_mixed = low(low_back(attention(projected[:, :model_width], projected[:, model_width:2 * model_width], projected[:, 2 * model_width:], target_seg, target_seg)))
    after_self = states + low_back(matmul(self_mixed, self_output))
    lowered_two = low(layer_norm(after_self, second_gain, second_shift))
    cross_asked = low(low_back(matmul(lowered_two, cross_query)))
    key_value = low(low_back(matmul(low(source), cross_keyval)))
    cross_mixed = low(low_back(attention(cross_asked, key_value[:, :model_width], key_value[:, model_width:], target_seg, source_seg)))
    after_cross = after_self + low_back(matmul(cross_mixed, cross_output))
    lowered_three = low(layer_norm(after_cross, third_gain, third_shift))
    hidden = low_back(matmul(lowered_three, hidden_up) + hidden_bias)
    activated = low(jax.nn.gelu(hidden))
    return after_cross + low_back(matmul(activated, hidden_down) + output_bias)

def reference(target_states, source_states, target_segments, source_segments, output_grad, self_project, self_output, cross_query, cross_keyval, cross_output, hidden_up, hidden_bias, hidden_down, output_bias, first_gain, first_shift, second_gain, second_shift, third_gain, third_shift):
    params = tuple((weight.astype(jnp.float32) for weight in (self_project, self_output, cross_query, cross_keyval, cross_output, hidden_up, hidden_bias, hidden_down, output_bias, first_gain, first_shift, second_gain, second_shift, third_gain, third_shift)))

    def one_row(totals, inputs_now):
        states, source, target_seg, source_seg, out_grad = inputs_now

        def forward(states_in, source_in, params_in):
            return forward_row(states_in, source_in, params_in, target_seg, source_seg)
        result, pullback = jax.vjp(forward, states.astype(jnp.float32), source.astype(jnp.float32), params)
        grad_states, grad_src, grad_params = pullback(out_grad.astype(jnp.float32))
        totals = jax.tree.map(lambda left, right: left + right, totals, grad_params)
        return (totals, (result.astype(jnp.bfloat16), grad_states, grad_src))
    start = tuple((jnp.zeros(weight.shape, jnp.float32) for weight in params))
    totals, (layer_output, grad_target, grad_source) = lax.scan(one_row, start, (target_states, source_states, target_segments, source_segments, output_grad))
    return (layer_output, grad_target, grad_source, totals[0], totals[1], totals[2], totals[3], totals[4], totals[5], totals[6], totals[7], totals[8], totals[9], totals[10], totals[11], totals[12], totals[13], totals[14])
```

```python
import jax
import jax.numpy as jnp
from jax import lax
from jax.sharding import PartitionSpec as P

HEADS = 8
HD = 64


def layer_norm(value, gain, shift):
    row_mean = jnp.mean(value, -1, keepdims=True)
    centered = value - row_mean
    variance = jnp.mean(centered * centered, -1, keepdims=True)
    inverse = lax.rsqrt(variance + 1e-05)
    normed = centered * inverse
    return (normed * gain + shift, normed, inverse)


def norm_back(upstream, normed, inverse, gain):
    scaled = upstream * gain
    first_mean = jnp.mean(scaled, -1, keepdims=True)
    second_mean = jnp.mean(scaled * normed, -1, keepdims=True)
    grad_input = inverse * (scaled - first_mean - normed * second_mean)
    return (grad_input, jnp.sum(upstream * normed, 0), jnp.sum(upstream, 0))


def matmul(left, right):
    return jnp.dot(left, right, preferred_element_type=jnp.float32)


def transposed(left, right):
    return lax.dot_general(
        left, right, (((0,), (0,)), ((), ())), preferred_element_type=jnp.float32
    )


def against(left, right):
    return lax.dot_general(
        left, right, (((1,), (1,)), ((), ())), preferred_element_type=jnp.float32
    )


def head_split(value):
    return value.reshape(value.shape[0], HEADS, HD)


def head_join(value):
    return value.reshape(value.shape[0], HEADS * HD)


def scores_of(queries, key_rows, query_seg, key_seg):
    raw_scores = jnp.einsum(
        "qhd,khd->hqk", queries, key_rows, preferred_element_type=jnp.float32
    ) * HD ** (-0.5)
    same_seg = (query_seg[:, None] == key_seg[None, :])[None]
    return (raw_scores, same_seg)


def block_weights(queries, key_rows, query_seg, key_seg, log_total):
    raw_scores, same_seg = scores_of(queries, key_rows, query_seg, key_seg)
    return jnp.where(same_seg, jnp.exp(raw_scores - log_total[..., None]), 0.0)


def log_totals(queries, key_blocks, seg_blocks, query_seg):

    def log_advance(carry, inputs_now):
        row_max, row_total = carry
        key_rows, key_seg = inputs_now
        raw_scores, same_seg = scores_of(queries, key_rows, query_seg, key_seg)
        masked = jnp.where(same_seg, raw_scores, -1000000000.0)
        new_max = jnp.maximum(row_max, jnp.max(masked, -1))
        shifted = jnp.where(same_seg, jnp.exp(masked - new_max[..., None]), 0.0)
        return ((new_max, row_total * jnp.exp(row_max - new_max) + jnp.sum(shifted, -1)), None)

    start = (
        jnp.full((HEADS, queries.shape[0]), -1000000000.0, jnp.float32),
        jnp.zeros((HEADS, queries.shape[0]), jnp.float32),
    )
    (row_max, row_total), unused = lax.scan(log_advance, start, (key_blocks, seg_blocks))
    return row_max + jnp.log(row_total)


def weighted_sum(queries, key_blocks, value_blocks, seg_blocks, query_seg, log_total):

    def weighted_advance(carry, inputs_now):
        key_rows, value_rows, key_seg = inputs_now
        weights = block_weights(queries, key_rows, query_seg, key_seg, log_total).astype(
            jnp.bfloat16
        )
        return (
            carry
            + jnp.einsum("hqk,khd->qhd", weights, value_rows, preferred_element_type=jnp.float32),
            None,
        )

    total, unused = lax.scan(
        weighted_advance,
        jnp.zeros(queries.shape, jnp.float32),
        (key_blocks, value_blocks, seg_blocks),
    )
    return total


def grad_dots(queries, grad_heads, key_blocks, value_blocks, seg_blocks, query_seg, log_total):

    def grad_advance(carry, inputs_now):
        key_rows, value_rows, key_seg = inputs_now
        weights = block_weights(queries, key_rows, query_seg, key_seg, log_total)
        grad_weights = jnp.einsum(
            "qhd,khd->hqk", grad_heads, value_rows, preferred_element_type=jnp.float32
        )
        return (carry + jnp.sum(weights * grad_weights, -1), None)

    start = jnp.zeros((HEADS, queries.shape[0]), jnp.float32)
    total, unused = lax.scan(grad_advance, start, (key_blocks, value_blocks, seg_blocks))
    return total


def query_grads(
    queries, grad_heads, key_blocks, value_blocks, seg_blocks, query_seg, log_total, row_dots
):
    score_scale = HD ** (-0.5)

    def query_advance(carry, inputs_now):
        key_rows, value_rows, key_seg = inputs_now
        weights = block_weights(queries, key_rows, query_seg, key_seg, log_total)
        grad_weights = jnp.einsum(
            "qhd,khd->hqk", grad_heads, value_rows, preferred_element_type=jnp.float32
        )
        grad_scores = (weights * (grad_weights - row_dots[..., None])).astype(jnp.bfloat16)
        carry = (
            carry
            + jnp.einsum("hqk,khd->qhd", grad_scores, key_rows, preferred_element_type=jnp.float32)
            * score_scale
        )
        grad_keys = (
            jnp.einsum("hqk,qhd->khd", grad_scores, queries, preferred_element_type=jnp.float32)
            * score_scale
        )
        grad_values = jnp.einsum(
            "hqk,qhd->khd",
            weights.astype(jnp.bfloat16),
            grad_heads,
            preferred_element_type=jnp.float32,
        )
        return (carry, jnp.concatenate([head_join(grad_keys), head_join(grad_values)], 1))

    return lax.scan(
        query_advance, jnp.zeros(queries.shape, jnp.float32), (key_blocks, value_blocks, seg_blocks)
    )


BLOCK = 16
AXES = ("rows", "seq")


def device_pairs(flip):
    return [(device, device ^ flip) for device in range(32)]


def exchange(value, flip):
    return lax.ppermute(value, AXES, device_pairs(flip))


def device_index():
    return lax.axis_index("rows") * 2 + lax.axis_index("seq")


FLIP_Y, FLIP_CORE, FLIP_X, FLIP_Z = 1, 2, 4, 8


def gather_pair(left, right):
    width = left.shape[1]
    both = jnp.concatenate([left, right], 1)
    both = jnp.concatenate([both] + [exchange(both, FLIP_Z * i) for i in (1, 2, 3)], 0)
    out = []
    for value, first, second in (
        (both[:, :width], FLIP_X, FLIP_Y), (both[:, width:], FLIP_Y, FLIP_X)
    ):
        value = jnp.concatenate([value, exchange(value, first)], 0)
        other = exchange(value, second)
        order = [f + i * FLIP_Z for f in (0, first) for i in range(4)]
        order = order + [o + second for o in order]
        order = order + [o + FLIP_CORE for o in order]
        out.append(((value, other, exchange(value, FLIP_CORE), exchange(other, FLIP_CORE)), order))
    return out


def swapped(blocks):
    value = blocks.reshape((2,) * 5 + blocks.shape[1:])
    for axis in range(5):
        bit = (device_index() >> (4 - axis)) & 1
        value = jnp.where(bit == 1, jnp.flip(value, axis), value)
    return value.reshape(blocks.shape)


def natural(got):
    pieces, order = got
    whole = jnp.concatenate(pieces, 0).reshape(32, BLOCK, -1)
    whole = jnp.concatenate([whole[order.index(i)][None] for i in range(32)], 0)
    return swapped(whole).reshape(32 * BLOCK, -1)


def relative(value):
    return swapped(value.astype(jnp.bfloat16).reshape(32, BLOCK, -1))


def scatter_pair(left, right):
    out = []
    for value, first, second in ((left, FLIP_Y, FLIP_X), (right, FLIP_X, FLIP_Y)):
        parts = {i: value[i] for i in range(32)}
        for flip in (FLIP_CORE, first, second):
            kept = [i for i in sorted(parts) if not i & flip]
            sent = jnp.concatenate([parts[i | flip] for i in kept], 0)
            came = exchange(sent, flip)
            parts = {
                i: (
                    parts[i].astype(jnp.float32)
                    + came[n * BLOCK : (n + 1) * BLOCK].astype(jnp.float32)
                ).astype(jnp.bfloat16)
                for n, i in enumerate(kept)
            }
        out.append(parts)
    width = left.shape[2]
    total = jnp.concatenate([out[0][0], out[1][0]], 1).astype(jnp.float32)
    for i in (1, 2, 3):
        sent = jnp.concatenate([out[0][FLIP_Z * i], out[1][FLIP_Z * i]], 1)
        total = total + exchange(sent, FLIP_Z * i).astype(jnp.float32)
    return total[:, :width], total[:, width:]


def general_device(
    target_states,
    source_states,
    target_segments,
    source_segments,
    output_grad,
    self_project,
    self_output,
    cross_query,
    cross_keyval,
    cross_output,
    hidden_up,
    hidden_bias,
    hidden_down,
    output_bias,
    first_gain,
    first_shift,
    second_gain,
    second_shift,
    third_gain,
    third_shift,
):
    (
        full_project,
        full_output,
        full_query,
        full_keyval,
        full_crossout,
        full_up,
        full_upbias,
        full_down,
        full_downbias,
        gain_one,
        shift_one,
        gain_two,
        shift_two,
        gain_three,
        shift_three,
    ) = (
        lax.all_gather(self_project, ("rows", "seq"), axis=0, tiled=True),
        lax.all_gather(self_output, ("rows", "seq"), axis=0, tiled=True),
        lax.all_gather(cross_query, ("rows", "seq"), axis=0, tiled=True),
        lax.all_gather(cross_keyval, ("rows", "seq"), axis=0, tiled=True),
        lax.all_gather(cross_output, ("rows", "seq"), axis=0, tiled=True),
        lax.all_gather(hidden_up, ("rows", "seq"), axis=0, tiled=True),
        lax.all_gather(hidden_bias, ("rows", "seq"), axis=0, tiled=True),
        lax.all_gather(hidden_down, ("rows", "seq"), axis=0, tiled=True),
        lax.all_gather(output_bias, ("rows", "seq"), axis=0, tiled=True),
        lax.all_gather(first_gain, ("rows", "seq"), axis=0, tiled=True),
        lax.all_gather(first_shift, ("rows", "seq"), axis=0, tiled=True),
        lax.all_gather(second_gain, ("rows", "seq"), axis=0, tiled=True),
        lax.all_gather(second_shift, ("rows", "seq"), axis=0, tiled=True),
        lax.all_gather(third_gain, ("rows", "seq"), axis=0, tiled=True),
        lax.all_gather(third_shift, ("rows", "seq"), axis=0, tiled=True),
    )
    gain_one = gain_one.astype(jnp.float32)
    gain_two = gain_two.astype(jnp.float32)
    gain_three = gain_three.astype(jnp.float32)
    score_scale = HD ** (-0.5)
    states = target_states[0].astype(jnp.float32)
    local_rows = states.shape[0]
    model_width = states.shape[1]
    seq_count = lax.axis_size("seq")
    row_segments = target_segments[0]
    seq_length = row_segments.shape[0]
    own_segments = lax.dynamic_slice_in_dim(
        row_segments, lax.axis_index("seq") * local_rows, local_rows
    )
    block_rows = max(1, min(seq_count, 512 // local_rows)) * local_rows
    block_count = seq_length // block_rows
    seg_blocks = row_segments.reshape(block_count, block_rows)
    normed_value, normed_one, inverse_one = layer_norm(
        states, gain_one, shift_one.astype(jnp.float32)
    )
    lowered_one = normed_value.astype(jnp.bfloat16)
    projected = matmul(lowered_one, full_project).astype(jnp.bfloat16)
    query_flat = projected[:, :model_width]
    key_local = projected[:, model_width : 2 * model_width]
    value_local = projected[:, 2 * model_width :]
    queries = head_split(query_flat)
    key_all, value_all = (
        lax.all_gather(key_local, "seq", axis=0, tiled=True),
        lax.all_gather(value_local, "seq", axis=0, tiled=True),
    )
    key_blocks = key_all.reshape(block_count, block_rows, HEADS, HD)
    value_blocks = value_all.reshape(block_count, block_rows, HEADS, HD)
    log_total = log_totals(queries, key_blocks, seg_blocks, own_segments)
    self_mixed = head_join(
        weighted_sum(queries, key_blocks, value_blocks, seg_blocks, own_segments, log_total)
    ).astype(jnp.bfloat16)
    after_self = states + matmul(self_mixed, full_output)
    normed_value, normed_two, inverse_two = layer_norm(
        after_self, gain_two, shift_two.astype(jnp.float32)
    )
    lowered_two = normed_value.astype(jnp.bfloat16)
    cross_asked = matmul(lowered_two, full_query).astype(jnp.bfloat16)
    source_low = source_states[0]
    source_all = lax.all_gather(source_low, "seq", axis=0, tiled=True)
    key_value = matmul(source_all, full_keyval).astype(jnp.bfloat16)
    cross_key_heads = head_split(key_value[:, :model_width])
    cross_value_heads = head_split(key_value[:, model_width:])
    asked_heads = head_split(cross_asked)
    raw_scores, same_seg = scores_of(asked_heads, cross_key_heads, own_segments, source_segments[0])
    cross_probs = jax.nn.softmax(jnp.where(same_seg, raw_scores, -1000000000.0), axis=-1)
    cross_mixed = head_join(
        jnp.einsum(
            "hqk,khd->qhd",
            cross_probs.astype(jnp.bfloat16),
            cross_value_heads,
            preferred_element_type=jnp.float32,
        )
    ).astype(jnp.bfloat16)
    after_cross = after_self + matmul(cross_mixed, full_crossout)
    normed_value, normed_three, inverse_three = layer_norm(
        after_cross, gain_three, shift_three.astype(jnp.float32)
    )
    lowered_three = normed_value.astype(jnp.bfloat16)
    hidden = matmul(lowered_three, full_up) + full_upbias.astype(jnp.float32)
    activated = jax.nn.gelu(hidden).astype(jnp.bfloat16)
    layer_out = after_cross + matmul(activated, full_down) + full_downbias.astype(jnp.float32)
    grad_low = output_grad[0]
    out_grad = grad_low.astype(jnp.float32)
    grad_down = transposed(activated, grad_low)
    grad_downbias = jnp.sum(out_grad, 0)
    grad_act = against(grad_low, full_down)
    grad_hidden = jax.vjp(jax.nn.gelu, hidden)[1](grad_act)[0].astype(jnp.bfloat16)
    grad_upbias = jnp.sum(grad_hidden.astype(jnp.float32), 0)
    grad_up = transposed(lowered_three, grad_hidden)
    dx_three, grad_gain_three, grad_shift_three = norm_back(
        against(grad_hidden, full_up), normed_three, inverse_three, gain_three
    )
    grad_cross = out_grad + dx_three
    grad_cross_low = grad_cross.astype(jnp.bfloat16)
    grad_crossout = transposed(cross_mixed, grad_cross_low)
    grad_cross_heads = head_split(against(grad_cross_low, full_crossout).astype(jnp.bfloat16))
    grad_weights = jnp.einsum(
        "qhd,khd->hqk", grad_cross_heads, cross_value_heads, preferred_element_type=jnp.float32
    )
    grad_scores = (
        cross_probs * (grad_weights - jnp.sum(cross_probs * grad_weights, -1, keepdims=True))
    ).astype(jnp.bfloat16)
    grad_asked = head_join(
        jnp.einsum("hqk,khd->qhd", grad_scores, cross_key_heads, preferred_element_type=jnp.float32)
        * score_scale
    ).astype(jnp.bfloat16)
    grad_cross_keys = (
        jnp.einsum("hqk,qhd->khd", grad_scores, asked_heads, preferred_element_type=jnp.float32)
        * score_scale
    )
    grad_cross_values = jnp.einsum(
        "hqk,qhd->khd",
        cross_probs.astype(jnp.bfloat16),
        grad_cross_heads,
        preferred_element_type=jnp.float32,
    )
    pair_terms = jnp.concatenate([head_join(grad_cross_keys), head_join(grad_cross_values)], 1)
    pair_grad = lax.psum_scatter(
        pair_terms.astype(jnp.bfloat16), "seq", scatter_dimension=0, tiled=True
    )
    grad_keyval = transposed(source_low, pair_grad)
    grad_source = against(pair_grad, full_keyval)
    grad_query = transposed(lowered_two, grad_asked)
    dx_two, grad_gain_two, grad_shift_two = norm_back(
        against(grad_asked, full_query), normed_two, inverse_two, gain_two
    )
    grad_self = grad_cross + dx_two
    grad_self_low = grad_self.astype(jnp.bfloat16)
    grad_output = transposed(self_mixed, grad_self_low)
    grad_mixed = against(grad_self_low, full_output).astype(jnp.bfloat16)
    grad_heads = head_split(grad_mixed)
    row_dots = grad_dots(
        queries, grad_heads, key_blocks, value_blocks, seg_blocks, own_segments, log_total
    )
    grad_queries, key_terms = query_grads(
        queries, grad_heads, key_blocks, value_blocks, seg_blocks, own_segments, log_total, row_dots
    )
    summed = lax.psum_scatter(
        key_terms.reshape(seq_length, 2 * model_width).astype(jnp.bfloat16),
        "seq",
        scatter_dimension=0,
        tiled=True,
    )
    grad_projected = jnp.concatenate([head_join(grad_queries).astype(jnp.bfloat16), summed], 1)
    grad_project = transposed(lowered_one, grad_projected)
    dx_one, grad_gain_one, grad_shift_one = norm_back(
        against(grad_projected, full_project), normed_one, inverse_one, gain_one
    )
    grad_target = grad_self + dx_one
    shards = (
        lax.psum_scatter(grad_project, ("rows", "seq"), scatter_dimension=0, tiled=True),
        lax.psum_scatter(grad_output, ("rows", "seq"), scatter_dimension=0, tiled=True),
        lax.psum_scatter(grad_query, ("rows", "seq"), scatter_dimension=0, tiled=True),
        lax.psum_scatter(grad_keyval, ("rows", "seq"), scatter_dimension=0, tiled=True),
        lax.psum_scatter(grad_crossout, ("rows", "seq"), scatter_dimension=0, tiled=True),
        lax.psum_scatter(grad_up, ("rows", "seq"), scatter_dimension=0, tiled=True),
        lax.psum_scatter(grad_upbias, ("rows", "seq"), scatter_dimension=0, tiled=True),
        lax.psum_scatter(grad_down, ("rows", "seq"), scatter_dimension=0, tiled=True),
        lax.psum_scatter(grad_downbias, ("rows", "seq"), scatter_dimension=0, tiled=True),
        lax.psum_scatter(grad_gain_one, ("rows", "seq"), scatter_dimension=0, tiled=True),
        lax.psum_scatter(grad_shift_one, ("rows", "seq"), scatter_dimension=0, tiled=True),
        lax.psum_scatter(grad_gain_two, ("rows", "seq"), scatter_dimension=0, tiled=True),
        lax.psum_scatter(grad_shift_two, ("rows", "seq"), scatter_dimension=0, tiled=True),
        lax.psum_scatter(grad_gain_three, ("rows", "seq"), scatter_dimension=0, tiled=True),
        lax.psum_scatter(grad_shift_three, ("rows", "seq"), scatter_dimension=0, tiled=True),
    )
    return (layer_out.astype(jnp.bfloat16)[None], grad_target[None], grad_source[None]) + tuple(
        shards
    )


def fast_device(
    target_states,
    source_states,
    target_segments,
    source_segments,
    output_grad,
    self_project,
    self_output,
    cross_query,
    cross_keyval,
    cross_output,
    hidden_up,
    hidden_bias,
    hidden_down,
    output_bias,
    first_gain,
    first_shift,
    second_gain,
    second_shift,
    third_gain,
    third_shift,
):
    vectors = (
        output_bias, first_gain, first_shift, second_gain, second_shift, third_gain, third_shift
    )
    pad = jnp.zeros((BLOCK, 128 - len(vectors) - 4), jnp.bfloat16)
    vector_block = jnp.concatenate(
        [vector[:, None] for vector in vectors] + [hidden_bias.reshape(4, BLOCK).T, pad], 1
    )
    down_block = jnp.concatenate([hidden_down[i * BLOCK : (i + 1) * BLOCK] for i in range(4)], 1)
    left_one = self_project[:, :768]
    right_one = jnp.concatenate([self_project[:, 768:], vector_block], 1)
    left_two = jnp.concatenate([self_output, cross_query, cross_keyval, cross_output, hidden_up[:, :768]], 1)
    right_two = jnp.concatenate([hidden_up[:, 768:], down_block], 1)
    got_one = gather_pair(left_one, right_one)
    got_two = gather_pair(left_two, right_two)
    left_one, right_one = [natural(v) for v in got_one]
    left_two, right_two = [natural(v) for v in got_two]
    full_project = jnp.concatenate([left_one, right_one[:, :768]], 1)
    vector_rows = right_one[:, 768:768 + 128].T
    full_downbias, gain_one, shift_one, gain_two, shift_two, gain_three, shift_three = vector_rows[:7]
    full_upbias = vector_rows[7:11].reshape(4, 32, BLOCK).transpose(1, 0, 2).reshape(-1)
    full_output, full_query, full_keyval, full_crossout = (
        left_two[:, :512], left_two[:, 512:1024], left_two[:, 1024:2048], left_two[:, 2048:2560]
    )
    full_up = jnp.concatenate([left_two[:, 2560:], right_two[:, :1280]], 1)
    full_down = right_two[:, 1280:].reshape(32, BLOCK, 4, 512).transpose(0, 2, 1, 3).reshape(2048, 512)
    gain_one = gain_one.astype(jnp.float32)
    gain_two = gain_two.astype(jnp.float32)
    gain_three = gain_three.astype(jnp.float32)
    score_scale = HD ** (-0.5)
    states = target_states[0].astype(jnp.float32)
    local_rows = states.shape[0]
    model_width = states.shape[1]
    seq_count = lax.axis_size("seq")
    row_segments = target_segments[0]
    seq_length = row_segments.shape[0]
    own_segments = lax.dynamic_slice_in_dim(
        row_segments, lax.axis_index("seq") * local_rows, local_rows
    )
    block_rows = max(1, min(seq_count, 512 // local_rows)) * local_rows
    block_count = seq_length // block_rows
    seg_blocks = row_segments.reshape(block_count, block_rows)
    normed_value, normed_one, inverse_one = layer_norm(
        states, gain_one, shift_one.astype(jnp.float32)
    )
    lowered_one = normed_value.astype(jnp.bfloat16)
    projected = matmul(lowered_one, full_project).astype(jnp.bfloat16)
    query_flat = projected[:, :model_width]
    key_local = projected[:, model_width : 2 * model_width]
    value_local = projected[:, 2 * model_width :]
    queries = head_split(query_flat)
    key_all, value_all = (
        lax.all_gather(key_local, "seq", axis=0, tiled=True),
        lax.all_gather(value_local, "seq", axis=0, tiled=True),
    )
    key_blocks = key_all.reshape(block_count, block_rows, HEADS, HD)
    value_blocks = value_all.reshape(block_count, block_rows, HEADS, HD)
    log_total = log_totals(queries, key_blocks, seg_blocks, own_segments)
    self_mixed = head_join(
        weighted_sum(queries, key_blocks, value_blocks, seg_blocks, own_segments, log_total)
    ).astype(jnp.bfloat16)
    after_self = states + matmul(self_mixed, full_output)
    normed_value, normed_two, inverse_two = layer_norm(
        after_self, gain_two, shift_two.astype(jnp.float32)
    )
    lowered_two = normed_value.astype(jnp.bfloat16)
    cross_asked = matmul(lowered_two, full_query).astype(jnp.bfloat16)
    source_low = source_states[0]
    source_all = lax.all_gather(source_low, "seq", axis=0, tiled=True)
    key_value = matmul(source_all, full_keyval).astype(jnp.bfloat16)
    cross_key_heads = head_split(key_value[:, :model_width])
    cross_value_heads = head_split(key_value[:, model_width:])
    asked_heads = head_split(cross_asked)
    raw_scores, same_seg = scores_of(asked_heads, cross_key_heads, own_segments, source_segments[0])
    cross_probs = jax.nn.softmax(jnp.where(same_seg, raw_scores, -1000000000.0), axis=-1)
    cross_mixed = head_join(
        jnp.einsum(
            "hqk,khd->qhd",
            cross_probs.astype(jnp.bfloat16),
            cross_value_heads,
            preferred_element_type=jnp.float32,
        )
    ).astype(jnp.bfloat16)
    after_cross = after_self + matmul(cross_mixed, full_crossout)
    normed_value, normed_three, inverse_three = layer_norm(
        after_cross, gain_three, shift_three.astype(jnp.float32)
    )
    lowered_three = normed_value.astype(jnp.bfloat16)
    hidden = matmul(lowered_three, full_up) + full_upbias.astype(jnp.float32)
    activated = jax.nn.gelu(hidden).astype(jnp.bfloat16)
    layer_out = after_cross + matmul(activated, full_down) + full_downbias.astype(jnp.float32)
    grad_low = output_grad[0]
    out_grad = grad_low.astype(jnp.float32)
    grad_down = transposed(activated, grad_low)
    grad_downbias = jnp.sum(out_grad, 0)
    grad_act = against(grad_low, full_down)
    grad_hidden = jax.vjp(jax.nn.gelu, hidden)[1](grad_act)[0].astype(jnp.bfloat16)
    grad_upbias = jnp.sum(grad_hidden.astype(jnp.float32), 0)
    grad_up = transposed(lowered_three, grad_hidden)
    dx_three, grad_gain_three, grad_shift_three = norm_back(
        against(grad_hidden, full_up), normed_three, inverse_three, gain_three
    )
    grad_cross = out_grad + dx_three
    grad_cross_low = grad_cross.astype(jnp.bfloat16)
    grad_crossout = transposed(cross_mixed, grad_cross_low)
    grad_cross_heads = head_split(against(grad_cross_low, full_crossout).astype(jnp.bfloat16))
    grad_weights = jnp.einsum(
        "qhd,khd->hqk", grad_cross_heads, cross_value_heads, preferred_element_type=jnp.float32
    )
    grad_scores = (
        cross_probs * (grad_weights - jnp.sum(cross_probs * grad_weights, -1, keepdims=True))
    ).astype(jnp.bfloat16)
    grad_asked = head_join(
        jnp.einsum("hqk,khd->qhd", grad_scores, cross_key_heads, preferred_element_type=jnp.float32)
        * score_scale
    ).astype(jnp.bfloat16)
    grad_cross_keys = (
        jnp.einsum("hqk,qhd->khd", grad_scores, asked_heads, preferred_element_type=jnp.float32)
        * score_scale
    )
    grad_cross_values = jnp.einsum(
        "hqk,qhd->khd",
        cross_probs.astype(jnp.bfloat16),
        grad_cross_heads,
        preferred_element_type=jnp.float32,
    )
    pair_terms = jnp.concatenate([head_join(grad_cross_keys), head_join(grad_cross_values)], 1)
    pair_grad = lax.psum_scatter(
        pair_terms.astype(jnp.bfloat16), "seq", scatter_dimension=0, tiled=True
    )
    grad_keyval = transposed(source_low, pair_grad)
    grad_source = against(pair_grad, full_keyval)
    grad_query = transposed(lowered_two, grad_asked)
    dx_two, grad_gain_two, grad_shift_two = norm_back(
        against(grad_asked, full_query), normed_two, inverse_two, gain_two
    )
    grad_self = grad_cross + dx_two
    grad_self_low = grad_self.astype(jnp.bfloat16)
    grad_output = transposed(self_mixed, grad_self_low)
    grad_mixed = against(grad_self_low, full_output).astype(jnp.bfloat16)
    grad_heads = head_split(grad_mixed)
    row_dots = grad_dots(
        queries, grad_heads, key_blocks, value_blocks, seg_blocks, own_segments, log_total
    )
    grad_queries, key_terms = query_grads(
        queries, grad_heads, key_blocks, value_blocks, seg_blocks, own_segments, log_total, row_dots
    )
    summed = lax.psum_scatter(
        key_terms.reshape(seq_length, 2 * model_width).astype(jnp.bfloat16),
        "seq",
        scatter_dimension=0,
        tiled=True,
    )
    grad_projected = jnp.concatenate([head_join(grad_queries).astype(jnp.bfloat16), summed], 1)
    grad_project = transposed(lowered_one, grad_projected)
    dx_one, grad_gain_one, grad_shift_one = norm_back(
        against(grad_projected, full_project), normed_one, inverse_one, gain_one
    )
    grad_target = grad_self + dx_one
    vector_sums = jnp.stack(
        [grad_downbias, grad_gain_one, grad_shift_one, grad_gain_two, grad_shift_two,
         grad_gain_three, grad_shift_three], 1)
    bias_sums = grad_upbias.reshape(32, 4, BLOCK).transpose(0, 2, 1).reshape(512, 4)
    vector_sums = jnp.concatenate([vector_sums, bias_sums, jnp.zeros((512, 117), jnp.float32)], 1)
    down_sums = grad_down.reshape(32, 4, BLOCK, 512).transpose(0, 2, 1, 3).reshape(512, 2048)
    left_two = relative(grad_up)
    right_two = relative(down_sums)
    own_up, own_down = scatter_pair(left_two, right_two)
    left_one = relative(jnp.concatenate([grad_project, grad_keyval], 1))
    right_one = relative(jnp.concatenate([grad_output, grad_query, grad_crossout, vector_sums], 1))
    own_left, own_right = scatter_pair(left_one, right_one)
    own_down = jnp.concatenate([own_down[:, i * 512:(i + 1) * 512] for i in range(4)], 0)
    own_vectors = own_right[:, 1536:1536 + 11].T
    shards = (
        own_left[:, :1536], own_right[:, :512], own_right[:, 512:1024], own_left[:, 1536:],
        own_right[:, 1024:1536], own_up, own_vectors[7:11].reshape(64), own_down,
    ) + tuple(own_vectors[i] for i in range(7))
    return (layer_out.astype(jnp.bfloat16)[None], grad_target[None], grad_source[None]) + shards


def specs():
    in_specs = (
        P("rows", "seq", None),
        P("rows", "seq", None),
        P("rows", None),
        P("rows", None),
        P("rows", "seq", None),
        P(("rows", "seq"), None),
        P(("rows", "seq"), None),
        P(("rows", "seq"), None),
        P(("rows", "seq"), None),
        P(("rows", "seq"), None),
        P(("rows", "seq"), None),
        P(("rows", "seq")),
        P(("rows", "seq"), None),
        P(("rows", "seq")),
        P(("rows", "seq")),
        P(("rows", "seq")),
        P(("rows", "seq")),
        P(("rows", "seq")),
        P(("rows", "seq")),
        P(("rows", "seq")),
    )
    out_specs = (
        P("rows", "seq", None),
        P("rows", "seq", None),
        P("rows", "seq", None),
        P(("rows", "seq"), None),
        P(("rows", "seq"), None),
        P(("rows", "seq"), None),
        P(("rows", "seq"), None),
        P(("rows", "seq"), None),
        P(("rows", "seq"), None),
        P(("rows", "seq")),
        P(("rows", "seq"), None),
        P(("rows", "seq")),
        P(("rows", "seq")),
        P(("rows", "seq")),
        P(("rows", "seq")),
        P(("rows", "seq")),
        P(("rows", "seq")),
        P(("rows", "seq")),
    )
    return in_specs, out_specs


def solution(mesh):
    in_specs, out_specs = specs()
    fast = mesh.shape["rows"] == 16 and mesh.shape["seq"] == 2
    return jax.shard_map(
        fast_device if fast else general_device,
        mesh=mesh, in_specs=in_specs, out_specs=out_specs, check_vma=False,
    )
```

```python
import jax
import jax.numpy as jnp
from jax import lax
from jax.experimental import pallas as pl
from jax.experimental.pallas import tpu as pltpu
from jax.sharding import PartitionSpec as P

HEADS = 8
HD = 64


def layer_norm(value, gain, shift):
    row_mean = jnp.mean(value, -1, keepdims=True)
    centered = value - row_mean
    variance = jnp.mean(centered * centered, -1, keepdims=True)
    inverse = lax.rsqrt(variance + 1e-05)
    normed = centered * inverse
    return (normed * gain + shift, normed, inverse)


def norm_back(upstream, normed, inverse, gain):
    scaled = upstream * gain
    first_mean = jnp.mean(scaled, -1, keepdims=True)
    second_mean = jnp.mean(scaled * normed, -1, keepdims=True)
    grad_input = inverse * (scaled - first_mean - normed * second_mean)
    return (grad_input, jnp.sum(upstream * normed, 0), jnp.sum(upstream, 0))


def matmul(left, right):
    return jnp.dot(left, right, preferred_element_type=jnp.float32)


def transposed(left, right):
    return lax.dot_general(
        left, right, (((0,), (0,)), ((), ())), preferred_element_type=jnp.float32
    )


def against(left, right):
    return lax.dot_general(
        left, right, (((1,), (1,)), ((), ())), preferred_element_type=jnp.float32
    )


def head_split(value):
    return value.reshape(value.shape[0], HEADS, HD)


def head_join(value):
    return value.reshape(value.shape[0], HEADS * HD)


def scores_of(queries, key_rows, query_seg, key_seg):
    raw_scores = jnp.einsum(
        "qhd,khd->hqk", queries, key_rows, preferred_element_type=jnp.float32
    ) * HD ** (-0.5)
    same_seg = (query_seg[:, None] == key_seg[None, :])[None]
    return (raw_scores, same_seg)


def block_weights(queries, key_rows, query_seg, key_seg, log_total):
    raw_scores, same_seg = scores_of(queries, key_rows, query_seg, key_seg)
    return jnp.where(same_seg, jnp.exp(raw_scores - log_total[..., None]), 0.0)


def log_totals(queries, key_blocks, seg_blocks, query_seg):

    def log_advance(carry, inputs_now):
        row_max, row_total = carry
        key_rows, key_seg = inputs_now
        raw_scores, same_seg = scores_of(queries, key_rows, query_seg, key_seg)
        masked = jnp.where(same_seg, raw_scores, -1000000000.0)
        new_max = jnp.maximum(row_max, jnp.max(masked, -1))
        shifted = jnp.where(same_seg, jnp.exp(masked - new_max[..., None]), 0.0)
        return ((new_max, row_total * jnp.exp(row_max - new_max) + jnp.sum(shifted, -1)), None)

    start = (
        jnp.full((HEADS, queries.shape[0]), -1000000000.0, jnp.float32),
        jnp.zeros((HEADS, queries.shape[0]), jnp.float32),
    )
    (row_max, row_total), unused = lax.scan(log_advance, start, (key_blocks, seg_blocks))
    return row_max + jnp.log(row_total)


def weighted_sum(queries, key_blocks, value_blocks, seg_blocks, query_seg, log_total):

    def weighted_advance(carry, inputs_now):
        key_rows, value_rows, key_seg = inputs_now
        weights = block_weights(queries, key_rows, query_seg, key_seg, log_total).astype(
            jnp.bfloat16
        )
        return (
            carry
            + jnp.einsum("hqk,khd->qhd", weights, value_rows, preferred_element_type=jnp.float32),
            None,
        )

    total, unused = lax.scan(
        weighted_advance,
        jnp.zeros(queries.shape, jnp.float32),
        (key_blocks, value_blocks, seg_blocks),
    )
    return total


def grad_dots(queries, grad_heads, key_blocks, value_blocks, seg_blocks, query_seg, log_total):

    def grad_advance(carry, inputs_now):
        key_rows, value_rows, key_seg = inputs_now
        weights = block_weights(queries, key_rows, query_seg, key_seg, log_total)
        grad_weights = jnp.einsum(
            "qhd,khd->hqk", grad_heads, value_rows, preferred_element_type=jnp.float32
        )
        return (carry + jnp.sum(weights * grad_weights, -1), None)

    start = jnp.zeros((HEADS, queries.shape[0]), jnp.float32)
    total, unused = lax.scan(grad_advance, start, (key_blocks, value_blocks, seg_blocks))
    return total


def query_grads(
    queries, grad_heads, key_blocks, value_blocks, seg_blocks, query_seg, log_total, row_dots
):
    score_scale = HD ** (-0.5)

    def query_advance(carry, inputs_now):
        key_rows, value_rows, key_seg = inputs_now
        weights = block_weights(queries, key_rows, query_seg, key_seg, log_total)
        grad_weights = jnp.einsum(
            "qhd,khd->hqk", grad_heads, value_rows, preferred_element_type=jnp.float32
        )
        grad_scores = (weights * (grad_weights - row_dots[..., None])).astype(jnp.bfloat16)
        carry = (
            carry
            + jnp.einsum("hqk,khd->qhd", grad_scores, key_rows, preferred_element_type=jnp.float32)
            * score_scale
        )
        grad_keys = (
            jnp.einsum("hqk,qhd->khd", grad_scores, queries, preferred_element_type=jnp.float32)
            * score_scale
        )
        grad_values = jnp.einsum(
            "hqk,qhd->khd",
            weights.astype(jnp.bfloat16),
            grad_heads,
            preferred_element_type=jnp.float32,
        )
        return (carry, jnp.concatenate([head_join(grad_keys), head_join(grad_values)], 1))

    return lax.scan(
        query_advance, jnp.zeros(queries.shape, jnp.float32), (key_blocks, value_blocks, seg_blocks)
    )


def general_device(
    target_states,
    source_states,
    target_segments,
    source_segments,
    output_grad,
    self_project,
    self_output,
    cross_query,
    cross_keyval,
    cross_output,
    hidden_up,
    hidden_bias,
    hidden_down,
    output_bias,
    first_gain,
    first_shift,
    second_gain,
    second_shift,
    third_gain,
    third_shift,
):
    (
        full_project,
        full_output,
        full_query,
        full_keyval,
        full_crossout,
        full_up,
        full_upbias,
        full_down,
        full_downbias,
        gain_one,
        shift_one,
        gain_two,
        shift_two,
        gain_three,
        shift_three,
    ) = (
        lax.all_gather(self_project, ("rows", "seq"), axis=0, tiled=True),
        lax.all_gather(self_output, ("rows", "seq"), axis=0, tiled=True),
        lax.all_gather(cross_query, ("rows", "seq"), axis=0, tiled=True),
        lax.all_gather(cross_keyval, ("rows", "seq"), axis=0, tiled=True),
        lax.all_gather(cross_output, ("rows", "seq"), axis=0, tiled=True),
        lax.all_gather(hidden_up, ("rows", "seq"), axis=0, tiled=True),
        lax.all_gather(hidden_bias, ("rows", "seq"), axis=0, tiled=True),
        lax.all_gather(hidden_down, ("rows", "seq"), axis=0, tiled=True),
        lax.all_gather(output_bias, ("rows", "seq"), axis=0, tiled=True),
        lax.all_gather(first_gain, ("rows", "seq"), axis=0, tiled=True),
        lax.all_gather(first_shift, ("rows", "seq"), axis=0, tiled=True),
        lax.all_gather(second_gain, ("rows", "seq"), axis=0, tiled=True),
        lax.all_gather(second_shift, ("rows", "seq"), axis=0, tiled=True),
        lax.all_gather(third_gain, ("rows", "seq"), axis=0, tiled=True),
        lax.all_gather(third_shift, ("rows", "seq"), axis=0, tiled=True),
    )
    gain_one = gain_one.astype(jnp.float32)
    gain_two = gain_two.astype(jnp.float32)
    gain_three = gain_three.astype(jnp.float32)
    score_scale = HD ** (-0.5)
    states = target_states[0].astype(jnp.float32)
    local_rows = states.shape[0]
    model_width = states.shape[1]
    seq_count = lax.axis_size("seq")
    row_segments = target_segments[0]
    seq_length = row_segments.shape[0]
    own_segments = lax.dynamic_slice_in_dim(
        row_segments, lax.axis_index("seq") * local_rows, local_rows
    )
    block_rows = max(1, min(seq_count, 512 // local_rows)) * local_rows
    block_count = seq_length // block_rows
    seg_blocks = row_segments.reshape(block_count, block_rows)
    normed_value, normed_one, inverse_one = layer_norm(
        states, gain_one, shift_one.astype(jnp.float32)
    )
    lowered_one = normed_value.astype(jnp.bfloat16)
    projected = matmul(lowered_one, full_project).astype(jnp.bfloat16)
    query_flat = projected[:, :model_width]
    key_local = projected[:, model_width : 2 * model_width]
    value_local = projected[:, 2 * model_width :]
    queries = head_split(query_flat)
    key_all, value_all = (
        lax.all_gather(key_local, "seq", axis=0, tiled=True),
        lax.all_gather(value_local, "seq", axis=0, tiled=True),
    )
    key_blocks = key_all.reshape(block_count, block_rows, HEADS, HD)
    value_blocks = value_all.reshape(block_count, block_rows, HEADS, HD)
    log_total = log_totals(queries, key_blocks, seg_blocks, own_segments)
    self_mixed = head_join(
        weighted_sum(queries, key_blocks, value_blocks, seg_blocks, own_segments, log_total)
    ).astype(jnp.bfloat16)
    after_self = states + matmul(self_mixed, full_output)
    normed_value, normed_two, inverse_two = layer_norm(
        after_self, gain_two, shift_two.astype(jnp.float32)
    )
    lowered_two = normed_value.astype(jnp.bfloat16)
    cross_asked = matmul(lowered_two, full_query).astype(jnp.bfloat16)
    source_low = source_states[0]
    source_all = lax.all_gather(source_low, "seq", axis=0, tiled=True)
    key_value = matmul(source_all, full_keyval).astype(jnp.bfloat16)
    cross_key_heads = head_split(key_value[:, :model_width])
    cross_value_heads = head_split(key_value[:, model_width:])
    asked_heads = head_split(cross_asked)
    raw_scores, same_seg = scores_of(asked_heads, cross_key_heads, own_segments, source_segments[0])
    cross_probs = jax.nn.softmax(jnp.where(same_seg, raw_scores, -1000000000.0), axis=-1)
    cross_mixed = head_join(
        jnp.einsum(
            "hqk,khd->qhd",
            cross_probs.astype(jnp.bfloat16),
            cross_value_heads,
            preferred_element_type=jnp.float32,
        )
    ).astype(jnp.bfloat16)
    after_cross = after_self + matmul(cross_mixed, full_crossout)
    normed_value, normed_three, inverse_three = layer_norm(
        after_cross, gain_three, shift_three.astype(jnp.float32)
    )
    lowered_three = normed_value.astype(jnp.bfloat16)
    hidden = matmul(lowered_three, full_up) + full_upbias.astype(jnp.float32)
    activated = jax.nn.gelu(hidden).astype(jnp.bfloat16)
    layer_out = after_cross + matmul(activated, full_down) + full_downbias.astype(jnp.float32)
    grad_low = output_grad[0]
    out_grad = grad_low.astype(jnp.float32)
    grad_down = transposed(activated, grad_low)
    grad_downbias = jnp.sum(out_grad, 0)
    grad_act = against(grad_low, full_down)
    grad_hidden = jax.vjp(jax.nn.gelu, hidden)[1](grad_act)[0].astype(jnp.bfloat16)
    grad_upbias = jnp.sum(grad_hidden.astype(jnp.float32), 0)
    grad_up = transposed(lowered_three, grad_hidden)
    dx_three, grad_gain_three, grad_shift_three = norm_back(
        against(grad_hidden, full_up), normed_three, inverse_three, gain_three
    )
    grad_cross = out_grad + dx_three
    grad_cross_low = grad_cross.astype(jnp.bfloat16)
    grad_crossout = transposed(cross_mixed, grad_cross_low)
    grad_cross_heads = head_split(against(grad_cross_low, full_crossout).astype(jnp.bfloat16))
    grad_weights = jnp.einsum(
        "qhd,khd->hqk", grad_cross_heads, cross_value_heads, preferred_element_type=jnp.float32
    )
    grad_scores = (
        cross_probs * (grad_weights - jnp.sum(cross_probs * grad_weights, -1, keepdims=True))
    ).astype(jnp.bfloat16)
    grad_asked = head_join(
        jnp.einsum("hqk,khd->qhd", grad_scores, cross_key_heads, preferred_element_type=jnp.float32)
        * score_scale
    ).astype(jnp.bfloat16)
    grad_cross_keys = (
        jnp.einsum("hqk,qhd->khd", grad_scores, asked_heads, preferred_element_type=jnp.float32)
        * score_scale
    )
    grad_cross_values = jnp.einsum(
        "hqk,qhd->khd",
        cross_probs.astype(jnp.bfloat16),
        grad_cross_heads,
        preferred_element_type=jnp.float32,
    )
    pair_terms = jnp.concatenate([head_join(grad_cross_keys), head_join(grad_cross_values)], 1)
    pair_grad = lax.psum_scatter(
        pair_terms.astype(jnp.bfloat16), "seq", scatter_dimension=0, tiled=True
    )
    grad_keyval = transposed(source_low, pair_grad)
    grad_source = against(pair_grad, full_keyval)
    grad_query = transposed(lowered_two, grad_asked)
    dx_two, grad_gain_two, grad_shift_two = norm_back(
        against(grad_asked, full_query), normed_two, inverse_two, gain_two
    )
    grad_self = grad_cross + dx_two
    grad_self_low = grad_self.astype(jnp.bfloat16)
    grad_output = transposed(self_mixed, grad_self_low)
    grad_mixed = against(grad_self_low, full_output).astype(jnp.bfloat16)
    grad_heads = head_split(grad_mixed)
    row_dots = grad_dots(
        queries, grad_heads, key_blocks, value_blocks, seg_blocks, own_segments, log_total
    )
    grad_queries, key_terms = query_grads(
        queries, grad_heads, key_blocks, value_blocks, seg_blocks, own_segments, log_total, row_dots
    )
    summed = lax.psum_scatter(
        key_terms.reshape(seq_length, 2 * model_width).astype(jnp.bfloat16),
        "seq",
        scatter_dimension=0,
        tiled=True,
    )
    grad_projected = jnp.concatenate([head_join(grad_queries).astype(jnp.bfloat16), summed], 1)
    grad_project = transposed(lowered_one, grad_projected)
    dx_one, grad_gain_one, grad_shift_one = norm_back(
        against(grad_projected, full_project), normed_one, inverse_one, gain_one
    )
    grad_target = grad_self + dx_one
    shards = (
        lax.psum_scatter(grad_project, ("rows", "seq"), scatter_dimension=0, tiled=True),
        lax.psum_scatter(grad_output, ("rows", "seq"), scatter_dimension=0, tiled=True),
        lax.psum_scatter(grad_query, ("rows", "seq"), scatter_dimension=0, tiled=True),
        lax.psum_scatter(grad_keyval, ("rows", "seq"), scatter_dimension=0, tiled=True),
        lax.psum_scatter(grad_crossout, ("rows", "seq"), scatter_dimension=0, tiled=True),
        lax.psum_scatter(grad_up, ("rows", "seq"), scatter_dimension=0, tiled=True),
        lax.psum_scatter(grad_upbias, ("rows", "seq"), scatter_dimension=0, tiled=True),
        lax.psum_scatter(grad_down, ("rows", "seq"), scatter_dimension=0, tiled=True),
        lax.psum_scatter(grad_downbias, ("rows", "seq"), scatter_dimension=0, tiled=True),
        lax.psum_scatter(grad_gain_one, ("rows", "seq"), scatter_dimension=0, tiled=True),
        lax.psum_scatter(grad_shift_one, ("rows", "seq"), scatter_dimension=0, tiled=True),
        lax.psum_scatter(grad_gain_two, ("rows", "seq"), scatter_dimension=0, tiled=True),
        lax.psum_scatter(grad_shift_two, ("rows", "seq"), scatter_dimension=0, tiled=True),
        lax.psum_scatter(grad_gain_three, ("rows", "seq"), scatter_dimension=0, tiled=True),
        lax.psum_scatter(grad_shift_three, ("rows", "seq"), scatter_dimension=0, tiled=True),
    )
    return (layer_out.astype(jnp.bfloat16)[None], grad_target[None], grad_source[None]) + tuple(
        shards
    )


F32, BF16 = jnp.float32, jnp.bfloat16
BLOCK = 16
AXES = ("rows", "seq")
FLIP_Y, FLIP_CORE, FLIP_X, FLIP_Z = 1, 2, 4, 8
MODEL, FEED, OWN, WINDOW, HALF_SOURCE = 512, 2048, 512, 256, 192
KEYS, SOURCES = OWN + WINDOW, 2 * HALF_SOURCE
TILE = 128
MASKED = -1000000000.0
SCALE = HD ** (-0.5)


def exchange(value, flip):
    return lax.ppermute(value, AXES, [(device, device ^ flip) for device in range(32)])


def gather_pair(both, width):
    both = jnp.concatenate([both] + [exchange(both, FLIP_Z * i) for i in (1, 2, 3)], 0)
    out = []
    for value, first, second in (
        (both[:, :width], FLIP_X, FLIP_Y), (both[:, width:], FLIP_Y, FLIP_X)
    ):
        value = jnp.concatenate([value, exchange(value, first)], 0)
        other = exchange(value, second)
        out.append([value, other, exchange(value, FLIP_CORE), exchange(other, FLIP_CORE)])
    return out[0] + out[1]


def scatter_steps(kept, sent, first, second):
    came = exchange(sent, FLIP_CORE)
    for flip in (first, second):
        half = kept.shape[0] // 2
        sent = kept[half:] + came[half:]
        kept = kept[:half] + came[:half]
        came = exchange(sent, flip)
    return kept + came


def scatter_pair(left, right):
    left = scatter_steps(left[0], left[1], FLIP_Y, FLIP_X)
    right = scatter_steps(right[0], right[1], FLIP_X, FLIP_Y)
    both = jnp.concatenate([left, right], 1)
    return [both[:BLOCK]] + [
        exchange(both[BLOCK * i : BLOCK * (i + 1)], FLIP_Z * i) for i in (1, 2, 3)
    ]


def block_flips(first, second):
    return [
        (core * 2 + b, (a * 4 + z) * BLOCK, core * FLIP_CORE + b * second + a * first + z * FLIP_Z)
        for core in (0, 1) for b in (0, 1) for a in (0, 1) for z in range(4)
    ]


LEFT_FLIPS, RIGHT_FLIPS = block_flips(FLIP_X, FLIP_Y), block_flips(FLIP_Y, FLIP_X)


def nn(left, right):
    return jnp.dot(left, right, preferred_element_type=F32)


def load_blocks(me, flips, pieces, columns, target, target_columns, semaphore):
    for piece, row, flip in flips:
        place = pl.multiple_of((me ^ flip) * BLOCK, BLOCK)
        pltpu.make_async_copy(
            pieces[piece].at[pl.ds(row, BLOCK), columns],
            target.at[pl.ds(place, BLOCK), target_columns],
            semaphore,
        ).start()


def wait_all(target, semaphore):
    pltpu.make_async_copy(target, target, semaphore).wait()


def store_blocks(me, flips, source, columns, targets, target_columns, semaphore):
    for piece, row, flip in flips:
        place = pl.multiple_of((me ^ flip) * BLOCK, BLOCK)
        pltpu.make_async_copy(
            source.at[pl.ds(place, BLOCK), columns],
            targets[piece // 2].at[pl.ds((piece % 2) * 128 + row, BLOCK), target_columns],
            semaphore,
        ).start()


def normed_rows(value):
    centered = value - jnp.mean(value, -1, keepdims=True)
    inverse = lax.rsqrt(jnp.mean(centered * centered, -1, keepdims=True) + 1e-05)
    return centered * inverse, inverse


def norm_back_rows(upstream, normed, inverse, gain):
    scaled = upstream * gain
    first_mean = jnp.mean(scaled, -1, keepdims=True)
    second_mean = jnp.mean(scaled * normed, -1, keepdims=True)
    return inverse * (scaled - first_mean - normed * second_mean)


def column_sum(value):
    return jnp.sum(value, 0, keepdims=True)


def own_segments_of(index, segments):
    return jnp.where(index == 0, segments[:, :OWN], segments[:, OWN:]).astype(F32)


def key_segments_of(index, segments):
    near = jnp.where(index == 0, segments[:, OWN:KEYS], segments[:, OWN - WINDOW : OWN])
    return jnp.concatenate([own_segments_of(index, segments), near.astype(F32)], 1)


def spread(row):
    return jnp.broadcast_to(row, (TILE, row.shape[1])).T


def lane_half(shape, half):
    lanes = lax.broadcasted_iota(jnp.int32, shape, 1)
    return (lanes < HD) if half == 0 else (lanes >= HD)


def attend(queries, keys, values, mixed, log_rows, query_seg, key_row):
    (key_ref, key_at), (value_ref, value_at) = keys, values
    count = key_row.shape[1]

    def block(index, unused):
        rows = pl.ds(pl.multiple_of(index * TILE, TILE), TILE)
        same = jnp.concatenate([query_seg[rows, :]] * (count // TILE), 1) == key_row
        bias = jnp.where(same, 0.0, MASKED)
        lanes = lax.broadcasted_iota(jnp.int32, (TILE, TILE), 1)
        logs = jnp.zeros((TILE, TILE), F32)
        for pair in range(HEADS // 2):
            at = pair * TILE
            query = queries[rows, at : at + TILE]
            key = key_ref[:, key_at + at : key_at + at + TILE]
            value = value_ref[:, value_at + at : value_at + at + TILE]
            halves = []
            for half in range(2):
                masked = jnp.where(lane_half(query.shape, half), query, jnp.zeros_like(query))
                scores = against(masked, key) + bias
                top = jnp.max(scores, -1, keepdims=True)
                weights = jnp.exp(scores - top)
                total = jnp.sum(weights, -1, keepdims=True)
                halves.append(nn(weights.astype(BF16), value) * (1.0 / total))
                logs = jnp.where(lanes == pair * 2 + half, top + jnp.log(total), logs)
            mixed[rows, at : at + TILE] = jnp.where(
                lane_half(halves[0].shape, 0), halves[0], halves[1]
            ).astype(BF16)
        log_rows[:, rows] = logs.T[:HEADS]
        return unused

    lax.fori_loop(0, OWN // TILE, block, 0)


def head_dots(upstream, mixed):
    head = lax.broadcasted_iota(jnp.int32, (HEADS, MODEL), 1) // HD
    ones = (head == lax.broadcasted_iota(jnp.int32, (HEADS, MODEL), 0)).astype(F32)
    return lax.dot_general(
        ones, upstream.astype(F32) * mixed.astype(F32), (((1,), (1,)), ((), ())),
        precision=lax.Precision.HIGHEST, preferred_element_type=F32,
    )


def attend_back(
    queries, upstream, keys, values, log_rows, dot_rows, query_row, key_seg, query_grad, pair_grad
):
    (key_ref, key_at), (value_ref, value_at) = keys, values
    query_grad[...] = jnp.zeros_like(query_grad)

    def block(index, unused):
        rows = pl.ds(pl.multiple_of(index * TILE, TILE), TILE)
        same = jnp.concatenate([key_seg[rows, :]] * (OWN // TILE), 1) == query_row
        bias = jnp.where(same, 0.0, MASKED)
        for pair in range(HEADS // 2):
            at = pair * TILE
            query = queries[:, at : at + TILE]
            grad = upstream[:, at : at + TILE]
            key = key_ref[rows, key_at + at : key_at + at + TILE]
            value = value_ref[rows, value_at + at : value_at + at + TILE]
            total = jnp.zeros((OWN, TILE), F32)
            key_parts, value_parts = [], []
            for half in range(2):
                head = pair * 2 + half
                keep = lane_half(key.shape, half)
                one_key = jnp.where(keep, key, jnp.zeros_like(key))
                one_value = jnp.where(keep, value, jnp.zeros_like(value))
                weights = jnp.exp(against(one_key, query) + (bias - log_rows[head : head + 1, :]))
                grads = against(one_value, grad) - dot_rows[head : head + 1, :]
                score_grad = (weights * grads).astype(BF16)
                value_parts.append(nn(weights.astype(BF16), grad))
                key_parts.append(nn(score_grad, query))
                total = total + transposed(score_grad, one_key)
            query_grad[:, at : at + TILE] += total
            keep = lane_half(key_parts[0].shape, 0)
            pair_grad[rows, at : at + TILE] = jnp.where(keep, *key_parts).astype(BF16)
            pair_grad[rows, MODEL + at : MODEL + at + TILE] = jnp.where(keep, *value_parts).astype(BF16)
        return unused

    lax.fori_loop(0, key_seg.shape[0] // TILE, block, 0)


def pack_body(
    place, vectors, project, output, query, keyval, crossout, up, down, states,
    one, two, three, window, semaphore
):
    me, side = place[0], place[1]
    send = pltpu.make_async_copy(
        states.at[pl.ds(pl.multiple_of((1 - side) * WINDOW, WINDOW), WINDOW), :], window, semaphore
    )
    send.start()
    values = jnp.broadcast_to(vectors[...].astype(F32), (8, 256))
    lanes = lax.broadcasted_iota(jnp.int32, (8, TILE), 1)
    rows = lax.broadcasted_iota(jnp.int32, (8, TILE), 0)
    packed = jnp.zeros((8, TILE), F32)
    spot, wide = (me & 7) * 16, (me & 1) * 64
    for row in range(7):
        moved = pltpu.roll(values, spot + 256 - 16 * row, 1)[:, :TILE]
        inside = jnp.logical_and(lanes >= spot, lanes < spot + 16)
        packed = jnp.where(jnp.logical_and(rows == row, inside), moved, packed)
    moved = pltpu.roll(values, wide + 256 - 112, 1)[:, :TILE]
    inside = jnp.logical_and(lanes >= wide, lanes < wide + 64)
    packed = jnp.where(jnp.logical_and(rows == 7, inside), moved, packed)
    one[:, :1536] = project[...]
    one[:, 1536:] = jnp.concatenate([packed, jnp.zeros((8, TILE), F32)], 0).astype(BF16)
    two[:, :512] = output[...]
    two[:, 512:1024] = query[...]
    two[:, 1024:2048] = keyval[...]
    two[:, 2048:] = crossout[...]
    three[:, :FEED] = up[...]
    for part in range(4):
        three[:, FEED + part * 512 : FEED + (part + 1) * 512] = down[part * BLOCK : (part + 1) * BLOCK, :]
    send.wait()


def self_body(place, segments, states, window, *refs):
    pieces, refs = refs[:8], refs[8:]
    queries, pair, mixed, log_rows, lowered, vectors, up_bias, weight, packed, query_seg, sems = refs
    me, side = place[0], place[1]
    load_blocks(me, RIGHT_FLIPS, pieces[4:], slice(768, 896), packed, slice(0, 128), sems.at[0])
    load_blocks(me, LEFT_FLIPS, pieces[:4], slice(0, 768), weight, slice(0, 768), sems.at[1])
    load_blocks(me, RIGHT_FLIPS, pieces[4:], slice(0, 768), weight, slice(768, 1536), sems.at[2])
    query_seg[...] = spread(own_segments_of(side, segments[...]))
    key_row = key_segments_of(side, segments[...])
    wait_all(packed, sems.at[0])
    for tile in range(4):
        total = jnp.zeros((8, TILE), F32)
        for i in range(8):
            total = total + packed[(tile * 8 + i) * BLOCK : (tile * 8 + i + 1) * BLOCK, :].astype(F32)[:8]
        vectors[:, tile * TILE : (tile + 1) * TILE] = total
    for tile in range(16):
        total = (
            packed[2 * tile * BLOCK : (2 * tile + 1) * BLOCK, :].astype(F32)
            + packed[(2 * tile + 1) * BLOCK : (2 * tile + 2) * BLOCK, :].astype(F32)
        )
        up_bias[:, tile * TILE : (tile + 1) * TILE] = total[7:8]
    gain, shift = vectors[1:2, :], vectors[2:3, :]
    for i in range(KEYS // TILE):
        rows = slice(i * TILE, (i + 1) * TILE)
        value = states[rows, :] if i < 4 else window[(i - 4) * TILE : (i - 3) * TILE, :]
        lowered[rows, :] = (normed_rows(value.astype(F32))[0] * gain + shift).astype(BF16)
    wait_all(weight.at[:, :768], sems.at[1])
    wait_all(weight.at[:, 768:], sems.at[2])
    for i in range(KEYS // 256):
        rows = slice(i * 256, (i + 1) * 256)
        if i < 2:
            queries[rows, :] = (nn(lowered[rows, :], weight[:, :512]) .astype(BF16) * SCALE).astype(BF16)
        pair[rows, :] = nn(lowered[rows, :], weight[:, 512:]).astype(BF16)
    attend(queries, (pair, 0), (pair, MODEL), mixed, log_rows, query_seg, key_row)


def cross_body(place, segments, source_segments, states, own_source, other_source, self_mixed, vectors, *refs):
    pieces, refs = refs[:8], refs[8:]
    after_self, lowered, queries, pair, mixed, log_rows, after_cross, source, weight, query_seg, sems = refs
    me, side = place[0], place[1]
    load_blocks(me, LEFT_FLIPS, pieces[:4], slice(0, 1280), weight, slice(0, 1280), sems.at[0])
    load_blocks(me, RIGHT_FLIPS, pieces[4:], slice(0, 1280), weight, slice(1280, 2560), sems.at[1])
    query_seg[...] = spread(own_segments_of(side, segments[...]))
    key_row = source_segments[...].astype(F32)
    source[:HALF_SOURCE, :] = jnp.where(side == 0, own_source[...], other_source[...])
    source[HALF_SOURCE:, :] = jnp.where(side == 0, other_source[...], own_source[...])
    gain, shift = vectors[3:4, :], vectors[4:5, :]
    wait_all(weight.at[:, :1280], sems.at[0])
    wait_all(weight.at[:, 1280:], sems.at[1])
    pair[...] = nn(source[...], weight[:, 1024:2048]).astype(BF16)
    for i in range(2):
        rows = slice(i * 256, (i + 1) * 256)
        value = states[rows, :].astype(F32) + nn(self_mixed[rows, :], weight[:, :512])
        after_self[rows, :] = value
        lowered[rows, :] = (normed_rows(value)[0] * gain + shift).astype(BF16)
        queries[rows, :] = (nn(lowered[rows, :], weight[:, 512:1024]).astype(BF16) * SCALE).astype(BF16)
    attend(queries, (pair, 0), (pair, MODEL), mixed, log_rows, query_seg, key_row)
    for i in range(2):
        rows = slice(i * 256, (i + 1) * 256)
        after_cross[rows, :] = after_self[rows, :] + nn(mixed[rows, :], weight[:, 2048:])


CHUNK = 512


def feed_body(place, after_cross, output_grad, vectors, up_bias, *refs):
    pieces, refs = refs[:8], refs[8:]
    (
        layer_out, after_grad, up_keep, up_send, down_keep, down_send, sums, bias_sums,
        up, down, lowered, flipped, total, back, up_grad, down_grad, sems,
    ) = refs
    me = place[0]
    load_blocks(me, LEFT_FLIPS, pieces[:4], slice(0, FEED), up, slice(0, FEED), sems.at[0])
    for part in range(4):
        for piece, row, flip in RIGHT_FLIPS:
            spot = pl.multiple_of((me ^ flip) * 64 + part * BLOCK, BLOCK)
            pltpu.make_async_copy(
                pieces[4 + piece].at[pl.ds(row, BLOCK), slice(part * 512, (part + 1) * 512)],
                down.at[pl.ds(spot, BLOCK), :],
                sems.at[1],
            ).start()
    gain, shift = vectors[5:6, :], vectors[6:7, :]
    for i in range(4):
        rows = slice(i * TILE, (i + 1) * TILE)
        low = (normed_rows(after_cross[rows, :])[0] * gain + shift).astype(BF16)
        lowered[rows, :] = low
    flipped[...] = lowered[...].T
    total[...] = jnp.zeros_like(total)
    back[...] = jnp.zeros_like(back)
    wait_all(up, sems.at[0])
    wait_all(down, sems.at[1])

    def chunk(index, unused):
        at = pl.ds(pl.multiple_of(index * CHUNK, CHUNK), CHUNK)
        hidden = nn(lowered[...], up[:, at]) + up_bias[:, at]
        square = hidden * hidden
        inner = 0.7978845608028654 * hidden * (1.0 + 0.044715 * square)
        curve = jnp.tanh(inner)
        half = 0.5 * (1.0 + curve)
        activated = (hidden * half).astype(BF16)
        slope = half + (0.5 * 0.7978845608028654) * hidden * (1.0 - curve * curve) * (
            1.0 + (3 * 0.044715) * square
        )
        total[...] += nn(activated, down[at, :])
        down_grad[at, :] = transposed(activated, output_grad[...]).astype(BF16)
        grad_hidden = (against(output_grad[...], down[at, :]) * slope).astype(BF16)
        bias_sums[:, at] = column_sum(grad_hidden.astype(F32))
        up_grad[:, at] = nn(flipped[...], grad_hidden).astype(BF16)
        back[...] += against(grad_hidden, up[:, at])
        return unused

    lax.fori_loop(0, FEED // CHUNK, chunk, 0)
    store_blocks(me, LEFT_FLIPS, up_grad, slice(0, FEED), (up_keep, up_send), slice(0, FEED), sems.at[2])
    for part in range(4):
        for piece, row, flip in RIGHT_FLIPS:
            spot = pl.multiple_of((me ^ flip) * 64 + part * BLOCK, BLOCK)
            pltpu.make_async_copy(
                down_grad.at[pl.ds(spot, BLOCK), :],
                (down_keep, down_send)[piece // 2].at[
                    pl.ds((piece % 2) * 128 + row, BLOCK), slice(part * 512, (part + 1) * 512)
                ],
                sems.at[3],
            ).start()
    gain_sum, shift_sum, bias_sum = (jnp.zeros((1, MODEL), F32) for _ in range(3))
    for i in range(4):
        rows = slice(i * TILE, (i + 1) * TILE)
        value, grad = after_cross[rows, :], output_grad[rows, :].astype(F32)
        layer_out[rows, :] = (value + total[rows, :] + vectors[0:1, :]).astype(BF16)
        normed, inverse = normed_rows(value)
        upstream = back[rows, :]
        after_grad[rows, :] = grad + norm_back_rows(upstream, normed, inverse, gain)
        gain_sum, shift_sum = gain_sum + column_sum(upstream * normed), shift_sum + column_sum(upstream)
        bias_sum = bias_sum + column_sum(grad)
    zero = jnp.zeros((1, MODEL), F32)
    sums[...] = jnp.concatenate([bias_sum, zero, zero, zero, zero, gain_sum, shift_sum, zero], 0)
    wait_all(up_grad, sems.at[2])
    wait_all(down_grad, sems.at[3])


def cross_back_body(
    place, segments, source_segments, own_source, other_source, after_self, lowered, queries, pair,
    mixed, log_rows, after_grad, vectors, sums, *refs
):
    pieces, refs = refs[:8], refs[8:]
    (
        self_grad, source_own, source_send, left_keep, left_send, right_keep, right_send, new_sums,
        source, weight, upstream, query_grad, pair_grad, left_grad, right_grad, key_seg, sems,
    ) = refs
    me, side = place[0], place[1]
    load_blocks(me, RIGHT_FLIPS, pieces[4:], slice(0, 1280), weight, slice(1280, 2560), sems.at[1])
    load_blocks(me, LEFT_FLIPS, pieces[:4], slice(0, 1280), weight, slice(0, 1280), sems.at[0])
    key_seg[...] = spread(source_segments[...].astype(F32))
    query_row = own_segments_of(side, segments[...])
    source[:HALF_SOURCE, :] = jnp.where(side == 0, own_source[...], other_source[...])
    source[HALF_SOURCE:, :] = jnp.where(side == 0, other_source[...], own_source[...])
    wait_all(weight.at[:, 1280:], sems.at[1])
    wait_all(weight.at[:, :1280], sems.at[0])
    grad_low = after_grad[...].astype(BF16)
    upstream[...] = against(grad_low, weight[:, 2048:]).astype(BF16)
    left_grad[:, :512] = transposed(mixed[...], grad_low).astype(BF16)
    dot_rows = head_dots(upstream[...], mixed[...])
    attend_back(
        queries, upstream, (pair, 0), (pair, MODEL), log_rows, dot_rows, query_row, key_seg,
        query_grad, pair_grad,
    )
    asked = (query_grad[...] * SCALE).astype(BF16)
    left_grad[:, 512:] = transposed(lowered[...], asked).astype(BF16)
    right_grad[...] = transposed(source[...], pair_grad[...]).astype(BF16)
    store_blocks(me, LEFT_FLIPS, left_grad, slice(0, 1024), (left_keep, left_send), slice(0, 1024), sems.at[2])
    store_blocks(me, RIGHT_FLIPS, right_grad, slice(0, 1024), (right_keep, right_send), slice(0, 1024), sems.at[3])
    back = against(pair_grad[...], weight[:, 1024:2048])
    first, second = back[:HALF_SOURCE], back[HALF_SOURCE:]
    source_own[...] = jnp.where(side == 0, first, second)
    source_send[...] = jnp.where(side == 0, second, first).astype(BF16)
    gain = vectors[3:4, :]
    gain_sum, shift_sum = jnp.zeros((1, MODEL), F32), jnp.zeros((1, MODEL), F32)
    for i in range(2):
        rows = slice(i * 256, (i + 1) * 256)
        normed, inverse = normed_rows(after_self[rows, :])
        up = against(asked[rows, :], weight[:, 512:1024])
        self_grad[rows, :] = after_grad[rows, :] + norm_back_rows(up, normed, inverse, gain)
        gain_sum, shift_sum = gain_sum + column_sum(up * normed), shift_sum + column_sum(up)
    zero = jnp.zeros((1, MODEL), F32)
    new_sums[...] = sums[...] + jnp.concatenate(
        [zero, zero, zero, gain_sum, shift_sum, zero, zero, zero], 0
    )
    wait_all(left_grad, sems.at[2])
    wait_all(right_grad, sems.at[3])


def self_back_body(
    place, segments, states, window, lowered, queries, pair, mixed, log_rows, self_grad, vectors,
    sums, bias_sums, *refs
):
    pieces, more, refs = refs[:8], refs[8:12], refs[12:]
    (
        own_back, send_back, left_keep, left_send, right_keep, right_send,
        weight, output, upstream, query_grad, pair_grad, left_grad, right_grad, key_seg, sems,
    ) = refs
    me, side = place[0], place[1]
    load_blocks(me, LEFT_FLIPS, more, slice(0, 512), output, slice(0, 512), sems.at[4])
    load_blocks(me, LEFT_FLIPS, pieces[:4], slice(0, 768), weight, slice(0, 768), sems.at[0])
    load_blocks(me, RIGHT_FLIPS, pieces[4:], slice(0, 768), weight, slice(768, 1536), sems.at[1])
    key_seg[...] = spread(key_segments_of(side, segments[...]))
    query_row = own_segments_of(side, segments[...])
    wait_all(output, sems.at[4])
    grad_low = self_grad[...].astype(BF16)
    upstream[...] = against(grad_low, output[...]).astype(BF16)
    right_grad[:, 512:1024] = transposed(mixed[...], grad_low).astype(BF16)
    dot_rows = head_dots(upstream[...], mixed[...])
    attend_back(
        queries, upstream, (pair, 0), (pair, MODEL), log_rows, dot_rows, query_row, key_seg,
        query_grad, pair_grad,
    )
    wait_all(weight.at[:, :768], sems.at[0])
    wait_all(weight.at[:, 768:], sems.at[1])
    asked = (query_grad[...] * SCALE).astype(BF16)
    left_grad[:, :512] = transposed(lowered[:OWN, :], asked).astype(BF16)
    left_grad[:, 512:] = transposed(lowered[...], pair_grad[:, :512]).astype(BF16)
    right_grad[:, :512] = transposed(lowered[...], pair_grad[:, 512:]).astype(BF16)
    store_blocks(me, LEFT_FLIPS, left_grad, slice(0, 1024), (left_keep, left_send), slice(0, 1024), sems.at[2])
    gain_sum, shift_sum = jnp.zeros((1, MODEL), F32), jnp.zeros((1, MODEL), F32)
    for i in range(3):
        rows = slice(i * 256, (i + 1) * 256)
        back = against(pair_grad[rows, :], weight[:, 512:])
        if i < 2:
            back = back + against(asked[rows, :], weight[:, :512])
            own_back[rows, :] = back
            value = states[rows, :]
        else:
            send_back[...] = back.astype(BF16)
            value = window[...]
        normed = normed_rows(value.astype(F32))[0]
        gain_sum, shift_sum = gain_sum + column_sum(back * normed), shift_sum + column_sum(back)
    zero = jnp.zeros((1, MODEL), F32)
    sums = sums[...] + jnp.concatenate([zero, gain_sum, shift_sum, zero, zero, zero, zero, zero], 0)
    last = lax.broadcasted_iota(jnp.int32, (8, TILE), 0) == 7
    for device in range(32):
        tile, wide = device // 8 * TILE, device // 2 * TILE
        value = jnp.where(last, bias_sums[:, wide : wide + TILE], sums[:, tile : tile + TILE])
        high = value.astype(BF16).astype(F32)
        right_grad[device * BLOCK : (device + 1) * BLOCK, 1024:] = jnp.concatenate(
            [high, value - high], 0
        ).astype(BF16)
    store_blocks(me, RIGHT_FLIPS, right_grad, slice(0, 1152), (right_keep, right_send), slice(0, 1152), sems.at[3])
    wait_all(left_grad, sems.at[2])
    wait_all(right_grad, sems.at[3])


def target_body(place, back, came, states, self_grad, vectors, out):
    gain = vectors[1:2, :]
    for i in range(4):
        rows = slice(i * TILE, (i + 1) * TILE)
        here = (i < 2) == (place[1] == 1)
        extra = came[(i % 2) * TILE : (i % 2 + 1) * TILE, :].astype(F32)
        upstream = back[rows, :] + jnp.where(here, extra, 0.0)
        normed, inverse = normed_rows(states[rows, :].astype(F32))
        out[rows, :] = self_grad[rows, :] + norm_back_rows(upstream, normed, inverse, gain)


def finish_body(place, *refs):
    feed, cross, last, outs = refs[:4], refs[4:8], refs[8:12], refs[12:]
    project, output, query, keyval, crossout, up, down, small = outs
    me = place[0]

    def total(parts, begin, end):
        value = parts[0][:, begin:end].astype(F32)
        for part in parts[1:]:
            value = value + part[:, begin:end].astype(F32)
        return value

    up[...] = total(feed, 0, FEED)
    for part in range(4):
        down[part * BLOCK : (part + 1) * BLOCK, :] = total(feed, FEED + part * 512, FEED + (part + 1) * 512)
    crossout[...] = total(cross, 0, 512)
    query[...] = total(cross, 512, 1024)
    keyval[...] = total(cross, 1024, 2048)
    project[...] = total(last, 0, 1536)
    output[...] = total(last, 1536, 2048)
    value = total(last, 2048, 2176)
    value = value[:8] + value[8:]
    narrow = pltpu.roll(value, (TILE - (me & 7) * 16) & 127, 1)
    wide = pltpu.roll(value, (TILE - (me & 1) * 64) & 127, 1)
    last_row = lax.broadcasted_iota(jnp.int32, (8, TILE), 0) == 7
    small[...] = jnp.where(last_row, wide, narrow)


def shape_of(*shape, dtype=BF16):
    return jax.ShapeDtypeStruct(shape, dtype)


VMEM_SPEC = pl.BlockSpec(memory_space=pltpu.VMEM)
ANY_SPEC = pl.BlockSpec(memory_space=pl.ANY)
SMEM_SPEC = pl.BlockSpec(memory_space=pltpu.SMEM)


def call(body, name, place, inputs, pieces, outs, scratch, flops, any_outs=(), any_ins=()):
    return pl.pallas_call(
        body,
        name=name,
        out_shape=outs,
        in_specs=[SMEM_SPEC]
        + [ANY_SPEC if i in any_ins else VMEM_SPEC for i in range(len(inputs))]
        + [ANY_SPEC] * len(pieces),
        out_specs=[ANY_SPEC if i in any_outs else VMEM_SPEC for i in range(len(outs))],
        scratch_shapes=scratch,
        compiler_params=pltpu.CompilerParams(vmem_limit_bytes=40 * 2**20),
        cost_estimate=pl.CostEstimate(flops=flops, bytes_accessed=4 * 2**20, transcendentals=0),
    )(place, *inputs, *pieces)


def fast_device(
    target_states, source_states, target_segments, source_segments, output_grad, self_project,
    self_output, cross_query, cross_keyval, cross_output, hidden_up, hidden_bias, hidden_down,
    output_bias, first_gain, first_shift, second_gain, second_shift, third_gain, third_shift,
):
    vmem, dma = pltpu.VMEM, pltpu.SemaphoreType.DMA
    side = lax.axis_index("seq")
    place = jnp.stack([lax.axis_index("rows") * 2 + side, side]).astype(jnp.int32)
    states, grad = target_states[0], output_grad[0]
    small = jnp.concatenate([
        output_bias, first_gain, first_shift, second_gain, second_shift, third_gain, third_shift,
        hidden_bias, jnp.zeros((80,), BF16),
    ]).reshape(1, 256)
    one, two, three, near = call(
        pack_body, "pack", place,
        [small, self_project, self_output, cross_query, cross_keyval, cross_output, hidden_up, hidden_down, states],
        [], [shape_of(16, 1664), shape_of(16, 2560), shape_of(16, 4096), shape_of(WINDOW, MODEL)],
        [dma], 1000000, any_outs=(3,), any_ins=(8,),
    )
    window = exchange(near, FLIP_Y)
    pieces_one = gather_pair(one, 768)
    pieces_two = gather_pair(two, 1280)
    pieces_three = gather_pair(three, FEED)
    half = source_states.shape[1]
    own_source = jnp.pad(source_states[0], ((0, HALF_SOURCE - half), (0, 0)))
    other_source = exchange(own_source, FLIP_Y)
    gap = jnp.full((1, HALF_SOURCE - half), -1, jnp.int32)
    source_seg = jnp.concatenate([source_segments[:, :half], gap, source_segments[:, half:], gap], 1)

    queries, pair, mixed, logs, lowered, vectors, up_bias = call(
        self_body, "self_forward", place, [target_segments, states, window], pieces_one,
        [
            shape_of(OWN, MODEL), shape_of(KEYS, 2 * MODEL), shape_of(OWN, MODEL), shape_of(HEADS, OWN, dtype=F32),
            shape_of(KEYS, MODEL), shape_of(8, MODEL, dtype=F32), shape_of(1, FEED, dtype=F32),
        ],
        [vmem((MODEL, 1536), BF16), vmem((MODEL, TILE), BF16), vmem((OWN, TILE), F32), dma((3,))],
        5000000000,
    )
    after_self, lowered_two, queries_two, pair_two, mixed_two, logs_two, after_cross = call(
        cross_body, "cross_forward", place,
        [target_segments, source_seg, states, own_source, other_source, mixed, vectors], pieces_two,
        [
            shape_of(OWN, MODEL, dtype=F32), shape_of(OWN, MODEL), shape_of(OWN, MODEL), shape_of(SOURCES, 2 * MODEL),
            shape_of(OWN, MODEL), shape_of(HEADS, OWN, dtype=F32), shape_of(OWN, MODEL, dtype=F32),
        ],
        [vmem((SOURCES, MODEL), BF16), vmem((MODEL, 2560), BF16), vmem((OWN, TILE), F32), dma((2,))],
        5000000000,
    )
    layer_out, after_grad, up_keep, up_send, down_keep, down_send, sums, bias_sums = call(
        feed_body, "feed", place, [after_cross, grad, vectors, up_bias], pieces_three,
        [shape_of(OWN, MODEL), shape_of(OWN, MODEL, dtype=F32)] + [shape_of(256, FEED)] * 4
        + [shape_of(8, MODEL, dtype=F32), shape_of(1, FEED, dtype=F32)],
        [
            vmem((MODEL, FEED), BF16), vmem((FEED, MODEL), BF16), vmem((OWN, MODEL), BF16), vmem((MODEL, OWN), BF16),
            vmem((OWN, MODEL), F32), vmem((OWN, MODEL), F32), vmem((MODEL, FEED), BF16), vmem((FEED, MODEL), BF16),
            dma((4,)),
        ],
        10000000000, any_outs=(2, 3, 4, 5),
    )
    feed = scatter_pair((up_keep, up_send), (down_keep, down_send))
    self_grad, source_own, source_send, *cross_sends, sums = call(
        cross_back_body, "cross_backward", place,
        [
            target_segments, source_seg, own_source, other_source, after_self, lowered_two, queries_two, pair_two,
            mixed_two, logs_two, after_grad, vectors, sums,
        ],
        pieces_two,
        [shape_of(OWN, MODEL, dtype=F32), shape_of(HALF_SOURCE, MODEL, dtype=F32), shape_of(HALF_SOURCE, MODEL)]
        + [shape_of(256, 1024)] * 4 + [shape_of(8, MODEL, dtype=F32)],
        [
            vmem((SOURCES, MODEL), BF16), vmem((MODEL, 2560), BF16), vmem((OWN, MODEL), BF16), vmem((OWN, MODEL), F32),
            vmem((SOURCES, 2 * MODEL), BF16), vmem((MODEL, 1024), BF16), vmem((MODEL, 1024), BF16),
            vmem((SOURCES, TILE), F32), dma((4,)),
        ],
        8000000000, any_outs=(3, 4, 5, 6),
    )
    cross = scatter_pair(cross_sends[:2], cross_sends[2:])
    source_came = exchange(source_send, FLIP_Y)
    grad_source = source_own[:half] + source_came[:half].astype(F32)
    own_back, send_back, *last_sends = call(
        self_back_body, "self_backward", place,
        [target_segments, states, window, lowered, queries, pair, mixed, logs, self_grad, vectors, sums, bias_sums],
        pieces_one + pieces_two[:4],
        [shape_of(OWN, MODEL, dtype=F32), shape_of(WINDOW, MODEL)] + [shape_of(256, 1024)] * 2
        + [shape_of(256, 1152)] * 2,
        [
            vmem((MODEL, 1536), BF16), vmem((MODEL, MODEL), BF16), vmem((OWN, MODEL), BF16), vmem((OWN, MODEL), F32),
            vmem((KEYS, 2 * MODEL), BF16), vmem((MODEL, 1024), BF16), vmem((MODEL, 1152), BF16),
            vmem((KEYS, TILE), F32), dma((5,)),
        ],
        12000000000, any_outs=(2, 3, 4, 5),
    )
    last = scatter_pair(last_sends[:2], last_sends[2:])
    (grad_target,) = call(
        target_body, "target_grad", place, [own_back, exchange(send_back, FLIP_Y), states, self_grad, vectors], [],
        [shape_of(OWN, MODEL, dtype=F32)], [], 1000000,
    )
    *grads, small = call(
        finish_body, "finish", place, feed + cross + last, [],
        [
            shape_of(16, 1536, dtype=F32), shape_of(16, 512, dtype=F32), shape_of(16, 512, dtype=F32),
            shape_of(16, 1024, dtype=F32), shape_of(16, 512, dtype=F32), shape_of(16, 2048, dtype=F32),
            shape_of(64, 512, dtype=F32), shape_of(8, TILE, dtype=F32),
        ],
        [], 1000000,
    )
    project, output, query, keyval, crossout, up, down = grads
    rows = [small[i, :16] for i in range(7)]
    return (
        layer_out[None], grad_target[None], grad_source[None], project, output, query, keyval, crossout, up,
        small[7, :64], down, *rows,
    )


def specs():
    in_specs = (
        P("rows", "seq", None),
        P("rows", "seq", None),
        P("rows", None),
        P("rows", None),
        P("rows", "seq", None),
        P(("rows", "seq"), None),
        P(("rows", "seq"), None),
        P(("rows", "seq"), None),
        P(("rows", "seq"), None),
        P(("rows", "seq"), None),
        P(("rows", "seq"), None),
        P(("rows", "seq")),
        P(("rows", "seq"), None),
        P(("rows", "seq")),
        P(("rows", "seq")),
        P(("rows", "seq")),
        P(("rows", "seq")),
        P(("rows", "seq")),
        P(("rows", "seq")),
        P(("rows", "seq")),
    )
    out_specs = (
        P("rows", "seq", None),
        P("rows", "seq", None),
        P("rows", "seq", None),
        P(("rows", "seq"), None),
        P(("rows", "seq"), None),
        P(("rows", "seq"), None),
        P(("rows", "seq"), None),
        P(("rows", "seq"), None),
        P(("rows", "seq"), None),
        P(("rows", "seq")),
        P(("rows", "seq"), None),
        P(("rows", "seq")),
        P(("rows", "seq")),
        P(("rows", "seq")),
        P(("rows", "seq")),
        P(("rows", "seq")),
        P(("rows", "seq")),
        P(("rows", "seq")),
    )
    return in_specs, out_specs


def solution(mesh):
    in_specs, out_specs = specs()
    fast = mesh.shape["rows"] == 16 and mesh.shape["seq"] == 2
    return jax.shard_map(
        fast_device if fast else general_device,
        mesh=mesh, in_specs=in_specs, out_specs=out_specs, check_vma=False,
    )
```

```python
import jax
import jax.numpy as jnp
from jax import lax
from jax.experimental import pallas as pl
from jax.experimental.pallas import tpu as pltpu
from jax.sharding import PartitionSpec as P

HEADS = 8
HD = 64


def layer_norm(value, gain, shift):
    row_mean = jnp.mean(value, -1, keepdims=True)
    centered = value - row_mean
    variance = jnp.mean(centered * centered, -1, keepdims=True)
    inverse = lax.rsqrt(variance + 1e-05)
    normed = centered * inverse
    return (normed * gain + shift, normed, inverse)


def norm_back(upstream, normed, inverse, gain):
    scaled = upstream * gain
    first_mean = jnp.mean(scaled, -1, keepdims=True)
    second_mean = jnp.mean(scaled * normed, -1, keepdims=True)
    grad_input = inverse * (scaled - first_mean - normed * second_mean)
    return (grad_input, jnp.sum(upstream * normed, 0), jnp.sum(upstream, 0))


def matmul(left, right):
    return jnp.dot(left, right, preferred_element_type=jnp.float32)


def transposed(left, right):
    return lax.dot_general(
        left, right, (((0,), (0,)), ((), ())), preferred_element_type=jnp.float32
    )


def against(left, right):
    return lax.dot_general(
        left, right, (((1,), (1,)), ((), ())), preferred_element_type=jnp.float32
    )


def head_split(value):
    return value.reshape(value.shape[0], HEADS, HD)


def head_join(value):
    return value.reshape(value.shape[0], HEADS * HD)


def scores_of(queries, key_rows, query_seg, key_seg):
    raw_scores = jnp.einsum(
        "qhd,khd->hqk", queries, key_rows, preferred_element_type=jnp.float32
    ) * HD ** (-0.5)
    same_seg = (query_seg[:, None] == key_seg[None, :])[None]
    return (raw_scores, same_seg)


def block_weights(queries, key_rows, query_seg, key_seg, log_total):
    raw_scores, same_seg = scores_of(queries, key_rows, query_seg, key_seg)
    return jnp.where(same_seg, jnp.exp(raw_scores - log_total[..., None]), 0.0)


def log_totals(queries, key_blocks, seg_blocks, query_seg):

    def log_advance(carry, inputs_now):
        row_max, row_total = carry
        key_rows, key_seg = inputs_now
        raw_scores, same_seg = scores_of(queries, key_rows, query_seg, key_seg)
        masked = jnp.where(same_seg, raw_scores, -1000000000.0)
        new_max = jnp.maximum(row_max, jnp.max(masked, -1))
        shifted = jnp.where(same_seg, jnp.exp(masked - new_max[..., None]), 0.0)
        return ((new_max, row_total * jnp.exp(row_max - new_max) + jnp.sum(shifted, -1)), None)

    start = (
        jnp.full((HEADS, queries.shape[0]), -1000000000.0, jnp.float32),
        jnp.zeros((HEADS, queries.shape[0]), jnp.float32),
    )
    (row_max, row_total), unused = lax.scan(log_advance, start, (key_blocks, seg_blocks))
    return row_max + jnp.log(row_total)


def weighted_sum(queries, key_blocks, value_blocks, seg_blocks, query_seg, log_total):

    def weighted_advance(carry, inputs_now):
        key_rows, value_rows, key_seg = inputs_now
        weights = block_weights(queries, key_rows, query_seg, key_seg, log_total).astype(
            jnp.bfloat16
        )
        return (
            carry
            + jnp.einsum("hqk,khd->qhd", weights, value_rows, preferred_element_type=jnp.float32),
            None,
        )

    total, unused = lax.scan(
        weighted_advance,
        jnp.zeros(queries.shape, jnp.float32),
        (key_blocks, value_blocks, seg_blocks),
    )
    return total


def grad_dots(queries, grad_heads, key_blocks, value_blocks, seg_blocks, query_seg, log_total):

    def grad_advance(carry, inputs_now):
        key_rows, value_rows, key_seg = inputs_now
        weights = block_weights(queries, key_rows, query_seg, key_seg, log_total)
        grad_weights = jnp.einsum(
            "qhd,khd->hqk", grad_heads, value_rows, preferred_element_type=jnp.float32
        )
        return (carry + jnp.sum(weights * grad_weights, -1), None)

    start = jnp.zeros((HEADS, queries.shape[0]), jnp.float32)
    total, unused = lax.scan(grad_advance, start, (key_blocks, value_blocks, seg_blocks))
    return total


def query_grads(
    queries, grad_heads, key_blocks, value_blocks, seg_blocks, query_seg, log_total, row_dots
):
    score_scale = HD ** (-0.5)

    def query_advance(carry, inputs_now):
        key_rows, value_rows, key_seg = inputs_now
        weights = block_weights(queries, key_rows, query_seg, key_seg, log_total)
        grad_weights = jnp.einsum(
            "qhd,khd->hqk", grad_heads, value_rows, preferred_element_type=jnp.float32
        )
        grad_scores = (weights * (grad_weights - row_dots[..., None])).astype(jnp.bfloat16)
        carry = (
            carry
            + jnp.einsum("hqk,khd->qhd", grad_scores, key_rows, preferred_element_type=jnp.float32)
            * score_scale
        )
        grad_keys = (
            jnp.einsum("hqk,qhd->khd", grad_scores, queries, preferred_element_type=jnp.float32)
            * score_scale
        )
        grad_values = jnp.einsum(
            "hqk,qhd->khd",
            weights.astype(jnp.bfloat16),
            grad_heads,
            preferred_element_type=jnp.float32,
        )
        return (carry, jnp.concatenate([head_join(grad_keys), head_join(grad_values)], 1))

    return lax.scan(
        query_advance, jnp.zeros(queries.shape, jnp.float32), (key_blocks, value_blocks, seg_blocks)
    )


def general_device(
    target_states,
    source_states,
    target_segments,
    source_segments,
    output_grad,
    self_project,
    self_output,
    cross_query,
    cross_keyval,
    cross_output,
    hidden_up,
    hidden_bias,
    hidden_down,
    output_bias,
    first_gain,
    first_shift,
    second_gain,
    second_shift,
    third_gain,
    third_shift,
):
    (
        full_project,
        full_output,
        full_query,
        full_keyval,
        full_crossout,
        full_up,
        full_upbias,
        full_down,
        full_downbias,
        gain_one,
        shift_one,
        gain_two,
        shift_two,
        gain_three,
        shift_three,
    ) = (
        lax.all_gather(self_project, ("rows", "seq"), axis=0, tiled=True),
        lax.all_gather(self_output, ("rows", "seq"), axis=0, tiled=True),
        lax.all_gather(cross_query, ("rows", "seq"), axis=0, tiled=True),
        lax.all_gather(cross_keyval, ("rows", "seq"), axis=0, tiled=True),
        lax.all_gather(cross_output, ("rows", "seq"), axis=0, tiled=True),
        lax.all_gather(hidden_up, ("rows", "seq"), axis=0, tiled=True),
        lax.all_gather(hidden_bias, ("rows", "seq"), axis=0, tiled=True),
        lax.all_gather(hidden_down, ("rows", "seq"), axis=0, tiled=True),
        lax.all_gather(output_bias, ("rows", "seq"), axis=0, tiled=True),
        lax.all_gather(first_gain, ("rows", "seq"), axis=0, tiled=True),
        lax.all_gather(first_shift, ("rows", "seq"), axis=0, tiled=True),
        lax.all_gather(second_gain, ("rows", "seq"), axis=0, tiled=True),
        lax.all_gather(second_shift, ("rows", "seq"), axis=0, tiled=True),
        lax.all_gather(third_gain, ("rows", "seq"), axis=0, tiled=True),
        lax.all_gather(third_shift, ("rows", "seq"), axis=0, tiled=True),
    )
    gain_one = gain_one.astype(jnp.float32)
    gain_two = gain_two.astype(jnp.float32)
    gain_three = gain_three.astype(jnp.float32)
    score_scale = HD ** (-0.5)
    states = target_states[0].astype(jnp.float32)
    local_rows = states.shape[0]
    model_width = states.shape[1]
    seq_count = lax.axis_size("seq")
    row_segments = target_segments[0]
    seq_length = row_segments.shape[0]
    own_segments = lax.dynamic_slice_in_dim(
        row_segments, lax.axis_index("seq") * local_rows, local_rows
    )
    block_rows = max(1, min(seq_count, 512 // local_rows)) * local_rows
    block_count = seq_length // block_rows
    seg_blocks = row_segments.reshape(block_count, block_rows)
    normed_value, normed_one, inverse_one = layer_norm(
        states, gain_one, shift_one.astype(jnp.float32)
    )
    lowered_one = normed_value.astype(jnp.bfloat16)
    projected = matmul(lowered_one, full_project).astype(jnp.bfloat16)
    query_flat = projected[:, :model_width]
    key_local = projected[:, model_width : 2 * model_width]
    value_local = projected[:, 2 * model_width :]
    queries = head_split(query_flat)
    key_all, value_all = (
        lax.all_gather(key_local, "seq", axis=0, tiled=True),
        lax.all_gather(value_local, "seq", axis=0, tiled=True),
    )
    key_blocks = key_all.reshape(block_count, block_rows, HEADS, HD)
    value_blocks = value_all.reshape(block_count, block_rows, HEADS, HD)
    log_total = log_totals(queries, key_blocks, seg_blocks, own_segments)
    self_mixed = head_join(
        weighted_sum(queries, key_blocks, value_blocks, seg_blocks, own_segments, log_total)
    ).astype(jnp.bfloat16)
    after_self = states + matmul(self_mixed, full_output)
    normed_value, normed_two, inverse_two = layer_norm(
        after_self, gain_two, shift_two.astype(jnp.float32)
    )
    lowered_two = normed_value.astype(jnp.bfloat16)
    cross_asked = matmul(lowered_two, full_query).astype(jnp.bfloat16)
    source_low = source_states[0]
    source_all = lax.all_gather(source_low, "seq", axis=0, tiled=True)
    key_value = matmul(source_all, full_keyval).astype(jnp.bfloat16)
    cross_key_heads = head_split(key_value[:, :model_width])
    cross_value_heads = head_split(key_value[:, model_width:])
    asked_heads = head_split(cross_asked)
    raw_scores, same_seg = scores_of(asked_heads, cross_key_heads, own_segments, source_segments[0])
    cross_probs = jax.nn.softmax(jnp.where(same_seg, raw_scores, -1000000000.0), axis=-1)
    cross_mixed = head_join(
        jnp.einsum(
            "hqk,khd->qhd",
            cross_probs.astype(jnp.bfloat16),
            cross_value_heads,
            preferred_element_type=jnp.float32,
        )
    ).astype(jnp.bfloat16)
    after_cross = after_self + matmul(cross_mixed, full_crossout)
    normed_value, normed_three, inverse_three = layer_norm(
        after_cross, gain_three, shift_three.astype(jnp.float32)
    )
    lowered_three = normed_value.astype(jnp.bfloat16)
    hidden = matmul(lowered_three, full_up) + full_upbias.astype(jnp.float32)
    activated = jax.nn.gelu(hidden).astype(jnp.bfloat16)
    layer_out = after_cross + matmul(activated, full_down) + full_downbias.astype(jnp.float32)
    grad_low = output_grad[0]
    out_grad = grad_low.astype(jnp.float32)
    grad_down = transposed(activated, grad_low)
    grad_downbias = jnp.sum(out_grad, 0)
    grad_act = against(grad_low, full_down)
    grad_hidden = jax.vjp(jax.nn.gelu, hidden)[1](grad_act)[0].astype(jnp.bfloat16)
    grad_upbias = jnp.sum(grad_hidden.astype(jnp.float32), 0)
    grad_up = transposed(lowered_three, grad_hidden)
    dx_three, grad_gain_three, grad_shift_three = norm_back(
        against(grad_hidden, full_up), normed_three, inverse_three, gain_three
    )
    grad_cross = out_grad + dx_three
    grad_cross_low = grad_cross.astype(jnp.bfloat16)
    grad_crossout = transposed(cross_mixed, grad_cross_low)
    grad_cross_heads = head_split(against(grad_cross_low, full_crossout).astype(jnp.bfloat16))
    grad_weights = jnp.einsum(
        "qhd,khd->hqk", grad_cross_heads, cross_value_heads, preferred_element_type=jnp.float32
    )
    grad_scores = (
        cross_probs * (grad_weights - jnp.sum(cross_probs * grad_weights, -1, keepdims=True))
    ).astype(jnp.bfloat16)
    grad_asked = head_join(
        jnp.einsum("hqk,khd->qhd", grad_scores, cross_key_heads, preferred_element_type=jnp.float32)
        * score_scale
    ).astype(jnp.bfloat16)
    grad_cross_keys = (
        jnp.einsum("hqk,qhd->khd", grad_scores, asked_heads, preferred_element_type=jnp.float32)
        * score_scale
    )
    grad_cross_values = jnp.einsum(
        "hqk,qhd->khd",
        cross_probs.astype(jnp.bfloat16),
        grad_cross_heads,
        preferred_element_type=jnp.float32,
    )
    pair_terms = jnp.concatenate([head_join(grad_cross_keys), head_join(grad_cross_values)], 1)
    pair_grad = lax.psum_scatter(
        pair_terms.astype(jnp.bfloat16), "seq", scatter_dimension=0, tiled=True
    )
    grad_keyval = transposed(source_low, pair_grad)
    grad_source = against(pair_grad, full_keyval)
    grad_query = transposed(lowered_two, grad_asked)
    dx_two, grad_gain_two, grad_shift_two = norm_back(
        against(grad_asked, full_query), normed_two, inverse_two, gain_two
    )
    grad_self = grad_cross + dx_two
    grad_self_low = grad_self.astype(jnp.bfloat16)
    grad_output = transposed(self_mixed, grad_self_low)
    grad_mixed = against(grad_self_low, full_output).astype(jnp.bfloat16)
    grad_heads = head_split(grad_mixed)
    row_dots = grad_dots(
        queries, grad_heads, key_blocks, value_blocks, seg_blocks, own_segments, log_total
    )
    grad_queries, key_terms = query_grads(
        queries, grad_heads, key_blocks, value_blocks, seg_blocks, own_segments, log_total, row_dots
    )
    summed = lax.psum_scatter(
        key_terms.reshape(seq_length, 2 * model_width).astype(jnp.bfloat16),
        "seq",
        scatter_dimension=0,
        tiled=True,
    )
    grad_projected = jnp.concatenate([head_join(grad_queries).astype(jnp.bfloat16), summed], 1)
    grad_project = transposed(lowered_one, grad_projected)
    dx_one, grad_gain_one, grad_shift_one = norm_back(
        against(grad_projected, full_project), normed_one, inverse_one, gain_one
    )
    grad_target = grad_self + dx_one
    shards = (
        lax.psum_scatter(grad_project, ("rows", "seq"), scatter_dimension=0, tiled=True),
        lax.psum_scatter(grad_output, ("rows", "seq"), scatter_dimension=0, tiled=True),
        lax.psum_scatter(grad_query, ("rows", "seq"), scatter_dimension=0, tiled=True),
        lax.psum_scatter(grad_keyval, ("rows", "seq"), scatter_dimension=0, tiled=True),
        lax.psum_scatter(grad_crossout, ("rows", "seq"), scatter_dimension=0, tiled=True),
        lax.psum_scatter(grad_up, ("rows", "seq"), scatter_dimension=0, tiled=True),
        lax.psum_scatter(grad_upbias, ("rows", "seq"), scatter_dimension=0, tiled=True),
        lax.psum_scatter(grad_down, ("rows", "seq"), scatter_dimension=0, tiled=True),
        lax.psum_scatter(grad_downbias, ("rows", "seq"), scatter_dimension=0, tiled=True),
        lax.psum_scatter(grad_gain_one, ("rows", "seq"), scatter_dimension=0, tiled=True),
        lax.psum_scatter(grad_shift_one, ("rows", "seq"), scatter_dimension=0, tiled=True),
        lax.psum_scatter(grad_gain_two, ("rows", "seq"), scatter_dimension=0, tiled=True),
        lax.psum_scatter(grad_shift_two, ("rows", "seq"), scatter_dimension=0, tiled=True),
        lax.psum_scatter(grad_gain_three, ("rows", "seq"), scatter_dimension=0, tiled=True),
        lax.psum_scatter(grad_shift_three, ("rows", "seq"), scatter_dimension=0, tiled=True),
    )
    return (layer_out.astype(jnp.bfloat16)[None], grad_target[None], grad_source[None]) + tuple(
        shards
    )


F32, BF16 = jnp.float32, jnp.bfloat16
BLOCK = 16
AXES = ("rows", "seq")
FLIP_Y, FLIP_CORE, FLIP_X, FLIP_Z = 1, 2, 4, 8
MODEL, FEED, OWN, WINDOW, HALF_SOURCE = 512, 2048, 512, 256, 192
KEYS, SOURCES = OWN + WINDOW, 2 * HALF_SOURCE
TILE = 128
MASKED = -1000000000.0
SCALE = HD ** (-0.5)


def exchange(value, flip):
    return lax.ppermute(value, AXES, [(device, device ^ flip) for device in range(32)])


def exchange_side(value, step):
    flips = (FLIP_X, FLIP_Y) if step == 0 else (FLIP_Y, FLIP_X)
    return lax.ppermute(value, AXES, [(device, device ^ flips[device >> 1 & 1]) for device in range(32)])


def tied(values, *others):
    return lax.optimization_barrier((values, others))[0]


def along_z(block):
    return [exchange(block, FLIP_Z * i) for i in Z_ORDER]


Z_ORDER = (1, 2, 3)


def join(*parts):
    return jnp.concatenate(parts, 0)


def both_cores(halves):
    return halves + [exchange(half, FLIP_CORE) for half in halves]


def add_halves(kept, came):
    half = kept.shape[0] // 2
    return kept[half:] + came[half:], kept[:half] + came[:half]


def z_blocks(both):
    blocks = [both[BLOCK * i : BLOCK * (i + 1)] for i in range(4)]
    return [blocks[0]] + [exchange(block, FLIP_Z * i) for i, block in zip(Z_ORDER, blocks[1:])]


def block_places(me):
    out = []
    for other in (0, 1):
        core = (me >> 1 & 1) ^ other
        first, second = FLIP_X - 3 * core, FLIP_Y + 3 * core
        for b in (0, 1):
            for a in (0, 1):
                for i, z in enumerate((0,) + Z_ORDER):
                    owner = me ^ (other * FLIP_CORE + b * second + a * first + z * FLIP_Z)
                    out.append((other * 2 + b, (a * 4 + i) * BLOCK, owner))
    return out


def nn(left, right):
    return jnp.dot(left, right, preferred_element_type=F32)


def load_blocks(me, pieces, columns, target, target_columns, semaphore):
    for piece, row, owner in block_places(me):
        pltpu.make_async_copy(
            pieces[piece].at[pl.ds(row, BLOCK), columns],
            target.at[pl.ds(pl.multiple_of(owner * BLOCK, BLOCK), BLOCK), target_columns],
            semaphore,
        ).start()


def wait_all(target, semaphore):
    pltpu.make_async_copy(target, target, semaphore).wait()


def store_blocks(me, source, columns, targets, target_columns, semaphore):
    for piece, row, owner in block_places(me):
        pltpu.make_async_copy(
            source.at[pl.ds(pl.multiple_of(owner * BLOCK, BLOCK), BLOCK), columns],
            targets[piece // 2].at[pl.ds((piece % 2) * 128 + row, BLOCK), target_columns],
            semaphore,
        ).start()


def normed_rows(value):
    centered = value - jnp.mean(value, -1, keepdims=True)
    inverse = lax.rsqrt(jnp.mean(centered * centered, -1, keepdims=True) + 1e-05)
    return centered * inverse, inverse


def norm_back_rows(upstream, normed, inverse, gain):
    scaled = upstream * gain
    first_mean = jnp.mean(scaled, -1, keepdims=True)
    second_mean = jnp.mean(scaled * normed, -1, keepdims=True)
    return inverse * (scaled - first_mean - normed * second_mean)


def column_sum(value):
    return jnp.sum(value, 0, keepdims=True)


def own_segments_of(index, segments):
    return jnp.where(index == 0, segments[:, :OWN], segments[:, OWN:]).astype(F32)


def key_segments_of(index, segments):
    near = jnp.where(index == 0, segments[:, OWN:KEYS], segments[:, OWN - WINDOW : OWN])
    return jnp.concatenate([own_segments_of(index, segments), near.astype(F32)], 1)


def spread(row):
    return jnp.broadcast_to(row, (TILE, row.shape[1])).T


def lane_half(shape, half):
    lanes = lax.broadcasted_iota(jnp.int32, shape, 1)
    return (lanes < HD) if half == 0 else (lanes >= HD)


def attend(queries, keys, values, mixed, log_rows, query_seg, key_row):
    (key_ref, key_at), (value_ref, value_at) = keys, values
    count = key_row.shape[1]

    def block(index, unused):
        rows = pl.ds(pl.multiple_of(index * TILE, TILE), TILE)
        same = jnp.concatenate([query_seg[rows, :]] * (count // TILE), 1) == key_row
        bias = jnp.where(same, 0.0, MASKED)
        lanes = lax.broadcasted_iota(jnp.int32, (TILE, TILE), 1)
        logs = jnp.zeros((TILE, TILE), F32)
        for pair in range(HEADS // 2):
            at = pair * TILE
            query = queries[rows, at : at + TILE]
            key = key_ref[:, key_at + at : key_at + at + TILE]
            value = value_ref[:, value_at + at : value_at + at + TILE]
            halves = []
            for half in range(2):
                masked = jnp.where(lane_half(query.shape, half), query, jnp.zeros_like(query))
                scores = against(masked, key) + bias
                top = jnp.max(scores, -1, keepdims=True)
                weights = jnp.exp(scores - top)
                total = jnp.sum(weights, -1, keepdims=True)
                halves.append(nn(weights.astype(BF16), value) * (1.0 / total))
                logs = jnp.where(lanes == pair * 2 + half, top + jnp.log(total), logs)
            mixed[rows, at : at + TILE] = jnp.where(
                lane_half(halves[0].shape, 0), halves[0], halves[1]
            ).astype(BF16)
        log_rows[:, rows] = logs.T[:HEADS]
        return unused

    lax.fori_loop(0, OWN // TILE, block, 0)


def head_dots(upstream, mixed):
    head = lax.broadcasted_iota(jnp.int32, (HEADS, MODEL), 1) // HD
    ones = (head == lax.broadcasted_iota(jnp.int32, (HEADS, MODEL), 0)).astype(F32)
    return lax.dot_general(
        ones, upstream.astype(F32) * mixed.astype(F32), (((1,), (1,)), ((), ())),
        precision=lax.Precision.HIGHEST, preferred_element_type=F32,
    )


def attend_back(
    queries, upstream, keys, values, log_rows, dot_rows, query_row, key_seg, query_grad, pair_grad, pairs
):
    (key_ref, key_at), (value_ref, value_at) = keys, values
    query_grad[...] = jnp.zeros_like(query_grad)

    def block(index, unused):
        rows = pl.ds(pl.multiple_of(index * TILE, TILE), TILE)
        same = jnp.concatenate([key_seg[rows, :]] * (OWN // TILE), 1) == query_row
        bias = jnp.where(same, 0.0, MASKED)
        for pair in pairs:
            at, to = pair * TILE, (pair - pairs[0]) * TILE
            query = queries[:, at : at + TILE]
            grad = upstream[:, at : at + TILE]
            key = key_ref[rows, key_at + at : key_at + at + TILE]
            value = value_ref[rows, value_at + at : value_at + at + TILE]
            total = jnp.zeros((OWN, TILE), F32)
            key_parts, value_parts = [], []
            for half in range(2):
                head = pair * 2 + half
                keep = lane_half(key.shape, half)
                one_key = jnp.where(keep, key, jnp.zeros_like(key))
                one_value = jnp.where(keep, value, jnp.zeros_like(value))
                weights = jnp.exp(against(one_key, query) + (bias - log_rows[head : head + 1, :]))
                grads = against(one_value, grad) - dot_rows[head : head + 1, :]
                score_grad = (weights * grads).astype(BF16)
                value_parts.append(nn(weights.astype(BF16), grad))
                key_parts.append(nn(score_grad, query))
                total = total + transposed(score_grad, one_key)
            query_grad[:, to : to + TILE] += total
            keep = lane_half(key_parts[0].shape, 0)
            pair_grad[rows, to : to + TILE] = jnp.where(keep, *key_parts).astype(BF16)
            to = to + len(pairs) * TILE
            pair_grad[rows, to : to + TILE] = jnp.where(keep, *value_parts).astype(BF16)
        return unused

    lax.fori_loop(0, key_seg.shape[0] // TILE, block, 0)


def pack_body(
    place, vectors, project, output, query, keyval, crossout, up, down, states, source,
    one, two, three, near, own_source, block, semaphores
):
    me, side = place[0], place[1]
    copies = [
        (project, one.at[:, :1536]),
        (output, two.at[:, :512]),
        (query, two.at[:, 512:1024]),
        (keyval, two.at[:, 1024:2048]),
        (crossout, two.at[:, 2048:]),
        (up, three.at[:, :FEED]),
    ] + [
        (down.at[part * BLOCK : (part + 1) * BLOCK, :], three.at[:, FEED + part * 512 : FEED + (part + 1) * 512])
        for part in range(4)
    ] + [
        (states.at[pl.ds(pl.multiple_of((1 - side) * WINDOW, WINDOW), WINDOW), :], near)
    ]
    copies = [pltpu.make_async_copy(*copy, semaphores.at[i]) for i, copy in enumerate(copies)]
    for copy in copies:
        copy.start()
    gap = jnp.zeros((HALF_SOURCE - source.shape[0], MODEL), F32)
    own_source[...] = jnp.concatenate([source[...].astype(F32), gap], 0).astype(BF16)
    values = jnp.broadcast_to(vectors[...].astype(F32), (8, 256))
    lanes = lax.broadcasted_iota(jnp.int32, (8, TILE), 1)
    rows = lax.broadcasted_iota(jnp.int32, (8, TILE), 0)
    packed = jnp.zeros((8, TILE), F32)
    spot, wide = (me & 7) * 16, (me & 1) * 64
    for row in range(7):
        moved = pltpu.roll(values, spot + 256 - 16 * row, 1)[:, :TILE]
        inside = jnp.logical_and(lanes >= spot, lanes < spot + 16)
        packed = jnp.where(jnp.logical_and(rows == row, inside), moved, packed)
    moved = pltpu.roll(values, wide + 256 - 112, 1)[:, :TILE]
    inside = jnp.logical_and(lanes >= wide, lanes < wide + 64)
    packed = jnp.where(jnp.logical_and(rows == 7, inside), moved, packed)
    block[...] = jnp.concatenate([packed, jnp.zeros((8, TILE), F32)], 0).astype(BF16)
    last = pltpu.make_async_copy(block, one.at[:, 1536:], semaphores.at[len(copies)])
    last.start()
    for copy in copies + [last]:
        copy.wait()


def self_body(place, states, window, *refs):
    pieces, refs = refs[:4], refs[4:]
    queries, pair, lowered, vectors, up_bias, weight, packed, sems = refs
    me = place[0]
    load_blocks(me, pieces, slice(1536, 1664), packed, slice(0, 128), sems.at[0])
    load_blocks(me, pieces, slice(0, 1536), weight, slice(0, 1536), sems.at[1])
    wait_all(packed, sems.at[0])
    for tile in range(4):
        total = jnp.zeros((8, TILE), F32)
        for i in range(8):
            total = total + packed[(tile * 8 + i) * BLOCK : (tile * 8 + i + 1) * BLOCK, :].astype(F32)[:8]
        vectors[:, tile * TILE : (tile + 1) * TILE] = total
    for tile in range(16):
        total = (
            packed[2 * tile * BLOCK : (2 * tile + 1) * BLOCK, :].astype(F32)
            + packed[(2 * tile + 1) * BLOCK : (2 * tile + 2) * BLOCK, :].astype(F32)
        )
        up_bias[:, tile * TILE : (tile + 1) * TILE] = total[7:8]
    gain, shift = vectors[1:2, :], vectors[2:3, :]
    for i in range(KEYS // TILE):
        rows = slice(i * TILE, (i + 1) * TILE)
        value = states[rows, :] if i < 4 else window[(i - 4) * TILE : (i - 3) * TILE, :]
        lowered[rows, :] = (normed_rows(value.astype(F32))[0] * gain + shift).astype(BF16)
    wait_all(weight, sems.at[1])
    for i in range(KEYS // 256):
        rows = slice(i * 256, (i + 1) * 256)
        if i < 2:
            queries[rows, :] = (nn(lowered[rows, :], weight[:, :512]) .astype(BF16) * SCALE).astype(BF16)
        pair[rows, :] = nn(lowered[rows, :], weight[:, 512:]).astype(BF16)


def self_mix_body(place, segments, queries, pair, mixed, log_rows, query_seg):
    query_seg[...] = spread(own_segments_of(place[1], segments[...]))
    key_row = key_segments_of(place[1], segments[...])
    attend(queries, (pair, 0), (pair, MODEL), mixed, log_rows, query_seg, key_row)


def cross_body(place, states, own_source, other_source, self_mixed, vectors, *refs):
    pieces, refs = refs[:4], refs[4:]
    after_self, lowered, queries, pair, weight, source, sems = refs
    me, side = place[0], place[1]
    load_blocks(me, pieces, slice(0, 2560), weight, slice(0, 2560), sems.at[0])
    source[:HALF_SOURCE, :] = jnp.where(side == 0, own_source[...], other_source[...])
    source[HALF_SOURCE:, :] = jnp.where(side == 0, other_source[...], own_source[...])
    gain, shift = vectors[3:4, :], vectors[4:5, :]
    wait_all(weight, sems.at[0])
    pair[...] = nn(source[...], weight[:, 1024:2048]).astype(BF16)
    for i in range(2):
        rows = slice(i * 256, (i + 1) * 256)
        value = states[rows, :].astype(F32) + nn(self_mixed[rows, :], weight[:, :512])
        after_self[rows, :] = value
        lowered[rows, :] = (normed_rows(value)[0] * gain + shift).astype(BF16)
        queries[rows, :] = (nn(lowered[rows, :], weight[:, 512:1024]).astype(BF16) * SCALE).astype(BF16)


def cross_mix_body(
    place, segments, source_segments, queries, pair, after_self, weight, mixed, log_rows, after_cross, query_seg
):
    query_seg[...] = spread(own_segments_of(place[1], segments[...]))
    attend(queries, (pair, 0), (pair, MODEL), mixed, log_rows, query_seg, source_segments[...].astype(F32))
    for i in range(2):
        rows = slice(i * 256, (i + 1) * 256)
        after_cross[rows, :] = after_self[rows, :] + nn(mixed[rows, :], weight[:, 2048:])


CHUNK = 512


def feed_body(place, after_cross, output_grad, vectors, up_bias, *refs):
    pieces, refs = refs[:4], refs[4:]
    (
        layer_out, after_grad, kept, sent, sums, bias_sums,
        up, down, lowered, flipped, total, back, up_grad, down_grad, sems,
    ) = refs
    me = place[0]
    load_blocks(me, pieces, slice(0, FEED), up, slice(0, FEED), sems.at[0])
    for part in range(4):
        for piece, row, owner in block_places(me):
            spot = pl.multiple_of(owner * 64 + part * BLOCK, BLOCK)
            pltpu.make_async_copy(
                pieces[piece].at[pl.ds(row, BLOCK), slice(FEED + part * 512, FEED + (part + 1) * 512)],
                down.at[pl.ds(spot, BLOCK), :],
                sems.at[1],
            ).start()
    gain, shift = vectors[5:6, :], vectors[6:7, :]
    for i in range(4):
        rows = slice(i * TILE, (i + 1) * TILE)
        low = (normed_rows(after_cross[rows, :])[0] * gain + shift).astype(BF16)
        lowered[rows, :] = low
    flipped[...] = lowered[...].T
    total[...] = jnp.zeros_like(total)
    back[...] = jnp.zeros_like(back)
    wait_all(up, sems.at[0])
    wait_all(down, sems.at[1])

    def chunk(index, unused):
        at = pl.ds(pl.multiple_of(index * CHUNK, CHUNK), CHUNK)
        hidden = nn(lowered[...], up[:, at]) + up_bias[:, at]
        square = hidden * hidden
        inner = 0.7978845608028654 * hidden * (1.0 + 0.044715 * square)
        curve = jnp.tanh(inner)
        half = 0.5 * (1.0 + curve)
        activated = (hidden * half).astype(BF16)
        slope = half + (0.5 * 0.7978845608028654) * hidden * (1.0 - curve * curve) * (
            1.0 + (3 * 0.044715) * square
        )
        total[...] += nn(activated, down[at, :])
        down_grad[at, :] = transposed(activated, output_grad[...]).astype(BF16)
        grad_hidden = (against(output_grad[...], down[at, :]) * slope).astype(BF16)
        bias_sums[:, at] = column_sum(grad_hidden.astype(F32))
        up_grad[:, at] = nn(flipped[...], grad_hidden).astype(BF16)
        back[...] += against(grad_hidden, up[:, at])
        return unused

    lax.fori_loop(0, FEED // CHUNK, chunk, 0)
    store_blocks(me, up_grad, slice(0, FEED), (kept, sent), slice(0, FEED), sems.at[2])
    for part in range(4):
        for piece, row, owner in block_places(me):
            spot = pl.multiple_of(owner * 64 + part * BLOCK, BLOCK)
            pltpu.make_async_copy(
                down_grad.at[pl.ds(spot, BLOCK), :],
                (kept, sent)[piece // 2].at[
                    pl.ds((piece % 2) * 128 + row, BLOCK), slice(FEED + part * 512, FEED + (part + 1) * 512)
                ],
                sems.at[3],
            ).start()
    gain_sum, shift_sum, bias_sum = (jnp.zeros((1, MODEL), F32) for _ in range(3))
    for i in range(4):
        rows = slice(i * TILE, (i + 1) * TILE)
        value, grad = after_cross[rows, :], output_grad[rows, :].astype(F32)
        layer_out[rows, :] = (value + total[rows, :] + vectors[0:1, :]).astype(BF16)
        normed, inverse = normed_rows(value)
        upstream = back[rows, :]
        after_grad[rows, :] = grad + norm_back_rows(upstream, normed, inverse, gain)
        gain_sum, shift_sum = gain_sum + column_sum(upstream * normed), shift_sum + column_sum(upstream)
        bias_sum = bias_sum + column_sum(grad)
    zero = jnp.zeros((1, MODEL), F32)
    sums[...] = jnp.concatenate([bias_sum, zero, zero, zero, zero, gain_sum, shift_sum, zero], 0)
    wait_all(up_grad, sems.at[2])
    wait_all(down_grad, sems.at[3])


def cross_back_body(
    place, segments, source_segments, own_source, other_source, queries, pair, mixed, log_rows, after_grad, weight,
    asked, source_own, source_send, grads, upstream, query_grad, pair_grad, source, key_seg,
):
    side = place[1]
    key_seg[...] = spread(source_segments[...].astype(F32))
    query_row = own_segments_of(side, segments[...])
    source[:HALF_SOURCE, :] = jnp.where(side == 0, own_source[...], other_source[...])
    source[HALF_SOURCE:, :] = jnp.where(side == 0, other_source[...], own_source[...])
    grad_low = after_grad[...].astype(BF16)
    upstream[...] = against(grad_low, weight[:, 2048:]).astype(BF16)
    dot_rows = head_dots(upstream[...], mixed[...])
    grads[:, :512] = transposed(mixed[...], grad_low).astype(BF16)
    attend_back(
        queries, upstream, (pair, 0), (pair, MODEL), log_rows, dot_rows, query_row, key_seg,
        query_grad, pair_grad, (0, 1, 2, 3),
    )
    asked[...] = (query_grad[...] * SCALE).astype(BF16)
    grads[:, 512:] = transposed(source[...], pair_grad[...]).astype(BF16)
    back = against(pair_grad[...], weight[:, 1024:2048])
    first, second = back[:HALF_SOURCE], back[HALF_SOURCE:]
    source_own[...] = jnp.where(side == 0, first, second)
    source_send[...] = jnp.where(side == 0, second, first).astype(BF16)


def cross_weight_body(
    place, after_self, lowered, self_mixed, after_grad, asked, vectors, sums, weight, some_grads, *refs
):
    self_grad, upstream, dot_rows, kept, sent, new_sums, grads, sems = refs
    me = place[0]
    store_blocks(me, some_grads, slice(0, 1536), (kept, sent), slice(0, 1536), sems.at[0])
    gain = vectors[3:4, :]
    gain_sum, shift_sum = jnp.zeros((1, MODEL), F32), jnp.zeros((1, MODEL), F32)
    for i in range(2):
        rows = slice(i * 256, (i + 1) * 256)
        normed, inverse = normed_rows(after_self[rows, :])
        up = against(asked[rows, :], weight[:, 512:1024])
        self_grad[rows, :] = after_grad[rows, :] + norm_back_rows(up, normed, inverse, gain)
        gain_sum, shift_sum = gain_sum + column_sum(up * normed), shift_sum + column_sum(up)
    grads[:, :512] = transposed(lowered[...], asked[...]).astype(BF16)
    grad_low = self_grad[...].astype(BF16)
    grads[:, 512:] = transposed(self_mixed[...], grad_low).astype(BF16)
    store_blocks(me, grads, slice(0, 1024), (kept, sent), slice(1536, 2560), sems.at[1])
    upstream[...] = against(grad_low, weight[:, :512]).astype(BF16)
    dot_rows[...] = head_dots(upstream[...], self_mixed[...])
    zero = jnp.zeros((1, MODEL), F32)
    new_sums[...] = sums[...] + jnp.concatenate(
        [zero, zero, zero, gain_sum, shift_sum, zero, zero, zero], 0
    )
    wait_all(some_grads, sems.at[0])
    wait_all(grads, sems.at[1])


def project_grads(lowered, asked, pair_grad, weight, at, grads, back):
    grads[:, :256] = transposed(lowered[:OWN, :], asked).astype(BF16)
    grads[:, 256:512] = transposed(lowered[...], pair_grad[:, :256]).astype(BF16)
    grads[:, 512:768] = transposed(lowered[...], pair_grad[:, 256:]).astype(BF16)
    for i in range(3):
        rows = slice(i * 256, (i + 1) * 256)
        part = against(pair_grad[rows, :256], weight[:, 512 + at : 768 + at]) + against(
            pair_grad[rows, 256:], weight[:, 1024 + at : 1280 + at]
        )
        if i < 2:
            part = part + against(asked[rows, :], weight[:, at : at + 256])
        back(rows, part)


def self_back_body(
    place, segments, lowered, queries, pair, log_rows, upstream, dot_rows, weight,
    part_back, left_keep, left_send, query_grad, pair_grad, left_grad, key_seg, sems,
):
    key_seg[...] = spread(key_segments_of(place[1], segments[...]))
    query_row = own_segments_of(place[1], segments[...])
    attend_back(
        queries, upstream, (pair, 0), (pair, MODEL), log_rows, dot_rows, query_row, key_seg,
        query_grad, pair_grad, (0, 1),
    )

    def keep(rows, part):
        part_back[rows, :] = part

    project_grads(lowered, (query_grad[...] * SCALE).astype(BF16), pair_grad, weight, 0, left_grad, keep)
    store_blocks(place[0], left_grad, slice(0, 768), (left_keep, left_send), slice(0, 768), sems.at[0])
    wait_all(left_grad, sems.at[0])


def self_last_body(
    place, segments, states, window, lowered, queries, pair, log_rows, upstream, dot_rows, weight, part_back,
    sums, bias_sums, *refs
):
    own_back, send_back, right_keep, right_send, query_grad, pair_grad, right_grad, key_seg, sems = refs
    key_seg[...] = spread(key_segments_of(place[1], segments[...]))
    query_row = own_segments_of(place[1], segments[...])
    attend_back(
        queries, upstream, (pair, 0), (pair, MODEL), log_rows, dot_rows, query_row, key_seg,
        query_grad, pair_grad, (2, 3),
    )
    gain_sum, shift_sum = [jnp.zeros((1, MODEL), F32)], [jnp.zeros((1, MODEL), F32)]

    def finish(rows, part):
        part = part + part_back[rows, :]
        if rows.start < OWN:
            own_back[rows, :] = part
            value = states[rows, :]
        else:
            send_back[...] = part.astype(BF16)
            value = window[...]
        normed = normed_rows(value.astype(F32))[0]
        gain_sum[0], shift_sum[0] = gain_sum[0] + column_sum(part * normed), shift_sum[0] + column_sum(part)

    project_grads(lowered, (query_grad[...] * SCALE).astype(BF16), pair_grad, weight, 256, right_grad, finish)
    zero = jnp.zeros((1, MODEL), F32)
    sums = sums[...] + jnp.concatenate([zero, gain_sum[0], shift_sum[0], zero, zero, zero, zero, zero], 0)
    last = lax.broadcasted_iota(jnp.int32, (8, TILE), 0) == 7
    for device in range(32):
        tile, wide = device // 8 * TILE, device // 2 * TILE
        value = jnp.where(last, bias_sums[:, wide : wide + TILE], sums[:, tile : tile + TILE])
        high = value.astype(BF16).astype(F32)
        right_grad[device * BLOCK : (device + 1) * BLOCK, 768:] = jnp.concatenate(
            [high, value - high], 0
        ).astype(BF16)
    store_blocks(place[0], right_grad, slice(0, 896), (right_keep, right_send), slice(0, 896), sems.at[0])
    wait_all(right_grad, sems.at[0])


def target_body(place, back, came, states, self_grad, vectors, out):
    gain = vectors[1:2, :]
    for i in range(4):
        rows = slice(i * TILE, (i + 1) * TILE)
        here = (i < 2) == (place[1] == 1)
        extra = came[(i % 2) * TILE : (i % 2 + 1) * TILE, :].astype(F32)
        upstream = back[rows, :] + jnp.where(here, extra, 0.0)
        normed, inverse = normed_rows(states[rows, :].astype(F32))
        out[rows, :] = self_grad[rows, :] + norm_back_rows(upstream, normed, inverse, gain)


def finish_body(place, *refs):
    feed, cross, last, outs = refs[:4], refs[4:8], refs[8:12], refs[12:]
    project, output, query, keyval, crossout, up, down, *small = outs
    me = place[0]

    def total(parts, begin, end):
        value = parts[0][:, begin:end].astype(F32)
        for part in parts[1:]:
            value = value + part[:, begin:end].astype(F32)
        return value

    up[...] = total(feed, 0, FEED)
    for part in range(4):
        down[part * BLOCK : (part + 1) * BLOCK, :] = total(feed, FEED + part * 512, FEED + (part + 1) * 512)
    crossout[...] = total(cross, 0, 512)
    keyval[...] = total(cross, 512, 1536)
    query[...] = total(cross, 1536, 2048)
    output[...] = total(cross, 2048, 2560)
    for part in range(6):
        to = part // 2 * 512 + part % 2 * 256
        at = part // 2 * 256 + part % 2 * 768
        project[:, to : to + 256] = total(last, at, at + 256)
    value = total(last, 1536, 1664)
    value = value[:8] + value[8:]
    narrow = pltpu.roll(value, (TILE - (me & 7) * 16) & 127, 1)
    wide = pltpu.roll(value, (TILE - (me & 1) * 64) & 127, 1)
    for row in range(7):
        small[row][...] = narrow[row : row + 1, :16]
    small[7][...] = wide[7:8, :64]


def shape_of(*shape, dtype=BF16):
    return jax.ShapeDtypeStruct(shape, dtype)


VMEM_SPEC = pl.BlockSpec(memory_space=pltpu.VMEM)
ANY_SPEC = pl.BlockSpec(memory_space=pl.ANY)
HBM_SPEC = pl.BlockSpec(memory_space=pltpu.HBM)
SMEM_SPEC = pl.BlockSpec(memory_space=pltpu.SMEM)


def call(body, name, place, inputs, pieces, outs, scratch, flops, any_outs=(), any_ins=(), vmem=40):
    return pl.pallas_call(
        body,
        name=name,
        out_shape=outs,
        in_specs=[SMEM_SPEC]
        + [HBM_SPEC if i in any_ins else VMEM_SPEC for i in range(len(inputs))]
        + [ANY_SPEC] * len(pieces),
        out_specs=[ANY_SPEC if i in any_outs else VMEM_SPEC for i in range(len(outs))],
        scratch_shapes=scratch,
        compiler_params=pltpu.CompilerParams(vmem_limit_bytes=vmem * 2**20),
        cost_estimate=pl.CostEstimate(flops=flops, bytes_accessed=4 * 2**20, transcendentals=0),
    )(place, *inputs, *pieces)


def fast_device(
    target_states, source_states, target_segments, source_segments, output_grad, self_project,
    self_output, cross_query, cross_keyval, cross_output, hidden_up, hidden_bias, hidden_down,
    output_bias, first_gain, first_shift, second_gain, second_shift, third_gain, third_shift,
):
    vmem, dma = pltpu.VMEM, pltpu.SemaphoreType.DMA
    side = lax.axis_index("seq")
    place = jnp.stack([lax.axis_index("rows") * 2 + side, side]).astype(jnp.int32)
    states, grad = target_states[0], output_grad[0]
    small = jnp.pad(hidden_bias, (112, 80))
    for i, vector in enumerate(
        (output_bias, first_gain, first_shift, second_gain, second_shift, third_gain, third_shift)
    ):
        small = small + jnp.pad(vector, (16 * i, 240 - 16 * i))
    small = small.reshape(1, 256)
    one, two, three, near, own_source = call(
        pack_body, "pack", place,
        [
            small, self_project, self_output, cross_query, cross_keyval, cross_output, hidden_up, hidden_down, states,
            source_states[0],
        ],
        [],
        [
            shape_of(16, 1664), shape_of(16, 2560), shape_of(16, 4096), shape_of(WINDOW, MODEL),
            shape_of(HALF_SOURCE, MODEL),
        ],
        [vmem((BLOCK, TILE), BF16), dma((12,))], 1000000, any_ins=range(1, 9), vmem=60,
    )
    parts_one = along_z(one)
    window = exchange(near, FLIP_Y)
    one = join(one, *parts_one)
    came = exchange_side(one, 0)
    two, window = tied((two, window), came)
    parts_two = along_z(two)
    one = tied(join(one, came), window)
    other = exchange_side(one, 1)
    parts_two = tied(parts_two, other)
    pieces_one = both_cores([one, other])
    two = join(two, *parts_two)
    came = exchange_side(two, 0)
    half = source_states.shape[1]
    gap = jnp.full((1, HALF_SOURCE - half), -1, jnp.int32)
    source_seg = jnp.concatenate([source_segments[:, :half], gap, source_segments[:, half:], gap], 1)

    queries, pair, lowered, vectors, up_bias, weight_one = call(
        self_body, "self_lower", place, [states, window], pieces_one,
        [
            shape_of(OWN, MODEL), shape_of(KEYS, 2 * MODEL), shape_of(KEYS, MODEL), shape_of(8, MODEL, dtype=F32),
            shape_of(1, FEED, dtype=F32), shape_of(MODEL, 1536),
        ],
        [vmem((MODEL, TILE), BF16), dma((3,))], 3000000000,
    )
    came, two, three, sent_source = tied((came, two, three, own_source), queries)
    parts_three = along_z(three)
    other_source = exchange(sent_source, FLIP_Y)
    two = join(two, came)
    two_core = exchange(two, FLIP_CORE)
    other = exchange_side(two, 1)
    mixed, logs = call(
        self_mix_body, "self_mix", place, [target_segments, queries, pair], [],
        [shape_of(OWN, MODEL), shape_of(HEADS, OWN, dtype=F32)], [vmem((OWN, TILE), F32)], 8000000000,
    )
    other, two_core, parts_three, three, other_source = tied(
        (other, two_core, parts_three, three, other_source), mixed
    )
    pieces_two = [two, other, two_core, exchange(other, FLIP_CORE)]
    three = join(three, *parts_three)
    came = exchange_side(three, 0)
    after_self, lowered_two, queries_two, pair_two, weight_two = call(
        cross_body, "cross_lower", place, [states, own_source, other_source, mixed, vectors], pieces_two,
        [
            shape_of(OWN, MODEL, dtype=F32), shape_of(OWN, MODEL), shape_of(OWN, MODEL), shape_of(SOURCES, 2 * MODEL),
            shape_of(MODEL, 2560),
        ],
        [vmem((SOURCES, MODEL), BF16), dma((2,))], 3000000000,
    )
    came, three = tied((came, three), queries_two)
    three = join(three, came)
    three_core = exchange(three, FLIP_CORE)
    other = exchange_side(three, 1)
    mixed_two, logs_two, after_cross = call(
        cross_mix_body, "cross_mix", place,
        [target_segments, source_seg, queries_two, pair_two, after_self, weight_two], [],
        [shape_of(OWN, MODEL), shape_of(HEADS, OWN, dtype=F32), shape_of(OWN, MODEL, dtype=F32)],
        [vmem((OWN, TILE), F32)], 8000000000,
    )
    three_core, other = tied((three_core, other), after_cross)
    pieces_three = [three, other, three_core, exchange(other, FLIP_CORE)]
    layer_out, after_grad, feed_kept, feed_sent, sums, bias_sums = call(
        feed_body, "feed", place, [after_cross, grad, vectors, up_bias], pieces_three,
        [shape_of(OWN, MODEL), shape_of(OWN, MODEL, dtype=F32)] + [shape_of(256, 2 * FEED)] * 2
        + [shape_of(8, MODEL, dtype=F32), shape_of(1, FEED, dtype=F32)],
        [
            vmem((MODEL, FEED), BF16), vmem((FEED, MODEL), BF16), vmem((OWN, MODEL), BF16), vmem((MODEL, OWN), BF16),
            vmem((OWN, MODEL), F32), vmem((OWN, MODEL), F32), vmem((MODEL, FEED), BF16), vmem((FEED, MODEL), BF16),
            dma((4,)),
        ],
        10000000000, any_outs=(2, 3),
    )
    feed_sent, feed_kept = add_halves(feed_kept, exchange(feed_sent, FLIP_CORE))
    after_grad = tied(after_grad, feed_sent)
    feed_came = exchange_side(feed_sent, 1)
    asked, source_own, source_send, some_grads = call(
        cross_back_body, "cross_backward", place,
        [
            target_segments, source_seg, own_source, other_source, queries_two, pair_two, mixed_two, logs_two,
            after_grad, weight_two,
        ],
        [],
        [
            shape_of(OWN, MODEL), shape_of(HALF_SOURCE, MODEL, dtype=F32), shape_of(HALF_SOURCE, MODEL),
            shape_of(MODEL, 1536),
        ],
        [
            vmem((OWN, MODEL), BF16), vmem((OWN, MODEL), F32), vmem((SOURCES, 2 * MODEL), BF16),
            vmem((SOURCES, MODEL), BF16), vmem((SOURCES, TILE), F32),
        ],
        10000000000,
    )
    feed_came = tied(feed_came, asked)
    feed_sent, feed_kept = add_halves(feed_kept, feed_came)
    asked = tied(asked, feed_sent)
    feed_came = exchange_side(feed_sent, 0)
    self_grad, upstream, dot_rows, cross_kept, cross_sent, sums = call(
        cross_weight_body, "cross_weights", place,
        [after_self, lowered_two, mixed, after_grad, asked, vectors, sums, weight_two, some_grads], [],
        [shape_of(OWN, MODEL, dtype=F32), shape_of(OWN, MODEL), shape_of(HEADS, OWN, dtype=F32)]
        + [shape_of(256, 2560)] * 2 + [shape_of(8, MODEL, dtype=F32)],
        [vmem((MODEL, 1024), BF16), dma((2,))],
        6000000000, any_outs=(3, 4),
    )
    feed_came = tied(feed_came, upstream)
    cross_kept, cross_sent, source_send = tied((cross_kept, cross_sent, source_send), feed_came)
    feed = z_blocks(feed_kept + feed_came)
    cross_sent, cross_kept = add_halves(cross_kept, exchange(cross_sent, FLIP_CORE))
    source_came = exchange(source_send, FLIP_Y)
    cross_came = exchange_side(cross_sent, 1)
    upstream = tied(upstream, feed[0], cross_sent)
    part_back, *left_sends = call(
        self_back_body, "self_backward", place,
        [target_segments, lowered, queries, pair, logs, upstream, dot_rows, weight_one], [],
        [shape_of(KEYS, MODEL, dtype=F32)] + [shape_of(256, 768)] * 2,
        [
            vmem((OWN, 256), F32), vmem((KEYS, 512), BF16), vmem((MODEL, 768), BF16), vmem((KEYS, TILE), F32), dma((1,)),
        ],
        8000000000, any_outs=(1, 2),
    )
    cross_came, feed, source_own, source_came = tied((cross_came, feed, source_own, source_came), part_back)
    left_sends = tied(left_sends, cross_came, feed, source_came)
    cross_sent, cross_kept = add_halves(cross_kept, cross_came)
    left_sent, left_kept = add_halves(left_sends[0], exchange(left_sends[1], FLIP_CORE))
    cross_came, left_came = exchange_side(cross_sent, 0), exchange_side(left_sent, 1)
    part_back = tied(part_back, cross_sent, left_sent)
    own_back, send_back, *right_sends = call(
        self_last_body, "self_last", place,
        [
            target_segments, states, window, lowered, queries, pair, logs, upstream, dot_rows, weight_one, part_back,
            sums, bias_sums,
        ],
        [],
        [shape_of(OWN, MODEL, dtype=F32), shape_of(WINDOW, MODEL)] + [shape_of(256, 896)] * 2,
        [
            vmem((OWN, 256), F32), vmem((KEYS, 512), BF16), vmem((MODEL, 896), BF16), vmem((KEYS, TILE), F32), dma((1,)),
        ],
        8000000000, any_outs=(2, 3),
    )
    cross_came, left_came, source_own = tied((cross_came, left_came, source_own), own_back)
    right_sends, send_back = tied((right_sends, send_back), cross_came, left_came)
    right_sent, right_kept = add_halves(right_sends[0], exchange(right_sends[1], FLIP_CORE))
    cross_kept, left_kept = tied((cross_kept, left_kept), right_sent)
    right_came, came = exchange_side(right_sent, 1), exchange(send_back, FLIP_Y)
    left_sent, left_kept = add_halves(left_kept, left_came)
    left_came = exchange_side(left_sent, 0)
    cross = z_blocks(cross_kept + cross_came)
    right_sent, right_kept = add_halves(right_kept, right_came)
    right_came = exchange_side(right_sent, 0)
    came, source_own = tied((came, source_own), right_sent)
    grad_source = source_own[:half] + source_came[:half].astype(F32)
    (grad_target,) = call(
        target_body, "target_grad", place, [own_back, came, states, self_grad, vectors], [],
        [shape_of(OWN, MODEL, dtype=F32)], [], 1000000,
    )
    last = z_blocks(jnp.concatenate([left_kept + left_came, right_kept + right_came], 1))
    project, output, query, keyval, crossout, up, down, *small = call(
        finish_body, "finish", place, feed + cross + last, [],
        [
            shape_of(16, 1536, dtype=F32), shape_of(16, 512, dtype=F32), shape_of(16, 512, dtype=F32),
            shape_of(16, 1024, dtype=F32), shape_of(16, 512, dtype=F32), shape_of(16, 2048, dtype=F32),
            shape_of(64, 512, dtype=F32),
        ]
        + [shape_of(1, 16, dtype=F32)] * 7 + [shape_of(1, 64, dtype=F32)],
        [], 1000000,
    )
    *rows, up_sum = [row[0] for row in small]
    return (
        layer_out[None], grad_target[None], grad_source[None], project, output, query, keyval, crossout, up,
        up_sum, down, *rows,
    )


def specs():
    in_specs = (
        P("rows", "seq", None),
        P("rows", "seq", None),
        P("rows", None),
        P("rows", None),
        P("rows", "seq", None),
        P(("rows", "seq"), None),
        P(("rows", "seq"), None),
        P(("rows", "seq"), None),
        P(("rows", "seq"), None),
        P(("rows", "seq"), None),
        P(("rows", "seq"), None),
        P(("rows", "seq")),
        P(("rows", "seq"), None),
        P(("rows", "seq")),
        P(("rows", "seq")),
        P(("rows", "seq")),
        P(("rows", "seq")),
        P(("rows", "seq")),
        P(("rows", "seq")),
        P(("rows", "seq")),
    )
    out_specs = (
        P("rows", "seq", None),
        P("rows", "seq", None),
        P("rows", "seq", None),
        P(("rows", "seq"), None),
        P(("rows", "seq"), None),
        P(("rows", "seq"), None),
        P(("rows", "seq"), None),
        P(("rows", "seq"), None),
        P(("rows", "seq"), None),
        P(("rows", "seq")),
        P(("rows", "seq"), None),
        P(("rows", "seq")),
        P(("rows", "seq")),
        P(("rows", "seq")),
        P(("rows", "seq")),
        P(("rows", "seq")),
        P(("rows", "seq")),
        P(("rows", "seq")),
    )
    return in_specs, out_specs


def solution(mesh):
    in_specs, out_specs = specs()
    fast = mesh.shape["rows"] == 16 and mesh.shape["seq"] == 2
    return jax.shard_map(
        fast_device if fast else general_device,
        mesh=mesh, in_specs=in_specs, out_specs=out_specs, check_vma=False,
    )
```

```python
import jax
import jax.numpy as jnp
from jax import lax
from jax.experimental import pallas as pl
from jax.experimental.pallas import tpu as pltpu
from jax.sharding import PartitionSpec as P

HEADS = 8
HD = 64


def layer_norm(value, gain, shift):
    row_mean = jnp.mean(value, -1, keepdims=True)
    centered = value - row_mean
    variance = jnp.mean(centered * centered, -1, keepdims=True)
    inverse = lax.rsqrt(variance + 1e-05)
    normed = centered * inverse
    return (normed * gain + shift, normed, inverse)


def norm_back(upstream, normed, inverse, gain):
    scaled = upstream * gain
    first_mean = jnp.mean(scaled, -1, keepdims=True)
    second_mean = jnp.mean(scaled * normed, -1, keepdims=True)
    grad_input = inverse * (scaled - first_mean - normed * second_mean)
    return (grad_input, jnp.sum(upstream * normed, 0), jnp.sum(upstream, 0))


def matmul(left, right):
    return jnp.dot(left, right, preferred_element_type=jnp.float32)


def transposed(left, right):
    return lax.dot_general(
        left, right, (((0,), (0,)), ((), ())), preferred_element_type=jnp.float32
    )


def against(left, right):
    return lax.dot_general(
        left, right, (((1,), (1,)), ((), ())), preferred_element_type=jnp.float32
    )


def head_split(value):
    return value.reshape(value.shape[0], HEADS, HD)


def head_join(value):
    return value.reshape(value.shape[0], HEADS * HD)


def scores_of(queries, key_rows, query_seg, key_seg):
    raw_scores = jnp.einsum(
        "qhd,khd->hqk", queries, key_rows, preferred_element_type=jnp.float32
    ) * HD ** (-0.5)
    same_seg = (query_seg[:, None] == key_seg[None, :])[None]
    return (raw_scores, same_seg)


def block_weights(queries, key_rows, query_seg, key_seg, log_total):
    raw_scores, same_seg = scores_of(queries, key_rows, query_seg, key_seg)
    return jnp.where(same_seg, jnp.exp(raw_scores - log_total[..., None]), 0.0)


def log_totals(queries, key_blocks, seg_blocks, query_seg):

    def log_advance(carry, inputs_now):
        row_max, row_total = carry
        key_rows, key_seg = inputs_now
        raw_scores, same_seg = scores_of(queries, key_rows, query_seg, key_seg)
        masked = jnp.where(same_seg, raw_scores, -1000000000.0)
        new_max = jnp.maximum(row_max, jnp.max(masked, -1))
        shifted = jnp.where(same_seg, jnp.exp(masked - new_max[..., None]), 0.0)
        return ((new_max, row_total * jnp.exp(row_max - new_max) + jnp.sum(shifted, -1)), None)

    start = (
        jnp.full((HEADS, queries.shape[0]), -1000000000.0, jnp.float32),
        jnp.zeros((HEADS, queries.shape[0]), jnp.float32),
    )
    (row_max, row_total), unused = lax.scan(log_advance, start, (key_blocks, seg_blocks))
    return row_max + jnp.log(row_total)


def weighted_sum(queries, key_blocks, value_blocks, seg_blocks, query_seg, log_total):

    def weighted_advance(carry, inputs_now):
        key_rows, value_rows, key_seg = inputs_now
        weights = block_weights(queries, key_rows, query_seg, key_seg, log_total).astype(
            jnp.bfloat16
        )
        return (
            carry
            + jnp.einsum("hqk,khd->qhd", weights, value_rows, preferred_element_type=jnp.float32),
            None,
        )

    total, unused = lax.scan(
        weighted_advance,
        jnp.zeros(queries.shape, jnp.float32),
        (key_blocks, value_blocks, seg_blocks),
    )
    return total


def grad_dots(queries, grad_heads, key_blocks, value_blocks, seg_blocks, query_seg, log_total):

    def grad_advance(carry, inputs_now):
        key_rows, value_rows, key_seg = inputs_now
        weights = block_weights(queries, key_rows, query_seg, key_seg, log_total)
        grad_weights = jnp.einsum(
            "qhd,khd->hqk", grad_heads, value_rows, preferred_element_type=jnp.float32
        )
        return (carry + jnp.sum(weights * grad_weights, -1), None)

    start = jnp.zeros((HEADS, queries.shape[0]), jnp.float32)
    total, unused = lax.scan(grad_advance, start, (key_blocks, value_blocks, seg_blocks))
    return total


def query_grads(
    queries, grad_heads, key_blocks, value_blocks, seg_blocks, query_seg, log_total, row_dots
):
    score_scale = HD ** (-0.5)

    def query_advance(carry, inputs_now):
        key_rows, value_rows, key_seg = inputs_now
        weights = block_weights(queries, key_rows, query_seg, key_seg, log_total)
        grad_weights = jnp.einsum(
            "qhd,khd->hqk", grad_heads, value_rows, preferred_element_type=jnp.float32
        )
        grad_scores = (weights * (grad_weights - row_dots[..., None])).astype(jnp.bfloat16)
        carry = (
            carry
            + jnp.einsum("hqk,khd->qhd", grad_scores, key_rows, preferred_element_type=jnp.float32)
            * score_scale
        )
        grad_keys = (
            jnp.einsum("hqk,qhd->khd", grad_scores, queries, preferred_element_type=jnp.float32)
            * score_scale
        )
        grad_values = jnp.einsum(
            "hqk,qhd->khd",
            weights.astype(jnp.bfloat16),
            grad_heads,
            preferred_element_type=jnp.float32,
        )
        return (carry, jnp.concatenate([head_join(grad_keys), head_join(grad_values)], 1))

    return lax.scan(
        query_advance, jnp.zeros(queries.shape, jnp.float32), (key_blocks, value_blocks, seg_blocks)
    )


def general_device(
    target_states,
    source_states,
    target_segments,
    source_segments,
    output_grad,
    self_project,
    self_output,
    cross_query,
    cross_keyval,
    cross_output,
    hidden_up,
    hidden_bias,
    hidden_down,
    output_bias,
    first_gain,
    first_shift,
    second_gain,
    second_shift,
    third_gain,
    third_shift,
):
    (
        full_project,
        full_output,
        full_query,
        full_keyval,
        full_crossout,
        full_up,
        full_upbias,
        full_down,
        full_downbias,
        gain_one,
        shift_one,
        gain_two,
        shift_two,
        gain_three,
        shift_three,
    ) = (
        lax.all_gather(self_project, ("rows", "seq"), axis=0, tiled=True),
        lax.all_gather(self_output, ("rows", "seq"), axis=0, tiled=True),
        lax.all_gather(cross_query, ("rows", "seq"), axis=0, tiled=True),
        lax.all_gather(cross_keyval, ("rows", "seq"), axis=0, tiled=True),
        lax.all_gather(cross_output, ("rows", "seq"), axis=0, tiled=True),
        lax.all_gather(hidden_up, ("rows", "seq"), axis=0, tiled=True),
        lax.all_gather(hidden_bias, ("rows", "seq"), axis=0, tiled=True),
        lax.all_gather(hidden_down, ("rows", "seq"), axis=0, tiled=True),
        lax.all_gather(output_bias, ("rows", "seq"), axis=0, tiled=True),
        lax.all_gather(first_gain, ("rows", "seq"), axis=0, tiled=True),
        lax.all_gather(first_shift, ("rows", "seq"), axis=0, tiled=True),
        lax.all_gather(second_gain, ("rows", "seq"), axis=0, tiled=True),
        lax.all_gather(second_shift, ("rows", "seq"), axis=0, tiled=True),
        lax.all_gather(third_gain, ("rows", "seq"), axis=0, tiled=True),
        lax.all_gather(third_shift, ("rows", "seq"), axis=0, tiled=True),
    )
    gain_one = gain_one.astype(jnp.float32)
    gain_two = gain_two.astype(jnp.float32)
    gain_three = gain_three.astype(jnp.float32)
    score_scale = HD ** (-0.5)
    states = target_states[0].astype(jnp.float32)
    local_rows = states.shape[0]
    model_width = states.shape[1]
    seq_count = lax.axis_size("seq")
    row_segments = target_segments[0]
    seq_length = row_segments.shape[0]
    own_segments = lax.dynamic_slice_in_dim(
        row_segments, lax.axis_index("seq") * local_rows, local_rows
    )
    block_rows = max(1, min(seq_count, 512 // local_rows)) * local_rows
    block_count = seq_length // block_rows
    seg_blocks = row_segments.reshape(block_count, block_rows)
    normed_value, normed_one, inverse_one = layer_norm(
        states, gain_one, shift_one.astype(jnp.float32)
    )
    lowered_one = normed_value.astype(jnp.bfloat16)
    projected = matmul(lowered_one, full_project).astype(jnp.bfloat16)
    query_flat = projected[:, :model_width]
    key_local = projected[:, model_width : 2 * model_width]
    value_local = projected[:, 2 * model_width :]
    queries = head_split(query_flat)
    key_all, value_all = (
        lax.all_gather(key_local, "seq", axis=0, tiled=True),
        lax.all_gather(value_local, "seq", axis=0, tiled=True),
    )
    key_blocks = key_all.reshape(block_count, block_rows, HEADS, HD)
    value_blocks = value_all.reshape(block_count, block_rows, HEADS, HD)
    log_total = log_totals(queries, key_blocks, seg_blocks, own_segments)
    self_mixed = head_join(
        weighted_sum(queries, key_blocks, value_blocks, seg_blocks, own_segments, log_total)
    ).astype(jnp.bfloat16)
    after_self = states + matmul(self_mixed, full_output)
    normed_value, normed_two, inverse_two = layer_norm(
        after_self, gain_two, shift_two.astype(jnp.float32)
    )
    lowered_two = normed_value.astype(jnp.bfloat16)
    cross_asked = matmul(lowered_two, full_query).astype(jnp.bfloat16)
    source_low = source_states[0]
    source_all = lax.all_gather(source_low, "seq", axis=0, tiled=True)
    key_value = matmul(source_all, full_keyval).astype(jnp.bfloat16)
    cross_key_heads = head_split(key_value[:, :model_width])
    cross_value_heads = head_split(key_value[:, model_width:])
    asked_heads = head_split(cross_asked)
    raw_scores, same_seg = scores_of(asked_heads, cross_key_heads, own_segments, source_segments[0])
    cross_probs = jax.nn.softmax(jnp.where(same_seg, raw_scores, -1000000000.0), axis=-1)
    cross_mixed = head_join(
        jnp.einsum(
            "hqk,khd->qhd",
            cross_probs.astype(jnp.bfloat16),
            cross_value_heads,
            preferred_element_type=jnp.float32,
        )
    ).astype(jnp.bfloat16)
    after_cross = after_self + matmul(cross_mixed, full_crossout)
    normed_value, normed_three, inverse_three = layer_norm(
        after_cross, gain_three, shift_three.astype(jnp.float32)
    )
    lowered_three = normed_value.astype(jnp.bfloat16)
    hidden = matmul(lowered_three, full_up) + full_upbias.astype(jnp.float32)
    activated = jax.nn.gelu(hidden).astype(jnp.bfloat16)
    layer_out = after_cross + matmul(activated, full_down) + full_downbias.astype(jnp.float32)
    grad_low = output_grad[0]
    out_grad = grad_low.astype(jnp.float32)
    grad_down = transposed(activated, grad_low)
    grad_downbias = jnp.sum(out_grad, 0)
    grad_act = against(grad_low, full_down)
    grad_hidden = jax.vjp(jax.nn.gelu, hidden)[1](grad_act)[0].astype(jnp.bfloat16)
    grad_upbias = jnp.sum(grad_hidden.astype(jnp.float32), 0)
    grad_up = transposed(lowered_three, grad_hidden)
    dx_three, grad_gain_three, grad_shift_three = norm_back(
        against(grad_hidden, full_up), normed_three, inverse_three, gain_three
    )
    grad_cross = out_grad + dx_three
    grad_cross_low = grad_cross.astype(jnp.bfloat16)
    grad_crossout = transposed(cross_mixed, grad_cross_low)
    grad_cross_heads = head_split(against(grad_cross_low, full_crossout).astype(jnp.bfloat16))
    grad_weights = jnp.einsum(
        "qhd,khd->hqk", grad_cross_heads, cross_value_heads, preferred_element_type=jnp.float32
    )
    grad_scores = (
        cross_probs * (grad_weights - jnp.sum(cross_probs * grad_weights, -1, keepdims=True))
    ).astype(jnp.bfloat16)
    grad_asked = head_join(
        jnp.einsum("hqk,khd->qhd", grad_scores, cross_key_heads, preferred_element_type=jnp.float32)
        * score_scale
    ).astype(jnp.bfloat16)
    grad_cross_keys = (
        jnp.einsum("hqk,qhd->khd", grad_scores, asked_heads, preferred_element_type=jnp.float32)
        * score_scale
    )
    grad_cross_values = jnp.einsum(
        "hqk,qhd->khd",
        cross_probs.astype(jnp.bfloat16),
        grad_cross_heads,
        preferred_element_type=jnp.float32,
    )
    pair_terms = jnp.concatenate([head_join(grad_cross_keys), head_join(grad_cross_values)], 1)
    pair_grad = lax.psum_scatter(
        pair_terms.astype(jnp.bfloat16), "seq", scatter_dimension=0, tiled=True
    )
    grad_keyval = transposed(source_low, pair_grad)
    grad_source = against(pair_grad, full_keyval)
    grad_query = transposed(lowered_two, grad_asked)
    dx_two, grad_gain_two, grad_shift_two = norm_back(
        against(grad_asked, full_query), normed_two, inverse_two, gain_two
    )
    grad_self = grad_cross + dx_two
    grad_self_low = grad_self.astype(jnp.bfloat16)
    grad_output = transposed(self_mixed, grad_self_low)
    grad_mixed = against(grad_self_low, full_output).astype(jnp.bfloat16)
    grad_heads = head_split(grad_mixed)
    row_dots = grad_dots(
        queries, grad_heads, key_blocks, value_blocks, seg_blocks, own_segments, log_total
    )
    grad_queries, key_terms = query_grads(
        queries, grad_heads, key_blocks, value_blocks, seg_blocks, own_segments, log_total, row_dots
    )
    summed = lax.psum_scatter(
        key_terms.reshape(seq_length, 2 * model_width).astype(jnp.bfloat16),
        "seq",
        scatter_dimension=0,
        tiled=True,
    )
    grad_projected = jnp.concatenate([head_join(grad_queries).astype(jnp.bfloat16), summed], 1)
    grad_project = transposed(lowered_one, grad_projected)
    dx_one, grad_gain_one, grad_shift_one = norm_back(
        against(grad_projected, full_project), normed_one, inverse_one, gain_one
    )
    grad_target = grad_self + dx_one
    shards = (
        lax.psum_scatter(grad_project, ("rows", "seq"), scatter_dimension=0, tiled=True),
        lax.psum_scatter(grad_output, ("rows", "seq"), scatter_dimension=0, tiled=True),
        lax.psum_scatter(grad_query, ("rows", "seq"), scatter_dimension=0, tiled=True),
        lax.psum_scatter(grad_keyval, ("rows", "seq"), scatter_dimension=0, tiled=True),
        lax.psum_scatter(grad_crossout, ("rows", "seq"), scatter_dimension=0, tiled=True),
        lax.psum_scatter(grad_up, ("rows", "seq"), scatter_dimension=0, tiled=True),
        lax.psum_scatter(grad_upbias, ("rows", "seq"), scatter_dimension=0, tiled=True),
        lax.psum_scatter(grad_down, ("rows", "seq"), scatter_dimension=0, tiled=True),
        lax.psum_scatter(grad_downbias, ("rows", "seq"), scatter_dimension=0, tiled=True),
        lax.psum_scatter(grad_gain_one, ("rows", "seq"), scatter_dimension=0, tiled=True),
        lax.psum_scatter(grad_shift_one, ("rows", "seq"), scatter_dimension=0, tiled=True),
        lax.psum_scatter(grad_gain_two, ("rows", "seq"), scatter_dimension=0, tiled=True),
        lax.psum_scatter(grad_shift_two, ("rows", "seq"), scatter_dimension=0, tiled=True),
        lax.psum_scatter(grad_gain_three, ("rows", "seq"), scatter_dimension=0, tiled=True),
        lax.psum_scatter(grad_shift_three, ("rows", "seq"), scatter_dimension=0, tiled=True),
    )
    return (layer_out.astype(jnp.bfloat16)[None], grad_target[None], grad_source[None]) + tuple(
        shards
    )


F32, BF16 = jnp.float32, jnp.bfloat16
BLOCK = 16
AXES = ("rows", "seq")
FLIP_Y, FLIP_CORE, FLIP_X, FLIP_Z = 1, 2, 4, 8
MODEL, FEED, OWN, WINDOW, HALF_SOURCE = 512, 2048, 512, 256, 192
KEYS, SOURCES = OWN + WINDOW, 2 * HALF_SOURCE
TILE = 128
MASKED = -1000000000.0
SCALE = HD ** (-0.5)


def exchange(value, flip):
    return lax.ppermute(value, AXES, [(device, device ^ flip) for device in range(32)])


def exchange_side(value, step):
    flips = (FLIP_X, FLIP_Y) if step == 0 else (FLIP_Y, FLIP_X)
    return lax.ppermute(value, AXES, [(device, device ^ flips[device >> 1 & 1]) for device in range(32)])


def tied(values, *others):
    return lax.optimization_barrier((values, others))[0]


def along_z(block):
    return [exchange(block, FLIP_Z * i) for i in Z_ORDER]


Z_ORDER = (1, 2, 3)


def join(*parts):
    return jnp.concatenate(parts, 0)


def both_cores(halves):
    return halves + [exchange(half, FLIP_CORE) for half in halves]


def add_halves(kept, came):
    half = kept.shape[0] // 2
    return kept[half:] + came[half:], kept[:half] + came[:half]


def z_blocks(both):
    size = both.shape[0] // 4
    blocks = [both[size * i : size * (i + 1)] for i in range(4)]
    return [blocks[0]] + [exchange(block, FLIP_Z * i) for i, block in zip(Z_ORDER, blocks[1:])]


def block_places(me):
    out = []
    for other in (0, 1):
        core = (me >> 1 & 1) ^ other
        first, second = FLIP_X - 3 * core, FLIP_Y + 3 * core
        for b in (0, 1):
            for a in (0, 1):
                for i, z in enumerate((0,) + Z_ORDER):
                    owner = me ^ (other * FLIP_CORE + b * second + a * first + z * FLIP_Z)
                    out.append((other * 2 + b, a * 4 + i, owner))
    return out


def nn(left, right):
    return jnp.dot(left, right, preferred_element_type=F32)


def block_rows(owner, size=BLOCK):
    return pl.ds(pl.multiple_of(owner * size, size), size)


def load_blocks(me, pieces, columns, target):
    for piece, row, owner in block_places(me):
        target[block_rows(owner), :] = pieces[piece][row * BLOCK : (row + 1) * BLOCK, columns]


def store_blocks(me, source, targets, columns):
    for piece, row, owner in block_places(me):
        at = (piece % 2 * 8 + row) * BLOCK
        targets[piece // 2][at : at + BLOCK, columns] = source[block_rows(owner), :]


def normed_rows(value):
    centered = value - jnp.mean(value, -1, keepdims=True)
    inverse = lax.rsqrt(jnp.mean(centered * centered, -1, keepdims=True) + 1e-05)
    return centered * inverse, inverse


def norm_back_rows(upstream, normed, inverse, gain):
    scaled = upstream * gain
    first_mean = jnp.mean(scaled, -1, keepdims=True)
    second_mean = jnp.mean(scaled * normed, -1, keepdims=True)
    return inverse * (scaled - first_mean - normed * second_mean)


def column_sum(value):
    return jnp.sum(value, 0, keepdims=True)


def own_segments_of(index, segments):
    return jnp.where(index == 0, segments[:, :OWN], segments[:, OWN:]).astype(F32)


def key_segments_of(index, segments):
    near = jnp.where(index == 0, segments[:, OWN:KEYS], segments[:, OWN - WINDOW : OWN])
    return jnp.concatenate([own_segments_of(index, segments), near.astype(F32)], 1)


def spread(row):
    return jnp.broadcast_to(row, (TILE, row.shape[1])).T


def lane_half(shape, half):
    lanes = lax.broadcasted_iota(jnp.int32, shape, 1)
    return (lanes < HD) if half == 0 else (lanes >= HD)


def half_masks(value):
    keep, zero = lane_half(value.shape, 0), jnp.zeros_like(value)
    return jnp.concatenate([jnp.where(keep, value, zero), jnp.where(keep, zero, value)], 0)


def self_jobs(side):
    near, far = pl.multiple_of((1 - side) * 256, 256), pl.multiple_of(side * 256, 256)
    skip_near, skip_far = pl.multiple_of((1 - side) * TILE, TILE), pl.multiple_of(side * TILE, TILE)
    return [
        (pl.ds(near, 256), [(skip_near, 384), (OWN, WINDOW)], 256),
        (pl.ds(far, 256), [(skip_far, 384)], 256),
    ]


def attend(queries, pair_ref, mixed, log_rows, query_seg, key_row, jobs):
    for rows, spans, size in jobs:

        def keys_of(ref, lanes):
            parts = [ref[pl.ds(start, count), lanes] for start, count in spans]
            return parts[0] if len(parts) == 1 else jnp.concatenate(parts, 0)

        segments = [key_row[:, pl.ds(start, count)] for start, count in spans]
        segments = segments[0] if len(segments) == 1 else jnp.concatenate(segments, 1)
        same = jnp.concatenate([query_seg[rows, :]] * (segments.shape[1] // TILE), 1) == segments
        bias = jnp.where(same, 0.0, MASKED)
        lanes = lax.broadcasted_iota(jnp.int32, (size, TILE), 1)
        logs = jnp.zeros((size, TILE), F32)
        for pair in range(HEADS // 2):
            at = slice(pair * TILE, (pair + 1) * TILE)
            scores = against(half_masks(queries[rows, at]), keys_of(pair_ref, at))
            weights, scales = [], []
            for half in range(2):
                part = scores[half * size : (half + 1) * size] + bias
                top = jnp.max(part, -1, keepdims=True)
                part = jnp.exp(part - top)
                total = jnp.sum(part, -1, keepdims=True)
                weights.append(part.astype(BF16))
                scales.append(1.0 / total)
                logs = jnp.where(lanes == pair * 2 + half, top + jnp.log(total), logs)
            values = keys_of(pair_ref, slice(MODEL + pair * TILE, MODEL + (pair + 1) * TILE))
            out = nn(jnp.concatenate(weights, 0), values)
            keep = lane_half((size, TILE), 0)
            mixed[rows, at] = jnp.where(keep, out[:size] * scales[0], out[size:] * scales[1]).astype(BF16)
        log_rows[:, rows] = logs.T[:HEADS]


def head_dots(upstream, mixed):
    head = lax.broadcasted_iota(jnp.int32, (HEADS, MODEL), 1) // HD
    ones = (head == lax.broadcasted_iota(jnp.int32, (HEADS, MODEL), 0)).astype(F32)
    return lax.dot_general(
        ones, upstream.astype(F32) * mixed.astype(F32), (((1,), (1,)), ((), ())),
        precision=lax.Precision.HIGHEST, preferred_element_type=F32,
    )


def attend_back(
    queries, upstream, pair_ref, log_rows, dot_rows, query_row, key_seg, query_grad, pair_grad, pairs, jobs
):
    query_grad[...] = jnp.zeros_like(query_grad)
    for key_start, size, start, count in jobs:
        rows, across = pl.ds(key_start, size), pl.ds(start, count)
        same = jnp.concatenate([key_seg[rows, :]] * (count // TILE), 1) == query_row[:, across]
        bias = jnp.where(same, 0.0, MASKED)
        for pair in pairs:
            at, to = pair * TILE, (pair - pairs[0]) * TILE
            query = queries[across, at : at + TILE]
            grad = upstream[across, at : at + TILE]
            keys = half_masks(pair_ref[rows, at : at + TILE])
            values = half_masks(pair_ref[rows, MODEL + at : MODEL + at + TILE])
            scores, grads = against(keys, query), against(values, grad)
            weights, score_grads = [], []
            for half in range(2):
                head, part = pair * 2 + half, slice(half * size, (half + 1) * size)
                weight = jnp.exp(scores[part] + (bias - log_rows[head : head + 1, across]))
                score_grads.append((weight * (grads[part] - dot_rows[head : head + 1, across])).astype(BF16))
                weights.append(weight.astype(BF16))
            score_grad = jnp.concatenate(score_grads, 0)
            value_part = nn(jnp.concatenate(weights, 0), grad)
            key_part = nn(score_grad, query)
            query_grad[across, to : to + TILE] += transposed(score_grad, keys)
            keep = lane_half((size, TILE), 0)
            pair_grad[rows, to : to + TILE] = jnp.where(keep, key_part[:size], key_part[size:]).astype(BF16)
            to = to + len(pairs) * TILE
            pair_grad[rows, to : to + TILE] = jnp.where(keep, value_part[:size], value_part[size:]).astype(BF16)


def self_back_jobs(side):
    near = pl.multiple_of((1 - side) * 256, 256)
    return [(0, 256, 0, 384), (256, 256, TILE, 384), (OWN, WINDOW, near, 256)]


def pack_body(
    place, vectors, project, output, query, keyval, crossout, up, down, states, source,
    one, three, near, own_source, block, semaphores
):
    me, side = place[0], place[1]
    copies = [
        (project, one.at[:, :1536]),
        (output, one.at[:, 1664:2176]),
        (query, one.at[:, 2176:2688]),
        (keyval, one.at[:, 2688:3712]),
        (crossout, one.at[:, 3712:]),
        (down, three.at[64:]),
    ] + [
        (up.at[:, part * 512 : (part + 1) * 512], three.at[part * BLOCK : (part + 1) * BLOCK, :])
        for part in range(4)
    ] + [
        (states.at[pl.ds(pl.multiple_of((1 - side) * WINDOW, WINDOW), WINDOW), :], near.at[:WINDOW])
    ]
    copies = [pltpu.make_async_copy(*copy, semaphores.at[i]) for i, copy in enumerate(copies)]
    for copy in copies:
        copy.start()
    gap = jnp.zeros((HALF_SOURCE - source.shape[0], MODEL), F32)
    padded = jnp.concatenate([source[...].astype(F32), gap], 0).astype(BF16)
    own_source[...] = padded
    near[WINDOW:, :] = padded
    values = jnp.broadcast_to(vectors[...].astype(F32), (8, 256))
    lanes = lax.broadcasted_iota(jnp.int32, (8, TILE), 1)
    rows = lax.broadcasted_iota(jnp.int32, (8, TILE), 0)
    packed = jnp.zeros((8, TILE), F32)
    spot, wide = (me & 7) * 16, (me & 1) * 64
    for row in range(7):
        moved = pltpu.roll(values, spot + 256 - 16 * row, 1)[:, :TILE]
        inside = jnp.logical_and(lanes >= spot, lanes < spot + 16)
        packed = jnp.where(jnp.logical_and(rows == row, inside), moved, packed)
    moved = pltpu.roll(values, wide + 256 - 112, 1)[:, :TILE]
    inside = jnp.logical_and(lanes >= wide, lanes < wide + 64)
    packed = jnp.where(jnp.logical_and(rows == 7, inside), moved, packed)
    block[...] = jnp.concatenate([packed, jnp.zeros((8, TILE), F32)], 0).astype(BF16)
    last = pltpu.make_async_copy(block, one.at[:, 1536:1664], semaphores.at[len(copies)])
    last.start()
    for copy in copies + [last]:
        copy.wait()


def self_body(place, states, window, *refs):
    pieces, refs = refs[:4], refs[4:]
    queries, pair, lowered, vectors, up_bias, weight, weight_two, packed = refs
    me = place[0]
    load_blocks(me, pieces, slice(1536, 1664), packed)
    load_blocks(me, pieces, slice(0, 1536), weight)
    load_blocks(me, pieces, slice(1664, 4224), weight_two)
    for tile in range(4):
        total = jnp.zeros((8, TILE), F32)
        for i in range(8):
            total = total + packed[(tile * 8 + i) * BLOCK : (tile * 8 + i + 1) * BLOCK, :].astype(F32)[:8]
        vectors[:, tile * TILE : (tile + 1) * TILE] = total
    for tile in range(16):
        total = (
            packed[2 * tile * BLOCK : (2 * tile + 1) * BLOCK, :].astype(F32)
            + packed[(2 * tile + 1) * BLOCK : (2 * tile + 2) * BLOCK, :].astype(F32)
        )
        up_bias[:, tile * TILE : (tile + 1) * TILE] = total[7:8]
    gain, shift = vectors[1:2, :], vectors[2:3, :]
    for i in range(KEYS // TILE):
        rows = slice(i * TILE, (i + 1) * TILE)
        value = states[rows, :] if i < 4 else window[(i - 4) * TILE : (i - 3) * TILE, :]
        lowered[rows, :] = (normed_rows(value.astype(F32))[0] * gain + shift).astype(BF16)
    for i in range(KEYS // 256):
        rows = slice(i * 256, (i + 1) * 256)
        if i < 2:
            queries[rows, :] = (nn(lowered[rows, :], weight[:, :512]) .astype(BF16) * SCALE).astype(BF16)
        pair[rows, :] = nn(lowered[rows, :], weight[:, 512:]).astype(BF16)


def forward_body(
    place, segments, source_segments, states, own_source, other_source, vectors, weight, self_queries, self_pair,
    self_mixed, self_logs, after_self, lowered, queries, pair, mixed, logs, after_cross,
    query_seg, key_row, source_row, source,
):
    self_mix(place, segments, self_queries, self_pair, self_mixed, self_logs, query_seg, key_row)
    cross_lower(
        place, states, own_source, other_source, self_mixed, vectors, after_self, lowered, queries, pair, weight, source
    )
    source_row[...] = source_segments[...].astype(F32)
    attend(queries, pair, mixed, logs, query_seg, source_row, [(pl.ds(0, OWN), [(0, SOURCES)], OWN)])
    for i in range(2):
        rows = slice(i * 256, (i + 1) * 256)
        after_cross[rows, :] = after_self[rows, :] + nn(mixed[rows, :], weight[:, 2048:])


def self_mix(place, segments, queries, pair, mixed, log_rows, query_seg, key_row):
    query_seg[...] = spread(own_segments_of(place[1], segments[...]))
    key_row[...] = key_segments_of(place[1], segments[...])
    attend(queries, pair, mixed, log_rows, query_seg, key_row, self_jobs(place[1]))


def cross_lower(
    place, states, own_source, other_source, self_mixed, vectors, after_self, lowered, queries, pair, weight, source
):
    side = place[1]
    source[:HALF_SOURCE, :] = jnp.where(side == 0, own_source[...], other_source[...])
    source[HALF_SOURCE:, :] = jnp.where(side == 0, other_source[...], own_source[...])
    gain, shift = vectors[3:4, :], vectors[4:5, :]
    pair[...] = nn(source[...], weight[:, 1024:2048]).astype(BF16)
    for i in range(2):
        rows = slice(i * 256, (i + 1) * 256)
        value = states[rows, :].astype(F32) + nn(self_mixed[rows, :], weight[:, :512])
        after_self[rows, :] = value
        lowered[rows, :] = (normed_rows(value)[0] * gain + shift).astype(BF16)
        queries[rows, :] = (nn(lowered[rows, :], weight[:, 512:1024]).astype(BF16) * SCALE).astype(BF16)


CHUNK = 512


def feed_body(place, after_cross, output_grad, vectors, up_bias, *refs):
    pieces, refs = refs[:4], refs[4:]
    (
        total, back, kept, sent, bias_sums, ups, downs, lowered, flipped, up_grads, down_grads,
    ) = refs
    me = place[0]
    places = block_places(me)

    def chunk_of(z):
        return pl.multiple_of(((me >> 3) ^ z) * CHUNK, CHUNK)

    gain, shift = vectors[5:6, :], vectors[6:7, :]
    for i in range(4):
        rows = slice(i * TILE, (i + 1) * TILE)
        low = (normed_rows(after_cross[rows, :])[0] * gain + shift).astype(BF16)
        lowered[rows, :] = low
    flipped[...] = lowered[...].T
    grad_low = output_grad[...]
    for i, z in enumerate((0,) + Z_ORDER):
        at = pl.ds(chunk_of(z), CHUNK)
        z_row = pl.multiple_of(((me >> 3) ^ z) * BLOCK, BLOCK)
        up, down, up_grad, down_grad = ups.at[i], downs.at[i], up_grads.at[i], down_grads.at[i]
        for piece, row, owner in places:
            up[block_rows(owner), :] = pieces[piece][pl.ds(row * 128 + z_row, BLOCK), :]
            if row % 4 == i:
                down[pl.ds(pl.multiple_of((owner & 7) * 64, 64), 64), :] = pieces[piece][
                    row * 128 + 64 : (row + 1) * 128, :
                ]
        hidden = nn(lowered[...], up[...]) + up_bias[:, at]
        square = hidden * hidden
        inner = 0.7978845608028654 * hidden * (1.0 + 0.044715 * square)
        curve = jnp.tanh(inner)
        half = 0.5 * (1.0 + curve)
        activated = (hidden * half).astype(BF16)
        slope = half + (0.5 * 0.7978845608028654) * hidden * (1.0 - curve * curve) * (
            1.0 + (3 * 0.044715) * square
        )
        down_grad[...] = transposed(activated, grad_low).astype(BF16)
        for piece, row, owner in places:
            if row % 4 == i:
                to = (piece % 2 * 8 + row) * 128
                (kept, sent)[piece // 2][to + 64 : to + 128, :] = down_grad[
                    pl.ds(pl.multiple_of((owner & 7) * 64, 64), 64), :
                ]
        grad_hidden = (against(grad_low, down[...]) * slope).astype(BF16)
        bias_sums[:, at] = column_sum(grad_hidden.astype(F32))
        up_grad[...] = nn(flipped[...], grad_hidden).astype(BF16)
        for piece, row, owner in places:
            to = (piece % 2 * 8 + row) * 128
            (kept, sent)[piece // 2][pl.ds(to + z_row, BLOCK), :] = up_grad[block_rows(owner), :]
        if i:
            total[...] += nn(activated, down[...])
            back[...] += against(grad_hidden, up[...])
        else:
            total[...] = nn(activated, down[...])
            back[...] = against(grad_hidden, up[...])


def feed_last_body(place, after_cross, output_grad, vectors, total, back, layer_out, after_grad, sums):
    gain = vectors[5:6, :]
    gain_sum, shift_sum, bias_sum = (jnp.zeros((1, MODEL), F32) for _ in range(3))
    for i in range(4):
        rows = slice(i * TILE, (i + 1) * TILE)
        value, grad = after_cross[rows, :], output_grad[rows, :].astype(F32)
        layer_out[rows, :] = (value + total[rows, :] + vectors[0:1, :]).astype(BF16)
        normed, inverse = normed_rows(value)
        upstream = back[rows, :]
        after_grad[rows, :] = grad + norm_back_rows(upstream, normed, inverse, gain)
        gain_sum, shift_sum = gain_sum + column_sum(upstream * normed), shift_sum + column_sum(upstream)
        bias_sum = bias_sum + column_sum(grad)
    zero = jnp.zeros((1, MODEL), F32)
    sums[...] = jnp.concatenate([bias_sum, zero, zero, zero, zero, gain_sum, shift_sum, zero], 0)


def cross_back_body(
    place, segments, source_segments, own_source, other_source, queries, pair, mixed, log_rows, after_grad, weight,
    asked, source_own, source_send, grads, upstream, query_grad, pair_grad, source, key_seg, query_row,
):
    side = place[1]
    key_seg[...] = spread(source_segments[...].astype(F32))
    query_row[...] = own_segments_of(side, segments[...])
    source[:HALF_SOURCE, :] = jnp.where(side == 0, own_source[...], other_source[...])
    source[HALF_SOURCE:, :] = jnp.where(side == 0, other_source[...], own_source[...])
    grad_low = after_grad[...].astype(BF16)
    upstream[...] = against(grad_low, weight[:, 2048:]).astype(BF16)
    dot_rows = head_dots(upstream[...], mixed[...])
    grads[:, :512] = transposed(mixed[...], grad_low).astype(BF16)
    attend_back(
        queries, upstream, pair, log_rows, dot_rows, query_row, key_seg, query_grad, pair_grad, (0, 1, 2, 3),
        [(0, SOURCES, 0, OWN)],
    )
    asked[...] = (query_grad[...] * SCALE).astype(BF16)
    grads[:, 512:] = transposed(source[...], pair_grad[...]).astype(BF16)
    back = against(pair_grad[...], weight[:, 1024:2048])
    first, second = back[:HALF_SOURCE], back[HALF_SOURCE:]
    source_own[...] = jnp.where(side == 0, first, second)
    source_send[...] = jnp.where(side == 0, second, first).astype(BF16)


def cross_weight_body(
    place, after_self, lowered, self_mixed, after_grad, asked, vectors, sums, weight, some_grads, *refs
):
    self_grad, upstream, dot_rows, kept, sent, new_sums, grads = refs
    me = place[0]
    store_blocks(me, some_grads, (kept, sent), slice(0, 1536))
    gain = vectors[3:4, :]
    gain_sum, shift_sum = jnp.zeros((1, MODEL), F32), jnp.zeros((1, MODEL), F32)
    for i in range(2):
        rows = slice(i * 256, (i + 1) * 256)
        normed, inverse = normed_rows(after_self[rows, :])
        up = against(asked[rows, :], weight[:, 512:1024])
        self_grad[rows, :] = after_grad[rows, :] + norm_back_rows(up, normed, inverse, gain)
        gain_sum, shift_sum = gain_sum + column_sum(up * normed), shift_sum + column_sum(up)
    grads[:, :512] = transposed(lowered[...], asked[...]).astype(BF16)
    grad_low = self_grad[...].astype(BF16)
    grads[:, 512:] = transposed(self_mixed[...], grad_low).astype(BF16)
    store_blocks(me, grads, (kept, sent), slice(1536, 2560))
    upstream[...] = against(grad_low, weight[:, :512]).astype(BF16)
    dot_rows[...] = head_dots(upstream[...], self_mixed[...])
    zero = jnp.zeros((1, MODEL), F32)
    new_sums[...] = sums[...] + jnp.concatenate(
        [zero, zero, zero, gain_sum, shift_sum, zero, zero, zero], 0
    )


def project_grads(lowered, asked, pair_grad, weight, at, grads, back):
    grads[:, :256] = transposed(lowered[:OWN, :], asked).astype(BF16)
    grads[:, 256:512] = transposed(lowered[...], pair_grad[:, :256]).astype(BF16)
    grads[:, 512:768] = transposed(lowered[...], pair_grad[:, 256:]).astype(BF16)
    for i in range(3):
        rows = slice(i * 256, (i + 1) * 256)
        part = against(pair_grad[rows, :256], weight[:, 512 + at : 768 + at]) + against(
            pair_grad[rows, 256:], weight[:, 1024 + at : 1280 + at]
        )
        if i < 2:
            part = part + against(asked[rows, :], weight[:, at : at + 256])
        back(rows, part)


def self_back_body(
    place, segments, lowered, queries, pair, log_rows, upstream, dot_rows, weight,
    part_back, left_grad, query_grad, pair_grad, key_seg, query_row,
):
    key_seg[...] = spread(key_segments_of(place[1], segments[...]))
    query_row[...] = own_segments_of(place[1], segments[...])
    attend_back(
        queries, upstream, pair, log_rows, dot_rows, query_row, key_seg, query_grad, pair_grad, (0, 1),
        self_back_jobs(place[1]),
    )

    def keep(rows, part):
        part_back[rows, :] = part

    project_grads(lowered, (query_grad[...] * SCALE).astype(BF16), pair_grad, weight, 0, left_grad, keep)


def self_last_body(
    place, segments, states, window, lowered, queries, pair, log_rows, upstream, dot_rows, weight, part_back,
    sums, bias_sums, left_grad, *refs
):
    own_back, send_back, kept, sent, query_grad, pair_grad, right_grad, key_seg, query_row = refs
    store_blocks(place[0], left_grad, (kept, sent), slice(0, 768))
    key_seg[...] = spread(key_segments_of(place[1], segments[...]))
    query_row[...] = own_segments_of(place[1], segments[...])
    attend_back(
        queries, upstream, pair, log_rows, dot_rows, query_row, key_seg, query_grad, pair_grad, (2, 3),
        self_back_jobs(place[1]),
    )
    gain_sum, shift_sum = [jnp.zeros((1, MODEL), F32)], [jnp.zeros((1, MODEL), F32)]

    def finish(rows, part):
        part = part + part_back[rows, :]
        if rows.start < OWN:
            own_back[rows, :] = part
            value = states[rows, :]
        else:
            send_back[...] = part.astype(BF16)
            value = window[...]
        normed = normed_rows(value.astype(F32))[0]
        gain_sum[0], shift_sum[0] = gain_sum[0] + column_sum(part * normed), shift_sum[0] + column_sum(part)

    project_grads(lowered, (query_grad[...] * SCALE).astype(BF16), pair_grad, weight, 256, right_grad, finish)
    zero = jnp.zeros((1, MODEL), F32)
    sums = sums[...] + jnp.concatenate([zero, gain_sum[0], shift_sum[0], zero, zero, zero, zero, zero], 0)
    last = lax.broadcasted_iota(jnp.int32, (8, TILE), 0) == 7
    for device in range(32):
        tile, wide = device // 8 * TILE, device // 2 * TILE
        value = jnp.where(last, bias_sums[:, wide : wide + TILE], sums[:, tile : tile + TILE])
        high = value.astype(BF16).astype(F32)
        right_grad[device * BLOCK : (device + 1) * BLOCK, 768:] = jnp.concatenate(
            [high, value - high], 0
        ).astype(BF16)
    store_blocks(place[0], right_grad, (kept, sent), slice(768, 1664))


def target_body(place, back, came, states, self_grad, vectors, out):
    gain = vectors[1:2, :]
    for i in range(4):
        rows = slice(i * TILE, (i + 1) * TILE)
        here = (i < 2) == (place[1] == 1)
        extra = came[(i % 2) * TILE : (i % 2 + 1) * TILE, :].astype(F32)
        upstream = back[rows, :] + jnp.where(here, extra, 0.0)
        normed, inverse = normed_rows(states[rows, :].astype(F32))
        out[rows, :] = self_grad[rows, :] + norm_back_rows(upstream, normed, inverse, gain)


def finish_body(place, *refs):
    feed, cross, last, outs = refs[:4], refs[4:8], refs[8:12], refs[12:]
    project, output, query, keyval, crossout, up, down, *small = outs
    me = place[0]

    def total(parts, begin, end, rows=slice(None)):
        value = parts[0][rows, begin:end].astype(F32)
        for part in parts[1:]:
            value = value + part[rows, begin:end].astype(F32)
        return value

    for part in range(4):
        rows = slice(part * BLOCK, (part + 1) * BLOCK)
        up[:, part * 512 : (part + 1) * 512] = total(feed, 0, MODEL, rows)
    down[...] = total(feed, 0, MODEL, slice(64, 128))
    crossout[...] = total(cross, 0, 512)
    keyval[...] = total(cross, 512, 1536)
    query[...] = total(cross, 1536, 2048)
    output[...] = total(cross, 2048, 2560)
    for part in range(6):
        to = part // 2 * 512 + part % 2 * 256
        at = part // 2 * 256 + part % 2 * 768
        project[:, to : to + 256] = total(last, at, at + 256)
    value = total(last, 1536, 1664)
    value = value[:8] + value[8:]
    narrow = pltpu.roll(value, (TILE - (me & 7) * 16) & 127, 1)
    wide = pltpu.roll(value, (TILE - (me & 1) * 64) & 127, 1)
    for row in range(7):
        small[row][...] = narrow[row : row + 1, :16]
    small[7][...] = wide[7:8, :64]


def shape_of(*shape, dtype=BF16):
    return jax.ShapeDtypeStruct(shape, dtype)


VMEM_SPEC = pl.BlockSpec(memory_space=pltpu.VMEM)
ANY_SPEC = pl.BlockSpec(memory_space=pl.ANY)
HBM_SPEC = pl.BlockSpec(memory_space=pltpu.HBM)
SMEM_SPEC = pl.BlockSpec(memory_space=pltpu.SMEM)


def call(body, name, place, inputs, pieces, outs, scratch, flops, any_outs=(), any_ins=(), vmem=40):
    return pl.pallas_call(
        body,
        name=name,
        out_shape=outs,
        in_specs=[SMEM_SPEC]
        + [HBM_SPEC if i in any_ins else VMEM_SPEC for i in range(len(inputs))]
        + [VMEM_SPEC] * len(pieces),
        out_specs=[ANY_SPEC if i in any_outs else VMEM_SPEC for i in range(len(outs))],
        scratch_shapes=scratch,
        compiler_params=pltpu.CompilerParams(vmem_limit_bytes=vmem * 2**20),
        cost_estimate=pl.CostEstimate(flops=flops, bytes_accessed=4 * 2**20, transcendentals=0),
    )(place, *inputs, *pieces)


def fast_device(
    target_states, source_states, target_segments, source_segments, output_grad, self_project,
    self_output, cross_query, cross_keyval, cross_output, hidden_up, hidden_bias, hidden_down,
    output_bias, first_gain, first_shift, second_gain, second_shift, third_gain, third_shift,
):
    vmem, dma = pltpu.VMEM, pltpu.SemaphoreType.DMA
    side = lax.axis_index("seq")
    place = jnp.stack([lax.axis_index("rows") * 2 + side, side]).astype(jnp.int32)
    states, grad = target_states[0], output_grad[0]
    small = jnp.pad(hidden_bias, (112, 80))
    for i, vector in enumerate(
        (output_bias, first_gain, first_shift, second_gain, second_shift, third_gain, third_shift)
    ):
        small = small + jnp.pad(vector, (16 * i, 240 - 16 * i))
    small = small.reshape(1, 256)
    one, three, near, own_source = call(
        pack_body, "pack", place,
        [
            small, self_project, self_output, cross_query, cross_keyval, cross_output, hidden_up, hidden_down, states,
            source_states[0],
        ],
        [],
        [
            shape_of(16, 4224), shape_of(128, MODEL), shape_of(WINDOW + HALF_SOURCE, MODEL),
            shape_of(HALF_SOURCE, MODEL),
        ],
        [vmem((BLOCK, TILE), BF16), dma((12,))], 1000000, any_ins=range(1, 9), vmem=60,
    )
    parts = along_z(one)
    near = exchange(near, FLIP_Y)
    one = join(one, *parts)
    one = tied(one, near)
    came = exchange_side(one, 0)
    three, one = tied((three, one), came)
    parts_three = along_z(three)
    one = join(one, came)
    one_core = exchange(one, FLIP_CORE)
    other = exchange_side(one, 1)
    other = tied(other, parts_three)
    window, other_source = near[:WINDOW], near[WINDOW:]
    pieces_one = [one, other, one_core, exchange(other, FLIP_CORE)]
    three = join(three, *parts_three)
    came = exchange_side(three, 0)
    half = source_states.shape[1]
    gap = jnp.full((1, HALF_SOURCE - half), -1, jnp.int32)
    source_seg = jnp.concatenate([source_segments[:, :half], gap, source_segments[:, half:], gap], 1)

    queries, pair, lowered, vectors, up_bias, weight_one, weight_two = call(
        self_body, "self_lower", place, [states, window], pieces_one,
        [
            shape_of(OWN, MODEL), shape_of(KEYS, 2 * MODEL), shape_of(KEYS, MODEL), shape_of(8, MODEL, dtype=F32),
            shape_of(1, FEED, dtype=F32), shape_of(MODEL, 1536), shape_of(MODEL, 2560),
        ],
        [vmem((MODEL, TILE), BF16)], 5000000000,
    )
    came, three = tied((came, three), queries)
    three = join(three, came)
    three_core = exchange(three, FLIP_CORE)
    other = exchange_side(three, 1)
    queries = tied(queries, three)
    mixed, logs, after_self, lowered_two, queries_two, pair_two, mixed_two, logs_two, after_cross = call(
        forward_body, "forward", place,
        [
            target_segments, source_seg, states, own_source, other_source, vectors, weight_two, queries, pair,
        ],
        [],
        [
            shape_of(OWN, MODEL), shape_of(HEADS, OWN, dtype=F32), shape_of(OWN, MODEL, dtype=F32), shape_of(OWN, MODEL),
            shape_of(OWN, MODEL), shape_of(SOURCES, 2 * MODEL), shape_of(OWN, MODEL), shape_of(HEADS, OWN, dtype=F32),
            shape_of(OWN, MODEL, dtype=F32),
        ],
        [
            vmem((OWN, TILE), F32), vmem((1, KEYS), F32), vmem((1, SOURCES), F32), vmem((SOURCES, MODEL), BF16),
        ],
        20000000000,
    )
    three_core, other = tied((three_core, other), after_cross)
    pieces_three = [three, other, three_core, exchange(other, FLIP_CORE)]
    total, back, feed_kept, feed_sent, bias_sums = call(
        feed_body, "feed", place, [after_cross, grad, vectors, up_bias], pieces_three,
        [shape_of(OWN, MODEL, dtype=F32)] * 2 + [shape_of(2048, MODEL)] * 2 + [shape_of(1, FEED, dtype=F32)],
        [
            vmem((4, MODEL, CHUNK), BF16), vmem((4, CHUNK, MODEL), BF16), vmem((OWN, MODEL), BF16),
            vmem((MODEL, OWN), BF16), vmem((4, MODEL, CHUNK), BF16), vmem((4, CHUNK, MODEL), BF16),
        ],
        10000000000,
    )
    feed_came = exchange(feed_sent, FLIP_CORE)
    layer_out, after_grad, sums = call(
        feed_last_body, "feed_last", place, [after_cross, grad, vectors, total, back], [],
        [shape_of(OWN, MODEL), shape_of(OWN, MODEL, dtype=F32), shape_of(8, MODEL, dtype=F32)], [], 2000000000,
    )
    feed_came = tied(feed_came, after_grad)
    feed_sent, feed_kept = add_halves(feed_kept, feed_came)
    after_grad = tied(after_grad, feed_sent)
    feed_came = exchange_side(feed_sent, 1)
    asked, source_own, source_send, some_grads = call(
        cross_back_body, "cross_backward", place,
        [
            target_segments, source_seg, own_source, other_source, queries_two, pair_two, mixed_two, logs_two,
            after_grad, weight_two,
        ],
        [],
        [
            shape_of(OWN, MODEL), shape_of(HALF_SOURCE, MODEL, dtype=F32), shape_of(HALF_SOURCE, MODEL),
            shape_of(MODEL, 1536),
        ],
        [
            vmem((OWN, MODEL), BF16), vmem((OWN, MODEL), F32), vmem((SOURCES, 2 * MODEL), BF16),
            vmem((SOURCES, MODEL), BF16), vmem((SOURCES, TILE), F32), vmem((1, OWN), F32),
        ],
        10000000000,
    )
    self_grad, upstream, dot_rows, cross_kept, cross_sent, sums = call(
        cross_weight_body, "cross_weights", place,
        [after_self, lowered_two, mixed, after_grad, asked, vectors, sums, weight_two, some_grads], [],
        [shape_of(OWN, MODEL, dtype=F32), shape_of(OWN, MODEL), shape_of(HEADS, OWN, dtype=F32)]
        + [shape_of(256, 2560)] * 2 + [shape_of(8, MODEL, dtype=F32)],
        [vmem((MODEL, 1024), BF16)], 6000000000,
    )
    feed_came = tied(feed_came, upstream)
    feed_sent, feed_kept = add_halves(feed_kept, feed_came)
    cross_sent = tied(cross_sent, feed_sent)
    feed_came, cross_came = exchange_side(feed_sent, 0), exchange(cross_sent, FLIP_CORE)
    upstream = tied(upstream, feed_sent)
    part_back, left_grad = call(
        self_back_body, "self_backward", place,
        [target_segments, lowered, queries, pair, logs, upstream, dot_rows, weight_one], [],
        [shape_of(KEYS, MODEL, dtype=F32), shape_of(MODEL, 768)],
        [
            vmem((OWN, 256), F32), vmem((KEYS, 512), BF16), vmem((KEYS, TILE), F32), vmem((1, OWN), F32),
        ],
        8000000000,
    )
    feed_came, cross_came, source_send = tied((feed_came, cross_came, source_send), part_back)
    cross_sent, cross_kept = add_halves(cross_kept, cross_came)
    feed = z_blocks(feed_kept + feed_came)
    cross_came, source_came = exchange_side(cross_sent, 1), exchange(source_send, FLIP_Y)
    part_back = tied(part_back, cross_sent, feed[0])
    own_back, send_back, last_kept, last_sent = call(
        self_last_body, "self_last", place,
        [
            target_segments, states, window, lowered, queries, pair, logs, upstream, dot_rows, weight_one, part_back,
            sums, bias_sums, left_grad,
        ],
        [],
        [shape_of(OWN, MODEL, dtype=F32), shape_of(WINDOW, MODEL)] + [shape_of(256, 1664)] * 2,
        [
            vmem((OWN, 256), F32), vmem((KEYS, 512), BF16), vmem((MODEL, 896), BF16), vmem((KEYS, TILE), F32),
            vmem((1, OWN), F32),
        ],
        8000000000,
    )
    cross_came, source_came, feed = tied((cross_came, source_came, feed), own_back)
    cross_sent, cross_kept = add_halves(cross_kept, cross_came)
    last_sent, send_back = tied((last_sent, send_back), cross_sent)
    cross_came = exchange_side(cross_sent, 0)
    last_sent, last_kept = add_halves(last_kept, exchange(last_sent, FLIP_CORE))
    cross_came = tied(cross_came, last_sent)
    last_came, came = exchange_side(last_sent, 1), exchange(send_back, FLIP_Y)
    cross = z_blocks(cross_kept + cross_came)
    last_sent, last_kept = add_halves(last_kept, last_came)
    last_came = exchange_side(last_sent, 0)
    came, source_own, source_came = tied((came, source_own, source_came), last_sent)
    grad_source = source_own[:half] + source_came[:half].astype(F32)
    (grad_target,) = call(
        target_body, "target_grad", place, [own_back, came, states, self_grad, vectors], [],
        [shape_of(OWN, MODEL, dtype=F32)], [], 1000000,
    )
    last = z_blocks(last_kept + last_came)
    project, output, query, keyval, crossout, up, down, *small = call(
        finish_body, "finish", place, feed + cross + last, [],
        [
            shape_of(16, 1536, dtype=F32), shape_of(16, 512, dtype=F32), shape_of(16, 512, dtype=F32),
            shape_of(16, 1024, dtype=F32), shape_of(16, 512, dtype=F32), shape_of(16, 2048, dtype=F32),
            shape_of(64, 512, dtype=F32),
        ]
        + [shape_of(1, 16, dtype=F32)] * 7 + [shape_of(1, 64, dtype=F32)],
        [], 1000000,
    )
    *rows, up_sum = [row[0] for row in small]
    return (
        layer_out[None], grad_target[None], grad_source[None], project, output, query, keyval, crossout, up,
        up_sum, down, *rows,
    )


def specs():
    in_specs = (
        P("rows", "seq", None),
        P("rows", "seq", None),
        P("rows", None),
        P("rows", None),
        P("rows", "seq", None),
        P(("rows", "seq"), None),
        P(("rows", "seq"), None),
        P(("rows", "seq"), None),
        P(("rows", "seq"), None),
        P(("rows", "seq"), None),
        P(("rows", "seq"), None),
        P(("rows", "seq")),
        P(("rows", "seq"), None),
        P(("rows", "seq")),
        P(("rows", "seq")),
        P(("rows", "seq")),
        P(("rows", "seq")),
        P(("rows", "seq")),
        P(("rows", "seq")),
        P(("rows", "seq")),
    )
    out_specs = (
        P("rows", "seq", None),
        P("rows", "seq", None),
        P("rows", "seq", None),
        P(("rows", "seq"), None),
        P(("rows", "seq"), None),
        P(("rows", "seq"), None),
        P(("rows", "seq"), None),
        P(("rows", "seq"), None),
        P(("rows", "seq"), None),
        P(("rows", "seq")),
        P(("rows", "seq"), None),
        P(("rows", "seq")),
        P(("rows", "seq")),
        P(("rows", "seq")),
        P(("rows", "seq")),
        P(("rows", "seq")),
        P(("rows", "seq")),
        P(("rows", "seq")),
    )
    return in_specs, out_specs


def solution(mesh):
    in_specs, out_specs = specs()
    fast = mesh.shape["rows"] == 16 and mesh.shape["seq"] == 2
    return jax.shard_map(
        fast_device if fast else general_device,
        mesh=mesh, in_specs=in_specs, out_specs=out_specs, check_vma=False,
    )
```

```python
import jax
import jax.numpy as jnp
from jax import lax
from jax.experimental import pallas as pl
from jax.experimental.pallas import tpu as pltpu
from jax.sharding import PartitionSpec as P

HEADS = 8
HD = 64


def layer_norm(value, gain, shift):
    row_mean = jnp.mean(value, -1, keepdims=True)
    centered = value - row_mean
    variance = jnp.mean(centered * centered, -1, keepdims=True)
    inverse = lax.rsqrt(variance + 1e-05)
    normed = centered * inverse
    return (normed * gain + shift, normed, inverse)


def norm_back(upstream, normed, inverse, gain):
    scaled = upstream * gain
    first_mean = jnp.mean(scaled, -1, keepdims=True)
    second_mean = jnp.mean(scaled * normed, -1, keepdims=True)
    grad_input = inverse * (scaled - first_mean - normed * second_mean)
    return (grad_input, jnp.sum(upstream * normed, 0), jnp.sum(upstream, 0))


def matmul(left, right):
    return jnp.dot(left, right, preferred_element_type=jnp.float32)


def transposed(left, right):
    return lax.dot_general(
        left, right, (((0,), (0,)), ((), ())), preferred_element_type=jnp.float32
    )


def against(left, right):
    return lax.dot_general(
        left, right, (((1,), (1,)), ((), ())), preferred_element_type=jnp.float32
    )


def head_split(value):
    return value.reshape(value.shape[0], HEADS, HD)


def head_join(value):
    return value.reshape(value.shape[0], HEADS * HD)


def scores_of(queries, key_rows, query_seg, key_seg):
    raw_scores = jnp.einsum(
        "qhd,khd->hqk", queries, key_rows, preferred_element_type=jnp.float32
    ) * HD ** (-0.5)
    same_seg = (query_seg[:, None] == key_seg[None, :])[None]
    return (raw_scores, same_seg)


def block_weights(queries, key_rows, query_seg, key_seg, log_total):
    raw_scores, same_seg = scores_of(queries, key_rows, query_seg, key_seg)
    return jnp.where(same_seg, jnp.exp(raw_scores - log_total[..., None]), 0.0)


def log_totals(queries, key_blocks, seg_blocks, query_seg):

    def log_advance(carry, inputs_now):
        row_max, row_total = carry
        key_rows, key_seg = inputs_now
        raw_scores, same_seg = scores_of(queries, key_rows, query_seg, key_seg)
        masked = jnp.where(same_seg, raw_scores, -1000000000.0)
        new_max = jnp.maximum(row_max, jnp.max(masked, -1))
        shifted = jnp.where(same_seg, jnp.exp(masked - new_max[..., None]), 0.0)
        return ((new_max, row_total * jnp.exp(row_max - new_max) + jnp.sum(shifted, -1)), None)

    start = (
        jnp.full((HEADS, queries.shape[0]), -1000000000.0, jnp.float32),
        jnp.zeros((HEADS, queries.shape[0]), jnp.float32),
    )
    (row_max, row_total), unused = lax.scan(log_advance, start, (key_blocks, seg_blocks))
    return row_max + jnp.log(row_total)


def weighted_sum(queries, key_blocks, value_blocks, seg_blocks, query_seg, log_total):

    def weighted_advance(carry, inputs_now):
        key_rows, value_rows, key_seg = inputs_now
        weights = block_weights(queries, key_rows, query_seg, key_seg, log_total).astype(
            jnp.bfloat16
        )
        return (
            carry
            + jnp.einsum("hqk,khd->qhd", weights, value_rows, preferred_element_type=jnp.float32),
            None,
        )

    total, unused = lax.scan(
        weighted_advance,
        jnp.zeros(queries.shape, jnp.float32),
        (key_blocks, value_blocks, seg_blocks),
    )
    return total


def grad_dots(queries, grad_heads, key_blocks, value_blocks, seg_blocks, query_seg, log_total):

    def grad_advance(carry, inputs_now):
        key_rows, value_rows, key_seg = inputs_now
        weights = block_weights(queries, key_rows, query_seg, key_seg, log_total)
        grad_weights = jnp.einsum(
            "qhd,khd->hqk", grad_heads, value_rows, preferred_element_type=jnp.float32
        )
        return (carry + jnp.sum(weights * grad_weights, -1), None)

    start = jnp.zeros((HEADS, queries.shape[0]), jnp.float32)
    total, unused = lax.scan(grad_advance, start, (key_blocks, value_blocks, seg_blocks))
    return total


def query_grads(
    queries, grad_heads, key_blocks, value_blocks, seg_blocks, query_seg, log_total, row_dots
):
    score_scale = HD ** (-0.5)

    def query_advance(carry, inputs_now):
        key_rows, value_rows, key_seg = inputs_now
        weights = block_weights(queries, key_rows, query_seg, key_seg, log_total)
        grad_weights = jnp.einsum(
            "qhd,khd->hqk", grad_heads, value_rows, preferred_element_type=jnp.float32
        )
        grad_scores = (weights * (grad_weights - row_dots[..., None])).astype(jnp.bfloat16)
        carry = (
            carry
            + jnp.einsum("hqk,khd->qhd", grad_scores, key_rows, preferred_element_type=jnp.float32)
            * score_scale
        )
        grad_keys = (
            jnp.einsum("hqk,qhd->khd", grad_scores, queries, preferred_element_type=jnp.float32)
            * score_scale
        )
        grad_values = jnp.einsum(
            "hqk,qhd->khd",
            weights.astype(jnp.bfloat16),
            grad_heads,
            preferred_element_type=jnp.float32,
        )
        return (carry, jnp.concatenate([head_join(grad_keys), head_join(grad_values)], 1))

    return lax.scan(
        query_advance, jnp.zeros(queries.shape, jnp.float32), (key_blocks, value_blocks, seg_blocks)
    )


def general_device(
    target_states,
    source_states,
    target_segments,
    source_segments,
    output_grad,
    self_project,
    self_output,
    cross_query,
    cross_keyval,
    cross_output,
    hidden_up,
    hidden_bias,
    hidden_down,
    output_bias,
    first_gain,
    first_shift,
    second_gain,
    second_shift,
    third_gain,
    third_shift,
):
    (
        full_project,
        full_output,
        full_query,
        full_keyval,
        full_crossout,
        full_up,
        full_upbias,
        full_down,
        full_downbias,
        gain_one,
        shift_one,
        gain_two,
        shift_two,
        gain_three,
        shift_three,
    ) = (
        lax.all_gather(self_project, ("rows", "seq"), axis=0, tiled=True),
        lax.all_gather(self_output, ("rows", "seq"), axis=0, tiled=True),
        lax.all_gather(cross_query, ("rows", "seq"), axis=0, tiled=True),
        lax.all_gather(cross_keyval, ("rows", "seq"), axis=0, tiled=True),
        lax.all_gather(cross_output, ("rows", "seq"), axis=0, tiled=True),
        lax.all_gather(hidden_up, ("rows", "seq"), axis=0, tiled=True),
        lax.all_gather(hidden_bias, ("rows", "seq"), axis=0, tiled=True),
        lax.all_gather(hidden_down, ("rows", "seq"), axis=0, tiled=True),
        lax.all_gather(output_bias, ("rows", "seq"), axis=0, tiled=True),
        lax.all_gather(first_gain, ("rows", "seq"), axis=0, tiled=True),
        lax.all_gather(first_shift, ("rows", "seq"), axis=0, tiled=True),
        lax.all_gather(second_gain, ("rows", "seq"), axis=0, tiled=True),
        lax.all_gather(second_shift, ("rows", "seq"), axis=0, tiled=True),
        lax.all_gather(third_gain, ("rows", "seq"), axis=0, tiled=True),
        lax.all_gather(third_shift, ("rows", "seq"), axis=0, tiled=True),
    )
    gain_one = gain_one.astype(jnp.float32)
    gain_two = gain_two.astype(jnp.float32)
    gain_three = gain_three.astype(jnp.float32)
    score_scale = HD ** (-0.5)
    states = target_states[0].astype(jnp.float32)
    local_rows = states.shape[0]
    model_width = states.shape[1]
    seq_count = lax.axis_size("seq")
    row_segments = target_segments[0]
    seq_length = row_segments.shape[0]
    own_segments = lax.dynamic_slice_in_dim(
        row_segments, lax.axis_index("seq") * local_rows, local_rows
    )
    block_rows = max(1, min(seq_count, 512 // local_rows)) * local_rows
    block_count = seq_length // block_rows
    seg_blocks = row_segments.reshape(block_count, block_rows)
    normed_value, normed_one, inverse_one = layer_norm(
        states, gain_one, shift_one.astype(jnp.float32)
    )
    lowered_one = normed_value.astype(jnp.bfloat16)
    projected = matmul(lowered_one, full_project).astype(jnp.bfloat16)
    query_flat = projected[:, :model_width]
    key_local = projected[:, model_width : 2 * model_width]
    value_local = projected[:, 2 * model_width :]
    queries = head_split(query_flat)
    key_all, value_all = (
        lax.all_gather(key_local, "seq", axis=0, tiled=True),
        lax.all_gather(value_local, "seq", axis=0, tiled=True),
    )
    key_blocks = key_all.reshape(block_count, block_rows, HEADS, HD)
    value_blocks = value_all.reshape(block_count, block_rows, HEADS, HD)
    log_total = log_totals(queries, key_blocks, seg_blocks, own_segments)
    self_mixed = head_join(
        weighted_sum(queries, key_blocks, value_blocks, seg_blocks, own_segments, log_total)
    ).astype(jnp.bfloat16)
    after_self = states + matmul(self_mixed, full_output)
    normed_value, normed_two, inverse_two = layer_norm(
        after_self, gain_two, shift_two.astype(jnp.float32)
    )
    lowered_two = normed_value.astype(jnp.bfloat16)
    cross_asked = matmul(lowered_two, full_query).astype(jnp.bfloat16)
    source_low = source_states[0]
    source_all = lax.all_gather(source_low, "seq", axis=0, tiled=True)
    key_value = matmul(source_all, full_keyval).astype(jnp.bfloat16)
    cross_key_heads = head_split(key_value[:, :model_width])
    cross_value_heads = head_split(key_value[:, model_width:])
    asked_heads = head_split(cross_asked)
    raw_scores, same_seg = scores_of(asked_heads, cross_key_heads, own_segments, source_segments[0])
    cross_probs = jax.nn.softmax(jnp.where(same_seg, raw_scores, -1000000000.0), axis=-1)
    cross_mixed = head_join(
        jnp.einsum(
            "hqk,khd->qhd",
            cross_probs.astype(jnp.bfloat16),
            cross_value_heads,
            preferred_element_type=jnp.float32,
        )
    ).astype(jnp.bfloat16)
    after_cross = after_self + matmul(cross_mixed, full_crossout)
    normed_value, normed_three, inverse_three = layer_norm(
        after_cross, gain_three, shift_three.astype(jnp.float32)
    )
    lowered_three = normed_value.astype(jnp.bfloat16)
    hidden = matmul(lowered_three, full_up) + full_upbias.astype(jnp.float32)
    activated = jax.nn.gelu(hidden).astype(jnp.bfloat16)
    layer_out = after_cross + matmul(activated, full_down) + full_downbias.astype(jnp.float32)
    grad_low = output_grad[0]
    out_grad = grad_low.astype(jnp.float32)
    grad_down = transposed(activated, grad_low)
    grad_downbias = jnp.sum(out_grad, 0)
    grad_act = against(grad_low, full_down)
    grad_hidden = jax.vjp(jax.nn.gelu, hidden)[1](grad_act)[0].astype(jnp.bfloat16)
    grad_upbias = jnp.sum(grad_hidden.astype(jnp.float32), 0)
    grad_up = transposed(lowered_three, grad_hidden)
    dx_three, grad_gain_three, grad_shift_three = norm_back(
        against(grad_hidden, full_up), normed_three, inverse_three, gain_three
    )
    grad_cross = out_grad + dx_three
    grad_cross_low = grad_cross.astype(jnp.bfloat16)
    grad_crossout = transposed(cross_mixed, grad_cross_low)
    grad_cross_heads = head_split(against(grad_cross_low, full_crossout).astype(jnp.bfloat16))
    grad_weights = jnp.einsum(
        "qhd,khd->hqk", grad_cross_heads, cross_value_heads, preferred_element_type=jnp.float32
    )
    grad_scores = (
        cross_probs * (grad_weights - jnp.sum(cross_probs * grad_weights, -1, keepdims=True))
    ).astype(jnp.bfloat16)
    grad_asked = head_join(
        jnp.einsum("hqk,khd->qhd", grad_scores, cross_key_heads, preferred_element_type=jnp.float32)
        * score_scale
    ).astype(jnp.bfloat16)
    grad_cross_keys = (
        jnp.einsum("hqk,qhd->khd", grad_scores, asked_heads, preferred_element_type=jnp.float32)
        * score_scale
    )
    grad_cross_values = jnp.einsum(
        "hqk,qhd->khd",
        cross_probs.astype(jnp.bfloat16),
        grad_cross_heads,
        preferred_element_type=jnp.float32,
    )
    pair_terms = jnp.concatenate([head_join(grad_cross_keys), head_join(grad_cross_values)], 1)
    pair_grad = lax.psum_scatter(
        pair_terms.astype(jnp.bfloat16), "seq", scatter_dimension=0, tiled=True
    )
    grad_keyval = transposed(source_low, pair_grad)
    grad_source = against(pair_grad, full_keyval)
    grad_query = transposed(lowered_two, grad_asked)
    dx_two, grad_gain_two, grad_shift_two = norm_back(
        against(grad_asked, full_query), normed_two, inverse_two, gain_two
    )
    grad_self = grad_cross + dx_two
    grad_self_low = grad_self.astype(jnp.bfloat16)
    grad_output = transposed(self_mixed, grad_self_low)
    grad_mixed = against(grad_self_low, full_output).astype(jnp.bfloat16)
    grad_heads = head_split(grad_mixed)
    row_dots = grad_dots(
        queries, grad_heads, key_blocks, value_blocks, seg_blocks, own_segments, log_total
    )
    grad_queries, key_terms = query_grads(
        queries, grad_heads, key_blocks, value_blocks, seg_blocks, own_segments, log_total, row_dots
    )
    summed = lax.psum_scatter(
        key_terms.reshape(seq_length, 2 * model_width).astype(jnp.bfloat16),
        "seq",
        scatter_dimension=0,
        tiled=True,
    )
    grad_projected = jnp.concatenate([head_join(grad_queries).astype(jnp.bfloat16), summed], 1)
    grad_project = transposed(lowered_one, grad_projected)
    dx_one, grad_gain_one, grad_shift_one = norm_back(
        against(grad_projected, full_project), normed_one, inverse_one, gain_one
    )
    grad_target = grad_self + dx_one
    shards = (
        lax.psum_scatter(grad_project, ("rows", "seq"), scatter_dimension=0, tiled=True),
        lax.psum_scatter(grad_output, ("rows", "seq"), scatter_dimension=0, tiled=True),
        lax.psum_scatter(grad_query, ("rows", "seq"), scatter_dimension=0, tiled=True),
        lax.psum_scatter(grad_keyval, ("rows", "seq"), scatter_dimension=0, tiled=True),
        lax.psum_scatter(grad_crossout, ("rows", "seq"), scatter_dimension=0, tiled=True),
        lax.psum_scatter(grad_up, ("rows", "seq"), scatter_dimension=0, tiled=True),
        lax.psum_scatter(grad_upbias, ("rows", "seq"), scatter_dimension=0, tiled=True),
        lax.psum_scatter(grad_down, ("rows", "seq"), scatter_dimension=0, tiled=True),
        lax.psum_scatter(grad_downbias, ("rows", "seq"), scatter_dimension=0, tiled=True),
        lax.psum_scatter(grad_gain_one, ("rows", "seq"), scatter_dimension=0, tiled=True),
        lax.psum_scatter(grad_shift_one, ("rows", "seq"), scatter_dimension=0, tiled=True),
        lax.psum_scatter(grad_gain_two, ("rows", "seq"), scatter_dimension=0, tiled=True),
        lax.psum_scatter(grad_shift_two, ("rows", "seq"), scatter_dimension=0, tiled=True),
        lax.psum_scatter(grad_gain_three, ("rows", "seq"), scatter_dimension=0, tiled=True),
        lax.psum_scatter(grad_shift_three, ("rows", "seq"), scatter_dimension=0, tiled=True),
    )
    return (layer_out.astype(jnp.bfloat16)[None], grad_target[None], grad_source[None]) + tuple(
        shards
    )


F32, BF16 = jnp.float32, jnp.bfloat16
BLOCK = 16
AXES = ("rows", "seq")
FLIP_Y, FLIP_CORE, FLIP_X, FLIP_Z = 1, 2, 4, 8
MODEL, FEED, OWN, WINDOW, HALF_SOURCE = 512, 2048, 512, 256, 192
KEYS, SOURCES = OWN + WINDOW, 2 * HALF_SOURCE
TILE = 128
MASKED = -1000000000.0
SCALE = HD ** (-0.5)


def exchange(value, flip):
    return lax.ppermute(value, AXES, [(device, device ^ flip) for device in range(32)])


def exchange_side(value, step):
    flips = (FLIP_X, FLIP_Y) if step == 0 else (FLIP_Y, FLIP_X)
    return lax.ppermute(value, AXES, [(device, device ^ flips[device >> 1 & 1]) for device in range(32)])


def tied(values, *others):
    return lax.optimization_barrier((values, others))[0]


def along_z(block):
    return [exchange(block, FLIP_Z * i) for i in Z_ORDER]


Z_ORDER = (1, 2, 3)


def join(*parts):
    return jnp.concatenate(parts, 0)


def both_cores(halves):
    return halves + [exchange(half, FLIP_CORE) for half in halves]


def add_halves(kept, came):
    half = kept.shape[0] // 2
    return kept[half:] + came[half:], kept[:half] + came[:half]


def z_blocks(both):
    size = both.shape[0] // 4
    blocks = [both[size * i : size * (i + 1)] for i in range(4)]
    return [blocks[0]] + [exchange(block, FLIP_Z * i) for i, block in zip(Z_ORDER, blocks[1:])]


def block_places(me):
    out = []
    for other in (0, 1):
        core = (me >> 1 & 1) ^ other
        first, second = FLIP_X - 3 * core, FLIP_Y + 3 * core
        for b in (0, 1):
            for a in (0, 1):
                for i, z in enumerate((0,) + Z_ORDER):
                    owner = me ^ (other * FLIP_CORE + b * second + a * first + z * FLIP_Z)
                    out.append((other * 2 + b, a * 4 + i, owner))
    return out


def nn(left, right):
    return jnp.dot(left, right, preferred_element_type=F32)


def block_rows(owner, size=BLOCK):
    return pl.ds(pl.multiple_of(owner * size, size), size)


def load_blocks(me, pieces, columns, target):
    for piece, row, owner in block_places(me):
        target[block_rows(owner), :] = pieces[piece][row * BLOCK : (row + 1) * BLOCK, columns]


def store_blocks(me, source, targets, columns):
    for piece, row, owner in block_places(me):
        at = (piece % 2 * 8 + row) * BLOCK
        targets[piece // 2][at : at + BLOCK, columns] = source[block_rows(owner), :]


def normed_rows(value):
    centered = value - jnp.mean(value, -1, keepdims=True)
    inverse = lax.rsqrt(jnp.mean(centered * centered, -1, keepdims=True) + 1e-05)
    return centered * inverse, inverse


def norm_back_rows(upstream, normed, inverse, gain):
    scaled = upstream * gain
    first_mean = jnp.mean(scaled, -1, keepdims=True)
    second_mean = jnp.mean(scaled * normed, -1, keepdims=True)
    return inverse * (scaled - first_mean - normed * second_mean)


def column_sum(value):
    return jnp.sum(value, 0, keepdims=True)


def own_segments_of(index, segments):
    return jnp.where(index == 0, segments[:, :OWN], segments[:, OWN:]).astype(F32)


def key_segments_of(index, segments):
    near = jnp.where(index == 0, segments[:, OWN:KEYS], segments[:, OWN - WINDOW : OWN])
    return jnp.concatenate([own_segments_of(index, segments), near.astype(F32)], 1)


def spread(row):
    return jnp.broadcast_to(row, (TILE, row.shape[1])).T


def lane_half(shape, half):
    lanes = lax.broadcasted_iota(jnp.int32, shape, 1)
    return (lanes < HD) if half == 0 else (lanes >= HD)


def half_masks(value):
    keep, zero = lane_half(value.shape, 0), jnp.zeros_like(value)
    return jnp.concatenate([jnp.where(keep, value, zero), jnp.where(keep, zero, value)], 0)


def self_jobs(side):
    near, far = pl.multiple_of((1 - side) * 256, 256), pl.multiple_of(side * 256, 256)
    skip_near, skip_far = pl.multiple_of((1 - side) * TILE, TILE), pl.multiple_of(side * TILE, TILE)
    return [
        (pl.ds(near, 256), [(skip_near, 384), (OWN, WINDOW)], 256),
        (pl.ds(far, 256), [(skip_far, 384)], 256),
    ]


def attend(queries, pair_ref, mixed, log_rows, query_seg, key_row, jobs):
    for rows, spans, size in jobs:

        def keys_of(ref, lanes):
            parts = [ref[pl.ds(start, count), lanes] for start, count in spans]
            return parts[0] if len(parts) == 1 else jnp.concatenate(parts, 0)

        segments = [key_row[:, pl.ds(start, count)] for start, count in spans]
        segments = segments[0] if len(segments) == 1 else jnp.concatenate(segments, 1)
        same = jnp.concatenate([query_seg[rows, :]] * (segments.shape[1] // TILE), 1) == segments
        bias = jnp.where(same, 0.0, MASKED)
        lanes = lax.broadcasted_iota(jnp.int32, (size, TILE), 1)
        logs = jnp.zeros((size, TILE), F32)
        for pair in range(HEADS // 2):
            at = slice(pair * TILE, (pair + 1) * TILE)
            scores = against(half_masks(queries[rows, at]), keys_of(pair_ref, at))
            weights, scales = [], []
            for half in range(2):
                part = scores[half * size : (half + 1) * size] + bias
                top = jnp.max(part, -1, keepdims=True)
                part = jnp.exp(part - top)
                total = jnp.sum(part, -1, keepdims=True)
                weights.append(part.astype(BF16))
                scales.append(1.0 / total)
                logs = jnp.where(lanes == pair * 2 + half, top + jnp.log(total), logs)
            values = keys_of(pair_ref, slice(MODEL + pair * TILE, MODEL + (pair + 1) * TILE))
            out = nn(jnp.concatenate(weights, 0), values)
            keep = lane_half((size, TILE), 0)
            mixed[rows, at] = jnp.where(keep, out[:size] * scales[0], out[size:] * scales[1]).astype(BF16)
        log_rows[:, rows] = logs.T[:HEADS]


def head_dots(upstream, mixed):
    head = lax.broadcasted_iota(jnp.int32, (HEADS, MODEL), 1) // HD
    ones = (head == lax.broadcasted_iota(jnp.int32, (HEADS, MODEL), 0)).astype(F32)
    return lax.dot_general(
        ones, upstream.astype(F32) * mixed.astype(F32), (((1,), (1,)), ((), ())),
        precision=lax.Precision.HIGHEST, preferred_element_type=F32,
    )


def attend_back(
    queries, upstream, pair_ref, log_rows, dot_rows, query_row, key_seg, query_grad, pair_grad, pairs, jobs
):
    query_grad[...] = jnp.zeros_like(query_grad)
    for key_start, size, start, count in jobs:
        rows, across = pl.ds(key_start, size), pl.ds(start, count)
        same = jnp.concatenate([key_seg[rows, :]] * (count // TILE), 1) == query_row[:, across]
        bias = jnp.where(same, 0.0, MASKED)
        for pair in pairs:
            at, to = pair * TILE, (pair - pairs[0]) * TILE
            query = queries[across, at : at + TILE]
            grad = upstream[across, at : at + TILE]
            keys = half_masks(pair_ref[rows, at : at + TILE])
            values = half_masks(pair_ref[rows, MODEL + at : MODEL + at + TILE])
            scores, grads = against(keys, query), against(values, grad)
            weights, score_grads = [], []
            for half in range(2):
                head, part = pair * 2 + half, slice(half * size, (half + 1) * size)
                weight = jnp.exp(scores[part] + (bias - log_rows[head : head + 1, across]))
                score_grads.append((weight * (grads[part] - dot_rows[head : head + 1, across])).astype(BF16))
                weights.append(weight.astype(BF16))
            score_grad = jnp.concatenate(score_grads, 0)
            value_part = nn(jnp.concatenate(weights, 0), grad)
            key_part = nn(score_grad, query)
            query_grad[across, to : to + TILE] += transposed(score_grad, keys)
            keep = lane_half((size, TILE), 0)
            pair_grad[rows, to : to + TILE] = jnp.where(keep, key_part[:size], key_part[size:]).astype(BF16)
            to = to + len(pairs) * TILE
            pair_grad[rows, to : to + TILE] = jnp.where(keep, value_part[:size], value_part[size:]).astype(BF16)


def self_back_jobs(side):
    near = pl.multiple_of((1 - side) * 256, 256)
    return [(0, 256, 0, 384), (256, 256, TILE, 384), (OWN, WINDOW, near, 256)]


def pack_body(
    place, vectors, project, output, query, keyval, crossout, up, down, states, source,
    one, three, near, own_source, block, semaphores
):
    me, side = place[0], place[1]
    copies = [
        (project, one.at[:, :1536]),
        (output, one.at[:, 1664:2176]),
        (query, one.at[:, 2176:2688]),
        (keyval, one.at[:, 2688:3712]),
        (crossout, one.at[:, 3712:]),
        (down, three.at[64:]),
    ] + [
        (up.at[:, part * 512 : (part + 1) * 512], three.at[part * BLOCK : (part + 1) * BLOCK, :])
        for part in range(4)
    ] + [
        (states.at[pl.ds(pl.multiple_of((1 - side) * WINDOW, WINDOW), WINDOW), :], near.at[:WINDOW])
    ]
    copies = [pltpu.make_async_copy(*copy, semaphores.at[i]) for i, copy in enumerate(copies)]
    for copy in copies:
        copy.start()
    gap = jnp.zeros((HALF_SOURCE - source.shape[0], MODEL), F32)
    padded = jnp.concatenate([source[...].astype(F32), gap], 0).astype(BF16)
    own_source[...] = padded
    near[WINDOW:, :] = padded
    values = jnp.broadcast_to(vectors[...].astype(F32), (8, 256))
    lanes = lax.broadcasted_iota(jnp.int32, (8, TILE), 1)
    rows = lax.broadcasted_iota(jnp.int32, (8, TILE), 0)
    packed = jnp.zeros((8, TILE), F32)
    spot, wide = (me & 7) * 16, (me & 1) * 64
    for row in range(7):
        moved = pltpu.roll(values, spot + 256 - 16 * row, 1)[:, :TILE]
        inside = jnp.logical_and(lanes >= spot, lanes < spot + 16)
        packed = jnp.where(jnp.logical_and(rows == row, inside), moved, packed)
    moved = pltpu.roll(values, wide + 256 - 112, 1)[:, :TILE]
    inside = jnp.logical_and(lanes >= wide, lanes < wide + 64)
    packed = jnp.where(jnp.logical_and(rows == 7, inside), moved, packed)
    block[...] = jnp.concatenate([packed, jnp.zeros((8, TILE), F32)], 0).astype(BF16)
    last = pltpu.make_async_copy(block, one.at[:, 1536:1664], semaphores.at[len(copies)])
    last.start()
    for copy in copies + [last]:
        copy.wait()


def self_body(place, states, window, *refs):
    pieces, refs = refs[:4], refs[4:]
    queries, pair, lowered, vectors, up_bias, weight, weight_two, packed = refs
    me = place[0]
    load_blocks(me, pieces, slice(1536, 1664), packed)
    load_blocks(me, pieces, slice(0, 1536), weight)
    load_blocks(me, pieces, slice(1664, 4224), weight_two)
    for tile in range(4):
        total = jnp.zeros((8, TILE), F32)
        for i in range(8):
            total = total + packed[(tile * 8 + i) * BLOCK : (tile * 8 + i + 1) * BLOCK, :].astype(F32)[:8]
        vectors[:, tile * TILE : (tile + 1) * TILE] = total
    for tile in range(16):
        total = (
            packed[2 * tile * BLOCK : (2 * tile + 1) * BLOCK, :].astype(F32)
            + packed[(2 * tile + 1) * BLOCK : (2 * tile + 2) * BLOCK, :].astype(F32)
        )
        up_bias[:, tile * TILE : (tile + 1) * TILE] = total[7:8]
    gain, shift = vectors[1:2, :], vectors[2:3, :]
    for i in range(KEYS // TILE):
        rows = slice(i * TILE, (i + 1) * TILE)
        value = states[rows, :] if i < 4 else window[(i - 4) * TILE : (i - 3) * TILE, :]
        lowered[rows, :] = (normed_rows(value.astype(F32))[0] * gain + shift).astype(BF16)
    for i in range(KEYS // 256):
        rows = slice(i * 256, (i + 1) * 256)
        if i < 2:
            queries[rows, :] = (nn(lowered[rows, :], weight[:, :512]) .astype(BF16) * SCALE).astype(BF16)
        pair[rows, :] = nn(lowered[rows, :], weight[:, 512:]).astype(BF16)


def forward_body(
    place, segments, source_segments, states, own_source, other_source, vectors, weight, self_queries, self_pair,
    self_mixed, self_logs, after_self, lowered, queries, pair, mixed, logs, after_cross,
    query_seg, key_row, source_row, source,
):
    self_mix(place, segments, self_queries, self_pair, self_mixed, self_logs, query_seg, key_row)
    cross_lower(
        place, states, own_source, other_source, self_mixed, vectors, after_self, lowered, queries, pair, weight, source
    )
    source_row[...] = source_segments[...].astype(F32)
    attend(queries, pair, mixed, logs, query_seg, source_row, [(pl.ds(0, OWN), [(0, SOURCES)], OWN)])
    for i in range(2):
        rows = slice(i * 256, (i + 1) * 256)
        after_cross[rows, :] = after_self[rows, :] + nn(mixed[rows, :], weight[:, 2048:])


def self_mix(place, segments, queries, pair, mixed, log_rows, query_seg, key_row):
    query_seg[...] = spread(own_segments_of(place[1], segments[...]))
    key_row[...] = key_segments_of(place[1], segments[...])
    attend(queries, pair, mixed, log_rows, query_seg, key_row, self_jobs(place[1]))


def cross_lower(
    place, states, own_source, other_source, self_mixed, vectors, after_self, lowered, queries, pair, weight, source
):
    side = place[1]
    source[:HALF_SOURCE, :] = jnp.where(side == 0, own_source[...], other_source[...])
    source[HALF_SOURCE:, :] = jnp.where(side == 0, other_source[...], own_source[...])
    gain, shift = vectors[3:4, :], vectors[4:5, :]
    pair[...] = nn(source[...], weight[:, 1024:2048]).astype(BF16)
    for i in range(2):
        rows = slice(i * 256, (i + 1) * 256)
        value = states[rows, :].astype(F32) + nn(self_mixed[rows, :], weight[:, :512])
        after_self[rows, :] = value
        lowered[rows, :] = (normed_rows(value)[0] * gain + shift).astype(BF16)
        queries[rows, :] = (nn(lowered[rows, :], weight[:, 512:1024]).astype(BF16) * SCALE).astype(BF16)


CHUNK = 512


def feed_body(place, after_cross, output_grad, vectors, up_bias, *refs):
    pieces, refs = refs[:4], refs[4:]
    (
        total, back, kept, sent, bias_sums, ups, downs, lowered, flipped, up_grads, down_grads,
    ) = refs
    me = place[0]
    places = block_places(me)

    def chunk_of(z):
        return pl.multiple_of(((me >> 3) ^ z) * CHUNK, CHUNK)

    gain, shift = vectors[5:6, :], vectors[6:7, :]
    for i in range(4):
        rows = slice(i * TILE, (i + 1) * TILE)
        low = (normed_rows(after_cross[rows, :])[0] * gain + shift).astype(BF16)
        lowered[rows, :] = low
    flipped[...] = lowered[...].T
    grad_low = output_grad[...]
    for i, z in enumerate((0,) + Z_ORDER):
        at = pl.ds(chunk_of(z), CHUNK)
        z_row = pl.multiple_of(((me >> 3) ^ z) * BLOCK, BLOCK)
        up, down, up_grad, down_grad = ups.at[i], downs.at[i], up_grads.at[i], down_grads.at[i]
        for piece, row, owner in places:
            up[block_rows(owner), :] = pieces[piece][pl.ds(row * 128 + z_row, BLOCK), :]
            if row % 4 == i:
                down[pl.ds(pl.multiple_of((owner & 7) * 64, 64), 64), :] = pieces[piece][
                    row * 128 + 64 : (row + 1) * 128, :
                ]
        hidden = nn(lowered[...], up[...]) + up_bias[:, at]
        square = hidden * hidden
        inner = 0.7978845608028654 * hidden * (1.0 + 0.044715 * square)
        curve = jnp.tanh(inner)
        half = 0.5 * (1.0 + curve)
        activated = (hidden * half).astype(BF16)
        slope = half + (0.5 * 0.7978845608028654) * hidden * (1.0 - curve * curve) * (
            1.0 + (3 * 0.044715) * square
        )
        down_grad[...] = transposed(activated, grad_low).astype(BF16)
        for piece, row, owner in places:
            if row % 4 == i:
                to = (piece % 2 * 8 + row) * 128
                (kept, sent)[piece // 2][to + 64 : to + 128, :] = down_grad[
                    pl.ds(pl.multiple_of((owner & 7) * 64, 64), 64), :
                ]
        grad_hidden = (against(grad_low, down[...]) * slope).astype(BF16)
        bias_sums[:, at] = column_sum(grad_hidden.astype(F32))
        up_grad[...] = nn(flipped[...], grad_hidden).astype(BF16)
        for piece, row, owner in places:
            to = (piece % 2 * 8 + row) * 128
            (kept, sent)[piece // 2][pl.ds(to + z_row, BLOCK), :] = up_grad[block_rows(owner), :]
        if i:
            total[...] += nn(activated, down[...])
            back[...] += against(grad_hidden, up[...])
        else:
            total[...] = nn(activated, down[...])
            back[...] = against(grad_hidden, up[...])


def feed_last_body(place, after_cross, output_grad, vectors, total, back, layer_out, after_grad, sums):
    gain = vectors[5:6, :]
    gain_sum, shift_sum, bias_sum = (jnp.zeros((1, MODEL), F32) for _ in range(3))
    for i in range(4):
        rows = slice(i * TILE, (i + 1) * TILE)
        value, grad = after_cross[rows, :], output_grad[rows, :].astype(F32)
        layer_out[rows, :] = (value + total[rows, :] + vectors[0:1, :]).astype(BF16)
        normed, inverse = normed_rows(value)
        upstream = back[rows, :]
        after_grad[rows, :] = grad + norm_back_rows(upstream, normed, inverse, gain)
        gain_sum, shift_sum = gain_sum + column_sum(upstream * normed), shift_sum + column_sum(upstream)
        bias_sum = bias_sum + column_sum(grad)
    zero = jnp.zeros((1, MODEL), F32)
    sums[...] = jnp.concatenate([bias_sum, zero, zero, zero, zero, gain_sum, shift_sum, zero], 0)


def cross_back_body(
    place, segments, source_segments, own_source, other_source, queries, pair, mixed, log_rows, after_grad, weight,
    asked, source_own, source_send, grads, upstream, query_grad, pair_grad, source, key_seg, query_row,
):
    side = place[1]
    key_seg[...] = spread(source_segments[...].astype(F32))
    query_row[...] = own_segments_of(side, segments[...])
    source[:HALF_SOURCE, :] = jnp.where(side == 0, own_source[...], other_source[...])
    source[HALF_SOURCE:, :] = jnp.where(side == 0, other_source[...], own_source[...])
    grad_low = after_grad[...].astype(BF16)
    upstream[...] = against(grad_low, weight[:, 2048:]).astype(BF16)
    dot_rows = head_dots(upstream[...], mixed[...])
    grads[:, :512] = transposed(mixed[...], grad_low).astype(BF16)
    attend_back(
        queries, upstream, pair, log_rows, dot_rows, query_row, key_seg, query_grad, pair_grad, (0, 1, 2, 3),
        [(0, SOURCES, 0, OWN)],
    )
    asked[...] = (query_grad[...] * SCALE).astype(BF16)
    grads[:, 512:] = transposed(source[...], pair_grad[...]).astype(BF16)
    back = against(pair_grad[...], weight[:, 1024:2048])
    first, second = back[:HALF_SOURCE], back[HALF_SOURCE:]
    source_own[...] = jnp.where(side == 0, first, second)
    source_send[...] = jnp.where(side == 0, second, first).astype(BF16)


def cross_weight_body(
    place, after_self, lowered, self_mixed, after_grad, asked, vectors, sums, weight, some_grads, *refs
):
    self_grad, upstream, dot_rows, kept, sent, new_sums, grads = refs
    me = place[0]
    store_blocks(me, some_grads, (kept, sent), slice(0, 1536))
    gain = vectors[3:4, :]
    gain_sum, shift_sum = jnp.zeros((1, MODEL), F32), jnp.zeros((1, MODEL), F32)
    for i in range(2):
        rows = slice(i * 256, (i + 1) * 256)
        normed, inverse = normed_rows(after_self[rows, :])
        up = against(asked[rows, :], weight[:, 512:1024])
        self_grad[rows, :] = after_grad[rows, :] + norm_back_rows(up, normed, inverse, gain)
        gain_sum, shift_sum = gain_sum + column_sum(up * normed), shift_sum + column_sum(up)
    grads[:, :512] = transposed(lowered[...], asked[...]).astype(BF16)
    grad_low = self_grad[...].astype(BF16)
    grads[:, 512:] = transposed(self_mixed[...], grad_low).astype(BF16)
    store_blocks(me, grads, (kept, sent), slice(1536, 2560))
    upstream[...] = against(grad_low, weight[:, :512]).astype(BF16)
    dot_rows[...] = head_dots(upstream[...], self_mixed[...])
    zero = jnp.zeros((1, MODEL), F32)
    new_sums[...] = sums[...] + jnp.concatenate(
        [zero, zero, zero, gain_sum, shift_sum, zero, zero, zero], 0
    )


def self_back_body(
    place, segments, states, window, lowered, queries, pair, log_rows, upstream, dot_rows, weight, sums, bias_sums,
    source_send, own_back, near_back, kept, sent, query_grad, pair_grad, grads, key_seg, query_row,
):
    near_back[WINDOW:, :] = source_send[...]
    key_seg[...] = spread(key_segments_of(place[1], segments[...]))
    query_row[...] = own_segments_of(place[1], segments[...])
    attend_back(
        queries, upstream, pair, log_rows, dot_rows, query_row, key_seg, query_grad, pair_grad, (0, 1, 2, 3),
        self_back_jobs(place[1]),
    )
    asked = (query_grad[...] * SCALE).astype(BF16)
    grads[:, :MODEL] = transposed(lowered[:OWN, :], asked).astype(BF16)
    grads[:, MODEL:1536] = transposed(lowered[...], pair_grad[...]).astype(BF16)
    gain_sum, shift_sum = jnp.zeros((1, MODEL), F32), jnp.zeros((1, MODEL), F32)
    for i in range(3):
        rows = slice(i * 256, (i + 1) * 256)
        part = against(pair_grad[rows, :], weight[:, MODEL:])
        if i < 2:
            part = part + against(asked[rows, :], weight[:, :MODEL])
            own_back[rows, :] = part
            value = states[rows, :]
        else:
            near_back[:WINDOW, :] = part.astype(BF16)
            value = window[...]
        normed = normed_rows(value.astype(F32))[0]
        gain_sum, shift_sum = gain_sum + column_sum(part * normed), shift_sum + column_sum(part)
    zero = jnp.zeros((1, MODEL), F32)
    sums = sums[...] + jnp.concatenate([zero, gain_sum, shift_sum, zero, zero, zero, zero, zero], 0)
    last = lax.broadcasted_iota(jnp.int32, (8, TILE), 0) == 7
    for device in range(32):
        tile, wide = device // 8 * TILE, device // 2 * TILE
        value = jnp.where(last, bias_sums[:, wide : wide + TILE], sums[:, tile : tile + TILE])
        high = value.astype(BF16).astype(F32)
        grads[device * BLOCK : (device + 1) * BLOCK, 1536:] = jnp.concatenate([high, value - high], 0).astype(BF16)
    store_blocks(place[0], grads, (kept, sent), slice(0, 1664))


def target_body(place, back, came, states, self_grad, vectors, out):
    gain = vectors[1:2, :]
    for i in range(4):
        rows = slice(i * TILE, (i + 1) * TILE)
        here = (i < 2) == (place[1] == 1)
        extra = came[(i % 2) * TILE : (i % 2 + 1) * TILE, :].astype(F32)
        upstream = back[rows, :] + jnp.where(here, extra, 0.0)
        normed, inverse = normed_rows(states[rows, :].astype(F32))
        out[rows, :] = self_grad[rows, :] + norm_back_rows(upstream, normed, inverse, gain)


def finish_body(place, *refs):
    feed, cross, last, outs = refs[:4], refs[4:8], refs[8:12], refs[12:]
    project, output, query, keyval, crossout, up, down, *small = outs
    me = place[0]

    def total(parts, begin, end, rows=slice(None)):
        value = parts[0][rows, begin:end].astype(F32)
        for part in parts[1:]:
            value = value + part[rows, begin:end].astype(F32)
        return value

    for part in range(4):
        rows = slice(part * BLOCK, (part + 1) * BLOCK)
        up[:, part * 512 : (part + 1) * 512] = total(feed, 0, MODEL, rows)
    down[...] = total(feed, 0, MODEL, slice(64, 128))
    crossout[...] = total(cross, 0, 512)
    keyval[...] = total(cross, 512, 1536)
    query[...] = total(cross, 1536, 2048)
    output[...] = total(cross, 2048, 2560)
    project[...] = total(last, 0, 1536)
    value = total(last, 1536, 1664)
    value = value[:8] + value[8:]
    narrow = pltpu.roll(value, (TILE - (me & 7) * 16) & 127, 1)
    wide = pltpu.roll(value, (TILE - (me & 1) * 64) & 127, 1)
    for row in range(7):
        small[row][...] = narrow[row : row + 1, :16]
    small[7][...] = wide[7:8, :64]


def shape_of(*shape, dtype=BF16):
    return jax.ShapeDtypeStruct(shape, dtype)


VMEM_SPEC = pl.BlockSpec(memory_space=pltpu.VMEM)
ANY_SPEC = pl.BlockSpec(memory_space=pl.ANY)
HBM_SPEC = pl.BlockSpec(memory_space=pltpu.HBM)
SMEM_SPEC = pl.BlockSpec(memory_space=pltpu.SMEM)


def call(body, name, place, inputs, pieces, outs, scratch, flops, any_outs=(), any_ins=(), vmem=40):
    return pl.pallas_call(
        body,
        name=name,
        out_shape=outs,
        in_specs=[SMEM_SPEC]
        + [HBM_SPEC if i in any_ins else VMEM_SPEC for i in range(len(inputs))]
        + [VMEM_SPEC] * len(pieces),
        out_specs=[ANY_SPEC if i in any_outs else VMEM_SPEC for i in range(len(outs))],
        scratch_shapes=scratch,
        compiler_params=pltpu.CompilerParams(vmem_limit_bytes=vmem * 2**20),
        cost_estimate=pl.CostEstimate(flops=flops, bytes_accessed=4 * 2**20, transcendentals=0),
    )(place, *inputs, *pieces)


def fast_device(
    target_states, source_states, target_segments, source_segments, output_grad, self_project,
    self_output, cross_query, cross_keyval, cross_output, hidden_up, hidden_bias, hidden_down,
    output_bias, first_gain, first_shift, second_gain, second_shift, third_gain, third_shift,
):
    vmem, dma = pltpu.VMEM, pltpu.SemaphoreType.DMA
    side = lax.axis_index("seq")
    place = jnp.stack([lax.axis_index("rows") * 2 + side, side]).astype(jnp.int32)
    states, grad = target_states[0], output_grad[0]
    small = jnp.pad(hidden_bias, (112, 80))
    for i, vector in enumerate(
        (output_bias, first_gain, first_shift, second_gain, second_shift, third_gain, third_shift)
    ):
        small = small + jnp.pad(vector, (16 * i, 240 - 16 * i))
    small = small.reshape(1, 256)
    one, three, near, own_source = call(
        pack_body, "pack", place,
        [
            small, self_project, self_output, cross_query, cross_keyval, cross_output, hidden_up, hidden_down, states,
            source_states[0],
        ],
        [],
        [
            shape_of(16, 4224), shape_of(128, MODEL), shape_of(WINDOW + HALF_SOURCE, MODEL),
            shape_of(HALF_SOURCE, MODEL),
        ],
        [vmem((BLOCK, TILE), BF16), dma((12,))], 1000000, any_ins=range(1, 9), vmem=60,
    )
    parts = along_z(one)
    near = exchange(near, FLIP_Y)
    one = join(one, *parts)
    one = tied(one, near)
    came = exchange_side(one, 0)
    three, one = tied((three, one), came)
    parts_three = along_z(three)
    one = join(one, came)
    one_core = exchange(one, FLIP_CORE)
    other = exchange_side(one, 1)
    other = tied(other, parts_three)
    window, other_source = near[:WINDOW], near[WINDOW:]
    pieces_one = [one, other, one_core, exchange(other, FLIP_CORE)]
    three = join(three, *parts_three)
    came = exchange_side(three, 0)
    half = source_states.shape[1]
    gap = jnp.full((1, HALF_SOURCE - half), -1, jnp.int32)
    source_seg = jnp.concatenate([source_segments[:, :half], gap, source_segments[:, half:], gap], 1)

    queries, pair, lowered, vectors, up_bias, weight_one, weight_two = call(
        self_body, "self_lower", place, [states, window], pieces_one,
        [
            shape_of(OWN, MODEL), shape_of(KEYS, 2 * MODEL), shape_of(KEYS, MODEL), shape_of(8, MODEL, dtype=F32),
            shape_of(1, FEED, dtype=F32), shape_of(MODEL, 1536), shape_of(MODEL, 2560),
        ],
        [vmem((MODEL, TILE), BF16)], 5000000000,
    )
    came, three = tied((came, three), queries)
    three = join(three, came)
    three_core = exchange(three, FLIP_CORE)
    other = exchange_side(three, 1)
    queries = tied(queries, three)
    mixed, logs, after_self, lowered_two, queries_two, pair_two, mixed_two, logs_two, after_cross = call(
        forward_body, "forward", place,
        [
            target_segments, source_seg, states, own_source, other_source, vectors, weight_two, queries, pair,
        ],
        [],
        [
            shape_of(OWN, MODEL), shape_of(HEADS, OWN, dtype=F32), shape_of(OWN, MODEL, dtype=F32), shape_of(OWN, MODEL),
            shape_of(OWN, MODEL), shape_of(SOURCES, 2 * MODEL), shape_of(OWN, MODEL), shape_of(HEADS, OWN, dtype=F32),
            shape_of(OWN, MODEL, dtype=F32),
        ],
        [
            vmem((OWN, TILE), F32), vmem((1, KEYS), F32), vmem((1, SOURCES), F32), vmem((SOURCES, MODEL), BF16),
        ],
        20000000000,
    )
    three_core, other = tied((three_core, other), after_cross)
    pieces_three = [three, other, three_core, exchange(other, FLIP_CORE)]
    total, back, feed_kept, feed_sent, bias_sums = call(
        feed_body, "feed", place, [after_cross, grad, vectors, up_bias], pieces_three,
        [shape_of(OWN, MODEL, dtype=F32)] * 2 + [shape_of(2048, MODEL)] * 2 + [shape_of(1, FEED, dtype=F32)],
        [
            vmem((4, MODEL, CHUNK), BF16), vmem((4, CHUNK, MODEL), BF16), vmem((OWN, MODEL), BF16),
            vmem((MODEL, OWN), BF16), vmem((4, MODEL, CHUNK), BF16), vmem((4, CHUNK, MODEL), BF16),
        ],
        10000000000,
    )
    feed_came = exchange(feed_sent, FLIP_CORE)
    layer_out, after_grad, sums = call(
        feed_last_body, "feed_last", place, [after_cross, grad, vectors, total, back], [],
        [shape_of(OWN, MODEL), shape_of(OWN, MODEL, dtype=F32), shape_of(8, MODEL, dtype=F32)], [], 2000000000,
    )
    feed_came = tied(feed_came, after_grad)
    feed_sent, feed_kept = add_halves(feed_kept, feed_came)
    after_grad = tied(after_grad, feed_sent)
    feed_came = exchange_side(feed_sent, 1)
    asked, source_own, source_send, some_grads = call(
        cross_back_body, "cross_backward", place,
        [
            target_segments, source_seg, own_source, other_source, queries_two, pair_two, mixed_two, logs_two,
            after_grad, weight_two,
        ],
        [],
        [
            shape_of(OWN, MODEL), shape_of(HALF_SOURCE, MODEL, dtype=F32), shape_of(HALF_SOURCE, MODEL),
            shape_of(MODEL, 1536),
        ],
        [
            vmem((OWN, MODEL), BF16), vmem((OWN, MODEL), F32), vmem((SOURCES, 2 * MODEL), BF16),
            vmem((SOURCES, MODEL), BF16), vmem((SOURCES, TILE), F32), vmem((1, OWN), F32),
        ],
        10000000000,
    )
    self_grad, upstream, dot_rows, cross_kept, cross_sent, sums = call(
        cross_weight_body, "cross_weights", place,
        [after_self, lowered_two, mixed, after_grad, asked, vectors, sums, weight_two, some_grads], [],
        [shape_of(OWN, MODEL, dtype=F32), shape_of(OWN, MODEL), shape_of(HEADS, OWN, dtype=F32)]
        + [shape_of(256, 2560)] * 2 + [shape_of(8, MODEL, dtype=F32)],
        [vmem((MODEL, 1024), BF16)], 6000000000,
    )
    cross_came = exchange(cross_sent, FLIP_CORE)
    feed_came = tied(feed_came, upstream)
    feed_sent, feed_kept = add_halves(feed_kept, feed_came)
    feed_came = exchange_side(feed_sent, 0)
    cross_came = tied(cross_came, feed_sent)
    cross_sent, cross_kept = add_halves(cross_kept, cross_came)
    cross_came = exchange_side(cross_sent, 1)
    upstream = tied(upstream, cross_sent)
    own_back, near_back, last_kept, last_sent = call(
        self_back_body, "self_backward", place,
        [
            target_segments, states, window, lowered, queries, pair, logs, upstream, dot_rows, weight_one, sums,
            bias_sums, source_send,
        ],
        [],
        [shape_of(OWN, MODEL, dtype=F32), shape_of(WINDOW + HALF_SOURCE, MODEL)] + [shape_of(256, 1664)] * 2,
        [
            vmem((OWN, MODEL), F32), vmem((KEYS, 2 * MODEL), BF16), vmem((MODEL, 1664), BF16), vmem((KEYS, TILE), F32),
            vmem((1, OWN), F32),
        ],
        16000000000,
    )
    last_came = exchange(last_sent, FLIP_CORE)
    cross_came, feed_came = tied((cross_came, feed_came), own_back)
    cross_sent, cross_kept = add_halves(cross_kept, cross_came)
    last_sent, last_kept = add_halves(last_kept, last_came)
    last_came, cross_came = exchange_side(last_sent, 1), exchange_side(cross_sent, 0)
    feed_came = tied(feed_came, last_sent)
    feed = z_blocks(feed_kept + feed_came)
    last_came = tied(last_came, feed[0])
    last_sent, last_kept = add_halves(last_kept, last_came)
    last_came = exchange_side(last_sent, 0)
    cross_came, feed, near_back = tied((cross_came, feed, near_back), last_sent)
    cross_kept = tied(cross_kept, feed)
    cross = z_blocks(cross_kept + cross_came)
    near_came = exchange(near_back, FLIP_Y)
    last_came = tied(last_came, cross[0])
    last = z_blocks(last_kept + last_came)
    came, source_came = near_came[:WINDOW], near_came[WINDOW:]
    grad_source = source_own[:half] + source_came[:half].astype(F32)
    (grad_target,) = call(
        target_body, "target_grad", place, [own_back, came, states, self_grad, vectors], [],
        [shape_of(OWN, MODEL, dtype=F32)], [], 1000000,
    )
    project, output, query, keyval, crossout, up, down, *small = call(
        finish_body, "finish", place, feed + cross + last, [],
        [
            shape_of(16, 1536, dtype=F32), shape_of(16, 512, dtype=F32), shape_of(16, 512, dtype=F32),
            shape_of(16, 1024, dtype=F32), shape_of(16, 512, dtype=F32), shape_of(16, 2048, dtype=F32),
            shape_of(64, 512, dtype=F32),
        ]
        + [shape_of(1, 16, dtype=F32)] * 7 + [shape_of(1, 64, dtype=F32)],
        [], 1000000,
    )
    *rows, up_sum = [row[0] for row in small]
    return (
        layer_out[None], grad_target[None], grad_source[None], project, output, query, keyval, crossout, up,
        up_sum, down, *rows,
    )


def specs():
    in_specs = (
        P("rows", "seq", None),
        P("rows", "seq", None),
        P("rows", None),
        P("rows", None),
        P("rows", "seq", None),
        P(("rows", "seq"), None),
        P(("rows", "seq"), None),
        P(("rows", "seq"), None),
        P(("rows", "seq"), None),
        P(("rows", "seq"), None),
        P(("rows", "seq"), None),
        P(("rows", "seq")),
        P(("rows", "seq"), None),
        P(("rows", "seq")),
        P(("rows", "seq")),
        P(("rows", "seq")),
        P(("rows", "seq")),
        P(("rows", "seq")),
        P(("rows", "seq")),
        P(("rows", "seq")),
    )
    out_specs = (
        P("rows", "seq", None),
        P("rows", "seq", None),
        P("rows", "seq", None),
        P(("rows", "seq"), None),
        P(("rows", "seq"), None),
        P(("rows", "seq"), None),
        P(("rows", "seq"), None),
        P(("rows", "seq"), None),
        P(("rows", "seq"), None),
        P(("rows", "seq")),
        P(("rows", "seq"), None),
        P(("rows", "seq")),
        P(("rows", "seq")),
        P(("rows", "seq")),
        P(("rows", "seq")),
        P(("rows", "seq")),
        P(("rows", "seq")),
        P(("rows", "seq")),
    )
    return in_specs, out_specs


def solution(mesh):
    in_specs, out_specs = specs()
    fast = mesh.shape["rows"] == 16 and mesh.shape["seq"] == 2
    return jax.shard_map(
        fast_device if fast else general_device,
        mesh=mesh, in_specs=in_specs, out_specs=out_specs, check_vma=False,
    )
```

```python
import jax
import jax.numpy as jnp
from jax import lax
from jax.experimental import pallas as pl
from jax.experimental.pallas import tpu as pltpu
from jax.sharding import PartitionSpec as P

HEADS = 8
HD = 64


def layer_norm(value, gain, shift):
    row_mean = jnp.mean(value, -1, keepdims=True)
    centered = value - row_mean
    variance = jnp.mean(centered * centered, -1, keepdims=True)
    inverse = lax.rsqrt(variance + 1e-05)
    normed = centered * inverse
    return (normed * gain + shift, normed, inverse)


def norm_back(upstream, normed, inverse, gain):
    scaled = upstream * gain
    first_mean = jnp.mean(scaled, -1, keepdims=True)
    second_mean = jnp.mean(scaled * normed, -1, keepdims=True)
    grad_input = inverse * (scaled - first_mean - normed * second_mean)
    return (grad_input, jnp.sum(upstream * normed, 0), jnp.sum(upstream, 0))


def matmul(left, right):
    return jnp.dot(left, right, preferred_element_type=jnp.float32)


def transposed(left, right):
    return lax.dot_general(
        left, right, (((0,), (0,)), ((), ())), preferred_element_type=jnp.float32
    )


def against(left, right):
    return lax.dot_general(
        left, right, (((1,), (1,)), ((), ())), preferred_element_type=jnp.float32
    )


def head_split(value):
    return value.reshape(value.shape[0], HEADS, HD)


def head_join(value):
    return value.reshape(value.shape[0], HEADS * HD)


def scores_of(queries, key_rows, query_seg, key_seg):
    raw_scores = jnp.einsum(
        "qhd,khd->hqk", queries, key_rows, preferred_element_type=jnp.float32
    ) * HD ** (-0.5)
    same_seg = (query_seg[:, None] == key_seg[None, :])[None]
    return (raw_scores, same_seg)


def block_weights(queries, key_rows, query_seg, key_seg, log_total):
    raw_scores, same_seg = scores_of(queries, key_rows, query_seg, key_seg)
    return jnp.where(same_seg, jnp.exp(raw_scores - log_total[..., None]), 0.0)


def log_totals(queries, key_blocks, seg_blocks, query_seg):

    def log_advance(carry, inputs_now):
        row_max, row_total = carry
        key_rows, key_seg = inputs_now
        raw_scores, same_seg = scores_of(queries, key_rows, query_seg, key_seg)
        masked = jnp.where(same_seg, raw_scores, -1000000000.0)
        new_max = jnp.maximum(row_max, jnp.max(masked, -1))
        shifted = jnp.where(same_seg, jnp.exp(masked - new_max[..., None]), 0.0)
        return ((new_max, row_total * jnp.exp(row_max - new_max) + jnp.sum(shifted, -1)), None)

    start = (
        jnp.full((HEADS, queries.shape[0]), -1000000000.0, jnp.float32),
        jnp.zeros((HEADS, queries.shape[0]), jnp.float32),
    )
    (row_max, row_total), unused = lax.scan(log_advance, start, (key_blocks, seg_blocks))
    return row_max + jnp.log(row_total)


def weighted_sum(queries, key_blocks, value_blocks, seg_blocks, query_seg, log_total):

    def weighted_advance(carry, inputs_now):
        key_rows, value_rows, key_seg = inputs_now
        weights = block_weights(queries, key_rows, query_seg, key_seg, log_total).astype(
            jnp.bfloat16
        )
        return (
            carry
            + jnp.einsum("hqk,khd->qhd", weights, value_rows, preferred_element_type=jnp.float32),
            None,
        )

    total, unused = lax.scan(
        weighted_advance,
        jnp.zeros(queries.shape, jnp.float32),
        (key_blocks, value_blocks, seg_blocks),
    )
    return total


def grad_dots(queries, grad_heads, key_blocks, value_blocks, seg_blocks, query_seg, log_total):

    def grad_advance(carry, inputs_now):
        key_rows, value_rows, key_seg = inputs_now
        weights = block_weights(queries, key_rows, query_seg, key_seg, log_total)
        grad_weights = jnp.einsum(
            "qhd,khd->hqk", grad_heads, value_rows, preferred_element_type=jnp.float32
        )
        return (carry + jnp.sum(weights * grad_weights, -1), None)

    start = jnp.zeros((HEADS, queries.shape[0]), jnp.float32)
    total, unused = lax.scan(grad_advance, start, (key_blocks, value_blocks, seg_blocks))
    return total


def query_grads(
    queries, grad_heads, key_blocks, value_blocks, seg_blocks, query_seg, log_total, row_dots
):
    score_scale = HD ** (-0.5)

    def query_advance(carry, inputs_now):
        key_rows, value_rows, key_seg = inputs_now
        weights = block_weights(queries, key_rows, query_seg, key_seg, log_total)
        grad_weights = jnp.einsum(
            "qhd,khd->hqk", grad_heads, value_rows, preferred_element_type=jnp.float32
        )
        grad_scores = (weights * (grad_weights - row_dots[..., None])).astype(jnp.bfloat16)
        carry = (
            carry
            + jnp.einsum("hqk,khd->qhd", grad_scores, key_rows, preferred_element_type=jnp.float32)
            * score_scale
        )
        grad_keys = (
            jnp.einsum("hqk,qhd->khd", grad_scores, queries, preferred_element_type=jnp.float32)
            * score_scale
        )
        grad_values = jnp.einsum(
            "hqk,qhd->khd",
            weights.astype(jnp.bfloat16),
            grad_heads,
            preferred_element_type=jnp.float32,
        )
        return (carry, jnp.concatenate([head_join(grad_keys), head_join(grad_values)], 1))

    return lax.scan(
        query_advance, jnp.zeros(queries.shape, jnp.float32), (key_blocks, value_blocks, seg_blocks)
    )


def general_device(
    target_states,
    source_states,
    target_segments,
    source_segments,
    output_grad,
    self_project,
    self_output,
    cross_query,
    cross_keyval,
    cross_output,
    hidden_up,
    hidden_bias,
    hidden_down,
    output_bias,
    first_gain,
    first_shift,
    second_gain,
    second_shift,
    third_gain,
    third_shift,
):
    (
        full_project,
        full_output,
        full_query,
        full_keyval,
        full_crossout,
        full_up,
        full_upbias,
        full_down,
        full_downbias,
        gain_one,
        shift_one,
        gain_two,
        shift_two,
        gain_three,
        shift_three,
    ) = (
        lax.all_gather(self_project, ("rows", "seq"), axis=0, tiled=True),
        lax.all_gather(self_output, ("rows", "seq"), axis=0, tiled=True),
        lax.all_gather(cross_query, ("rows", "seq"), axis=0, tiled=True),
        lax.all_gather(cross_keyval, ("rows", "seq"), axis=0, tiled=True),
        lax.all_gather(cross_output, ("rows", "seq"), axis=0, tiled=True),
        lax.all_gather(hidden_up, ("rows", "seq"), axis=0, tiled=True),
        lax.all_gather(hidden_bias, ("rows", "seq"), axis=0, tiled=True),
        lax.all_gather(hidden_down, ("rows", "seq"), axis=0, tiled=True),
        lax.all_gather(output_bias, ("rows", "seq"), axis=0, tiled=True),
        lax.all_gather(first_gain, ("rows", "seq"), axis=0, tiled=True),
        lax.all_gather(first_shift, ("rows", "seq"), axis=0, tiled=True),
        lax.all_gather(second_gain, ("rows", "seq"), axis=0, tiled=True),
        lax.all_gather(second_shift, ("rows", "seq"), axis=0, tiled=True),
        lax.all_gather(third_gain, ("rows", "seq"), axis=0, tiled=True),
        lax.all_gather(third_shift, ("rows", "seq"), axis=0, tiled=True),
    )
    gain_one = gain_one.astype(jnp.float32)
    gain_two = gain_two.astype(jnp.float32)
    gain_three = gain_three.astype(jnp.float32)
    score_scale = HD ** (-0.5)
    states = target_states[0].astype(jnp.float32)
    local_rows = states.shape[0]
    model_width = states.shape[1]
    seq_count = lax.axis_size("seq")
    row_segments = target_segments[0]
    seq_length = row_segments.shape[0]
    own_segments = lax.dynamic_slice_in_dim(
        row_segments, lax.axis_index("seq") * local_rows, local_rows
    )
    block_rows = max(1, min(seq_count, 512 // local_rows)) * local_rows
    block_count = seq_length // block_rows
    seg_blocks = row_segments.reshape(block_count, block_rows)
    normed_value, normed_one, inverse_one = layer_norm(
        states, gain_one, shift_one.astype(jnp.float32)
    )
    lowered_one = normed_value.astype(jnp.bfloat16)
    projected = matmul(lowered_one, full_project).astype(jnp.bfloat16)
    query_flat = projected[:, :model_width]
    key_local = projected[:, model_width : 2 * model_width]
    value_local = projected[:, 2 * model_width :]
    queries = head_split(query_flat)
    key_all, value_all = (
        lax.all_gather(key_local, "seq", axis=0, tiled=True),
        lax.all_gather(value_local, "seq", axis=0, tiled=True),
    )
    key_blocks = key_all.reshape(block_count, block_rows, HEADS, HD)
    value_blocks = value_all.reshape(block_count, block_rows, HEADS, HD)
    log_total = log_totals(queries, key_blocks, seg_blocks, own_segments)
    self_mixed = head_join(
        weighted_sum(queries, key_blocks, value_blocks, seg_blocks, own_segments, log_total)
    ).astype(jnp.bfloat16)
    after_self = states + matmul(self_mixed, full_output)
    normed_value, normed_two, inverse_two = layer_norm(
        after_self, gain_two, shift_two.astype(jnp.float32)
    )
    lowered_two = normed_value.astype(jnp.bfloat16)
    cross_asked = matmul(lowered_two, full_query).astype(jnp.bfloat16)
    source_low = source_states[0]
    source_all = lax.all_gather(source_low, "seq", axis=0, tiled=True)
    key_value = matmul(source_all, full_keyval).astype(jnp.bfloat16)
    cross_key_heads = head_split(key_value[:, :model_width])
    cross_value_heads = head_split(key_value[:, model_width:])
    asked_heads = head_split(cross_asked)
    raw_scores, same_seg = scores_of(asked_heads, cross_key_heads, own_segments, source_segments[0])
    cross_probs = jax.nn.softmax(jnp.where(same_seg, raw_scores, -1000000000.0), axis=-1)
    cross_mixed = head_join(
        jnp.einsum(
            "hqk,khd->qhd",
            cross_probs.astype(jnp.bfloat16),
            cross_value_heads,
            preferred_element_type=jnp.float32,
        )
    ).astype(jnp.bfloat16)
    after_cross = after_self + matmul(cross_mixed, full_crossout)
    normed_value, normed_three, inverse_three = layer_norm(
        after_cross, gain_three, shift_three.astype(jnp.float32)
    )
    lowered_three = normed_value.astype(jnp.bfloat16)
    hidden = matmul(lowered_three, full_up) + full_upbias.astype(jnp.float32)
    activated = jax.nn.gelu(hidden).astype(jnp.bfloat16)
    layer_out = after_cross + matmul(activated, full_down) + full_downbias.astype(jnp.float32)
    grad_low = output_grad[0]
    out_grad = grad_low.astype(jnp.float32)
    grad_down = transposed(activated, grad_low)
    grad_downbias = jnp.sum(out_grad, 0)
    grad_act = against(grad_low, full_down)
    grad_hidden = jax.vjp(jax.nn.gelu, hidden)[1](grad_act)[0].astype(jnp.bfloat16)
    grad_upbias = jnp.sum(grad_hidden.astype(jnp.float32), 0)
    grad_up = transposed(lowered_three, grad_hidden)
    dx_three, grad_gain_three, grad_shift_three = norm_back(
        against(grad_hidden, full_up), normed_three, inverse_three, gain_three
    )
    grad_cross = out_grad + dx_three
    grad_cross_low = grad_cross.astype(jnp.bfloat16)
    grad_crossout = transposed(cross_mixed, grad_cross_low)
    grad_cross_heads = head_split(against(grad_cross_low, full_crossout).astype(jnp.bfloat16))
    grad_weights = jnp.einsum(
        "qhd,khd->hqk", grad_cross_heads, cross_value_heads, preferred_element_type=jnp.float32
    )
    grad_scores = (
        cross_probs * (grad_weights - jnp.sum(cross_probs * grad_weights, -1, keepdims=True))
    ).astype(jnp.bfloat16)
    grad_asked = head_join(
        jnp.einsum("hqk,khd->qhd", grad_scores, cross_key_heads, preferred_element_type=jnp.float32)
        * score_scale
    ).astype(jnp.bfloat16)
    grad_cross_keys = (
        jnp.einsum("hqk,qhd->khd", grad_scores, asked_heads, preferred_element_type=jnp.float32)
        * score_scale
    )
    grad_cross_values = jnp.einsum(
        "hqk,qhd->khd",
        cross_probs.astype(jnp.bfloat16),
        grad_cross_heads,
        preferred_element_type=jnp.float32,
    )
    pair_terms = jnp.concatenate([head_join(grad_cross_keys), head_join(grad_cross_values)], 1)
    pair_grad = lax.psum_scatter(
        pair_terms.astype(jnp.bfloat16), "seq", scatter_dimension=0, tiled=True
    )
    grad_keyval = transposed(source_low, pair_grad)
    grad_source = against(pair_grad, full_keyval)
    grad_query = transposed(lowered_two, grad_asked)
    dx_two, grad_gain_two, grad_shift_two = norm_back(
        against(grad_asked, full_query), normed_two, inverse_two, gain_two
    )
    grad_self = grad_cross + dx_two
    grad_self_low = grad_self.astype(jnp.bfloat16)
    grad_output = transposed(self_mixed, grad_self_low)
    grad_mixed = against(grad_self_low, full_output).astype(jnp.bfloat16)
    grad_heads = head_split(grad_mixed)
    row_dots = grad_dots(
        queries, grad_heads, key_blocks, value_blocks, seg_blocks, own_segments, log_total
    )
    grad_queries, key_terms = query_grads(
        queries, grad_heads, key_blocks, value_blocks, seg_blocks, own_segments, log_total, row_dots
    )
    summed = lax.psum_scatter(
        key_terms.reshape(seq_length, 2 * model_width).astype(jnp.bfloat16),
        "seq",
        scatter_dimension=0,
        tiled=True,
    )
    grad_projected = jnp.concatenate([head_join(grad_queries).astype(jnp.bfloat16), summed], 1)
    grad_project = transposed(lowered_one, grad_projected)
    dx_one, grad_gain_one, grad_shift_one = norm_back(
        against(grad_projected, full_project), normed_one, inverse_one, gain_one
    )
    grad_target = grad_self + dx_one
    shards = (
        lax.psum_scatter(grad_project, ("rows", "seq"), scatter_dimension=0, tiled=True),
        lax.psum_scatter(grad_output, ("rows", "seq"), scatter_dimension=0, tiled=True),
        lax.psum_scatter(grad_query, ("rows", "seq"), scatter_dimension=0, tiled=True),
        lax.psum_scatter(grad_keyval, ("rows", "seq"), scatter_dimension=0, tiled=True),
        lax.psum_scatter(grad_crossout, ("rows", "seq"), scatter_dimension=0, tiled=True),
        lax.psum_scatter(grad_up, ("rows", "seq"), scatter_dimension=0, tiled=True),
        lax.psum_scatter(grad_upbias, ("rows", "seq"), scatter_dimension=0, tiled=True),
        lax.psum_scatter(grad_down, ("rows", "seq"), scatter_dimension=0, tiled=True),
        lax.psum_scatter(grad_downbias, ("rows", "seq"), scatter_dimension=0, tiled=True),
        lax.psum_scatter(grad_gain_one, ("rows", "seq"), scatter_dimension=0, tiled=True),
        lax.psum_scatter(grad_shift_one, ("rows", "seq"), scatter_dimension=0, tiled=True),
        lax.psum_scatter(grad_gain_two, ("rows", "seq"), scatter_dimension=0, tiled=True),
        lax.psum_scatter(grad_shift_two, ("rows", "seq"), scatter_dimension=0, tiled=True),
        lax.psum_scatter(grad_gain_three, ("rows", "seq"), scatter_dimension=0, tiled=True),
        lax.psum_scatter(grad_shift_three, ("rows", "seq"), scatter_dimension=0, tiled=True),
    )
    return (layer_out.astype(jnp.bfloat16)[None], grad_target[None], grad_source[None]) + tuple(
        shards
    )


F32, BF16 = jnp.float32, jnp.bfloat16
BLOCK = 16
AXES = ("rows", "seq")
FLIP_Y, FLIP_CORE, FLIP_X, FLIP_Z = 1, 2, 4, 8
MODEL, FEED, OWN, WINDOW, HALF_SOURCE = 512, 2048, 512, 256, 192
KEYS, SOURCES = OWN + WINDOW, 2 * HALF_SOURCE
TILE = 128
MASKED = -1000000000.0
SCALE = HD ** (-0.5)


def exchange(value, flip):
    return lax.ppermute(value, AXES, [(device, device ^ flip) for device in range(32)])


def exchange_side(value, step):
    flips = (FLIP_X, FLIP_Y) if step == 0 else (FLIP_Y, FLIP_X)
    return lax.ppermute(value, AXES, [(device, device ^ flips[device >> 1 & 1]) for device in range(32)])


def tied(values, *others):
    return lax.optimization_barrier((values, others))[0]


def along_z(block):
    return [exchange(block, FLIP_Z * i) for i in Z_ORDER]


Z_ORDER = (1, 2, 3)


def join(*parts):
    return jnp.concatenate(parts, 0)


def both_cores(halves):
    return halves + [exchange(half, FLIP_CORE) for half in halves]


def add_halves(kept, came):
    half = kept.shape[0] // 2
    return kept[half:] + came[half:], kept[:half] + came[:half]


def z_blocks(both):
    size = both.shape[0] // 4
    blocks = [both[size * i : size * (i + 1)] for i in range(4)]
    return [blocks[0]] + [exchange(block, FLIP_Z * i) for i, block in zip(Z_ORDER, blocks[1:])]


def block_places(me):
    out = []
    for other in (0, 1):
        core = (me >> 1 & 1) ^ other
        first, second = FLIP_X - 3 * core, FLIP_Y + 3 * core
        for b in (0, 1):
            for a in (0, 1):
                for i, z in enumerate((0,) + Z_ORDER):
                    owner = me ^ (other * FLIP_CORE + b * second + a * first + z * FLIP_Z)
                    out.append((other * 2 + b, a * 4 + i, owner))
    return out


def nn(left, right):
    return jnp.dot(left, right, preferred_element_type=F32)


def block_rows(owner, size=BLOCK):
    return pl.ds(pl.multiple_of(owner * size, size), size)


def load_blocks(me, pieces, columns, target):
    for piece, row, owner in block_places(me):
        target[block_rows(owner), :] = pieces[piece][row * BLOCK : (row + 1) * BLOCK, columns]


def store_blocks(me, source, targets, columns):
    for piece, row, owner in block_places(me):
        at = (piece % 2 * 8 + row) * BLOCK
        targets[piece // 2][at : at + BLOCK, columns] = source[block_rows(owner), :]


def normed_rows(value):
    centered = value - jnp.mean(value, -1, keepdims=True)
    inverse = lax.rsqrt(jnp.mean(centered * centered, -1, keepdims=True) + 1e-05)
    return centered * inverse, inverse


def norm_back_rows(upstream, normed, inverse, gain):
    scaled = upstream * gain
    first_mean = jnp.mean(scaled, -1, keepdims=True)
    second_mean = jnp.mean(scaled * normed, -1, keepdims=True)
    return inverse * (scaled - first_mean - normed * second_mean)


def column_sum(value):
    return jnp.sum(value, 0, keepdims=True)


def own_segments_of(index, segments):
    return jnp.where(index == 0, segments[:, :OWN], segments[:, OWN:]).astype(F32)


def key_segments_of(index, segments):
    near = jnp.where(index == 0, segments[:, OWN:KEYS], segments[:, OWN - WINDOW : OWN])
    return jnp.concatenate([own_segments_of(index, segments), near.astype(F32)], 1)


def spread(row):
    return jnp.broadcast_to(row, (TILE, row.shape[1])).T


def lane_half(shape, half):
    lanes = lax.broadcasted_iota(jnp.int32, shape, 1)
    return (lanes < HD) if half == 0 else (lanes >= HD)


def half_masks(value):
    keep, zero = lane_half(value.shape, 0), jnp.zeros_like(value)
    return jnp.concatenate([jnp.where(keep, value, zero), jnp.where(keep, zero, value)], 0)


def self_jobs(side):
    near, far = pl.multiple_of((1 - side) * 256, 256), pl.multiple_of(side * 256, 256)
    skip_near, skip_far = pl.multiple_of((1 - side) * TILE, TILE), pl.multiple_of(side * TILE, TILE)
    return [
        (pl.ds(near, 256), [(skip_near, 384), (OWN, WINDOW)], 256),
        (pl.ds(far, 256), [(skip_far, 384)], 256),
    ]


def attend(queries, pair_ref, mixed, log_rows, query_seg, key_row, jobs):
    for rows, spans, size in jobs:

        def keys_of(ref, lanes):
            parts = [ref[pl.ds(start, count), lanes] for start, count in spans]
            return parts[0] if len(parts) == 1 else jnp.concatenate(parts, 0)

        segments = [key_row[:, pl.ds(start, count)] for start, count in spans]
        segments = segments[0] if len(segments) == 1 else jnp.concatenate(segments, 1)
        same = jnp.concatenate([query_seg[rows, :]] * (segments.shape[1] // TILE), 1) == segments
        bias = jnp.where(same, 0.0, MASKED)
        lanes = lax.broadcasted_iota(jnp.int32, (size, TILE), 1)
        logs = jnp.zeros((size, TILE), F32)
        for pair in range(HEADS // 2):
            at = slice(pair * TILE, (pair + 1) * TILE)
            scores = against(half_masks(queries[rows, at]), keys_of(pair_ref, at))
            weights, scales = [], []
            for half in range(2):
                part = scores[half * size : (half + 1) * size] + bias
                top = jnp.max(part, -1, keepdims=True)
                part = jnp.exp(part - top)
                total = jnp.sum(part, -1, keepdims=True)
                weights.append(part.astype(BF16))
                scales.append(1.0 / total)
                logs = jnp.where(lanes == pair * 2 + half, top + jnp.log(total), logs)
            values = keys_of(pair_ref, slice(MODEL + pair * TILE, MODEL + (pair + 1) * TILE))
            out = nn(jnp.concatenate(weights, 0), values)
            keep = lane_half((size, TILE), 0)
            mixed[rows, at] = jnp.where(keep, out[:size] * scales[0], out[size:] * scales[1]).astype(BF16)
        log_rows[:, rows] = logs.T[:HEADS]


def head_dots(upstream, mixed):
    head = lax.broadcasted_iota(jnp.int32, (HEADS, MODEL), 1) // HD
    ones = (head == lax.broadcasted_iota(jnp.int32, (HEADS, MODEL), 0)).astype(F32)
    return lax.dot_general(
        ones, upstream.astype(F32) * mixed.astype(F32), (((1,), (1,)), ((), ())),
        precision=lax.Precision.HIGHEST, preferred_element_type=F32,
    )


def attend_back(queries, upstream, pair_ref, log_rows, dot_rows, query_row, key_seg, query_grad, pair_grad, jobs):
    query_grad[...] = jnp.zeros_like(query_grad)
    for key_start, size, start, count in jobs:
        rows, across = pl.ds(key_start, size), pl.ds(start, count)

        def heads(step, unused):
            same = jnp.concatenate([key_seg[rows, :]] * (count // TILE), 1) == query_row[:, across]
            bias = jnp.where(same, 0.0, MASKED)
            for pair in (step * 2, step * 2 + 1):
                at = pl.ds(pl.multiple_of(pair * TILE, TILE), TILE)
                value_at = pl.ds(pl.multiple_of(MODEL + pair * TILE, TILE), TILE)
                query = queries[across, at]
                grad = upstream[across, at]
                keys = half_masks(pair_ref[rows, at])
                values = half_masks(pair_ref[rows, value_at])
                scores, grads = against(keys, query), against(values, grad)
                weights, score_grads = [], []
                for half in range(2):
                    head, part = pl.ds(pair * 2 + half, 1), slice(half * size, (half + 1) * size)
                    weight = jnp.exp(scores[part] + (bias - log_rows[head, across]))
                    score_grads.append((weight * (grads[part] - dot_rows[head, across])).astype(BF16))
                    weights.append(weight.astype(BF16))
                score_grad = jnp.concatenate(score_grads, 0)
                value_part = nn(jnp.concatenate(weights, 0), grad)
                key_part = nn(score_grad, query)
                query_grad[across, at] += transposed(score_grad, keys)
                keep = lane_half((size, TILE), 0)
                pair_grad[rows, at] = jnp.where(keep, key_part[:size], key_part[size:]).astype(BF16)
                pair_grad[rows, value_at] = jnp.where(keep, value_part[:size], value_part[size:]).astype(BF16)
            return unused

        lax.fori_loop(0, HEADS // 4, heads, 0)


def self_back_jobs(side):
    near = pl.multiple_of((1 - side) * 256, 256)
    return [(0, 256, 0, 384), (256, 256, TILE, 384), (OWN, WINDOW, near, 256)]


def pack_body(
    place, vectors, project, output, query, keyval, crossout, up, down, states, source,
    one, three, near, own_source, block, semaphores
):
    me, side = place[0], place[1]
    copies = [
        (project, one.at[:, :1536]),
        (output, one.at[:, 1664:2176]),
        (query, one.at[:, 2176:2688]),
        (keyval, one.at[:, 2688:3712]),
        (crossout, one.at[:, 3712:]),
        (down, three.at[64:]),
    ] + [
        (up.at[:, part * 512 : (part + 1) * 512], three.at[part * BLOCK : (part + 1) * BLOCK, :])
        for part in range(4)
    ] + [
        (states.at[pl.ds(pl.multiple_of((1 - side) * WINDOW, WINDOW), WINDOW), :], near.at[:WINDOW])
    ]
    copies = [pltpu.make_async_copy(*copy, semaphores.at[i]) for i, copy in enumerate(copies)]
    for copy in copies:
        copy.start()
    gap = jnp.zeros((HALF_SOURCE - source.shape[0], MODEL), F32)
    padded = jnp.concatenate([source[...].astype(F32), gap], 0).astype(BF16)
    own_source[...] = padded
    near[WINDOW:, :] = padded
    values = jnp.broadcast_to(vectors[...].astype(F32), (8, 256))
    lanes = lax.broadcasted_iota(jnp.int32, (8, TILE), 1)
    rows = lax.broadcasted_iota(jnp.int32, (8, TILE), 0)
    packed = jnp.zeros((8, TILE), F32)
    spot, wide = (me & 7) * 16, (me & 1) * 64
    for row in range(7):
        moved = pltpu.roll(values, spot + 256 - 16 * row, 1)[:, :TILE]
        inside = jnp.logical_and(lanes >= spot, lanes < spot + 16)
        packed = jnp.where(jnp.logical_and(rows == row, inside), moved, packed)
    moved = pltpu.roll(values, wide + 256 - 112, 1)[:, :TILE]
    inside = jnp.logical_and(lanes >= wide, lanes < wide + 64)
    packed = jnp.where(jnp.logical_and(rows == 7, inside), moved, packed)
    block[...] = jnp.concatenate([packed, jnp.zeros((8, TILE), F32)], 0).astype(BF16)
    last = pltpu.make_async_copy(block, one.at[:, 1536:1664], semaphores.at[len(copies)])
    last.start()
    for copy in copies + [last]:
        copy.wait()


def self_body(place, states, window, *refs):
    pieces, refs = refs[:4], refs[4:]
    queries, pair, lowered, vectors, up_bias, weight, weight_two, packed = refs
    me = place[0]
    load_blocks(me, pieces, slice(1536, 1664), packed)
    load_blocks(me, pieces, slice(0, 1536), weight)
    load_blocks(me, pieces, slice(1664, 4224), weight_two)
    for tile in range(4):
        total = jnp.zeros((8, TILE), F32)
        for i in range(8):
            total = total + packed[(tile * 8 + i) * BLOCK : (tile * 8 + i + 1) * BLOCK, :].astype(F32)[:8]
        vectors[:, tile * TILE : (tile + 1) * TILE] = total
    for tile in range(16):
        total = (
            packed[2 * tile * BLOCK : (2 * tile + 1) * BLOCK, :].astype(F32)
            + packed[(2 * tile + 1) * BLOCK : (2 * tile + 2) * BLOCK, :].astype(F32)
        )
        up_bias[:, tile * TILE : (tile + 1) * TILE] = total[7:8]
    gain, shift = vectors[1:2, :], vectors[2:3, :]
    for i in range(KEYS // TILE):
        rows = slice(i * TILE, (i + 1) * TILE)
        value = states[rows, :] if i < 4 else window[(i - 4) * TILE : (i - 3) * TILE, :]
        lowered[rows, :] = (normed_rows(value.astype(F32))[0] * gain + shift).astype(BF16)
    for i in range(KEYS // 256):
        rows = slice(i * 256, (i + 1) * 256)
        if i < 2:
            queries[rows, :] = (nn(lowered[rows, :], weight[:, :512]) .astype(BF16) * SCALE).astype(BF16)
        pair[rows, :] = nn(lowered[rows, :], weight[:, 512:]).astype(BF16)


def forward_body(
    place, segments, source_segments, states, own_source, other_source, vectors, weight, self_queries, self_pair,
    self_mixed, self_logs, after_self, lowered, queries, pair, mixed, logs, after_cross,
    query_seg, key_row, source_row, source,
):
    self_mix(place, segments, self_queries, self_pair, self_mixed, self_logs, query_seg, key_row)
    cross_lower(
        place, states, own_source, other_source, self_mixed, vectors, after_self, lowered, queries, pair, weight, source
    )
    source_row[...] = source_segments[...].astype(F32)
    attend(queries, pair, mixed, logs, query_seg, source_row, [(pl.ds(0, OWN), [(0, SOURCES)], OWN)])
    for i in range(2):
        rows = slice(i * 256, (i + 1) * 256)
        after_cross[rows, :] = after_self[rows, :] + nn(mixed[rows, :], weight[:, 2048:])


def self_mix(place, segments, queries, pair, mixed, log_rows, query_seg, key_row):
    query_seg[...] = spread(own_segments_of(place[1], segments[...]))
    key_row[...] = key_segments_of(place[1], segments[...])
    attend(queries, pair, mixed, log_rows, query_seg, key_row, self_jobs(place[1]))


def cross_lower(
    place, states, own_source, other_source, self_mixed, vectors, after_self, lowered, queries, pair, weight, source
):
    side = place[1]
    source[:HALF_SOURCE, :] = jnp.where(side == 0, own_source[...], other_source[...])
    source[HALF_SOURCE:, :] = jnp.where(side == 0, other_source[...], own_source[...])
    gain, shift = vectors[3:4, :], vectors[4:5, :]
    pair[...] = nn(source[...], weight[:, 1024:2048]).astype(BF16)
    for i in range(2):
        rows = slice(i * 256, (i + 1) * 256)
        value = states[rows, :].astype(F32) + nn(self_mixed[rows, :], weight[:, :512])
        after_self[rows, :] = value
        lowered[rows, :] = (normed_rows(value)[0] * gain + shift).astype(BF16)
        queries[rows, :] = (nn(lowered[rows, :], weight[:, 512:1024]).astype(BF16) * SCALE).astype(BF16)


CHUNK, UNROLL = 512, 2


def feed_body(place, after_cross, output_grad, vectors, up_bias, *refs):
    pieces, refs = refs[:4], refs[4:]
    (
        total, back, kept, sent, bias_sums, ups, downs, lowered, flipped, up_grads, down_grads,
    ) = refs
    me = place[0]
    places = block_places(me)

    def chunk_of(z):
        return pl.multiple_of(((me >> 3) ^ z) * CHUNK, CHUNK)

    gain, shift = vectors[5:6, :], vectors[6:7, :]
    for i in range(4):
        rows = slice(i * TILE, (i + 1) * TILE)
        low = (normed_rows(after_cross[rows, :])[0] * gain + shift).astype(BF16)
        lowered[rows, :] = low
    flipped[...] = lowered[...].T
    grad_low = output_grad[...]
    total[...] = jnp.zeros_like(total)
    back[...] = jnp.zeros_like(back)

    def chunk(z):
        at = pl.ds(chunk_of(z), CHUNK)
        z_row = ((me >> 3) ^ z) * BLOCK
        up, down, up_grad, down_grad = ups.at[z], downs.at[z], up_grads.at[z], down_grads.at[z]
        for piece, row, owner in places:
            up[block_rows(owner), :] = pieces[piece][pl.ds(pl.multiple_of(row * 128 + z_row, BLOCK), BLOCK), :]
            if row % 4 == 0:
                start = pl.multiple_of((row + z) * 128 + 64, 64)
                down[block_rows(owner & 7, 64), :] = pieces[piece][pl.ds(start, 64), :]
        hidden = nn(lowered[...], up[...]) + up_bias[:, at]
        square = hidden * hidden
        inner = 0.7978845608028654 * hidden * (1.0 + 0.044715 * square)
        curve = jnp.tanh(inner)
        half = 0.5 * (1.0 + curve)
        activated = (hidden * half).astype(BF16)
        slope = half + (0.5 * 0.7978845608028654) * hidden * (1.0 - curve * curve) * (
            1.0 + (3 * 0.044715) * square
        )
        down_grad[...] = transposed(activated, grad_low).astype(BF16)
        for piece, row, owner in places:
            if row % 4 == 0:
                to = pl.multiple_of((piece % 2 * 8 + row + z) * 128 + 64, 64)
                (kept, sent)[piece // 2][pl.ds(to, 64), :] = down_grad[block_rows(owner & 7, 64), :]
        grad_hidden = (against(grad_low, down[...]) * slope).astype(BF16)
        bias_sums[:, at] = column_sum(grad_hidden.astype(F32))
        up_grad[...] = nn(flipped[...], grad_hidden).astype(BF16)
        for piece, row, owner in places:
            to = (piece % 2 * 8 + row) * 128
            (kept, sent)[piece // 2][pl.ds(pl.multiple_of(to + z_row, BLOCK), BLOCK), :] = up_grad[block_rows(owner), :]
        total[...] += nn(activated, down[...])
        back[...] += against(grad_hidden, up[...])

    def chunks(step, unused):
        for z in range(UNROLL):
            chunk(step * UNROLL + z)
        return unused

    lax.fori_loop(0, 4 // UNROLL, chunks, 0)


def feed_last_body(place, after_cross, output_grad, vectors, total, back, layer_out, after_grad, sums):
    gain = vectors[5:6, :]
    gain_sum, shift_sum, bias_sum = (jnp.zeros((1, MODEL), F32) for _ in range(3))
    for i in range(4):
        rows = slice(i * TILE, (i + 1) * TILE)
        value, grad = after_cross[rows, :], output_grad[rows, :].astype(F32)
        layer_out[rows, :] = (value + total[rows, :] + vectors[0:1, :]).astype(BF16)
        normed, inverse = normed_rows(value)
        upstream = back[rows, :]
        after_grad[rows, :] = grad + norm_back_rows(upstream, normed, inverse, gain)
        gain_sum, shift_sum = gain_sum + column_sum(upstream * normed), shift_sum + column_sum(upstream)
        bias_sum = bias_sum + column_sum(grad)
    zero = jnp.zeros((1, MODEL), F32)
    sums[...] = jnp.concatenate([bias_sum, zero, zero, zero, zero, gain_sum, shift_sum, zero], 0)


def cross_back_body(
    place, segments, source_segments, own_source, other_source, queries, pair, mixed, log_rows, after_grad, weight,
    asked, source_own, source_send, grads, upstream, query_grad, pair_grad, source, key_seg, query_row,
    dot_rows,
):
    side = place[1]
    key_seg[...] = spread(source_segments[...].astype(F32))
    query_row[...] = own_segments_of(side, segments[...])
    source[:HALF_SOURCE, :] = jnp.where(side == 0, own_source[...], other_source[...])
    source[HALF_SOURCE:, :] = jnp.where(side == 0, other_source[...], own_source[...])
    grad_low = after_grad[...].astype(BF16)
    upstream[...] = against(grad_low, weight[:, 2048:]).astype(BF16)
    dot_rows[...] = head_dots(upstream[...], mixed[...])
    grads[:, :512] = transposed(mixed[...], grad_low).astype(BF16)
    attend_back(
        queries, upstream, pair, log_rows, dot_rows, query_row, key_seg, query_grad, pair_grad,
        [(0, SOURCES, 0, OWN)],
    )
    asked[...] = (query_grad[...] * SCALE).astype(BF16)
    grads[:, 512:] = transposed(source[...], pair_grad[...]).astype(BF16)
    back = against(pair_grad[...], weight[:, 1024:2048])
    first, second = back[:HALF_SOURCE], back[HALF_SOURCE:]
    source_own[...] = jnp.where(side == 0, first, second)
    source_send[...] = jnp.where(side == 0, second, first).astype(BF16)


def cross_weight_body(
    place, after_self, lowered, self_mixed, after_grad, asked, vectors, sums, weight, some_grads, *refs
):
    self_grad, upstream, dot_rows, kept, sent, new_sums, grads = refs
    me = place[0]
    store_blocks(me, some_grads, (kept, sent), slice(0, 1536))
    gain = vectors[3:4, :]
    gain_sum, shift_sum = jnp.zeros((1, MODEL), F32), jnp.zeros((1, MODEL), F32)
    for i in range(2):
        rows = slice(i * 256, (i + 1) * 256)
        normed, inverse = normed_rows(after_self[rows, :])
        up = against(asked[rows, :], weight[:, 512:1024])
        self_grad[rows, :] = after_grad[rows, :] + norm_back_rows(up, normed, inverse, gain)
        gain_sum, shift_sum = gain_sum + column_sum(up * normed), shift_sum + column_sum(up)
    grads[:, :512] = transposed(lowered[...], asked[...]).astype(BF16)
    grad_low = self_grad[...].astype(BF16)
    grads[:, 512:] = transposed(self_mixed[...], grad_low).astype(BF16)
    store_blocks(me, grads, (kept, sent), slice(1536, 2560))
    upstream[...] = against(grad_low, weight[:, :512]).astype(BF16)
    dot_rows[...] = head_dots(upstream[...], self_mixed[...])
    zero = jnp.zeros((1, MODEL), F32)
    new_sums[...] = sums[...] + jnp.concatenate(
        [zero, zero, zero, gain_sum, shift_sum, zero, zero, zero], 0
    )


def self_back_body(
    place, segments, states, window, lowered, queries, pair, log_rows, upstream, dot_rows, weight, sums, bias_sums,
    source_send, own_back, near_back, kept, sent, query_grad, pair_grad, grads, key_seg, query_row,
):
    near_back[WINDOW:, :] = source_send[...]
    key_seg[...] = spread(key_segments_of(place[1], segments[...]))
    query_row[...] = own_segments_of(place[1], segments[...])
    attend_back(
        queries, upstream, pair, log_rows, dot_rows, query_row, key_seg, query_grad, pair_grad,
        self_back_jobs(place[1]),
    )
    asked = (query_grad[...] * SCALE).astype(BF16)
    grads[:, :MODEL] = transposed(lowered[:OWN, :], asked).astype(BF16)
    grads[:, MODEL:1536] = transposed(lowered[...], pair_grad[...]).astype(BF16)
    gain_sum, shift_sum = jnp.zeros((1, MODEL), F32), jnp.zeros((1, MODEL), F32)
    for i in range(3):
        rows = slice(i * 256, (i + 1) * 256)
        part = against(pair_grad[rows, :], weight[:, MODEL:])
        if i < 2:
            part = part + against(asked[rows, :], weight[:, :MODEL])
            own_back[rows, :] = part
            value = states[rows, :]
        else:
            near_back[:WINDOW, :] = part.astype(BF16)
            value = window[...]
        normed = normed_rows(value.astype(F32))[0]
        gain_sum, shift_sum = gain_sum + column_sum(part * normed), shift_sum + column_sum(part)
    zero = jnp.zeros((1, MODEL), F32)
    sums = sums[...] + jnp.concatenate([zero, gain_sum, shift_sum, zero, zero, zero, zero, zero], 0)
    last = lax.broadcasted_iota(jnp.int32, (8, TILE), 0) == 7
    for device in range(32):
        tile, wide = device // 8 * TILE, device // 2 * TILE
        value = jnp.where(last, bias_sums[:, wide : wide + TILE], sums[:, tile : tile + TILE])
        high = value.astype(BF16).astype(F32)
        grads[device * BLOCK : (device + 1) * BLOCK, 1536:] = jnp.concatenate([high, value - high], 0).astype(BF16)
    store_blocks(place[0], grads, (kept, sent), slice(0, 1664))


def target_body(place, back, came, states, self_grad, vectors, out):
    gain = vectors[1:2, :]
    for i in range(4):
        rows = slice(i * TILE, (i + 1) * TILE)
        here = (i < 2) == (place[1] == 1)
        extra = came[(i % 2) * TILE : (i % 2 + 1) * TILE, :].astype(F32)
        upstream = back[rows, :] + jnp.where(here, extra, 0.0)
        normed, inverse = normed_rows(states[rows, :].astype(F32))
        out[rows, :] = self_grad[rows, :] + norm_back_rows(upstream, normed, inverse, gain)


def finish_body(place, *refs):
    feed, cross, last, outs = refs[:4], refs[4:8], refs[8:12], refs[12:]
    project, output, query, keyval, crossout, up, down, *small = outs
    me = place[0]

    def total(parts, begin, end, rows=slice(None)):
        value = parts[0][rows, begin:end].astype(F32)
        for part in parts[1:]:
            value = value + part[rows, begin:end].astype(F32)
        return value

    for part in range(4):
        rows = slice(part * BLOCK, (part + 1) * BLOCK)
        up[:, part * 512 : (part + 1) * 512] = total(feed, 0, MODEL, rows)
    down[...] = total(feed, 0, MODEL, slice(64, 128))
    crossout[...] = total(cross, 0, 512)
    keyval[...] = total(cross, 512, 1536)
    query[...] = total(cross, 1536, 2048)
    output[...] = total(cross, 2048, 2560)
    project[...] = total(last, 0, 1536)
    value = total(last, 1536, 1664)
    value = value[:8] + value[8:]
    narrow = pltpu.roll(value, (TILE - (me & 7) * 16) & 127, 1)
    wide = pltpu.roll(value, (TILE - (me & 1) * 64) & 127, 1)
    for row in range(7):
        small[row][...] = narrow[row : row + 1, :16]
    small[7][...] = wide[7:8, :64]


def shape_of(*shape, dtype=BF16):
    return jax.ShapeDtypeStruct(shape, dtype)


VMEM_SPEC = pl.BlockSpec(memory_space=pltpu.VMEM)
ANY_SPEC = pl.BlockSpec(memory_space=pl.ANY)
HBM_SPEC = pl.BlockSpec(memory_space=pltpu.HBM)
SMEM_SPEC = pl.BlockSpec(memory_space=pltpu.SMEM)


def call(body, name, place, inputs, pieces, outs, scratch, flops, any_outs=(), any_ins=(), vmem=40):
    return pl.pallas_call(
        body,
        name=name,
        out_shape=outs,
        in_specs=[SMEM_SPEC]
        + [HBM_SPEC if i in any_ins else VMEM_SPEC for i in range(len(inputs))]
        + [VMEM_SPEC] * len(pieces),
        out_specs=[ANY_SPEC if i in any_outs else VMEM_SPEC for i in range(len(outs))],
        scratch_shapes=scratch,
        compiler_params=pltpu.CompilerParams(vmem_limit_bytes=vmem * 2**20),
        cost_estimate=pl.CostEstimate(flops=flops, bytes_accessed=4 * 2**20, transcendentals=0),
    )(place, *inputs, *pieces)


def fast_device(
    target_states, source_states, target_segments, source_segments, output_grad, self_project,
    self_output, cross_query, cross_keyval, cross_output, hidden_up, hidden_bias, hidden_down,
    output_bias, first_gain, first_shift, second_gain, second_shift, third_gain, third_shift,
):
    vmem, dma = pltpu.VMEM, pltpu.SemaphoreType.DMA
    side = lax.axis_index("seq")
    place = jnp.stack([lax.axis_index("rows") * 2 + side, side]).astype(jnp.int32)
    states, grad = target_states[0], output_grad[0]
    small = jnp.pad(hidden_bias, (112, 80))
    for i, vector in enumerate(
        (output_bias, first_gain, first_shift, second_gain, second_shift, third_gain, third_shift)
    ):
        small = small + jnp.pad(vector, (16 * i, 240 - 16 * i))
    small = small.reshape(1, 256)
    one, three, near, own_source = call(
        pack_body, "pack", place,
        [
            small, self_project, self_output, cross_query, cross_keyval, cross_output, hidden_up, hidden_down, states,
            source_states[0],
        ],
        [],
        [
            shape_of(16, 4224), shape_of(128, MODEL), shape_of(WINDOW + HALF_SOURCE, MODEL),
            shape_of(HALF_SOURCE, MODEL),
        ],
        [vmem((BLOCK, TILE), BF16), dma((12,))], 1000000, any_ins=range(1, 9), vmem=60,
    )
    parts = along_z(one)
    near = exchange(near, FLIP_Y)
    one = join(one, *parts)
    one = tied(one, near)
    came = exchange_side(one, 0)
    three, one = tied((three, one), came)
    parts_three = along_z(three)
    one = join(one, came)
    one_core = exchange(one, FLIP_CORE)
    other = exchange_side(one, 1)
    other = tied(other, parts_three)
    window, other_source = near[:WINDOW], near[WINDOW:]
    pieces_one = [one, other, one_core, exchange(other, FLIP_CORE)]
    three = join(three, *parts_three)
    came = exchange_side(three, 0)
    half = source_states.shape[1]
    gap = jnp.full((1, HALF_SOURCE - half), -1, jnp.int32)
    source_seg = jnp.concatenate([source_segments[:, :half], gap, source_segments[:, half:], gap], 1)

    queries, pair, lowered, vectors, up_bias, weight_one, weight_two = call(
        self_body, "self_lower", place, [states, window], pieces_one,
        [
            shape_of(OWN, MODEL), shape_of(KEYS, 2 * MODEL), shape_of(KEYS, MODEL), shape_of(8, MODEL, dtype=F32),
            shape_of(1, FEED, dtype=F32), shape_of(MODEL, 1536), shape_of(MODEL, 2560),
        ],
        [vmem((MODEL, TILE), BF16)], 5000000000,
    )
    came, three = tied((came, three), queries)
    three = join(three, came)
    three_core = exchange(three, FLIP_CORE)
    other = exchange_side(three, 1)
    queries = tied(queries, three)
    mixed, logs, after_self, lowered_two, queries_two, pair_two, mixed_two, logs_two, after_cross = call(
        forward_body, "forward", place,
        [
            target_segments, source_seg, states, own_source, other_source, vectors, weight_two, queries, pair,
        ],
        [],
        [
            shape_of(OWN, MODEL), shape_of(HEADS, OWN, dtype=F32), shape_of(OWN, MODEL, dtype=F32), shape_of(OWN, MODEL),
            shape_of(OWN, MODEL), shape_of(SOURCES, 2 * MODEL), shape_of(OWN, MODEL), shape_of(HEADS, OWN, dtype=F32),
            shape_of(OWN, MODEL, dtype=F32),
        ],
        [
            vmem((OWN, TILE), F32), vmem((1, KEYS), F32), vmem((1, SOURCES), F32), vmem((SOURCES, MODEL), BF16),
        ],
        20000000000,
    )
    three_core, other = tied((three_core, other), after_cross)
    pieces_three = [three, other, three_core, exchange(other, FLIP_CORE)]
    total, back, feed_kept, feed_sent, bias_sums = call(
        feed_body, "feed", place, [after_cross, grad, vectors, up_bias], pieces_three,
        [shape_of(OWN, MODEL, dtype=F32)] * 2 + [shape_of(2048, MODEL)] * 2 + [shape_of(1, FEED, dtype=F32)],
        [
            vmem((4, MODEL, CHUNK), BF16), vmem((4, CHUNK, MODEL), BF16), vmem((OWN, MODEL), BF16),
            vmem((MODEL, OWN), BF16), vmem((4, MODEL, CHUNK), BF16), vmem((4, CHUNK, MODEL), BF16),
        ],
        10000000000,
    )
    feed_came = exchange(feed_sent, FLIP_CORE)
    layer_out, after_grad, sums = call(
        feed_last_body, "feed_last", place, [after_cross, grad, vectors, total, back], [],
        [shape_of(OWN, MODEL), shape_of(OWN, MODEL, dtype=F32), shape_of(8, MODEL, dtype=F32)], [], 2000000000,
    )
    feed_came = tied(feed_came, after_grad)
    feed_sent, feed_kept = add_halves(feed_kept, feed_came)
    after_grad = tied(after_grad, feed_sent)
    feed_came = exchange_side(feed_sent, 1)
    asked, source_own, source_send, some_grads = call(
        cross_back_body, "cross_backward", place,
        [
            target_segments, source_seg, own_source, other_source, queries_two, pair_two, mixed_two, logs_two,
            after_grad, weight_two,
        ],
        [],
        [
            shape_of(OWN, MODEL), shape_of(HALF_SOURCE, MODEL, dtype=F32), shape_of(HALF_SOURCE, MODEL),
            shape_of(MODEL, 1536),
        ],
        [
            vmem((OWN, MODEL), BF16), vmem((OWN, MODEL), F32), vmem((SOURCES, 2 * MODEL), BF16),
            vmem((SOURCES, MODEL), BF16), vmem((SOURCES, TILE), F32), vmem((1, OWN), F32), vmem((HEADS, OWN), F32),
        ],
        10000000000,
    )
    self_grad, upstream, dot_rows, cross_kept, cross_sent, sums = call(
        cross_weight_body, "cross_weights", place,
        [after_self, lowered_two, mixed, after_grad, asked, vectors, sums, weight_two, some_grads], [],
        [shape_of(OWN, MODEL, dtype=F32), shape_of(OWN, MODEL), shape_of(HEADS, OWN, dtype=F32)]
        + [shape_of(256, 2560)] * 2 + [shape_of(8, MODEL, dtype=F32)],
        [vmem((MODEL, 1024), BF16)], 6000000000,
    )
    cross_came = exchange(cross_sent, FLIP_CORE)
    feed_came = tied(feed_came, upstream)
    feed_sent, feed_kept = add_halves(feed_kept, feed_came)
    feed_came = exchange_side(feed_sent, 0)
    cross_came = tied(cross_came, feed_sent)
    cross_sent, cross_kept = add_halves(cross_kept, cross_came)
    cross_came = exchange_side(cross_sent, 1)
    upstream = tied(upstream, cross_sent)
    own_back, near_back, last_kept, last_sent = call(
        self_back_body, "self_backward", place,
        [
            target_segments, states, window, lowered, queries, pair, logs, upstream, dot_rows, weight_one, sums,
            bias_sums, source_send,
        ],
        [],
        [shape_of(OWN, MODEL, dtype=F32), shape_of(WINDOW + HALF_SOURCE, MODEL)] + [shape_of(256, 1664)] * 2,
        [
            vmem((OWN, MODEL), F32), vmem((KEYS, 2 * MODEL), BF16), vmem((MODEL, 1664), BF16), vmem((KEYS, TILE), F32),
            vmem((1, OWN), F32),
        ],
        16000000000,
    )
    last_came = exchange(last_sent, FLIP_CORE)
    cross_came, feed_came = tied((cross_came, feed_came), own_back)
    cross_sent, cross_kept = add_halves(cross_kept, cross_came)
    last_sent, last_kept = add_halves(last_kept, last_came)
    last_came, cross_came = exchange_side(last_sent, 1), exchange_side(cross_sent, 0)
    feed_came = tied(feed_came, last_sent)
    feed = z_blocks(feed_kept + feed_came)
    last_came = tied(last_came, feed[0])
    last_sent, last_kept = add_halves(last_kept, last_came)
    last_came = exchange_side(last_sent, 0)
    cross_came, feed, near_back = tied((cross_came, feed, near_back), last_sent)
    cross_kept = tied(cross_kept, feed)
    cross = z_blocks(cross_kept + cross_came)
    near_came = exchange(near_back, FLIP_Y)
    last_came = tied(last_came, cross[0])
    last = z_blocks(last_kept + last_came)
    came, source_came = near_came[:WINDOW], near_came[WINDOW:]
    grad_source = source_own[:half] + source_came[:half].astype(F32)
    (grad_target,) = call(
        target_body, "target_grad", place, [own_back, came, states, self_grad, vectors], [],
        [shape_of(OWN, MODEL, dtype=F32)], [], 1000000,
    )
    project, output, query, keyval, crossout, up, down, *small = call(
        finish_body, "finish", place, feed + cross + last, [],
        [
            shape_of(16, 1536, dtype=F32), shape_of(16, 512, dtype=F32), shape_of(16, 512, dtype=F32),
            shape_of(16, 1024, dtype=F32), shape_of(16, 512, dtype=F32), shape_of(16, 2048, dtype=F32),
            shape_of(64, 512, dtype=F32),
        ]
        + [shape_of(1, 16, dtype=F32)] * 7 + [shape_of(1, 64, dtype=F32)],
        [], 1000000,
    )
    *rows, up_sum = [row[0] for row in small]
    return (
        layer_out[None], grad_target[None], grad_source[None], project, output, query, keyval, crossout, up,
        up_sum, down, *rows,
    )


def specs():
    in_specs = (
        P("rows", "seq", None),
        P("rows", "seq", None),
        P("rows", None),
        P("rows", None),
        P("rows", "seq", None),
        P(("rows", "seq"), None),
        P(("rows", "seq"), None),
        P(("rows", "seq"), None),
        P(("rows", "seq"), None),
        P(("rows", "seq"), None),
        P(("rows", "seq"), None),
        P(("rows", "seq")),
        P(("rows", "seq"), None),
        P(("rows", "seq")),
        P(("rows", "seq")),
        P(("rows", "seq")),
        P(("rows", "seq")),
        P(("rows", "seq")),
        P(("rows", "seq")),
        P(("rows", "seq")),
    )
    out_specs = (
        P("rows", "seq", None),
        P("rows", "seq", None),
        P("rows", "seq", None),
        P(("rows", "seq"), None),
        P(("rows", "seq"), None),
        P(("rows", "seq"), None),
        P(("rows", "seq"), None),
        P(("rows", "seq"), None),
        P(("rows", "seq"), None),
        P(("rows", "seq")),
        P(("rows", "seq"), None),
        P(("rows", "seq")),
        P(("rows", "seq")),
        P(("rows", "seq")),
        P(("rows", "seq")),
        P(("rows", "seq")),
        P(("rows", "seq")),
        P(("rows", "seq")),
    )
    return in_specs, out_specs


def solution(mesh):
    in_specs, out_specs = specs()
    fast = mesh.shape["rows"] == 16 and mesh.shape["seq"] == 2
    return jax.shard_map(
        fast_device if fast else general_device,
        mesh=mesh, in_specs=in_specs, out_specs=out_specs, check_vma=False,
    )
```

```python
import jax
import jax.numpy as jnp
from jax import lax
from jax.experimental import pallas as pl
from jax.experimental.pallas import tpu as pltpu
from jax.sharding import PartitionSpec as P

HEADS = 8
HD = 64


def layer_norm(value, gain, shift):
    row_mean = jnp.mean(value, -1, keepdims=True)
    centered = value - row_mean
    variance = jnp.mean(centered * centered, -1, keepdims=True)
    inverse = lax.rsqrt(variance + 1e-05)
    normed = centered * inverse
    return (normed * gain + shift, normed, inverse)


def norm_back(upstream, normed, inverse, gain):
    scaled = upstream * gain
    first_mean = jnp.mean(scaled, -1, keepdims=True)
    second_mean = jnp.mean(scaled * normed, -1, keepdims=True)
    grad_input = inverse * (scaled - first_mean - normed * second_mean)
    return (grad_input, jnp.sum(upstream * normed, 0), jnp.sum(upstream, 0))


def matmul(left, right):
    return jnp.dot(left, right, preferred_element_type=jnp.float32)


def transposed(left, right):
    return lax.dot_general(
        left, right, (((0,), (0,)), ((), ())), preferred_element_type=jnp.float32
    )


def against(left, right):
    return lax.dot_general(
        left, right, (((1,), (1,)), ((), ())), preferred_element_type=jnp.float32
    )


def head_split(value):
    return value.reshape(value.shape[0], HEADS, HD)


def head_join(value):
    return value.reshape(value.shape[0], HEADS * HD)


def scores_of(queries, key_rows, query_seg, key_seg):
    raw_scores = jnp.einsum(
        "qhd,khd->hqk", queries, key_rows, preferred_element_type=jnp.float32
    ) * HD ** (-0.5)
    same_seg = (query_seg[:, None] == key_seg[None, :])[None]
    return (raw_scores, same_seg)


def block_weights(queries, key_rows, query_seg, key_seg, log_total):
    raw_scores, same_seg = scores_of(queries, key_rows, query_seg, key_seg)
    return jnp.where(same_seg, jnp.exp(raw_scores - log_total[..., None]), 0.0)


def log_totals(queries, key_blocks, seg_blocks, query_seg):

    def log_advance(carry, inputs_now):
        row_max, row_total = carry
        key_rows, key_seg = inputs_now
        raw_scores, same_seg = scores_of(queries, key_rows, query_seg, key_seg)
        masked = jnp.where(same_seg, raw_scores, -1000000000.0)
        new_max = jnp.maximum(row_max, jnp.max(masked, -1))
        shifted = jnp.where(same_seg, jnp.exp(masked - new_max[..., None]), 0.0)
        return ((new_max, row_total * jnp.exp(row_max - new_max) + jnp.sum(shifted, -1)), None)

    start = (
        jnp.full((HEADS, queries.shape[0]), -1000000000.0, jnp.float32),
        jnp.zeros((HEADS, queries.shape[0]), jnp.float32),
    )
    (row_max, row_total), unused = lax.scan(log_advance, start, (key_blocks, seg_blocks))
    return row_max + jnp.log(row_total)


def weighted_sum(queries, key_blocks, value_blocks, seg_blocks, query_seg, log_total):

    def weighted_advance(carry, inputs_now):
        key_rows, value_rows, key_seg = inputs_now
        weights = block_weights(queries, key_rows, query_seg, key_seg, log_total).astype(
            jnp.bfloat16
        )
        return (
            carry
            + jnp.einsum("hqk,khd->qhd", weights, value_rows, preferred_element_type=jnp.float32),
            None,
        )

    total, unused = lax.scan(
        weighted_advance,
        jnp.zeros(queries.shape, jnp.float32),
        (key_blocks, value_blocks, seg_blocks),
    )
    return total


def grad_dots(queries, grad_heads, key_blocks, value_blocks, seg_blocks, query_seg, log_total):

    def grad_advance(carry, inputs_now):
        key_rows, value_rows, key_seg = inputs_now
        weights = block_weights(queries, key_rows, query_seg, key_seg, log_total)
        grad_weights = jnp.einsum(
            "qhd,khd->hqk", grad_heads, value_rows, preferred_element_type=jnp.float32
        )
        return (carry + jnp.sum(weights * grad_weights, -1), None)

    start = jnp.zeros((HEADS, queries.shape[0]), jnp.float32)
    total, unused = lax.scan(grad_advance, start, (key_blocks, value_blocks, seg_blocks))
    return total


def query_grads(
    queries, grad_heads, key_blocks, value_blocks, seg_blocks, query_seg, log_total, row_dots
):
    score_scale = HD ** (-0.5)

    def query_advance(carry, inputs_now):
        key_rows, value_rows, key_seg = inputs_now
        weights = block_weights(queries, key_rows, query_seg, key_seg, log_total)
        grad_weights = jnp.einsum(
            "qhd,khd->hqk", grad_heads, value_rows, preferred_element_type=jnp.float32
        )
        grad_scores = (weights * (grad_weights - row_dots[..., None])).astype(jnp.bfloat16)
        carry = (
            carry
            + jnp.einsum("hqk,khd->qhd", grad_scores, key_rows, preferred_element_type=jnp.float32)
            * score_scale
        )
        grad_keys = (
            jnp.einsum("hqk,qhd->khd", grad_scores, queries, preferred_element_type=jnp.float32)
            * score_scale
        )
        grad_values = jnp.einsum(
            "hqk,qhd->khd",
            weights.astype(jnp.bfloat16),
            grad_heads,
            preferred_element_type=jnp.float32,
        )
        return (carry, jnp.concatenate([head_join(grad_keys), head_join(grad_values)], 1))

    return lax.scan(
        query_advance, jnp.zeros(queries.shape, jnp.float32), (key_blocks, value_blocks, seg_blocks)
    )


def general_device(
    target_states,
    source_states,
    target_segments,
    source_segments,
    output_grad,
    self_project,
    self_output,
    cross_query,
    cross_keyval,
    cross_output,
    hidden_up,
    hidden_bias,
    hidden_down,
    output_bias,
    first_gain,
    first_shift,
    second_gain,
    second_shift,
    third_gain,
    third_shift,
):
    (
        full_project,
        full_output,
        full_query,
        full_keyval,
        full_crossout,
        full_up,
        full_upbias,
        full_down,
        full_downbias,
        gain_one,
        shift_one,
        gain_two,
        shift_two,
        gain_three,
        shift_three,
    ) = (
        lax.all_gather(self_project, ("rows", "seq"), axis=0, tiled=True),
        lax.all_gather(self_output, ("rows", "seq"), axis=0, tiled=True),
        lax.all_gather(cross_query, ("rows", "seq"), axis=0, tiled=True),
        lax.all_gather(cross_keyval, ("rows", "seq"), axis=0, tiled=True),
        lax.all_gather(cross_output, ("rows", "seq"), axis=0, tiled=True),
        lax.all_gather(hidden_up, ("rows", "seq"), axis=0, tiled=True),
        lax.all_gather(hidden_bias, ("rows", "seq"), axis=0, tiled=True),
        lax.all_gather(hidden_down, ("rows", "seq"), axis=0, tiled=True),
        lax.all_gather(output_bias, ("rows", "seq"), axis=0, tiled=True),
        lax.all_gather(first_gain, ("rows", "seq"), axis=0, tiled=True),
        lax.all_gather(first_shift, ("rows", "seq"), axis=0, tiled=True),
        lax.all_gather(second_gain, ("rows", "seq"), axis=0, tiled=True),
        lax.all_gather(second_shift, ("rows", "seq"), axis=0, tiled=True),
        lax.all_gather(third_gain, ("rows", "seq"), axis=0, tiled=True),
        lax.all_gather(third_shift, ("rows", "seq"), axis=0, tiled=True),
    )
    gain_one = gain_one.astype(jnp.float32)
    gain_two = gain_two.astype(jnp.float32)
    gain_three = gain_three.astype(jnp.float32)
    score_scale = HD ** (-0.5)
    states = target_states[0].astype(jnp.float32)
    local_rows = states.shape[0]
    model_width = states.shape[1]
    seq_count = lax.axis_size("seq")
    row_segments = target_segments[0]
    seq_length = row_segments.shape[0]
    own_segments = lax.dynamic_slice_in_dim(
        row_segments, lax.axis_index("seq") * local_rows, local_rows
    )
    block_rows = max(1, min(seq_count, 512 // local_rows)) * local_rows
    block_count = seq_length // block_rows
    seg_blocks = row_segments.reshape(block_count, block_rows)
    normed_value, normed_one, inverse_one = layer_norm(
        states, gain_one, shift_one.astype(jnp.float32)
    )
    lowered_one = normed_value.astype(jnp.bfloat16)
    projected = matmul(lowered_one, full_project).astype(jnp.bfloat16)
    query_flat = projected[:, :model_width]
    key_local = projected[:, model_width : 2 * model_width]
    value_local = projected[:, 2 * model_width :]
    queries = head_split(query_flat)
    key_all, value_all = (
        lax.all_gather(key_local, "seq", axis=0, tiled=True),
        lax.all_gather(value_local, "seq", axis=0, tiled=True),
    )
    key_blocks = key_all.reshape(block_count, block_rows, HEADS, HD)
    value_blocks = value_all.reshape(block_count, block_rows, HEADS, HD)
    log_total = log_totals(queries, key_blocks, seg_blocks, own_segments)
    self_mixed = head_join(
        weighted_sum(queries, key_blocks, value_blocks, seg_blocks, own_segments, log_total)
    ).astype(jnp.bfloat16)
    after_self = states + matmul(self_mixed, full_output)
    normed_value, normed_two, inverse_two = layer_norm(
        after_self, gain_two, shift_two.astype(jnp.float32)
    )
    lowered_two = normed_value.astype(jnp.bfloat16)
    cross_asked = matmul(lowered_two, full_query).astype(jnp.bfloat16)
    source_low = source_states[0]
    source_all = lax.all_gather(source_low, "seq", axis=0, tiled=True)
    key_value = matmul(source_all, full_keyval).astype(jnp.bfloat16)
    cross_key_heads = head_split(key_value[:, :model_width])
    cross_value_heads = head_split(key_value[:, model_width:])
    asked_heads = head_split(cross_asked)
    raw_scores, same_seg = scores_of(asked_heads, cross_key_heads, own_segments, source_segments[0])
    cross_probs = jax.nn.softmax(jnp.where(same_seg, raw_scores, -1000000000.0), axis=-1)
    cross_mixed = head_join(
        jnp.einsum(
            "hqk,khd->qhd",
            cross_probs.astype(jnp.bfloat16),
            cross_value_heads,
            preferred_element_type=jnp.float32,
        )
    ).astype(jnp.bfloat16)
    after_cross = after_self + matmul(cross_mixed, full_crossout)
    normed_value, normed_three, inverse_three = layer_norm(
        after_cross, gain_three, shift_three.astype(jnp.float32)
    )
    lowered_three = normed_value.astype(jnp.bfloat16)
    hidden = matmul(lowered_three, full_up) + full_upbias.astype(jnp.float32)
    activated = jax.nn.gelu(hidden).astype(jnp.bfloat16)
    layer_out = after_cross + matmul(activated, full_down) + full_downbias.astype(jnp.float32)
    grad_low = output_grad[0]
    out_grad = grad_low.astype(jnp.float32)
    grad_down = transposed(activated, grad_low)
    grad_downbias = jnp.sum(out_grad, 0)
    grad_act = against(grad_low, full_down)
    grad_hidden = jax.vjp(jax.nn.gelu, hidden)[1](grad_act)[0].astype(jnp.bfloat16)
    grad_upbias = jnp.sum(grad_hidden.astype(jnp.float32), 0)
    grad_up = transposed(lowered_three, grad_hidden)
    dx_three, grad_gain_three, grad_shift_three = norm_back(
        against(grad_hidden, full_up), normed_three, inverse_three, gain_three
    )
    grad_cross = out_grad + dx_three
    grad_cross_low = grad_cross.astype(jnp.bfloat16)
    grad_crossout = transposed(cross_mixed, grad_cross_low)
    grad_cross_heads = head_split(against(grad_cross_low, full_crossout).astype(jnp.bfloat16))
    grad_weights = jnp.einsum(
        "qhd,khd->hqk", grad_cross_heads, cross_value_heads, preferred_element_type=jnp.float32
    )
    grad_scores = (
        cross_probs * (grad_weights - jnp.sum(cross_probs * grad_weights, -1, keepdims=True))
    ).astype(jnp.bfloat16)
    grad_asked = head_join(
        jnp.einsum("hqk,khd->qhd", grad_scores, cross_key_heads, preferred_element_type=jnp.float32)
        * score_scale
    ).astype(jnp.bfloat16)
    grad_cross_keys = (
        jnp.einsum("hqk,qhd->khd", grad_scores, asked_heads, preferred_element_type=jnp.float32)
        * score_scale
    )
    grad_cross_values = jnp.einsum(
        "hqk,qhd->khd",
        cross_probs.astype(jnp.bfloat16),
        grad_cross_heads,
        preferred_element_type=jnp.float32,
    )
    pair_terms = jnp.concatenate([head_join(grad_cross_keys), head_join(grad_cross_values)], 1)
    pair_grad = lax.psum_scatter(
        pair_terms.astype(jnp.bfloat16), "seq", scatter_dimension=0, tiled=True
    )
    grad_keyval = transposed(source_low, pair_grad)
    grad_source = against(pair_grad, full_keyval)
    grad_query = transposed(lowered_two, grad_asked)
    dx_two, grad_gain_two, grad_shift_two = norm_back(
        against(grad_asked, full_query), normed_two, inverse_two, gain_two
    )
    grad_self = grad_cross + dx_two
    grad_self_low = grad_self.astype(jnp.bfloat16)
    grad_output = transposed(self_mixed, grad_self_low)
    grad_mixed = against(grad_self_low, full_output).astype(jnp.bfloat16)
    grad_heads = head_split(grad_mixed)
    row_dots = grad_dots(
        queries, grad_heads, key_blocks, value_blocks, seg_blocks, own_segments, log_total
    )
    grad_queries, key_terms = query_grads(
        queries, grad_heads, key_blocks, value_blocks, seg_blocks, own_segments, log_total, row_dots
    )
    summed = lax.psum_scatter(
        key_terms.reshape(seq_length, 2 * model_width).astype(jnp.bfloat16),
        "seq",
        scatter_dimension=0,
        tiled=True,
    )
    grad_projected = jnp.concatenate([head_join(grad_queries).astype(jnp.bfloat16), summed], 1)
    grad_project = transposed(lowered_one, grad_projected)
    dx_one, grad_gain_one, grad_shift_one = norm_back(
        against(grad_projected, full_project), normed_one, inverse_one, gain_one
    )
    grad_target = grad_self + dx_one
    shards = (
        lax.psum_scatter(grad_project, ("rows", "seq"), scatter_dimension=0, tiled=True),
        lax.psum_scatter(grad_output, ("rows", "seq"), scatter_dimension=0, tiled=True),
        lax.psum_scatter(grad_query, ("rows", "seq"), scatter_dimension=0, tiled=True),
        lax.psum_scatter(grad_keyval, ("rows", "seq"), scatter_dimension=0, tiled=True),
        lax.psum_scatter(grad_crossout, ("rows", "seq"), scatter_dimension=0, tiled=True),
        lax.psum_scatter(grad_up, ("rows", "seq"), scatter_dimension=0, tiled=True),
        lax.psum_scatter(grad_upbias, ("rows", "seq"), scatter_dimension=0, tiled=True),
        lax.psum_scatter(grad_down, ("rows", "seq"), scatter_dimension=0, tiled=True),
        lax.psum_scatter(grad_downbias, ("rows", "seq"), scatter_dimension=0, tiled=True),
        lax.psum_scatter(grad_gain_one, ("rows", "seq"), scatter_dimension=0, tiled=True),
        lax.psum_scatter(grad_shift_one, ("rows", "seq"), scatter_dimension=0, tiled=True),
        lax.psum_scatter(grad_gain_two, ("rows", "seq"), scatter_dimension=0, tiled=True),
        lax.psum_scatter(grad_shift_two, ("rows", "seq"), scatter_dimension=0, tiled=True),
        lax.psum_scatter(grad_gain_three, ("rows", "seq"), scatter_dimension=0, tiled=True),
        lax.psum_scatter(grad_shift_three, ("rows", "seq"), scatter_dimension=0, tiled=True),
    )
    return (layer_out.astype(jnp.bfloat16)[None], grad_target[None], grad_source[None]) + tuple(
        shards
    )


F32, BF16 = jnp.float32, jnp.bfloat16
BLOCK = 16
AXES = ("rows", "seq")
FLIP_Y, FLIP_CORE, FLIP_X, FLIP_Z = 1, 2, 4, 8
MODEL, FEED, OWN, WINDOW, HALF_SOURCE = 512, 2048, 512, 256, 192
KEYS, SOURCES = OWN + WINDOW, 2 * HALF_SOURCE
TILE = 128
MASKED = -1000000000.0
SCALE = HD ** (-0.5)


def exchange(value, flip):
    return lax.ppermute(value, AXES, [(device, device ^ flip) for device in range(32)])


def exchange_side(value, step):
    flips = (FLIP_X, FLIP_Y) if step == 0 else (FLIP_Y, FLIP_X)
    return lax.ppermute(value, AXES, [(device, device ^ flips[device >> 1 & 1]) for device in range(32)])


def tied(values, *others):
    return lax.optimization_barrier((values, others))[0]


def along_z(block):
    return [exchange(block, FLIP_Z * i) for i in Z_ORDER]


Z_ORDER = (1, 2, 3)


def join(*parts):
    return jnp.concatenate(parts, 0)


def both_cores(halves):
    return halves + [exchange(half, FLIP_CORE) for half in halves]


def add_halves(kept, came):
    half = kept.shape[0] // 2
    return kept[half:] + came[half:], kept[:half] + came[:half]


def z_blocks(both):
    size = both.shape[0] // 4
    blocks = [both[size * i : size * (i + 1)] for i in range(4)]
    return [blocks[0]] + [exchange(block, FLIP_Z * i) for i, block in zip(Z_ORDER, blocks[1:])]


def block_places(me):
    out = []
    for other in (0, 1):
        core = (me >> 1 & 1) ^ other
        first, second = FLIP_X - 3 * core, FLIP_Y + 3 * core
        for b in (0, 1):
            for a in (0, 1):
                for i, z in enumerate((0,) + Z_ORDER):
                    owner = me ^ (other * FLIP_CORE + b * second + a * first + z * FLIP_Z)
                    out.append((other * 2 + b, a * 4 + i, owner))
    return out


def nn(left, right):
    return jnp.dot(left, right, preferred_element_type=F32)


def block_rows(owner, size=BLOCK):
    return pl.ds(pl.multiple_of(owner * size, size), size)


def load_blocks(me, pieces, columns, target):
    for piece, row, owner in block_places(me):
        target[block_rows(owner), :] = pieces[piece][row * BLOCK : (row + 1) * BLOCK, columns]


def store_blocks(me, source, targets, columns):
    for piece, row, owner in block_places(me):
        at = (piece % 2 * 8 + row) * BLOCK
        targets[piece // 2][at : at + BLOCK, columns] = source[block_rows(owner), :]


def normed_rows(value):
    centered = value - jnp.mean(value, -1, keepdims=True)
    inverse = lax.rsqrt(jnp.mean(centered * centered, -1, keepdims=True) + 1e-05)
    return centered * inverse, inverse


def norm_back_rows(upstream, normed, inverse, gain):
    scaled = upstream * gain
    first_mean = jnp.mean(scaled, -1, keepdims=True)
    second_mean = jnp.mean(scaled * normed, -1, keepdims=True)
    return inverse * (scaled - first_mean - normed * second_mean)


def column_sum(value):
    return jnp.sum(value, 0, keepdims=True)


def own_segments_of(index, segments):
    return jnp.where(index == 0, segments[:, :OWN], segments[:, OWN:]).astype(F32)


def key_segments_of(index, segments):
    near = jnp.where(index == 0, segments[:, OWN:KEYS], segments[:, OWN - WINDOW : OWN])
    return jnp.concatenate([own_segments_of(index, segments), near.astype(F32)], 1)


def spread(row):
    return jnp.broadcast_to(row, (TILE, row.shape[1])).T


def lane_half(shape, half):
    lanes = lax.broadcasted_iota(jnp.int32, shape, 1)
    return (lanes < HD) if half == 0 else (lanes >= HD)


def half_masks(value):
    keep, zero = lane_half(value.shape, 0), jnp.zeros_like(value)
    return jnp.concatenate([jnp.where(keep, value, zero), jnp.where(keep, zero, value)], 0)


def self_jobs(side):
    near, far = pl.multiple_of((1 - side) * 256, 256), pl.multiple_of(side * 256, 256)
    skip_near, skip_far = pl.multiple_of((1 - side) * TILE, TILE), pl.multiple_of(side * TILE, TILE)
    return [
        (pl.ds(near, 256), [(skip_near, 384), (OWN, WINDOW)], 256),
        (pl.ds(far, 256), [(skip_far, 384)], 256),
    ]


def attend(queries, pair_ref, mixed, log_rows, query_seg, key_row, jobs):
    for rows, spans, size in jobs:

        def keys_of(ref, lanes):
            parts = [ref[pl.ds(start, count), lanes] for start, count in spans]
            return parts[0] if len(parts) == 1 else jnp.concatenate(parts, 0)

        segments = [key_row[:, pl.ds(start, count)] for start, count in spans]
        segments = segments[0] if len(segments) == 1 else jnp.concatenate(segments, 1)
        same = jnp.concatenate([query_seg[rows, :]] * (segments.shape[1] // TILE), 1) == segments
        bias = jnp.where(same, 0.0, MASKED)
        lanes = lax.broadcasted_iota(jnp.int32, (size, TILE), 1)
        logs = jnp.zeros((size, TILE), F32)
        for pair in range(HEADS // 2):
            at = slice(pair * TILE, (pair + 1) * TILE)
            scores = against(half_masks(queries[rows, at]), keys_of(pair_ref, at))
            weights, scales = [], []
            for half in range(2):
                part = scores[half * size : (half + 1) * size] + bias
                top = jnp.max(part, -1, keepdims=True)
                part = jnp.exp(part - top)
                total = jnp.sum(part, -1, keepdims=True)
                weights.append(part.astype(BF16))
                scales.append(1.0 / total)
                logs = jnp.where(lanes == pair * 2 + half, top + jnp.log(total), logs)
            values = keys_of(pair_ref, slice(MODEL + pair * TILE, MODEL + (pair + 1) * TILE))
            out = nn(jnp.concatenate(weights, 0), values)
            keep = lane_half((size, TILE), 0)
            mixed[rows, at] = jnp.where(keep, out[:size] * scales[0], out[size:] * scales[1]).astype(BF16)
        log_rows[:, rows] = logs.T[:HEADS]


def head_dots(upstream, mixed):
    head = lax.broadcasted_iota(jnp.int32, (HEADS, MODEL), 1) // HD
    ones = (head == lax.broadcasted_iota(jnp.int32, (HEADS, MODEL), 0)).astype(F32)
    return lax.dot_general(
        ones, upstream.astype(F32) * mixed.astype(F32), (((1,), (1,)), ((), ())),
        precision=lax.Precision.HIGHEST, preferred_element_type=F32,
    )


def attend_back(queries, upstream, pair_ref, log_rows, dot_rows, query_row, key_seg, query_grad, pair_grad, jobs):
    query_grad[...] = jnp.zeros_like(query_grad)
    for key_start, size, start, count in jobs:
        rows, across = pl.ds(key_start, size), pl.ds(start, count)

        def heads(step, unused):
            same = jnp.concatenate([key_seg[rows, :]] * (count // TILE), 1) == query_row[:, across]
            bias = jnp.where(same, 0.0, MASKED)
            for pair in (step * 2, step * 2 + 1):
                at = pl.ds(pl.multiple_of(pair * TILE, TILE), TILE)
                value_at = pl.ds(pl.multiple_of(MODEL + pair * TILE, TILE), TILE)
                query = queries[across, at]
                grad = upstream[across, at]
                keys = half_masks(pair_ref[rows, at])
                values = half_masks(pair_ref[rows, value_at])
                scores, grads = against(keys, query), against(values, grad)
                weights, score_grads = [], []
                for half in range(2):
                    head, part = pl.ds(pair * 2 + half, 1), slice(half * size, (half + 1) * size)
                    weight = jnp.exp(scores[part] + (bias - log_rows[head, across]))
                    score_grads.append((weight * (grads[part] - dot_rows[head, across])).astype(BF16))
                    weights.append(weight.astype(BF16))
                score_grad = jnp.concatenate(score_grads, 0)
                value_part = nn(jnp.concatenate(weights, 0), grad)
                key_part = nn(score_grad, query)
                query_grad[across, at] += transposed(score_grad, keys)
                keep = lane_half((size, TILE), 0)
                pair_grad[rows, at] = jnp.where(keep, key_part[:size], key_part[size:]).astype(BF16)
                pair_grad[rows, value_at] = jnp.where(keep, value_part[:size], value_part[size:]).astype(BF16)
            return unused

        lax.fori_loop(0, HEADS // 4, heads, 0)


def self_back_jobs(side):
    near = pl.multiple_of((1 - side) * 256, 256)
    return [(0, 256, 0, 384), (256, 256, TILE, 384), (OWN, WINDOW, near, 256)]


def pack_body(
    place, vectors, project, output, query, keyval, crossout, up, down, states, source,
    one, three, near, own_source, block, semaphores
):
    me, side = place[0], place[1]
    copies = [
        (project, one.at[:, :1536]),
        (output, one.at[:, 1664:2176]),
        (query, one.at[:, 2176:2688]),
        (keyval, one.at[:, 2688:3712]),
        (crossout, one.at[:, 3712:]),
        (down, three.at[64:]),
    ] + [
        (up.at[:, part * 512 : (part + 1) * 512], three.at[part * BLOCK : (part + 1) * BLOCK, :])
        for part in range(4)
    ] + [
        (states.at[pl.ds(pl.multiple_of((1 - side) * WINDOW, WINDOW), WINDOW), :], near.at[:WINDOW])
    ]
    copies = [pltpu.make_async_copy(*copy, semaphores.at[i]) for i, copy in enumerate(copies)]
    for copy in copies:
        copy.start()
    gap = jnp.zeros((HALF_SOURCE - source.shape[0], MODEL), F32)
    padded = jnp.concatenate([source[...].astype(F32), gap], 0).astype(BF16)
    own_source[...] = padded
    near[WINDOW:, :] = padded
    values = jnp.broadcast_to(vectors[...].astype(F32), (8, 256))
    lanes = lax.broadcasted_iota(jnp.int32, (8, TILE), 1)
    rows = lax.broadcasted_iota(jnp.int32, (8, TILE), 0)
    packed = jnp.zeros((8, TILE), F32)
    spot, wide = (me & 7) * 16, (me & 1) * 64
    for row in range(7):
        moved = pltpu.roll(values, spot + 256 - 16 * row, 1)[:, :TILE]
        inside = jnp.logical_and(lanes >= spot, lanes < spot + 16)
        packed = jnp.where(jnp.logical_and(rows == row, inside), moved, packed)
    moved = pltpu.roll(values, wide + 256 - 112, 1)[:, :TILE]
    inside = jnp.logical_and(lanes >= wide, lanes < wide + 64)
    packed = jnp.where(jnp.logical_and(rows == 7, inside), moved, packed)
    block[...] = jnp.concatenate([packed, jnp.zeros((8, TILE), F32)], 0).astype(BF16)
    last = pltpu.make_async_copy(block, one.at[:, 1536:1664], semaphores.at[len(copies)])
    last.start()
    for copy in copies + [last]:
        copy.wait()


def self_body(place, states, window, *refs):
    pieces, refs = refs[:4], refs[4:]
    queries, pair, lowered, vectors, up_bias, weight, weight_two, packed = refs
    me = place[0]
    load_blocks(me, pieces, slice(1536, 1664), packed)
    load_blocks(me, pieces, slice(0, 1536), weight)
    load_blocks(me, pieces, slice(1664, 4224), weight_two)
    for tile in range(4):
        total = jnp.zeros((8, TILE), F32)
        for i in range(8):
            total = total + packed[(tile * 8 + i) * BLOCK : (tile * 8 + i + 1) * BLOCK, :].astype(F32)[:8]
        vectors[:, tile * TILE : (tile + 1) * TILE] = total
    for tile in range(16):
        total = (
            packed[2 * tile * BLOCK : (2 * tile + 1) * BLOCK, :].astype(F32)
            + packed[(2 * tile + 1) * BLOCK : (2 * tile + 2) * BLOCK, :].astype(F32)
        )
        up_bias[:, tile * TILE : (tile + 1) * TILE] = total[7:8]
    gain, shift = vectors[1:2, :], vectors[2:3, :]
    for i in range(KEYS // TILE):
        rows = slice(i * TILE, (i + 1) * TILE)
        value = states[rows, :] if i < 4 else window[(i - 4) * TILE : (i - 3) * TILE, :]
        lowered[rows, :] = (normed_rows(value.astype(F32))[0] * gain + shift).astype(BF16)
    for i in range(KEYS // 256):
        rows = slice(i * 256, (i + 1) * 256)
        if i < 2:
            queries[rows, :] = (nn(lowered[rows, :], weight[:, :512]) .astype(BF16) * SCALE).astype(BF16)
        pair[rows, :] = nn(lowered[rows, :], weight[:, 512:]).astype(BF16)


def forward_body(
    place, segments, source_segments, states, own_source, other_source, vectors, weight, self_queries, self_pair,
    self_mixed, self_logs, after_self, lowered, queries, pair, mixed, logs, after_cross,
    query_seg, key_row, source_row, source,
):
    self_mix(place, segments, self_queries, self_pair, self_mixed, self_logs, query_seg, key_row)
    cross_lower(
        place, states, own_source, other_source, self_mixed, vectors, after_self, lowered, queries, pair, weight, source
    )
    source_row[...] = source_segments[...].astype(F32)
    attend(queries, pair, mixed, logs, query_seg, source_row, [(pl.ds(0, OWN), [(0, SOURCES)], OWN)])
    for i in range(2):
        rows = slice(i * 256, (i + 1) * 256)
        after_cross[rows, :] = after_self[rows, :] + nn(mixed[rows, :], weight[:, 2048:])


def self_mix(place, segments, queries, pair, mixed, log_rows, query_seg, key_row):
    query_seg[...] = spread(own_segments_of(place[1], segments[...]))
    key_row[...] = key_segments_of(place[1], segments[...])
    attend(queries, pair, mixed, log_rows, query_seg, key_row, self_jobs(place[1]))


def cross_lower(
    place, states, own_source, other_source, self_mixed, vectors, after_self, lowered, queries, pair, weight, source
):
    side = place[1]
    source[:HALF_SOURCE, :] = jnp.where(side == 0, own_source[...], other_source[...])
    source[HALF_SOURCE:, :] = jnp.where(side == 0, other_source[...], own_source[...])
    gain, shift = vectors[3:4, :], vectors[4:5, :]
    pair[...] = nn(source[...], weight[:, 1024:2048]).astype(BF16)
    for i in range(2):
        rows = slice(i * 256, (i + 1) * 256)
        value = states[rows, :].astype(F32) + nn(self_mixed[rows, :], weight[:, :512])
        after_self[rows, :] = value
        lowered[rows, :] = (normed_rows(value)[0] * gain + shift).astype(BF16)
        queries[rows, :] = (nn(lowered[rows, :], weight[:, 512:1024]).astype(BF16) * SCALE).astype(BF16)


CHUNK, UNROLL = 512, 2


def feed_body(place, after_cross, output_grad, vectors, up_bias, *refs):
    pieces, refs = refs[:4], refs[4:]
    (
        total, back, kept, sent, bias_sums, ups, downs, lowered, flipped, up_grads, down_grads,
    ) = refs
    me = place[0]
    places = block_places(me)

    def chunk_of(z):
        return pl.multiple_of(((me >> 3) ^ z) * CHUNK, CHUNK)

    gain, shift = vectors[5:6, :], vectors[6:7, :]
    for i in range(4):
        rows = slice(i * TILE, (i + 1) * TILE)
        low = (normed_rows(after_cross[rows, :])[0] * gain + shift).astype(BF16)
        lowered[rows, :] = low
    flipped[...] = lowered[...].T
    grad_low = output_grad[...]
    total[...] = jnp.zeros_like(total)
    back[...] = jnp.zeros_like(back)

    def chunk(z):
        at = pl.ds(chunk_of(z), CHUNK)
        mine = me >> 3
        z_row = (mine ^ z) * BLOCK
        up, down, up_grad, down_grad = ups.at[z], downs.at[z], up_grads.at[z], down_grads.at[z]
        swapped_z = (z & 1) * 2 + (z >> 1)
        for piece, row, owner in places:
            owner = (owner & 7) + (mine ^ (row % 2 * 2 + row % 4 // 2)) * FLIP_Z
            up[block_rows(owner), :] = pieces[piece][pl.ds(pl.multiple_of(row * 128 + z_row, BLOCK), BLOCK), :]
            if row % 4 == 0:
                start = pl.multiple_of((row + swapped_z) * 128 + 64, 64)
                down[block_rows(owner & 7, 64), :] = pieces[piece][pl.ds(start, 64), :]
        hidden = nn(lowered[...], up[...]) + up_bias[:, at]
        square = hidden * hidden
        inner = 0.7978845608028654 * hidden * (1.0 + 0.044715 * square)
        curve = jnp.tanh(inner)
        half = 0.5 * (1.0 + curve)
        activated = (hidden * half).astype(BF16)
        slope = half + (0.5 * 0.7978845608028654) * hidden * (1.0 - curve * curve) * (
            1.0 + (3 * 0.044715) * square
        )
        down_grad[...] = transposed(activated, grad_low).astype(BF16)
        for piece, row, owner in places:
            if row % 4 == 0:
                to = pl.multiple_of((piece % 2 * 8 + row + z) * 128 + 64, 64)
                (kept, sent)[piece // 2][pl.ds(to, 64), :] = down_grad[block_rows(owner & 7, 64), :]
        grad_hidden = (against(grad_low, down[...]) * slope).astype(BF16)
        bias_sums[:, at] = column_sum(grad_hidden.astype(F32))
        up_grad[...] = nn(flipped[...], grad_hidden).astype(BF16)
        for piece, row, owner in places:
            to = (piece % 2 * 8 + row) * 128
            (kept, sent)[piece // 2][pl.ds(pl.multiple_of(to + z_row, BLOCK), BLOCK), :] = up_grad[block_rows(owner), :]
        total[...] += nn(activated, down[...])
        back[...] += against(grad_hidden, up[...])

    def chunks(step, unused):
        for z in range(UNROLL):
            chunk(step * UNROLL + z)
        return unused

    lax.fori_loop(0, 4 // UNROLL, chunks, 0)


def feed_last_body(place, after_cross, output_grad, vectors, total, back, layer_out, after_grad, sums):
    gain = vectors[5:6, :]
    gain_sum, shift_sum, bias_sum = (jnp.zeros((1, MODEL), F32) for _ in range(3))
    for i in range(4):
        rows = slice(i * TILE, (i + 1) * TILE)
        value, grad = after_cross[rows, :], output_grad[rows, :].astype(F32)
        layer_out[rows, :] = (value + total[rows, :] + vectors[0:1, :]).astype(BF16)
        normed, inverse = normed_rows(value)
        upstream = back[rows, :]
        after_grad[rows, :] = grad + norm_back_rows(upstream, normed, inverse, gain)
        gain_sum, shift_sum = gain_sum + column_sum(upstream * normed), shift_sum + column_sum(upstream)
        bias_sum = bias_sum + column_sum(grad)
    zero = jnp.zeros((1, MODEL), F32)
    sums[...] = jnp.concatenate([bias_sum, zero, zero, zero, zero, gain_sum, shift_sum, zero], 0)


def cross_back_body(
    place, segments, source_segments, own_source, other_source, queries, pair, mixed, log_rows, after_grad, weight,
    asked, source_own, source_send, grads, upstream, query_grad, pair_grad, source, key_seg, query_row,
    dot_rows,
):
    side = place[1]
    key_seg[...] = spread(source_segments[...].astype(F32))
    query_row[...] = own_segments_of(side, segments[...])
    source[:HALF_SOURCE, :] = jnp.where(side == 0, own_source[...], other_source[...])
    source[HALF_SOURCE:, :] = jnp.where(side == 0, other_source[...], own_source[...])
    grad_low = after_grad[...].astype(BF16)
    upstream[...] = against(grad_low, weight[:, 2048:]).astype(BF16)
    dot_rows[...] = head_dots(upstream[...], mixed[...])
    grads[:, :512] = transposed(mixed[...], grad_low).astype(BF16)
    attend_back(
        queries, upstream, pair, log_rows, dot_rows, query_row, key_seg, query_grad, pair_grad,
        [(0, SOURCES, 0, OWN)],
    )
    asked[...] = (query_grad[...] * SCALE).astype(BF16)
    grads[:, 512:] = transposed(source[...], pair_grad[...]).astype(BF16)
    back = against(pair_grad[...], weight[:, 1024:2048])
    first, second = back[:HALF_SOURCE], back[HALF_SOURCE:]
    source_own[...] = jnp.where(side == 0, first, second)
    source_send[...] = jnp.where(side == 0, second, first).astype(BF16)


def cross_weight_body(
    place, after_self, lowered, self_mixed, after_grad, asked, vectors, sums, weight, some_grads, *refs
):
    self_grad, upstream, dot_rows, kept, sent, new_sums, grads = refs
    me = place[0]
    store_blocks(me, some_grads, (kept, sent), slice(0, 1536))
    gain = vectors[3:4, :]
    gain_sum, shift_sum = jnp.zeros((1, MODEL), F32), jnp.zeros((1, MODEL), F32)
    for i in range(2):
        rows = slice(i * 256, (i + 1) * 256)
        normed, inverse = normed_rows(after_self[rows, :])
        up = against(asked[rows, :], weight[:, 512:1024])
        self_grad[rows, :] = after_grad[rows, :] + norm_back_rows(up, normed, inverse, gain)
        gain_sum, shift_sum = gain_sum + column_sum(up * normed), shift_sum + column_sum(up)
    grads[:, :512] = transposed(lowered[...], asked[...]).astype(BF16)
    grad_low = self_grad[...].astype(BF16)
    grads[:, 512:] = transposed(self_mixed[...], grad_low).astype(BF16)
    store_blocks(me, grads, (kept, sent), slice(1536, 2560))
    upstream[...] = against(grad_low, weight[:, :512]).astype(BF16)
    dot_rows[...] = head_dots(upstream[...], self_mixed[...])
    zero = jnp.zeros((1, MODEL), F32)
    new_sums[...] = sums[...] + jnp.concatenate(
        [zero, zero, zero, gain_sum, shift_sum, zero, zero, zero], 0
    )


def self_back_body(
    place, segments, states, window, lowered, queries, pair, log_rows, upstream, dot_rows, weight, sums, bias_sums,
    source_send, own_back, near_back, kept, sent, query_grad, pair_grad, grads, key_seg, query_row,
):
    near_back[WINDOW:, :] = source_send[...]
    key_seg[...] = spread(key_segments_of(place[1], segments[...]))
    query_row[...] = own_segments_of(place[1], segments[...])
    attend_back(
        queries, upstream, pair, log_rows, dot_rows, query_row, key_seg, query_grad, pair_grad,
        self_back_jobs(place[1]),
    )
    asked = (query_grad[...] * SCALE).astype(BF16)
    grads[:, :MODEL] = transposed(lowered[:OWN, :], asked).astype(BF16)
    grads[:, MODEL:1536] = transposed(lowered[...], pair_grad[...]).astype(BF16)
    gain_sum, shift_sum = jnp.zeros((1, MODEL), F32), jnp.zeros((1, MODEL), F32)
    for i in range(3):
        rows = slice(i * 256, (i + 1) * 256)
        part = against(pair_grad[rows, :], weight[:, MODEL:])
        if i < 2:
            part = part + against(asked[rows, :], weight[:, :MODEL])
            own_back[rows, :] = part
            value = states[rows, :]
        else:
            near_back[:WINDOW, :] = part.astype(BF16)
            value = window[...]
        normed = normed_rows(value.astype(F32))[0]
        gain_sum, shift_sum = gain_sum + column_sum(part * normed), shift_sum + column_sum(part)
    zero = jnp.zeros((1, MODEL), F32)
    sums = sums[...] + jnp.concatenate([zero, gain_sum, shift_sum, zero, zero, zero, zero, zero], 0)
    last = lax.broadcasted_iota(jnp.int32, (8, TILE), 0) == 7
    for device in range(32):
        tile, wide = device // 8 * TILE, device // 2 * TILE
        value = jnp.where(last, bias_sums[:, wide : wide + TILE], sums[:, tile : tile + TILE])
        high = value.astype(BF16).astype(F32)
        grads[device * BLOCK : (device + 1) * BLOCK, 1536:] = jnp.concatenate([high, value - high], 0).astype(BF16)
    store_blocks(place[0], grads, (kept, sent), slice(0, 1664))


def target_body(place, back, came, states, self_grad, vectors, out):
    gain = vectors[1:2, :]
    for i in range(4):
        rows = slice(i * TILE, (i + 1) * TILE)
        here = (i < 2) == (place[1] == 1)
        extra = came[(i % 2) * TILE : (i % 2 + 1) * TILE, :].astype(F32)
        upstream = back[rows, :] + jnp.where(here, extra, 0.0)
        normed, inverse = normed_rows(states[rows, :].astype(F32))
        out[rows, :] = self_grad[rows, :] + norm_back_rows(upstream, normed, inverse, gain)


def finish_body(place, *refs):
    feed, cross, last, outs = refs[:4], refs[4:8], refs[8:12], refs[12:]
    project, output, query, keyval, crossout, up, down, *small = outs
    me = place[0]

    def total(parts, begin, end, rows=slice(None)):
        value = parts[0][rows, begin:end].astype(F32)
        for part in parts[1:]:
            value = value + part[rows, begin:end].astype(F32)
        return value

    for part in range(4):
        rows = slice(part * BLOCK, (part + 1) * BLOCK)
        up[:, part * 512 : (part + 1) * 512] = total(feed, 0, MODEL, rows)
    down[...] = total(feed, 0, MODEL, slice(64, 128))
    crossout[...] = total(cross, 0, 512)
    keyval[...] = total(cross, 512, 1536)
    query[...] = total(cross, 1536, 2048)
    output[...] = total(cross, 2048, 2560)
    project[...] = total(last, 0, 1536)
    value = total(last, 1536, 1664)
    value = value[:8] + value[8:]
    narrow = pltpu.roll(value, (TILE - (me & 7) * 16) & 127, 1)
    wide = pltpu.roll(value, (TILE - (me & 1) * 64) & 127, 1)
    for row in range(7):
        small[row][...] = narrow[row : row + 1, :16]
    small[7][...] = wide[7:8, :64]


def shape_of(*shape, dtype=BF16):
    return jax.ShapeDtypeStruct(shape, dtype)


VMEM_SPEC = pl.BlockSpec(memory_space=pltpu.VMEM)
ANY_SPEC = pl.BlockSpec(memory_space=pl.ANY)
HBM_SPEC = pl.BlockSpec(memory_space=pltpu.HBM)
SMEM_SPEC = pl.BlockSpec(memory_space=pltpu.SMEM)


def call(body, name, place, inputs, pieces, outs, scratch, flops, any_outs=(), any_ins=(), vmem=20):
    return pl.pallas_call(
        body,
        name=name,
        out_shape=outs,
        in_specs=[SMEM_SPEC]
        + [HBM_SPEC if i in any_ins else VMEM_SPEC for i in range(len(inputs))]
        + [VMEM_SPEC] * len(pieces),
        out_specs=[ANY_SPEC if i in any_outs else VMEM_SPEC for i in range(len(outs))],
        scratch_shapes=scratch,
        compiler_params=pltpu.CompilerParams(vmem_limit_bytes=vmem * 2**20),
        cost_estimate=pl.CostEstimate(flops=flops, bytes_accessed=4 * 2**20, transcendentals=0),
    )(place, *inputs, *pieces)


def fast_device(
    target_states, source_states, target_segments, source_segments, output_grad, self_project,
    self_output, cross_query, cross_keyval, cross_output, hidden_up, hidden_bias, hidden_down,
    output_bias, first_gain, first_shift, second_gain, second_shift, third_gain, third_shift,
):
    vmem, dma = pltpu.VMEM, pltpu.SemaphoreType.DMA
    side = lax.axis_index("seq")
    place = jnp.stack([lax.axis_index("rows") * 2 + side, side]).astype(jnp.int32)
    states, grad = target_states[0], output_grad[0]
    small = jnp.pad(hidden_bias, (112, 80))
    for i, vector in enumerate(
        (output_bias, first_gain, first_shift, second_gain, second_shift, third_gain, third_shift)
    ):
        small = small + jnp.pad(vector, (16 * i, 240 - 16 * i))
    small = small.reshape(1, 256)
    one, three, near, own_source = call(
        pack_body, "pack", place,
        [
            small, self_project, self_output, cross_query, cross_keyval, cross_output, hidden_up, hidden_down, states,
            source_states[0],
        ],
        [],
        [
            shape_of(16, 4224), shape_of(128, MODEL), shape_of(WINDOW + HALF_SOURCE, MODEL),
            shape_of(HALF_SOURCE, MODEL),
        ],
        [vmem((BLOCK, TILE), BF16), dma((12,))], 1000000, any_ins=range(1, 9), vmem=60,
    )
    parts = along_z(one)
    near = exchange(near, FLIP_Y)
    one = join(one, *parts)
    one = tied(one, near)
    came = exchange_side(one, 0)
    three = tied(three, one)
    far = exchange(three, 2 * FLIP_Z)
    came = tied(came, far)
    one = join(one, came)
    one_core = exchange(one, FLIP_CORE)
    other = exchange_side(one, 1)
    three = join(three, tied(far, one))
    three = join(three, exchange(three, FLIP_Z))
    came = exchange_side(three, 0)
    other = tied(other, came)
    window, other_source = near[:WINDOW], near[WINDOW:]
    pieces_one = [one, other, one_core, exchange(other, FLIP_CORE)]
    three = join(three, came)
    three_core = exchange(three, FLIP_CORE)
    three_other = exchange_side(three, 1)
    half = source_states.shape[1]
    gap = jnp.full((1, HALF_SOURCE - half), -1, jnp.int32)
    source_seg = jnp.concatenate([source_segments[:, :half], gap, source_segments[:, half:], gap], 1)

    queries, pair, lowered, vectors, up_bias, weight_one, weight_two = call(
        self_body, "self_lower", place, [states, window], pieces_one,
        [
            shape_of(OWN, MODEL), shape_of(KEYS, 2 * MODEL), shape_of(KEYS, MODEL), shape_of(8, MODEL, dtype=F32),
            shape_of(1, FEED, dtype=F32), shape_of(MODEL, 1536), shape_of(MODEL, 2560),
        ],
        [vmem((MODEL, TILE), BF16)], 1000,
    )
    mixed, logs, after_self, lowered_two, queries_two, pair_two, mixed_two, logs_two, after_cross = call(
        forward_body, "forward", place,
        [
            target_segments, source_seg, states, own_source, other_source, vectors, weight_two, queries, pair,
        ],
        [],
        [
            shape_of(OWN, MODEL), shape_of(HEADS, OWN, dtype=F32), shape_of(OWN, MODEL, dtype=F32), shape_of(OWN, MODEL),
            shape_of(OWN, MODEL), shape_of(SOURCES, 2 * MODEL), shape_of(OWN, MODEL), shape_of(HEADS, OWN, dtype=F32),
            shape_of(OWN, MODEL, dtype=F32),
        ],
        [
            vmem((OWN, TILE), F32), vmem((1, KEYS), F32), vmem((1, SOURCES), F32), vmem((SOURCES, MODEL), BF16),
        ],
        1000,
    )
    three_core, three_other = tied((three_core, three_other), after_cross)
    pieces_three = [three, three_other, three_core, exchange(three_other, FLIP_CORE)]
    total, back, feed_kept, feed_sent, bias_sums = call(
        feed_body, "feed", place, [after_cross, grad, vectors, up_bias], pieces_three,
        [shape_of(OWN, MODEL, dtype=F32)] * 2 + [shape_of(2048, MODEL)] * 2 + [shape_of(1, FEED, dtype=F32)],
        [
            vmem((4, MODEL, CHUNK), BF16), vmem((4, CHUNK, MODEL), BF16), vmem((OWN, MODEL), BF16),
            vmem((MODEL, OWN), BF16), vmem((4, MODEL, CHUNK), BF16), vmem((4, CHUNK, MODEL), BF16),
        ],
        10000000000,
    )
    feed_came = exchange(feed_sent, FLIP_CORE)
    layer_out, after_grad, sums = call(
        feed_last_body, "feed_last", place, [after_cross, grad, vectors, total, back], [],
        [shape_of(OWN, MODEL), shape_of(OWN, MODEL, dtype=F32), shape_of(8, MODEL, dtype=F32)], [], 2000000000,
    )
    feed_came = tied(feed_came, after_grad)
    feed_sent, feed_kept = add_halves(feed_kept, feed_came)
    after_grad = tied(after_grad, feed_sent)
    feed_came = exchange_side(feed_sent, 1)
    asked, source_own, source_send, some_grads = call(
        cross_back_body, "cross_backward", place,
        [
            target_segments, source_seg, own_source, other_source, queries_two, pair_two, mixed_two, logs_two,
            after_grad, weight_two,
        ],
        [],
        [
            shape_of(OWN, MODEL), shape_of(HALF_SOURCE, MODEL, dtype=F32), shape_of(HALF_SOURCE, MODEL),
            shape_of(MODEL, 1536),
        ],
        [
            vmem((OWN, MODEL), BF16), vmem((OWN, MODEL), F32), vmem((SOURCES, 2 * MODEL), BF16),
            vmem((SOURCES, MODEL), BF16), vmem((SOURCES, TILE), F32), vmem((1, OWN), F32), vmem((HEADS, OWN), F32),
        ],
        10000000000,
    )
    self_grad, upstream, dot_rows, cross_kept, cross_sent, sums = call(
        cross_weight_body, "cross_weights", place,
        [after_self, lowered_two, mixed, after_grad, asked, vectors, sums, weight_two, some_grads], [],
        [shape_of(OWN, MODEL, dtype=F32), shape_of(OWN, MODEL), shape_of(HEADS, OWN, dtype=F32)]
        + [shape_of(256, 2560)] * 2 + [shape_of(8, MODEL, dtype=F32)],
        [vmem((MODEL, 1024), BF16)], 6000000000,
    )
    cross_came = exchange(cross_sent, FLIP_CORE)
    feed_came = tied(feed_came, upstream)
    feed_sent, feed_kept = add_halves(feed_kept, feed_came)
    feed_came = exchange_side(feed_sent, 0)
    cross_came = tied(cross_came, feed_sent)
    cross_sent, cross_kept = add_halves(cross_kept, cross_came)
    cross_came = exchange_side(cross_sent, 1)
    upstream = tied(upstream, cross_sent)
    own_back, near_back, last_kept, last_sent = call(
        self_back_body, "self_backward", place,
        [
            target_segments, states, window, lowered, queries, pair, logs, upstream, dot_rows, weight_one, sums,
            bias_sums, source_send,
        ],
        [],
        [shape_of(OWN, MODEL, dtype=F32), shape_of(WINDOW + HALF_SOURCE, MODEL)] + [shape_of(256, 1664)] * 2,
        [
            vmem((OWN, MODEL), F32), vmem((KEYS, 2 * MODEL), BF16), vmem((MODEL, 1664), BF16), vmem((KEYS, TILE), F32),
            vmem((1, OWN), F32),
        ],
        16000000000,
    )
    last_came = exchange(last_sent, FLIP_CORE)
    cross_came, feed_came = tied((cross_came, feed_came), own_back)
    feed = z_blocks(feed_kept + feed_came)
    cross_came = tied(cross_came, feed[0])
    cross_sent, cross_kept = add_halves(cross_kept, cross_came)
    last_came = tied(last_came, feed[0])
    last_sent, last_kept = add_halves(last_kept, last_came)
    last_came, cross_came = exchange_side(last_sent, 1), exchange_side(cross_sent, 0)
    cross_kept = cross_kept + cross_came
    last_came = tied(last_came, cross_kept)
    last_sent, last_kept = add_halves(last_kept, last_came)
    last_came = exchange_side(last_sent, 0)
    feed, near_back = tied((feed, near_back), last_sent)
    cross_kept = tied(cross_kept, feed)
    cross = z_blocks(cross_kept)
    near_came = exchange(near_back, FLIP_Y)
    last_came = tied(last_came, cross[0])
    last = z_blocks(last_kept + last_came)
    came, source_came = near_came[:WINDOW], near_came[WINDOW:]
    grad_source = source_own[:half] + source_came[:half].astype(F32)
    (grad_target,) = call(
        target_body, "target_grad", place, [own_back, came, states, self_grad, vectors], [],
        [shape_of(OWN, MODEL, dtype=F32)], [], 1000000,
    )
    last = tied(last, grad_target, grad_source)
    project, output, query, keyval, crossout, up, down, *small = call(
        finish_body, "finish", place, feed + cross + last, [],
        [
            shape_of(16, 1536, dtype=F32), shape_of(16, 512, dtype=F32), shape_of(16, 512, dtype=F32),
            shape_of(16, 1024, dtype=F32), shape_of(16, 512, dtype=F32), shape_of(16, 2048, dtype=F32),
            shape_of(64, 512, dtype=F32),
        ]
        + [shape_of(1, 16, dtype=F32)] * 7 + [shape_of(1, 64, dtype=F32)],
        [], 1000000,
    )
    *rows, up_sum = [row[0] for row in small]
    return (
        layer_out[None], grad_target[None], grad_source[None], project, output, query, keyval, crossout, up,
        up_sum, down, *rows,
    )


def specs():
    in_specs = (
        P("rows", "seq", None),
        P("rows", "seq", None),
        P("rows", None),
        P("rows", None),
        P("rows", "seq", None),
        P(("rows", "seq"), None),
        P(("rows", "seq"), None),
        P(("rows", "seq"), None),
        P(("rows", "seq"), None),
        P(("rows", "seq"), None),
        P(("rows", "seq"), None),
        P(("rows", "seq")),
        P(("rows", "seq"), None),
        P(("rows", "seq")),
        P(("rows", "seq")),
        P(("rows", "seq")),
        P(("rows", "seq")),
        P(("rows", "seq")),
        P(("rows", "seq")),
        P(("rows", "seq")),
    )
    out_specs = (
        P("rows", "seq", None),
        P("rows", "seq", None),
        P("rows", "seq", None),
        P(("rows", "seq"), None),
        P(("rows", "seq"), None),
        P(("rows", "seq"), None),
        P(("rows", "seq"), None),
        P(("rows", "seq"), None),
        P(("rows", "seq"), None),
        P(("rows", "seq")),
        P(("rows", "seq"), None),
        P(("rows", "seq")),
        P(("rows", "seq")),
        P(("rows", "seq")),
        P(("rows", "seq")),
        P(("rows", "seq")),
        P(("rows", "seq")),
        P(("rows", "seq")),
    )
    return in_specs, out_specs


def solution(mesh):
    in_specs, out_specs = specs()
    fast = mesh.shape["rows"] == 16 and mesh.shape["seq"] == 2
    return jax.shard_map(
        fast_device if fast else general_device,
        mesh=mesh, in_specs=in_specs, out_specs=out_specs, check_vma=False,
    )
```

```python
import jax
import jax.numpy as jnp
from jax import lax
from jax.experimental import pallas as pl
from jax.experimental.pallas import tpu as pltpu
from jax.sharding import PartitionSpec as P

HEADS = 8
HD = 64


def layer_norm(value, gain, shift):
    row_mean = jnp.mean(value, -1, keepdims=True)
    centered = value - row_mean
    variance = jnp.mean(centered * centered, -1, keepdims=True)
    inverse = lax.rsqrt(variance + 1e-05)
    normed = centered * inverse
    return (normed * gain + shift, normed, inverse)


def norm_back(upstream, normed, inverse, gain):
    scaled = upstream * gain
    first_mean = jnp.mean(scaled, -1, keepdims=True)
    second_mean = jnp.mean(scaled * normed, -1, keepdims=True)
    grad_input = inverse * (scaled - first_mean - normed * second_mean)
    return (grad_input, jnp.sum(upstream * normed, 0), jnp.sum(upstream, 0))


def matmul(left, right):
    return jnp.dot(left, right, preferred_element_type=jnp.float32)


def transposed(left, right):
    return lax.dot_general(
        left, right, (((0,), (0,)), ((), ())), preferred_element_type=jnp.float32
    )


def against(left, right):
    return lax.dot_general(
        left, right, (((1,), (1,)), ((), ())), preferred_element_type=jnp.float32
    )


def head_split(value):
    return value.reshape(value.shape[0], HEADS, HD)


def head_join(value):
    return value.reshape(value.shape[0], HEADS * HD)


def scores_of(queries, key_rows, query_seg, key_seg):
    raw_scores = jnp.einsum(
        "qhd,khd->hqk", queries, key_rows, preferred_element_type=jnp.float32
    ) * HD ** (-0.5)
    same_seg = (query_seg[:, None] == key_seg[None, :])[None]
    return (raw_scores, same_seg)


def block_weights(queries, key_rows, query_seg, key_seg, log_total):
    raw_scores, same_seg = scores_of(queries, key_rows, query_seg, key_seg)
    return jnp.where(same_seg, jnp.exp(raw_scores - log_total[..., None]), 0.0)


def log_totals(queries, key_blocks, seg_blocks, query_seg):

    def log_advance(carry, inputs_now):
        row_max, row_total = carry
        key_rows, key_seg = inputs_now
        raw_scores, same_seg = scores_of(queries, key_rows, query_seg, key_seg)
        masked = jnp.where(same_seg, raw_scores, -1000000000.0)
        new_max = jnp.maximum(row_max, jnp.max(masked, -1))
        shifted = jnp.where(same_seg, jnp.exp(masked - new_max[..., None]), 0.0)
        return ((new_max, row_total * jnp.exp(row_max - new_max) + jnp.sum(shifted, -1)), None)

    start = (
        jnp.full((HEADS, queries.shape[0]), -1000000000.0, jnp.float32),
        jnp.zeros((HEADS, queries.shape[0]), jnp.float32),
    )
    (row_max, row_total), unused = lax.scan(log_advance, start, (key_blocks, seg_blocks))
    return row_max + jnp.log(row_total)


def weighted_sum(queries, key_blocks, value_blocks, seg_blocks, query_seg, log_total):

    def weighted_advance(carry, inputs_now):
        key_rows, value_rows, key_seg = inputs_now
        weights = block_weights(queries, key_rows, query_seg, key_seg, log_total).astype(
            jnp.bfloat16
        )
        return (
            carry
            + jnp.einsum("hqk,khd->qhd", weights, value_rows, preferred_element_type=jnp.float32),
            None,
        )

    total, unused = lax.scan(
        weighted_advance,
        jnp.zeros(queries.shape, jnp.float32),
        (key_blocks, value_blocks, seg_blocks),
    )
    return total


def grad_dots(queries, grad_heads, key_blocks, value_blocks, seg_blocks, query_seg, log_total):

    def grad_advance(carry, inputs_now):
        key_rows, value_rows, key_seg = inputs_now
        weights = block_weights(queries, key_rows, query_seg, key_seg, log_total)
        grad_weights = jnp.einsum(
            "qhd,khd->hqk", grad_heads, value_rows, preferred_element_type=jnp.float32
        )
        return (carry + jnp.sum(weights * grad_weights, -1), None)

    start = jnp.zeros((HEADS, queries.shape[0]), jnp.float32)
    total, unused = lax.scan(grad_advance, start, (key_blocks, value_blocks, seg_blocks))
    return total


def query_grads(
    queries, grad_heads, key_blocks, value_blocks, seg_blocks, query_seg, log_total, row_dots
):
    score_scale = HD ** (-0.5)

    def query_advance(carry, inputs_now):
        key_rows, value_rows, key_seg = inputs_now
        weights = block_weights(queries, key_rows, query_seg, key_seg, log_total)
        grad_weights = jnp.einsum(
            "qhd,khd->hqk", grad_heads, value_rows, preferred_element_type=jnp.float32
        )
        grad_scores = (weights * (grad_weights - row_dots[..., None])).astype(jnp.bfloat16)
        carry = (
            carry
            + jnp.einsum("hqk,khd->qhd", grad_scores, key_rows, preferred_element_type=jnp.float32)
            * score_scale
        )
        grad_keys = (
            jnp.einsum("hqk,qhd->khd", grad_scores, queries, preferred_element_type=jnp.float32)
            * score_scale
        )
        grad_values = jnp.einsum(
            "hqk,qhd->khd",
            weights.astype(jnp.bfloat16),
            grad_heads,
            preferred_element_type=jnp.float32,
        )
        return (carry, jnp.concatenate([head_join(grad_keys), head_join(grad_values)], 1))

    return lax.scan(
        query_advance, jnp.zeros(queries.shape, jnp.float32), (key_blocks, value_blocks, seg_blocks)
    )


def general_device(
    target_states,
    source_states,
    target_segments,
    source_segments,
    output_grad,
    self_project,
    self_output,
    cross_query,
    cross_keyval,
    cross_output,
    hidden_up,
    hidden_bias,
    hidden_down,
    output_bias,
    first_gain,
    first_shift,
    second_gain,
    second_shift,
    third_gain,
    third_shift,
):
    (
        full_project,
        full_output,
        full_query,
        full_keyval,
        full_crossout,
        full_up,
        full_upbias,
        full_down,
        full_downbias,
        gain_one,
        shift_one,
        gain_two,
        shift_two,
        gain_three,
        shift_three,
    ) = (
        lax.all_gather(self_project, ("rows", "seq"), axis=0, tiled=True),
        lax.all_gather(self_output, ("rows", "seq"), axis=0, tiled=True),
        lax.all_gather(cross_query, ("rows", "seq"), axis=0, tiled=True),
        lax.all_gather(cross_keyval, ("rows", "seq"), axis=0, tiled=True),
        lax.all_gather(cross_output, ("rows", "seq"), axis=0, tiled=True),
        lax.all_gather(hidden_up, ("rows", "seq"), axis=0, tiled=True),
        lax.all_gather(hidden_bias, ("rows", "seq"), axis=0, tiled=True),
        lax.all_gather(hidden_down, ("rows", "seq"), axis=0, tiled=True),
        lax.all_gather(output_bias, ("rows", "seq"), axis=0, tiled=True),
        lax.all_gather(first_gain, ("rows", "seq"), axis=0, tiled=True),
        lax.all_gather(first_shift, ("rows", "seq"), axis=0, tiled=True),
        lax.all_gather(second_gain, ("rows", "seq"), axis=0, tiled=True),
        lax.all_gather(second_shift, ("rows", "seq"), axis=0, tiled=True),
        lax.all_gather(third_gain, ("rows", "seq"), axis=0, tiled=True),
        lax.all_gather(third_shift, ("rows", "seq"), axis=0, tiled=True),
    )
    gain_one = gain_one.astype(jnp.float32)
    gain_two = gain_two.astype(jnp.float32)
    gain_three = gain_three.astype(jnp.float32)
    score_scale = HD ** (-0.5)
    states = target_states[0].astype(jnp.float32)
    local_rows = states.shape[0]
    model_width = states.shape[1]
    seq_count = lax.axis_size("seq")
    row_segments = target_segments[0]
    seq_length = row_segments.shape[0]
    own_segments = lax.dynamic_slice_in_dim(
        row_segments, lax.axis_index("seq") * local_rows, local_rows
    )
    block_rows = max(1, min(seq_count, 512 // local_rows)) * local_rows
    block_count = seq_length // block_rows
    seg_blocks = row_segments.reshape(block_count, block_rows)
    normed_value, normed_one, inverse_one = layer_norm(
        states, gain_one, shift_one.astype(jnp.float32)
    )
    lowered_one = normed_value.astype(jnp.bfloat16)
    projected = matmul(lowered_one, full_project).astype(jnp.bfloat16)
    query_flat = projected[:, :model_width]
    key_local = projected[:, model_width : 2 * model_width]
    value_local = projected[:, 2 * model_width :]
    queries = head_split(query_flat)
    key_all, value_all = (
        lax.all_gather(key_local, "seq", axis=0, tiled=True),
        lax.all_gather(value_local, "seq", axis=0, tiled=True),
    )
    key_blocks = key_all.reshape(block_count, block_rows, HEADS, HD)
    value_blocks = value_all.reshape(block_count, block_rows, HEADS, HD)
    log_total = log_totals(queries, key_blocks, seg_blocks, own_segments)
    self_mixed = head_join(
        weighted_sum(queries, key_blocks, value_blocks, seg_blocks, own_segments, log_total)
    ).astype(jnp.bfloat16)
    after_self = states + matmul(self_mixed, full_output)
    normed_value, normed_two, inverse_two = layer_norm(
        after_self, gain_two, shift_two.astype(jnp.float32)
    )
    lowered_two = normed_value.astype(jnp.bfloat16)
    cross_asked = matmul(lowered_two, full_query).astype(jnp.bfloat16)
    source_low = source_states[0]
    source_all = lax.all_gather(source_low, "seq", axis=0, tiled=True)
    key_value = matmul(source_all, full_keyval).astype(jnp.bfloat16)
    cross_key_heads = head_split(key_value[:, :model_width])
    cross_value_heads = head_split(key_value[:, model_width:])
    asked_heads = head_split(cross_asked)
    raw_scores, same_seg = scores_of(asked_heads, cross_key_heads, own_segments, source_segments[0])
    cross_probs = jax.nn.softmax(jnp.where(same_seg, raw_scores, -1000000000.0), axis=-1)
    cross_mixed = head_join(
        jnp.einsum(
            "hqk,khd->qhd",
            cross_probs.astype(jnp.bfloat16),
            cross_value_heads,
            preferred_element_type=jnp.float32,
        )
    ).astype(jnp.bfloat16)
    after_cross = after_self + matmul(cross_mixed, full_crossout)
    normed_value, normed_three, inverse_three = layer_norm(
        after_cross, gain_three, shift_three.astype(jnp.float32)
    )
    lowered_three = normed_value.astype(jnp.bfloat16)
    hidden = matmul(lowered_three, full_up) + full_upbias.astype(jnp.float32)
    activated = jax.nn.gelu(hidden).astype(jnp.bfloat16)
    layer_out = after_cross + matmul(activated, full_down) + full_downbias.astype(jnp.float32)
    grad_low = output_grad[0]
    out_grad = grad_low.astype(jnp.float32)
    grad_down = transposed(activated, grad_low)
    grad_downbias = jnp.sum(out_grad, 0)
    grad_act = against(grad_low, full_down)
    grad_hidden = jax.vjp(jax.nn.gelu, hidden)[1](grad_act)[0].astype(jnp.bfloat16)
    grad_upbias = jnp.sum(grad_hidden.astype(jnp.float32), 0)
    grad_up = transposed(lowered_three, grad_hidden)
    dx_three, grad_gain_three, grad_shift_three = norm_back(
        against(grad_hidden, full_up), normed_three, inverse_three, gain_three
    )
    grad_cross = out_grad + dx_three
    grad_cross_low = grad_cross.astype(jnp.bfloat16)
    grad_crossout = transposed(cross_mixed, grad_cross_low)
    grad_cross_heads = head_split(against(grad_cross_low, full_crossout).astype(jnp.bfloat16))
    grad_weights = jnp.einsum(
        "qhd,khd->hqk", grad_cross_heads, cross_value_heads, preferred_element_type=jnp.float32
    )
    grad_scores = (
        cross_probs * (grad_weights - jnp.sum(cross_probs * grad_weights, -1, keepdims=True))
    ).astype(jnp.bfloat16)
    grad_asked = head_join(
        jnp.einsum("hqk,khd->qhd", grad_scores, cross_key_heads, preferred_element_type=jnp.float32)
        * score_scale
    ).astype(jnp.bfloat16)
    grad_cross_keys = (
        jnp.einsum("hqk,qhd->khd", grad_scores, asked_heads, preferred_element_type=jnp.float32)
        * score_scale
    )
    grad_cross_values = jnp.einsum(
        "hqk,qhd->khd",
        cross_probs.astype(jnp.bfloat16),
        grad_cross_heads,
        preferred_element_type=jnp.float32,
    )
    pair_terms = jnp.concatenate([head_join(grad_cross_keys), head_join(grad_cross_values)], 1)
    pair_grad = lax.psum_scatter(
        pair_terms.astype(jnp.bfloat16), "seq", scatter_dimension=0, tiled=True
    )
    grad_keyval = transposed(source_low, pair_grad)
    grad_source = against(pair_grad, full_keyval)
    grad_query = transposed(lowered_two, grad_asked)
    dx_two, grad_gain_two, grad_shift_two = norm_back(
        against(grad_asked, full_query), normed_two, inverse_two, gain_two
    )
    grad_self = grad_cross + dx_two
    grad_self_low = grad_self.astype(jnp.bfloat16)
    grad_output = transposed(self_mixed, grad_self_low)
    grad_mixed = against(grad_self_low, full_output).astype(jnp.bfloat16)
    grad_heads = head_split(grad_mixed)
    row_dots = grad_dots(
        queries, grad_heads, key_blocks, value_blocks, seg_blocks, own_segments, log_total
    )
    grad_queries, key_terms = query_grads(
        queries, grad_heads, key_blocks, value_blocks, seg_blocks, own_segments, log_total, row_dots
    )
    summed = lax.psum_scatter(
        key_terms.reshape(seq_length, 2 * model_width).astype(jnp.bfloat16),
        "seq",
        scatter_dimension=0,
        tiled=True,
    )
    grad_projected = jnp.concatenate([head_join(grad_queries).astype(jnp.bfloat16), summed], 1)
    grad_project = transposed(lowered_one, grad_projected)
    dx_one, grad_gain_one, grad_shift_one = norm_back(
        against(grad_projected, full_project), normed_one, inverse_one, gain_one
    )
    grad_target = grad_self + dx_one
    shards = (
        lax.psum_scatter(grad_project, ("rows", "seq"), scatter_dimension=0, tiled=True),
        lax.psum_scatter(grad_output, ("rows", "seq"), scatter_dimension=0, tiled=True),
        lax.psum_scatter(grad_query, ("rows", "seq"), scatter_dimension=0, tiled=True),
        lax.psum_scatter(grad_keyval, ("rows", "seq"), scatter_dimension=0, tiled=True),
        lax.psum_scatter(grad_crossout, ("rows", "seq"), scatter_dimension=0, tiled=True),
        lax.psum_scatter(grad_up, ("rows", "seq"), scatter_dimension=0, tiled=True),
        lax.psum_scatter(grad_upbias, ("rows", "seq"), scatter_dimension=0, tiled=True),
        lax.psum_scatter(grad_down, ("rows", "seq"), scatter_dimension=0, tiled=True),
        lax.psum_scatter(grad_downbias, ("rows", "seq"), scatter_dimension=0, tiled=True),
        lax.psum_scatter(grad_gain_one, ("rows", "seq"), scatter_dimension=0, tiled=True),
        lax.psum_scatter(grad_shift_one, ("rows", "seq"), scatter_dimension=0, tiled=True),
        lax.psum_scatter(grad_gain_two, ("rows", "seq"), scatter_dimension=0, tiled=True),
        lax.psum_scatter(grad_shift_two, ("rows", "seq"), scatter_dimension=0, tiled=True),
        lax.psum_scatter(grad_gain_three, ("rows", "seq"), scatter_dimension=0, tiled=True),
        lax.psum_scatter(grad_shift_three, ("rows", "seq"), scatter_dimension=0, tiled=True),
    )
    return (layer_out.astype(jnp.bfloat16)[None], grad_target[None], grad_source[None]) + tuple(
        shards
    )


F32, BF16 = jnp.float32, jnp.bfloat16
BLOCK = 16
AXES = ("rows", "seq")
FLIP_Y, FLIP_CORE, FLIP_X, FLIP_Z = 1, 2, 4, 8
MODEL, FEED, OWN, WINDOW, HALF_SOURCE = 512, 2048, 512, 256, 192
KEYS, SOURCES = OWN + WINDOW, 2 * HALF_SOURCE
TILE = 128
MASKED = -1000000000.0
SCALE = HD ** (-0.5)


def exchange(value, flip):
    return lax.ppermute(value, AXES, [(device, device ^ flip) for device in range(32)])


def exchange_side(value, step):
    flips = (FLIP_X, FLIP_Y) if step == 0 else (FLIP_Y, FLIP_X)
    return lax.ppermute(value, AXES, [(device, device ^ flips[device >> 1 & 1]) for device in range(32)])


def tied(values, *others):
    return lax.optimization_barrier((values, others))[0]


def along_z(block):
    return [exchange(block, FLIP_Z * i) for i in Z_ORDER]


Z_ORDER = (1, 2, 3)


def join(*parts):
    return jnp.concatenate(parts, 0)


def both_cores(halves):
    return halves + [exchange(half, FLIP_CORE) for half in halves]


def add_halves(kept, came):
    half = kept.shape[0] // 2
    return kept[half:] + came[half:], kept[:half] + came[:half]


def z_blocks(both):
    size = both.shape[0] // 4
    blocks = [both[size * i : size * (i + 1)] for i in range(4)]
    return [blocks[0]] + [exchange(block, FLIP_Z * i) for i, block in zip(Z_ORDER, blocks[1:])]


def block_places(me):
    out = []
    for other in (0, 1):
        core = (me >> 1 & 1) ^ other
        first, second = FLIP_X - 3 * core, FLIP_Y + 3 * core
        for b in (0, 1):
            for a in (0, 1):
                for i, z in enumerate((0,) + Z_ORDER):
                    owner = me ^ (other * FLIP_CORE + b * second + a * first + z * FLIP_Z)
                    out.append((other * 2 + b, a * 4 + i, owner))
    return out


def nn(left, right):
    return jnp.dot(left, right, preferred_element_type=F32)


def block_rows(owner, size=BLOCK):
    return pl.ds(pl.multiple_of(owner * size, size), size)


def load_blocks(me, pieces, columns, target):
    for piece, row, owner in block_places(me):
        target[block_rows(owner), :] = pieces[piece][row * BLOCK : (row + 1) * BLOCK, columns]


def store_blocks(me, source, targets, columns):
    for piece, row, owner in block_places(me):
        at = (piece % 2 * 8 + row) * BLOCK
        targets[piece // 2][at : at + BLOCK, columns] = source[block_rows(owner), :]


def normed_rows(value):
    centered = value - jnp.mean(value, -1, keepdims=True)
    inverse = lax.rsqrt(jnp.mean(centered * centered, -1, keepdims=True) + 1e-05)
    return centered * inverse, inverse


def norm_back_rows(upstream, normed, inverse, gain):
    scaled = upstream * gain
    first_mean = jnp.mean(scaled, -1, keepdims=True)
    second_mean = jnp.mean(scaled * normed, -1, keepdims=True)
    return inverse * (scaled - first_mean - normed * second_mean)


def column_sum(value):
    return jnp.sum(value, 0, keepdims=True)


def own_segments_of(index, segments):
    return jnp.where(index == 0, segments[:, :OWN], segments[:, OWN:]).astype(F32)


def key_segments_of(index, segments):
    near = jnp.where(index == 0, segments[:, OWN:KEYS], segments[:, OWN - WINDOW : OWN])
    return jnp.concatenate([own_segments_of(index, segments), near.astype(F32)], 1)


def spread(row):
    return jnp.broadcast_to(row, (TILE, row.shape[1])).T


def lane_half(shape, half):
    lanes = lax.broadcasted_iota(jnp.int32, shape, 1)
    return (lanes < HD) if half == 0 else (lanes >= HD)


def half_masks(value):
    keep, zero = lane_half(value.shape, 0), jnp.zeros_like(value)
    return jnp.concatenate([jnp.where(keep, value, zero), jnp.where(keep, zero, value)], 0)


def self_jobs(side):
    near, far = pl.multiple_of((1 - side) * 256, 256), pl.multiple_of(side * 256, 256)
    skip_near, skip_far = pl.multiple_of((1 - side) * TILE, TILE), pl.multiple_of(side * TILE, TILE)
    return [
        (pl.ds(near, 256), [(skip_near, 384), (OWN, WINDOW)], 256),
        (pl.ds(far, 256), [(skip_far, 384)], 256),
    ]


def attend(queries, pair_ref, mixed, log_rows, query_seg, key_row, jobs):
    for rows, spans, size in jobs:

        def keys_of(ref, lanes):
            parts = [ref[pl.ds(start, count), lanes] for start, count in spans]
            return parts[0] if len(parts) == 1 else jnp.concatenate(parts, 0)

        segments = [key_row[:, pl.ds(start, count)] for start, count in spans]
        segments = segments[0] if len(segments) == 1 else jnp.concatenate(segments, 1)
        same = jnp.concatenate([query_seg[rows, :]] * (segments.shape[1] // TILE), 1) == segments
        bias = jnp.where(same, 0.0, MASKED)
        lanes = lax.broadcasted_iota(jnp.int32, (size, TILE), 1)
        logs = jnp.zeros((size, TILE), F32)
        for pair in range(HEADS // 2):
            at = slice(pair * TILE, (pair + 1) * TILE)
            scores = against(half_masks(queries[rows, at]), keys_of(pair_ref, at))
            weights, scales = [], []
            for half in range(2):
                part = scores[half * size : (half + 1) * size] + bias
                top = jnp.max(part, -1, keepdims=True)
                part = jnp.exp(part - top)
                total = jnp.sum(part, -1, keepdims=True)
                weights.append(part.astype(BF16))
                scales.append(1.0 / total)
                logs = jnp.where(lanes == pair * 2 + half, top + jnp.log(total), logs)
            values = keys_of(pair_ref, slice(MODEL + pair * TILE, MODEL + (pair + 1) * TILE))
            out = nn(jnp.concatenate(weights, 0), values)
            keep = lane_half((size, TILE), 0)
            mixed[rows, at] = jnp.where(keep, out[:size] * scales[0], out[size:] * scales[1]).astype(BF16)
        log_rows[:, rows] = logs.T[:HEADS]


def head_dots(upstream, mixed):
    head = lax.broadcasted_iota(jnp.int32, (HEADS, MODEL), 1) // HD
    ones = (head == lax.broadcasted_iota(jnp.int32, (HEADS, MODEL), 0)).astype(F32)
    return lax.dot_general(
        ones, upstream.astype(F32) * mixed.astype(F32), (((1,), (1,)), ((), ())),
        precision=lax.Precision.HIGHEST, preferred_element_type=F32,
    )


def attend_back(queries, upstream, pair_ref, log_rows, dot_rows, query_row, key_seg, query_grad, pair_grad, jobs):
    query_grad[...] = jnp.zeros_like(query_grad)
    for key_start, size, start, count in jobs:
        rows, across = pl.ds(key_start, size), pl.ds(start, count)

        def heads(step, unused):
            same = jnp.concatenate([key_seg[rows, :]] * (count // TILE), 1) == query_row[:, across]
            bias = jnp.where(same, 0.0, MASKED)
            for pair in (step * 2, step * 2 + 1):
                at = pl.ds(pl.multiple_of(pair * TILE, TILE), TILE)
                value_at = pl.ds(pl.multiple_of(MODEL + pair * TILE, TILE), TILE)
                query = queries[across, at]
                grad = upstream[across, at]
                keys = half_masks(pair_ref[rows, at])
                values = half_masks(pair_ref[rows, value_at])
                scores, grads = against(keys, query), against(values, grad)
                weights, score_grads = [], []
                for half in range(2):
                    head, part = pl.ds(pair * 2 + half, 1), slice(half * size, (half + 1) * size)
                    weight = jnp.exp(scores[part] + (bias - log_rows[head, across]))
                    score_grads.append((weight * (grads[part] - dot_rows[head, across])).astype(BF16))
                    weights.append(weight.astype(BF16))
                score_grad = jnp.concatenate(score_grads, 0)
                value_part = nn(jnp.concatenate(weights, 0), grad)
                key_part = nn(score_grad, query)
                query_grad[across, at] += transposed(score_grad, keys)
                keep = lane_half((size, TILE), 0)
                pair_grad[rows, at] = jnp.where(keep, key_part[:size], key_part[size:]).astype(BF16)
                pair_grad[rows, value_at] = jnp.where(keep, value_part[:size], value_part[size:]).astype(BF16)
            return unused

        lax.fori_loop(0, HEADS // 4, heads, 0)


def self_back_jobs(side):
    near = pl.multiple_of((1 - side) * 256, 256)
    return [(0, 256, 0, 384), (256, 256, TILE, 384), (OWN, WINDOW, near, 256)]


def pack_body(
    place, vectors, project, output, query, keyval, crossout, up, down, states, source,
    one, three, near, own_source, block, semaphores
):
    me, side = place[0], place[1]
    copies = [
        (project, one.at[:, :1536]),
        (output, one.at[:, 1664:2176]),
        (query, one.at[:, 2176:2688]),
        (keyval, one.at[:, 2688:3712]),
        (crossout, one.at[:, 3712:]),
        (down, three.at[64:]),
    ] + [
        (up.at[:, part * 512 : (part + 1) * 512], three.at[part * BLOCK : (part + 1) * BLOCK, :])
        for part in range(4)
    ] + [
        (states.at[pl.ds(pl.multiple_of((1 - side) * WINDOW, WINDOW), WINDOW), :], near.at[:WINDOW])
    ]
    copies = [pltpu.make_async_copy(*copy, semaphores.at[i]) for i, copy in enumerate(copies)]
    for copy in copies:
        copy.start()
    gap = jnp.zeros((HALF_SOURCE - source.shape[0], MODEL), F32)
    padded = jnp.concatenate([source[...].astype(F32), gap], 0).astype(BF16)
    own_source[...] = padded
    near[WINDOW:, :] = padded
    values = jnp.broadcast_to(vectors[...].astype(F32), (8, 256))
    lanes = lax.broadcasted_iota(jnp.int32, (8, TILE), 1)
    rows = lax.broadcasted_iota(jnp.int32, (8, TILE), 0)
    packed = jnp.zeros((8, TILE), F32)
    spot, wide = (me & 7) * 16, (me & 1) * 64
    for row in range(7):
        moved = pltpu.roll(values, spot + 256 - 16 * row, 1)[:, :TILE]
        inside = jnp.logical_and(lanes >= spot, lanes < spot + 16)
        packed = jnp.where(jnp.logical_and(rows == row, inside), moved, packed)
    moved = pltpu.roll(values, wide + 256 - 112, 1)[:, :TILE]
    inside = jnp.logical_and(lanes >= wide, lanes < wide + 64)
    packed = jnp.where(jnp.logical_and(rows == 7, inside), moved, packed)
    block[...] = jnp.concatenate([packed, jnp.zeros((8, TILE), F32)], 0).astype(BF16)
    last = pltpu.make_async_copy(block, one.at[:, 1536:1664], semaphores.at[len(copies)])
    last.start()
    for copy in copies + [last]:
        copy.wait()


def self_body(place, states, window, *refs):
    pieces, refs = refs[:4], refs[4:]
    queries, pair, lowered, vectors, up_bias, weight, weight_two, packed = refs
    me = place[0]
    load_blocks(me, pieces, slice(1536, 1664), packed)
    load_blocks(me, pieces, slice(0, 1536), weight)
    load_blocks(me, pieces, slice(1664, 4224), weight_two)
    for tile in range(4):
        total = jnp.zeros((8, TILE), F32)
        for i in range(8):
            total = total + packed[(tile * 8 + i) * BLOCK : (tile * 8 + i + 1) * BLOCK, :].astype(F32)[:8]
        vectors[:, tile * TILE : (tile + 1) * TILE] = total
    for tile in range(16):
        total = (
            packed[2 * tile * BLOCK : (2 * tile + 1) * BLOCK, :].astype(F32)
            + packed[(2 * tile + 1) * BLOCK : (2 * tile + 2) * BLOCK, :].astype(F32)
        )
        up_bias[:, tile * TILE : (tile + 1) * TILE] = total[7:8]
    gain, shift = vectors[1:2, :], vectors[2:3, :]
    for i in range(KEYS // TILE):
        rows = slice(i * TILE, (i + 1) * TILE)
        value = states[rows, :] if i < 4 else window[(i - 4) * TILE : (i - 3) * TILE, :]
        lowered[rows, :] = (normed_rows(value.astype(F32))[0] * gain + shift).astype(BF16)
    for i in range(KEYS // 256):
        rows = slice(i * 256, (i + 1) * 256)
        if i < 2:
            queries[rows, :] = (nn(lowered[rows, :], weight[:, :512]) .astype(BF16) * SCALE).astype(BF16)
        pair[rows, :] = nn(lowered[rows, :], weight[:, 512:]).astype(BF16)


def forward_body(
    place, segments, source_segments, states, own_source, other_source, vectors, weight, self_queries, self_pair,
    self_mixed, self_logs, after_self, lowered, queries, pair, mixed, logs, after_cross,
    query_seg, key_row, source_row, source,
):
    self_mix(place, segments, self_queries, self_pair, self_mixed, self_logs, query_seg, key_row)
    cross_lower(
        place, states, own_source, other_source, self_mixed, vectors, after_self, lowered, queries, pair, weight, source
    )
    source_row[...] = source_segments[...].astype(F32)
    attend(queries, pair, mixed, logs, query_seg, source_row, [(pl.ds(0, OWN), [(0, SOURCES)], OWN)])
    for i in range(2):
        rows = slice(i * 256, (i + 1) * 256)
        after_cross[rows, :] = after_self[rows, :] + nn(mixed[rows, :], weight[:, 2048:])


def self_mix(place, segments, queries, pair, mixed, log_rows, query_seg, key_row):
    query_seg[...] = spread(own_segments_of(place[1], segments[...]))
    key_row[...] = key_segments_of(place[1], segments[...])
    attend(queries, pair, mixed, log_rows, query_seg, key_row, self_jobs(place[1]))


def cross_lower(
    place, states, own_source, other_source, self_mixed, vectors, after_self, lowered, queries, pair, weight, source
):
    side = place[1]
    source[:HALF_SOURCE, :] = jnp.where(side == 0, own_source[...], other_source[...])
    source[HALF_SOURCE:, :] = jnp.where(side == 0, other_source[...], own_source[...])
    gain, shift = vectors[3:4, :], vectors[4:5, :]
    pair[...] = nn(source[...], weight[:, 1024:2048]).astype(BF16)
    for i in range(2):
        rows = slice(i * 256, (i + 1) * 256)
        value = states[rows, :].astype(F32) + nn(self_mixed[rows, :], weight[:, :512])
        after_self[rows, :] = value
        lowered[rows, :] = (normed_rows(value)[0] * gain + shift).astype(BF16)
        queries[rows, :] = (nn(lowered[rows, :], weight[:, 512:1024]).astype(BF16) * SCALE).astype(BF16)


CHUNK, UNROLL = 512, 2


def feed_front_body(place, after_cross, vectors, lowered, flipped):
    gain, shift = vectors[5:6, :], vectors[6:7, :]
    for i in range(4):
        rows = slice(i * TILE, (i + 1) * TILE)
        low = (normed_rows(after_cross[rows, :])[0] * gain + shift).astype(BF16)
        lowered[rows, :] = low
    flipped[...] = lowered[...].T


def feed_body(place, lowered, flipped, output_grad, up_bias, *refs):
    pieces, refs = refs[:4], refs[4:]
    (
        total, back, kept, sent, bias_sums, ups, downs, up_grads, down_grads,
    ) = refs
    me = place[0]
    places = block_places(me)

    def chunk_of(z):
        return pl.multiple_of(((me >> 3) ^ z) * CHUNK, CHUNK)

    grad_low = output_grad[...]
    total[...] = jnp.zeros_like(total)
    back[...] = jnp.zeros_like(back)

    def chunk(z):
        at = pl.ds(chunk_of(z), CHUNK)
        mine = me >> 3
        z_row = (mine ^ z) * BLOCK
        up, down, up_grad, down_grad = ups.at[z], downs.at[z], up_grads.at[z], down_grads.at[z]
        swapped_z = (z & 1) * 2 + (z >> 1)
        for piece, row, owner in places:
            owner = (owner & 7) + (mine ^ (row % 2 * 2 + row % 4 // 2)) * FLIP_Z
            up[block_rows(owner), :] = pieces[piece][pl.ds(pl.multiple_of(row * 128 + z_row, BLOCK), BLOCK), :]
            if row % 4 == 0:
                start = pl.multiple_of((row + swapped_z) * 128 + 64, 64)
                down[block_rows(owner & 7, 64), :] = pieces[piece][pl.ds(start, 64), :]
        hidden = nn(lowered[...], up[...]) + up_bias[:, at]
        square = hidden * hidden
        inner = 0.7978845608028654 * hidden * (1.0 + 0.044715 * square)
        curve = jnp.tanh(inner)
        half = 0.5 * (1.0 + curve)
        activated = (hidden * half).astype(BF16)
        slope = half + (0.5 * 0.7978845608028654) * hidden * (1.0 - curve * curve) * (
            1.0 + (3 * 0.044715) * square
        )
        down_grad[...] = transposed(activated, grad_low).astype(BF16)
        for piece, row, owner in places:
            if row % 4 == 0:
                to = pl.multiple_of((piece % 2 * 8 + row + z) * 128 + 64, 64)
                (kept, sent)[piece // 2][pl.ds(to, 64), :] = down_grad[block_rows(owner & 7, 64), :]
        grad_hidden = (against(grad_low, down[...]) * slope).astype(BF16)
        bias_sums[:, at] = column_sum(grad_hidden.astype(F32))
        up_grad[...] = nn(flipped[...], grad_hidden).astype(BF16)
        for piece, row, owner in places:
            to = (piece % 2 * 8 + row) * 128
            (kept, sent)[piece // 2][pl.ds(pl.multiple_of(to + z_row, BLOCK), BLOCK), :] = up_grad[block_rows(owner), :]
        total[...] += nn(activated, down[...])
        back[...] += against(grad_hidden, up[...])

    def chunks(step, unused):
        for z in range(UNROLL):
            chunk(step * UNROLL + z)
        return unused

    lax.fori_loop(0, 4 // UNROLL, chunks, 0)


def feed_last_body(
    place, after_cross, output_grad, vectors, total, back, mixed, weight,
    layer_out, after_grad, sums, mixed_grad, dot_rows, crossout_grad,
):
    gain = vectors[5:6, :]
    gain_sum, shift_sum, bias_sum = (jnp.zeros((1, MODEL), F32) for _ in range(3))
    for i in range(4):
        rows = slice(i * TILE, (i + 1) * TILE)
        value, grad = after_cross[rows, :], output_grad[rows, :].astype(F32)
        layer_out[rows, :] = (value + total[rows, :] + vectors[0:1, :]).astype(BF16)
        normed, inverse = normed_rows(value)
        upstream = back[rows, :]
        after_grad[rows, :] = grad + norm_back_rows(upstream, normed, inverse, gain)
        gain_sum, shift_sum = gain_sum + column_sum(upstream * normed), shift_sum + column_sum(upstream)
        bias_sum = bias_sum + column_sum(grad)
    zero = jnp.zeros((1, MODEL), F32)
    sums[...] = jnp.concatenate([bias_sum, zero, zero, zero, zero, gain_sum, shift_sum, zero], 0)
    grad_low = after_grad[...].astype(BF16)
    mixed_grad[...] = against(grad_low, weight[:, 2048:]).astype(BF16)
    dot_rows[...] = head_dots(mixed_grad[...], mixed[...])
    crossout_grad[...] = transposed(mixed[...], grad_low).astype(BF16)


def cross_back_body(
    place, segments, source_segments, own_source, other_source, queries, pair, log_rows, upstream, dot_rows, weight,
    asked, source_own, source_send, grads, query_grad, pair_grad, source, key_seg, query_row,
):
    side = place[1]
    key_seg[...] = spread(source_segments[...].astype(F32))
    query_row[...] = own_segments_of(side, segments[...])
    source[:HALF_SOURCE, :] = jnp.where(side == 0, own_source[...], other_source[...])
    source[HALF_SOURCE:, :] = jnp.where(side == 0, other_source[...], own_source[...])
    attend_back(
        queries, upstream, pair, log_rows, dot_rows, query_row, key_seg, query_grad, pair_grad,
        [(0, SOURCES, 0, OWN)],
    )
    asked[...] = (query_grad[...] * SCALE).astype(BF16)
    grads[...] = transposed(source[...], pair_grad[...]).astype(BF16)
    back = against(pair_grad[...], weight[:, 1024:2048])
    first, second = back[:HALF_SOURCE], back[HALF_SOURCE:]
    source_own[...] = jnp.where(side == 0, first, second)
    source_send[...] = jnp.where(side == 0, second, first).astype(BF16)


def cross_weight_body(
    place, after_self, lowered, self_mixed, after_grad, asked, vectors, sums, weight, crossout_grad, keyval_grad, *refs
):
    self_grad, upstream, dot_rows, kept, sent, new_sums, grads = refs
    me = place[0]
    store_blocks(me, crossout_grad, (kept, sent), slice(0, 512))
    store_blocks(me, keyval_grad, (kept, sent), slice(512, 1536))
    gain = vectors[3:4, :]
    gain_sum, shift_sum = jnp.zeros((1, MODEL), F32), jnp.zeros((1, MODEL), F32)
    for i in range(2):
        rows = slice(i * 256, (i + 1) * 256)
        normed, inverse = normed_rows(after_self[rows, :])
        up = against(asked[rows, :], weight[:, 512:1024])
        self_grad[rows, :] = after_grad[rows, :] + norm_back_rows(up, normed, inverse, gain)
        gain_sum, shift_sum = gain_sum + column_sum(up * normed), shift_sum + column_sum(up)
    grads[:, :512] = transposed(lowered[...], asked[...]).astype(BF16)
    grad_low = self_grad[...].astype(BF16)
    grads[:, 512:] = transposed(self_mixed[...], grad_low).astype(BF16)
    store_blocks(me, grads, (kept, sent), slice(1536, 2560))
    upstream[...] = against(grad_low, weight[:, :512]).astype(BF16)
    dot_rows[...] = head_dots(upstream[...], self_mixed[...])
    zero = jnp.zeros((1, MODEL), F32)
    new_sums[...] = sums[...] + jnp.concatenate(
        [zero, zero, zero, gain_sum, shift_sum, zero, zero, zero], 0
    )


def self_back_body(
    place, segments, states, window, lowered, queries, pair, log_rows, upstream, dot_rows, weight, sums, bias_sums,
    source_send, own_back, near_back, kept, sent, query_grad, pair_grad, grads, key_seg, query_row,
):
    near_back[WINDOW:, :] = source_send[...]
    key_seg[...] = spread(key_segments_of(place[1], segments[...]))
    query_row[...] = own_segments_of(place[1], segments[...])
    attend_back(
        queries, upstream, pair, log_rows, dot_rows, query_row, key_seg, query_grad, pair_grad,
        self_back_jobs(place[1]),
    )
    asked = (query_grad[...] * SCALE).astype(BF16)
    grads[:, :MODEL] = transposed(lowered[:OWN, :], asked).astype(BF16)
    grads[:, MODEL:1536] = transposed(lowered[...], pair_grad[...]).astype(BF16)
    gain_sum, shift_sum = jnp.zeros((1, MODEL), F32), jnp.zeros((1, MODEL), F32)
    for i in range(3):
        rows = slice(i * 256, (i + 1) * 256)
        part = against(pair_grad[rows, :], weight[:, MODEL:])
        if i < 2:
            part = part + against(asked[rows, :], weight[:, :MODEL])
            own_back[rows, :] = part
            value = states[rows, :]
        else:
            near_back[:WINDOW, :] = part.astype(BF16)
            value = window[...]
        normed = normed_rows(value.astype(F32))[0]
        gain_sum, shift_sum = gain_sum + column_sum(part * normed), shift_sum + column_sum(part)
    zero = jnp.zeros((1, MODEL), F32)
    sums = sums[...] + jnp.concatenate([zero, gain_sum, shift_sum, zero, zero, zero, zero, zero], 0)
    last = lax.broadcasted_iota(jnp.int32, (8, TILE), 0) == 7
    for device in range(32):
        tile, wide = device // 8 * TILE, device // 2 * TILE
        value = jnp.where(last, bias_sums[:, wide : wide + TILE], sums[:, tile : tile + TILE])
        high = value.astype(BF16).astype(F32)
        grads[device * BLOCK : (device + 1) * BLOCK, 1536:] = jnp.concatenate([high, value - high], 0).astype(BF16)
    store_blocks(place[0], grads, (kept, sent), slice(0, 1664))


def target_body(place, back, came, states, self_grad, vectors, out):
    gain = vectors[1:2, :]
    for i in range(4):
        rows = slice(i * TILE, (i + 1) * TILE)
        here = (i < 2) == (place[1] == 1)
        extra = came[(i % 2) * TILE : (i % 2 + 1) * TILE, :].astype(F32)
        upstream = back[rows, :] + jnp.where(here, extra, 0.0)
        normed, inverse = normed_rows(states[rows, :].astype(F32))
        out[rows, :] = self_grad[rows, :] + norm_back_rows(upstream, normed, inverse, gain)


def finish_body(place, *refs):
    feed, cross, last, outs = refs[:2], refs[2:6], refs[6:10], refs[10:]
    project, output, query, keyval, crossout, up, down, *small = outs
    me = place[0]

    def total(parts, begin, end, rows=slice(None)):
        value = parts[0][rows, begin:end].astype(F32)
        for part in parts[1:]:
            value = value + part[rows, begin:end].astype(F32)
        return value

    for part in range(4):
        rows = slice(part * BLOCK, (part + 1) * BLOCK)
        up[:, part * 512 : (part + 1) * 512] = total(feed, 0, MODEL, rows)
    down[...] = total(feed, 0, MODEL, slice(64, 128))
    crossout[...] = total(cross, 0, 512)
    keyval[...] = total(cross, 512, 1536)
    query[...] = total(cross, 1536, 2048)
    output[...] = total(cross, 2048, 2560)
    project[...] = total(last, 0, 1536)
    value = total(last, 1536, 1664)
    value = value[:8] + value[8:]
    narrow = pltpu.roll(value, (TILE - (me & 7) * 16) & 127, 1)
    wide = pltpu.roll(value, (TILE - (me & 1) * 64) & 127, 1)
    for row in range(7):
        small[row][...] = narrow[row : row + 1, :16]
    small[7][...] = wide[7:8, :64]


def shape_of(*shape, dtype=BF16):
    return jax.ShapeDtypeStruct(shape, dtype)


VMEM_SPEC = pl.BlockSpec(memory_space=pltpu.VMEM)
ANY_SPEC = pl.BlockSpec(memory_space=pl.ANY)
HBM_SPEC = pl.BlockSpec(memory_space=pltpu.HBM)
SMEM_SPEC = pl.BlockSpec(memory_space=pltpu.SMEM)


def call(body, name, place, inputs, pieces, outs, scratch, flops, any_outs=(), any_ins=(), vmem=20):
    return pl.pallas_call(
        body,
        name=name,
        out_shape=outs,
        in_specs=[SMEM_SPEC]
        + [HBM_SPEC if i in any_ins else VMEM_SPEC for i in range(len(inputs))]
        + [VMEM_SPEC] * len(pieces),
        out_specs=[ANY_SPEC if i in any_outs else VMEM_SPEC for i in range(len(outs))],
        scratch_shapes=scratch,
        compiler_params=pltpu.CompilerParams(vmem_limit_bytes=vmem * 2**20),
        cost_estimate=pl.CostEstimate(flops=flops, bytes_accessed=4 * 2**20, transcendentals=0),
    )(place, *inputs, *pieces)


def fast_device(
    target_states, source_states, target_segments, source_segments, output_grad, self_project,
    self_output, cross_query, cross_keyval, cross_output, hidden_up, hidden_bias, hidden_down,
    output_bias, first_gain, first_shift, second_gain, second_shift, third_gain, third_shift,
):
    vmem, dma = pltpu.VMEM, pltpu.SemaphoreType.DMA
    side = lax.axis_index("seq")
    place = jnp.stack([lax.axis_index("rows") * 2 + side, side]).astype(jnp.int32)
    states, grad = target_states[0], output_grad[0]
    small = jnp.pad(hidden_bias[None], ((0, 0), (112, 80)))
    for i, vector in enumerate(
        (output_bias, first_gain, first_shift, second_gain, second_shift, third_gain, third_shift)
    ):
        small = small + jnp.pad(vector[None], ((0, 0), (16 * i, 240 - 16 * i)))
    one, three, near, own_source = call(
        pack_body, "pack", place,
        [
            small, self_project, self_output, cross_query, cross_keyval, cross_output, hidden_up, hidden_down, states,
            source_states[0],
        ],
        [],
        [
            shape_of(16, 4224), shape_of(128, MODEL), shape_of(WINDOW + HALF_SOURCE, MODEL),
            shape_of(HALF_SOURCE, MODEL),
        ],
        [vmem((BLOCK, TILE), BF16), dma((12,))], 1000000, any_ins=range(1, 9), vmem=60,
    )
    parts = along_z(one)
    near = exchange(near, FLIP_Y)
    one = join(one, *parts)
    one = tied(one, near)
    came = exchange_side(one, 0)
    three = tied(three, one)
    far = exchange(three, 2 * FLIP_Z)
    came = tied(came, far)
    one = join(one, came)
    one_core = exchange(one, FLIP_CORE)
    other = exchange_side(one, 1)
    three = join(three, tied(far, one))
    three = join(three, exchange(three, FLIP_Z))
    came = exchange_side(three, 0)
    other = tied(other, came)
    window, other_source = near[:WINDOW], near[WINDOW:]
    pieces_one = [one, other, one_core, exchange(other, FLIP_CORE)]
    three = join(three, came)
    three_core = exchange(three, FLIP_CORE)
    three_other = exchange_side(three, 1)
    half = source_states.shape[1]
    gap = jnp.full((1, HALF_SOURCE - half), -1, jnp.int32)
    source_seg = jnp.concatenate([source_segments[:, :half], gap, source_segments[:, half:], gap], 1)

    queries, pair, lowered, vectors, up_bias, weight_one, weight_two = call(
        self_body, "self_lower", place, [states, window], pieces_one,
        [
            shape_of(OWN, MODEL), shape_of(KEYS, 2 * MODEL), shape_of(KEYS, MODEL), shape_of(8, MODEL, dtype=F32),
            shape_of(1, FEED, dtype=F32), shape_of(MODEL, 1536), shape_of(MODEL, 2560),
        ],
        [vmem((MODEL, TILE), BF16)], 1000,
    )
    mixed, logs, after_self, lowered_two, queries_two, pair_two, mixed_two, logs_two, after_cross = call(
        forward_body, "forward", place,
        [
            target_segments, source_seg, states, own_source, other_source, vectors, weight_two, queries, pair,
        ],
        [],
        [
            shape_of(OWN, MODEL), shape_of(HEADS, OWN, dtype=F32), shape_of(OWN, MODEL, dtype=F32), shape_of(OWN, MODEL),
            shape_of(OWN, MODEL), shape_of(SOURCES, 2 * MODEL), shape_of(OWN, MODEL), shape_of(HEADS, OWN, dtype=F32),
            shape_of(OWN, MODEL, dtype=F32),
        ],
        [
            vmem((OWN, TILE), F32), vmem((1, KEYS), F32), vmem((1, SOURCES), F32), vmem((SOURCES, MODEL), BF16),
        ],
        1000,
    )
    three_core, three_other = tied((three_core, three_other), after_cross)
    last_piece = exchange(three_other, FLIP_CORE)
    feed_in = call(
        feed_front_body, "feed_front", place, [tied(after_cross, three_other), vectors], [],
        [shape_of(OWN, MODEL), shape_of(MODEL, OWN)], [], 1000,
    )
    pieces_three = [three, three_other, three_core, tied(last_piece, feed_in)]
    total, back, feed_kept, feed_sent, bias_sums = call(
        feed_body, "feed", place, [*feed_in, grad, up_bias], pieces_three,
        [shape_of(OWN, MODEL, dtype=F32)] * 2 + [shape_of(2048, MODEL)] * 2 + [shape_of(1, FEED, dtype=F32)],
        [
            vmem((4, MODEL, CHUNK), BF16), vmem((4, CHUNK, MODEL), BF16), vmem((4, MODEL, CHUNK), BF16), vmem((4, CHUNK, MODEL), BF16),
        ],
        10000000000,
    )
    feed_came = exchange(feed_sent, FLIP_CORE)
    layer_out, after_grad, sums, upstream_two, dots_two, crossout_grad = call(
        feed_last_body, "feed_last", place, [after_cross, grad, vectors, total, back, mixed_two, weight_two], [],
        [
            shape_of(OWN, MODEL), shape_of(OWN, MODEL, dtype=F32), shape_of(8, MODEL, dtype=F32), shape_of(OWN, MODEL),
            shape_of(HEADS, OWN, dtype=F32), shape_of(MODEL, MODEL),
        ],
        [], 4000000000,
    )
    feed_came = tied(feed_came, after_grad)
    feed_sent, feed_kept = add_halves(feed_kept, feed_came)
    upstream_two = tied(upstream_two, feed_sent)
    feed_came = exchange_side(feed_sent, 1)
    asked, source_own, source_send, keyval_grad = call(
        cross_back_body, "cross_backward", place,
        [
            target_segments, source_seg, own_source, other_source, queries_two, pair_two, logs_two,
            upstream_two, dots_two, weight_two,
        ],
        [],
        [
            shape_of(OWN, MODEL), shape_of(HALF_SOURCE, MODEL, dtype=F32), shape_of(HALF_SOURCE, MODEL),
            shape_of(MODEL, 1024),
        ],
        [
            vmem((OWN, MODEL), F32), vmem((SOURCES, 2 * MODEL), BF16),
            vmem((SOURCES, MODEL), BF16), vmem((SOURCES, TILE), F32), vmem((1, OWN), F32),
        ],
        10000000000,
    )
    self_grad, upstream, dot_rows, cross_kept, cross_sent, sums = call(
        cross_weight_body, "cross_weights", place,
        [after_self, lowered_two, mixed, after_grad, asked, vectors, sums, weight_two, crossout_grad, keyval_grad],
        [],
        [shape_of(OWN, MODEL, dtype=F32), shape_of(OWN, MODEL), shape_of(HEADS, OWN, dtype=F32)]
        + [shape_of(256, 2560)] * 2 + [shape_of(8, MODEL, dtype=F32)],
        [vmem((MODEL, 1024), BF16)], 6000000000,
    )
    cross_came = exchange(cross_sent, FLIP_CORE)
    feed_came = tied(feed_came, upstream)
    feed_sent, feed_kept = add_halves(feed_kept, feed_came)
    feed_came = exchange_side(feed_sent, 0)
    cross_came = tied(cross_came, feed_sent)
    cross_sent, cross_kept = add_halves(cross_kept, cross_came)
    cross_came = exchange_side(cross_sent, 1)
    upstream = tied(upstream, cross_sent)
    own_back, near_back, last_kept, last_sent = call(
        self_back_body, "self_backward", place,
        [
            target_segments, states, window, lowered, queries, pair, logs, upstream, dot_rows, weight_one, sums,
            bias_sums, source_send,
        ],
        [],
        [shape_of(OWN, MODEL, dtype=F32), shape_of(WINDOW + HALF_SOURCE, MODEL)] + [shape_of(256, 1664)] * 2,
        [
            vmem((OWN, MODEL), F32), vmem((KEYS, 2 * MODEL), BF16), vmem((MODEL, 1664), BF16), vmem((KEYS, TILE), F32),
            vmem((1, OWN), F32),
        ],
        16000000000,
    )
    last_came = exchange(last_sent, FLIP_CORE)
    cross_came, feed_came = tied((cross_came, feed_came), own_back)
    feed_kept = feed_kept + feed_came
    feed_kept, feed_sent = (
        join(feed_kept[i * 128 : (i + 1) * 128], feed_kept[(i + 2) * 128 : (i + 3) * 128]) for i in range(2)
    )
    feed_came = exchange(feed_sent, FLIP_Z)
    cross_came = tied(cross_came, feed_sent)
    cross_sent, cross_kept = add_halves(cross_kept, cross_came)
    last_came = tied(last_came, feed_sent)
    last_sent, last_kept = add_halves(last_kept, last_came)
    last_came, cross_came = exchange_side(last_sent, 1), exchange_side(cross_sent, 0)
    feed_came = tied(feed_came, last_sent)
    feed_sent, feed_kept = add_halves(feed_kept, feed_came)
    feed = [feed_kept, exchange(feed_sent, 2 * FLIP_Z)]
    cross_came = tied(cross_came, feed_sent)
    cross_kept = cross_kept + cross_came
    last_came = tied(last_came, cross_kept)
    last_sent, last_kept = add_halves(last_kept, last_came)
    last_came = exchange_side(last_sent, 0)
    feed, near_back = tied((feed, near_back), last_sent)
    cross_kept = tied(cross_kept, feed)
    cross = z_blocks(cross_kept)
    near_came = exchange(near_back, FLIP_Y)
    last_came = tied(last_came, cross[0])
    last = z_blocks(last_kept + last_came)
    came, source_came = near_came[:WINDOW], near_came[WINDOW:]
    grad_source = source_own[:half] + source_came[:half].astype(F32)
    (grad_target,) = call(
        target_body, "target_grad", place, [own_back, came, states, self_grad, vectors], [],
        [shape_of(OWN, MODEL, dtype=F32)], [], 1000000,
    )
    last = tied(last, grad_target, grad_source)
    project, output, query, keyval, crossout, up, down, *small = call(
        finish_body, "finish", place, feed + cross + last, [],
        [
            shape_of(16, 1536, dtype=F32), shape_of(16, 512, dtype=F32), shape_of(16, 512, dtype=F32),
            shape_of(16, 1024, dtype=F32), shape_of(16, 512, dtype=F32), shape_of(16, 2048, dtype=F32),
            shape_of(64, 512, dtype=F32),
        ]
        + [shape_of(1, 16, dtype=F32)] * 7 + [shape_of(1, 64, dtype=F32)],
        [], 1000000,
    )
    *rows, up_sum = [row[0] for row in small]
    return (
        layer_out[None], grad_target[None], grad_source[None], project, output, query, keyval, crossout, up,
        up_sum, down, *rows,
    )


def specs():
    in_specs = (
        P("rows", "seq", None),
        P("rows", "seq", None),
        P("rows", None),
        P("rows", None),
        P("rows", "seq", None),
        P(("rows", "seq"), None),
        P(("rows", "seq"), None),
        P(("rows", "seq"), None),
        P(("rows", "seq"), None),
        P(("rows", "seq"), None),
        P(("rows", "seq"), None),
        P(("rows", "seq")),
        P(("rows", "seq"), None),
        P(("rows", "seq")),
        P(("rows", "seq")),
        P(("rows", "seq")),
        P(("rows", "seq")),
        P(("rows", "seq")),
        P(("rows", "seq")),
        P(("rows", "seq")),
    )
    out_specs = (
        P("rows", "seq", None),
        P("rows", "seq", None),
        P("rows", "seq", None),
        P(("rows", "seq"), None),
        P(("rows", "seq"), None),
        P(("rows", "seq"), None),
        P(("rows", "seq"), None),
        P(("rows", "seq"), None),
        P(("rows", "seq"), None),
        P(("rows", "seq")),
        P(("rows", "seq"), None),
        P(("rows", "seq")),
        P(("rows", "seq")),
        P(("rows", "seq")),
        P(("rows", "seq")),
        P(("rows", "seq")),
        P(("rows", "seq")),
        P(("rows", "seq")),
    )
    return in_specs, out_specs


def solution(mesh):
    in_specs, out_specs = specs()
    fast = mesh.shape["rows"] == 16 and mesh.shape["seq"] == 2
    return jax.shard_map(
        fast_device if fast else general_device,
        mesh=mesh, in_specs=in_specs, out_specs=out_specs, check_vma=False,
    )
```

```python
import jax
import jax.numpy as jnp
from jax import lax
from jax.experimental import pallas as pl
from jax.experimental.pallas import tpu as pltpu
from jax.sharding import PartitionSpec as P

HEADS = 8
HD = 64


def layer_norm(value, gain, shift):
    row_mean = jnp.mean(value, -1, keepdims=True)
    centered = value - row_mean
    variance = jnp.mean(centered * centered, -1, keepdims=True)
    inverse = lax.rsqrt(variance + 1e-05)
    normed = centered * inverse
    return (normed * gain + shift, normed, inverse)


def norm_back(upstream, normed, inverse, gain):
    scaled = upstream * gain
    first_mean = jnp.mean(scaled, -1, keepdims=True)
    second_mean = jnp.mean(scaled * normed, -1, keepdims=True)
    grad_input = inverse * (scaled - first_mean - normed * second_mean)
    return (grad_input, jnp.sum(upstream * normed, 0), jnp.sum(upstream, 0))


def matmul(left, right):
    return jnp.dot(left, right, preferred_element_type=jnp.float32)


def transposed(left, right):
    return lax.dot_general(
        left, right, (((0,), (0,)), ((), ())), preferred_element_type=jnp.float32
    )


def against(left, right):
    return lax.dot_general(
        left, right, (((1,), (1,)), ((), ())), preferred_element_type=jnp.float32
    )


def head_split(value):
    return value.reshape(value.shape[0], HEADS, HD)


def head_join(value):
    return value.reshape(value.shape[0], HEADS * HD)


def scores_of(queries, key_rows, query_seg, key_seg):
    raw_scores = jnp.einsum(
        "qhd,khd->hqk", queries, key_rows, preferred_element_type=jnp.float32
    ) * HD ** (-0.5)
    same_seg = (query_seg[:, None] == key_seg[None, :])[None]
    return (raw_scores, same_seg)


def block_weights(queries, key_rows, query_seg, key_seg, log_total):
    raw_scores, same_seg = scores_of(queries, key_rows, query_seg, key_seg)
    return jnp.where(same_seg, jnp.exp(raw_scores - log_total[..., None]), 0.0)


def log_totals(queries, key_blocks, seg_blocks, query_seg):

    def log_advance(carry, inputs_now):
        row_max, row_total = carry
        key_rows, key_seg = inputs_now
        raw_scores, same_seg = scores_of(queries, key_rows, query_seg, key_seg)
        masked = jnp.where(same_seg, raw_scores, -1000000000.0)
        new_max = jnp.maximum(row_max, jnp.max(masked, -1))
        shifted = jnp.where(same_seg, jnp.exp(masked - new_max[..., None]), 0.0)
        return ((new_max, row_total * jnp.exp(row_max - new_max) + jnp.sum(shifted, -1)), None)

    start = (
        jnp.full((HEADS, queries.shape[0]), -1000000000.0, jnp.float32),
        jnp.zeros((HEADS, queries.shape[0]), jnp.float32),
    )
    (row_max, row_total), unused = lax.scan(log_advance, start, (key_blocks, seg_blocks))
    return row_max + jnp.log(row_total)


def weighted_sum(queries, key_blocks, value_blocks, seg_blocks, query_seg, log_total):

    def weighted_advance(carry, inputs_now):
        key_rows, value_rows, key_seg = inputs_now
        weights = block_weights(queries, key_rows, query_seg, key_seg, log_total).astype(
            jnp.bfloat16
        )
        return (
            carry
            + jnp.einsum("hqk,khd->qhd", weights, value_rows, preferred_element_type=jnp.float32),
            None,
        )

    total, unused = lax.scan(
        weighted_advance,
        jnp.zeros(queries.shape, jnp.float32),
        (key_blocks, value_blocks, seg_blocks),
    )
    return total


def grad_dots(queries, grad_heads, key_blocks, value_blocks, seg_blocks, query_seg, log_total):

    def grad_advance(carry, inputs_now):
        key_rows, value_rows, key_seg = inputs_now
        weights = block_weights(queries, key_rows, query_seg, key_seg, log_total)
        grad_weights = jnp.einsum(
            "qhd,khd->hqk", grad_heads, value_rows, preferred_element_type=jnp.float32
        )
        return (carry + jnp.sum(weights * grad_weights, -1), None)

    start = jnp.zeros((HEADS, queries.shape[0]), jnp.float32)
    total, unused = lax.scan(grad_advance, start, (key_blocks, value_blocks, seg_blocks))
    return total


def query_grads(
    queries, grad_heads, key_blocks, value_blocks, seg_blocks, query_seg, log_total, row_dots
):
    score_scale = HD ** (-0.5)

    def query_advance(carry, inputs_now):
        key_rows, value_rows, key_seg = inputs_now
        weights = block_weights(queries, key_rows, query_seg, key_seg, log_total)
        grad_weights = jnp.einsum(
            "qhd,khd->hqk", grad_heads, value_rows, preferred_element_type=jnp.float32
        )
        grad_scores = (weights * (grad_weights - row_dots[..., None])).astype(jnp.bfloat16)
        carry = (
            carry
            + jnp.einsum("hqk,khd->qhd", grad_scores, key_rows, preferred_element_type=jnp.float32)
            * score_scale
        )
        grad_keys = (
            jnp.einsum("hqk,qhd->khd", grad_scores, queries, preferred_element_type=jnp.float32)
            * score_scale
        )
        grad_values = jnp.einsum(
            "hqk,qhd->khd",
            weights.astype(jnp.bfloat16),
            grad_heads,
            preferred_element_type=jnp.float32,
        )
        return (carry, jnp.concatenate([head_join(grad_keys), head_join(grad_values)], 1))

    return lax.scan(
        query_advance, jnp.zeros(queries.shape, jnp.float32), (key_blocks, value_blocks, seg_blocks)
    )


def general_device(
    target_states,
    source_states,
    target_segments,
    source_segments,
    output_grad,
    self_project,
    self_output,
    cross_query,
    cross_keyval,
    cross_output,
    hidden_up,
    hidden_bias,
    hidden_down,
    output_bias,
    first_gain,
    first_shift,
    second_gain,
    second_shift,
    third_gain,
    third_shift,
):
    (
        full_project,
        full_output,
        full_query,
        full_keyval,
        full_crossout,
        full_up,
        full_upbias,
        full_down,
        full_downbias,
        gain_one,
        shift_one,
        gain_two,
        shift_two,
        gain_three,
        shift_three,
    ) = (
        lax.all_gather(self_project, ("rows", "seq"), axis=0, tiled=True),
        lax.all_gather(self_output, ("rows", "seq"), axis=0, tiled=True),
        lax.all_gather(cross_query, ("rows", "seq"), axis=0, tiled=True),
        lax.all_gather(cross_keyval, ("rows", "seq"), axis=0, tiled=True),
        lax.all_gather(cross_output, ("rows", "seq"), axis=0, tiled=True),
        lax.all_gather(hidden_up, ("rows", "seq"), axis=0, tiled=True),
        lax.all_gather(hidden_bias, ("rows", "seq"), axis=0, tiled=True),
        lax.all_gather(hidden_down, ("rows", "seq"), axis=0, tiled=True),
        lax.all_gather(output_bias, ("rows", "seq"), axis=0, tiled=True),
        lax.all_gather(first_gain, ("rows", "seq"), axis=0, tiled=True),
        lax.all_gather(first_shift, ("rows", "seq"), axis=0, tiled=True),
        lax.all_gather(second_gain, ("rows", "seq"), axis=0, tiled=True),
        lax.all_gather(second_shift, ("rows", "seq"), axis=0, tiled=True),
        lax.all_gather(third_gain, ("rows", "seq"), axis=0, tiled=True),
        lax.all_gather(third_shift, ("rows", "seq"), axis=0, tiled=True),
    )
    gain_one = gain_one.astype(jnp.float32)
    gain_two = gain_two.astype(jnp.float32)
    gain_three = gain_three.astype(jnp.float32)
    score_scale = HD ** (-0.5)
    states = target_states[0].astype(jnp.float32)
    local_rows = states.shape[0]
    model_width = states.shape[1]
    seq_count = lax.axis_size("seq")
    row_segments = target_segments[0]
    seq_length = row_segments.shape[0]
    own_segments = lax.dynamic_slice_in_dim(
        row_segments, lax.axis_index("seq") * local_rows, local_rows
    )
    block_rows = max(1, min(seq_count, 512 // local_rows)) * local_rows
    block_count = seq_length // block_rows
    seg_blocks = row_segments.reshape(block_count, block_rows)
    normed_value, normed_one, inverse_one = layer_norm(
        states, gain_one, shift_one.astype(jnp.float32)
    )
    lowered_one = normed_value.astype(jnp.bfloat16)
    projected = matmul(lowered_one, full_project).astype(jnp.bfloat16)
    query_flat = projected[:, :model_width]
    key_local = projected[:, model_width : 2 * model_width]
    value_local = projected[:, 2 * model_width :]
    queries = head_split(query_flat)
    key_all, value_all = (
        lax.all_gather(key_local, "seq", axis=0, tiled=True),
        lax.all_gather(value_local, "seq", axis=0, tiled=True),
    )
    key_blocks = key_all.reshape(block_count, block_rows, HEADS, HD)
    value_blocks = value_all.reshape(block_count, block_rows, HEADS, HD)
    log_total = log_totals(queries, key_blocks, seg_blocks, own_segments)
    self_mixed = head_join(
        weighted_sum(queries, key_blocks, value_blocks, seg_blocks, own_segments, log_total)
    ).astype(jnp.bfloat16)
    after_self = states + matmul(self_mixed, full_output)
    normed_value, normed_two, inverse_two = layer_norm(
        after_self, gain_two, shift_two.astype(jnp.float32)
    )
    lowered_two = normed_value.astype(jnp.bfloat16)
    cross_asked = matmul(lowered_two, full_query).astype(jnp.bfloat16)
    source_low = source_states[0]
    source_all = lax.all_gather(source_low, "seq", axis=0, tiled=True)
    key_value = matmul(source_all, full_keyval).astype(jnp.bfloat16)
    cross_key_heads = head_split(key_value[:, :model_width])
    cross_value_heads = head_split(key_value[:, model_width:])
    asked_heads = head_split(cross_asked)
    raw_scores, same_seg = scores_of(asked_heads, cross_key_heads, own_segments, source_segments[0])
    cross_probs = jax.nn.softmax(jnp.where(same_seg, raw_scores, -1000000000.0), axis=-1)
    cross_mixed = head_join(
        jnp.einsum(
            "hqk,khd->qhd",
            cross_probs.astype(jnp.bfloat16),
            cross_value_heads,
            preferred_element_type=jnp.float32,
        )
    ).astype(jnp.bfloat16)
    after_cross = after_self + matmul(cross_mixed, full_crossout)
    normed_value, normed_three, inverse_three = layer_norm(
        after_cross, gain_three, shift_three.astype(jnp.float32)
    )
    lowered_three = normed_value.astype(jnp.bfloat16)
    hidden = matmul(lowered_three, full_up) + full_upbias.astype(jnp.float32)
    activated = jax.nn.gelu(hidden).astype(jnp.bfloat16)
    layer_out = after_cross + matmul(activated, full_down) + full_downbias.astype(jnp.float32)
    grad_low = output_grad[0]
    out_grad = grad_low.astype(jnp.float32)
    grad_down = transposed(activated, grad_low)
    grad_downbias = jnp.sum(out_grad, 0)
    grad_act = against(grad_low, full_down)
    grad_hidden = jax.vjp(jax.nn.gelu, hidden)[1](grad_act)[0].astype(jnp.bfloat16)
    grad_upbias = jnp.sum(grad_hidden.astype(jnp.float32), 0)
    grad_up = transposed(lowered_three, grad_hidden)
    dx_three, grad_gain_three, grad_shift_three = norm_back(
        against(grad_hidden, full_up), normed_three, inverse_three, gain_three
    )
    grad_cross = out_grad + dx_three
    grad_cross_low = grad_cross.astype(jnp.bfloat16)
    grad_crossout = transposed(cross_mixed, grad_cross_low)
    grad_cross_heads = head_split(against(grad_cross_low, full_crossout).astype(jnp.bfloat16))
    grad_weights = jnp.einsum(
        "qhd,khd->hqk", grad_cross_heads, cross_value_heads, preferred_element_type=jnp.float32
    )
    grad_scores = (
        cross_probs * (grad_weights - jnp.sum(cross_probs * grad_weights, -1, keepdims=True))
    ).astype(jnp.bfloat16)
    grad_asked = head_join(
        jnp.einsum("hqk,khd->qhd", grad_scores, cross_key_heads, preferred_element_type=jnp.float32)
        * score_scale
    ).astype(jnp.bfloat16)
    grad_cross_keys = (
        jnp.einsum("hqk,qhd->khd", grad_scores, asked_heads, preferred_element_type=jnp.float32)
        * score_scale
    )
    grad_cross_values = jnp.einsum(
        "hqk,qhd->khd",
        cross_probs.astype(jnp.bfloat16),
        grad_cross_heads,
        preferred_element_type=jnp.float32,
    )
    pair_terms = jnp.concatenate([head_join(grad_cross_keys), head_join(grad_cross_values)], 1)
    pair_grad = lax.psum_scatter(
        pair_terms.astype(jnp.bfloat16), "seq", scatter_dimension=0, tiled=True
    )
    grad_keyval = transposed(source_low, pair_grad)
    grad_source = against(pair_grad, full_keyval)
    grad_query = transposed(lowered_two, grad_asked)
    dx_two, grad_gain_two, grad_shift_two = norm_back(
        against(grad_asked, full_query), normed_two, inverse_two, gain_two
    )
    grad_self = grad_cross + dx_two
    grad_self_low = grad_self.astype(jnp.bfloat16)
    grad_output = transposed(self_mixed, grad_self_low)
    grad_mixed = against(grad_self_low, full_output).astype(jnp.bfloat16)
    grad_heads = head_split(grad_mixed)
    row_dots = grad_dots(
        queries, grad_heads, key_blocks, value_blocks, seg_blocks, own_segments, log_total
    )
    grad_queries, key_terms = query_grads(
        queries, grad_heads, key_blocks, value_blocks, seg_blocks, own_segments, log_total, row_dots
    )
    summed = lax.psum_scatter(
        key_terms.reshape(seq_length, 2 * model_width).astype(jnp.bfloat16),
        "seq",
        scatter_dimension=0,
        tiled=True,
    )
    grad_projected = jnp.concatenate([head_join(grad_queries).astype(jnp.bfloat16), summed], 1)
    grad_project = transposed(lowered_one, grad_projected)
    dx_one, grad_gain_one, grad_shift_one = norm_back(
        against(grad_projected, full_project), normed_one, inverse_one, gain_one
    )
    grad_target = grad_self + dx_one
    shards = (
        lax.psum_scatter(grad_project, ("rows", "seq"), scatter_dimension=0, tiled=True),
        lax.psum_scatter(grad_output, ("rows", "seq"), scatter_dimension=0, tiled=True),
        lax.psum_scatter(grad_query, ("rows", "seq"), scatter_dimension=0, tiled=True),
        lax.psum_scatter(grad_keyval, ("rows", "seq"), scatter_dimension=0, tiled=True),
        lax.psum_scatter(grad_crossout, ("rows", "seq"), scatter_dimension=0, tiled=True),
        lax.psum_scatter(grad_up, ("rows", "seq"), scatter_dimension=0, tiled=True),
        lax.psum_scatter(grad_upbias, ("rows", "seq"), scatter_dimension=0, tiled=True),
        lax.psum_scatter(grad_down, ("rows", "seq"), scatter_dimension=0, tiled=True),
        lax.psum_scatter(grad_downbias, ("rows", "seq"), scatter_dimension=0, tiled=True),
        lax.psum_scatter(grad_gain_one, ("rows", "seq"), scatter_dimension=0, tiled=True),
        lax.psum_scatter(grad_shift_one, ("rows", "seq"), scatter_dimension=0, tiled=True),
        lax.psum_scatter(grad_gain_two, ("rows", "seq"), scatter_dimension=0, tiled=True),
        lax.psum_scatter(grad_shift_two, ("rows", "seq"), scatter_dimension=0, tiled=True),
        lax.psum_scatter(grad_gain_three, ("rows", "seq"), scatter_dimension=0, tiled=True),
        lax.psum_scatter(grad_shift_three, ("rows", "seq"), scatter_dimension=0, tiled=True),
    )
    return (layer_out.astype(jnp.bfloat16)[None], grad_target[None], grad_source[None]) + tuple(
        shards
    )


F32, BF16 = jnp.float32, jnp.bfloat16
BLOCK = 16
AXES = ("rows", "seq")
FLIP_Y, FLIP_CORE, FLIP_X, FLIP_Z = 1, 2, 4, 8
MODEL, FEED, OWN, WINDOW, HALF_SOURCE = 512, 2048, 512, 256, 192
KEYS, SOURCES = OWN + WINDOW, 2 * HALF_SOURCE
TILE = 128
MASKED = -1000000000.0
SCALE = HD ** (-0.5)


def exchange(value, flip):
    return lax.ppermute(value, AXES, [(device, device ^ flip) for device in range(32)])


def exchange_side(value, step):
    flips = (FLIP_X, FLIP_Y) if step == 0 else (FLIP_Y, FLIP_X)
    return lax.ppermute(value, AXES, [(device, device ^ flips[device >> 1 & 1]) for device in range(32)])


def tied(values, *others):
    return lax.optimization_barrier((values, others))[0]


def along_z(block):
    return [exchange(block, FLIP_Z * i) for i in Z_ORDER]


Z_ORDER = (1, 2, 3)


def join(*parts):
    return jnp.concatenate(parts, 0)


def both_cores(halves):
    return halves + [exchange(half, FLIP_CORE) for half in halves]


def add_halves(kept, came):
    half = kept.shape[0] // 2
    return kept[half:] + came[half:], kept[:half] + came[:half]


def z_blocks(both):
    size = both.shape[0] // 4
    blocks = [both[size * i : size * (i + 1)] for i in range(4)]
    return [blocks[0]] + [exchange(block, FLIP_Z * i) for i, block in zip(Z_ORDER, blocks[1:])]


def block_places(me):
    out = []
    for other in (0, 1):
        core = (me >> 1 & 1) ^ other
        first, second = FLIP_X - 3 * core, FLIP_Y + 3 * core
        for b in (0, 1):
            for a in (0, 1):
                for i, z in enumerate((0,) + Z_ORDER):
                    owner = me ^ (other * FLIP_CORE + b * second + a * first + z * FLIP_Z)
                    out.append((other * 2 + b, a * 4 + i, owner))
    return out


def nn(left, right):
    return jnp.dot(left, right, preferred_element_type=F32)


def block_rows(owner, size=BLOCK):
    return pl.ds(pl.multiple_of(owner * size, size), size)


def load_blocks(me, pieces, columns, target):
    for piece, row, owner in block_places(me):
        target[block_rows(owner), :] = pieces[piece][row * BLOCK : (row + 1) * BLOCK, columns]


def store_blocks(me, source, targets, columns):
    for piece, row, owner in block_places(me):
        at = (piece % 2 * 8 + row) * BLOCK
        targets[piece // 2][at : at + BLOCK, columns] = source[block_rows(owner), :]


def normed_rows(value):
    centered = value - jnp.mean(value, -1, keepdims=True)
    inverse = lax.rsqrt(jnp.mean(centered * centered, -1, keepdims=True) + 1e-05)
    return centered * inverse, inverse


def norm_back_rows(upstream, normed, inverse, gain):
    scaled = upstream * gain
    first_mean = jnp.mean(scaled, -1, keepdims=True)
    second_mean = jnp.mean(scaled * normed, -1, keepdims=True)
    return inverse * (scaled - first_mean - normed * second_mean)


def column_sum(value):
    return jnp.sum(value, 0, keepdims=True)


def own_segments_of(index, segments):
    return jnp.where(index == 0, segments[:, :OWN], segments[:, OWN:]).astype(F32)


def key_segments_of(index, segments):
    near = jnp.where(index == 0, segments[:, OWN:KEYS], segments[:, OWN - WINDOW : OWN])
    return jnp.concatenate([own_segments_of(index, segments), near.astype(F32)], 1)


def spread(row):
    return jnp.broadcast_to(row, (TILE, row.shape[1])).T


def lane_half(shape, half):
    lanes = lax.broadcasted_iota(jnp.int32, shape, 1)
    return (lanes < HD) if half == 0 else (lanes >= HD)


def half_masks(value):
    keep, zero = lane_half(value.shape, 0), jnp.zeros_like(value)
    return jnp.concatenate([jnp.where(keep, value, zero), jnp.where(keep, zero, value)], 0)


def self_jobs(side):
    near, far = pl.multiple_of((1 - side) * 256, 256), pl.multiple_of(side * 256, 256)
    skip_near, skip_far = pl.multiple_of((1 - side) * TILE, TILE), pl.multiple_of(side * TILE, TILE)
    return [
        (pl.ds(near, 256), [(skip_near, 384), (OWN, WINDOW)], 256),
        (pl.ds(far, 256), [(skip_far, 384)], 256),
    ]


def attend(queries, pair_ref, mixed, log_rows, query_seg, key_row, jobs):
    for rows, spans, size in jobs:

        def keys_of(ref, lanes):
            parts = [ref[pl.ds(start, count), lanes] for start, count in spans]
            return parts[0] if len(parts) == 1 else jnp.concatenate(parts, 0)

        segments = [key_row[:, pl.ds(start, count)] for start, count in spans]
        segments = segments[0] if len(segments) == 1 else jnp.concatenate(segments, 1)
        same = jnp.concatenate([query_seg[rows, :]] * (segments.shape[1] // TILE), 1) == segments
        bias = jnp.where(same, 0.0, MASKED)
        lanes = lax.broadcasted_iota(jnp.int32, (size, TILE), 1)
        logs = jnp.zeros((size, TILE), F32)
        for pair in range(HEADS // 2):
            at = slice(pair * TILE, (pair + 1) * TILE)
            scores = against(half_masks(queries[rows, at]), keys_of(pair_ref, at))
            weights, scales = [], []
            for half in range(2):
                part = scores[half * size : (half + 1) * size] + bias
                top = jnp.max(part, -1, keepdims=True)
                part = jnp.exp(part - top)
                total = jnp.sum(part, -1, keepdims=True)
                weights.append(part.astype(BF16))
                scales.append(1.0 / total)
                logs = jnp.where(lanes == pair * 2 + half, top + jnp.log(total), logs)
            values = keys_of(pair_ref, slice(MODEL + pair * TILE, MODEL + (pair + 1) * TILE))
            out = nn(jnp.concatenate(weights, 0), values)
            keep = lane_half((size, TILE), 0)
            mixed[rows, at] = jnp.where(keep, out[:size] * scales[0], out[size:] * scales[1]).astype(BF16)
        log_rows[:, rows] = logs.T[:HEADS]


def head_dots(upstream, mixed):
    head = lax.broadcasted_iota(jnp.int32, (HEADS, MODEL), 1) // HD
    ones = (head == lax.broadcasted_iota(jnp.int32, (HEADS, MODEL), 0)).astype(F32)
    return lax.dot_general(
        ones, upstream.astype(F32) * mixed.astype(F32), (((1,), (1,)), ((), ())),
        precision=lax.Precision.HIGHEST, preferred_element_type=F32,
    )


def attend_back(queries, upstream, pair_ref, log_rows, dot_rows, query_row, key_seg, query_grad, pair_grad, jobs):
    query_grad[...] = jnp.zeros_like(query_grad)
    for key_start, size, start, count in jobs:
        rows, across = pl.ds(key_start, size), pl.ds(start, count)

        def heads(step, unused):
            same = jnp.concatenate([key_seg[rows, :]] * (count // TILE), 1) == query_row[:, across]
            bias = jnp.where(same, 0.0, MASKED)
            for pair in (step * 2, step * 2 + 1):
                at = pl.ds(pl.multiple_of(pair * TILE, TILE), TILE)
                value_at = pl.ds(pl.multiple_of(MODEL + pair * TILE, TILE), TILE)
                query = queries[across, at]
                grad = upstream[across, at]
                keys = half_masks(pair_ref[rows, at])
                values = half_masks(pair_ref[rows, value_at])
                scores, grads = against(keys, query), against(values, grad)
                weights, score_grads = [], []
                for half in range(2):
                    head, part = pl.ds(pair * 2 + half, 1), slice(half * size, (half + 1) * size)
                    weight = jnp.exp(scores[part] + (bias - log_rows[head, across]))
                    score_grads.append((weight * (grads[part] - dot_rows[head, across])).astype(BF16))
                    weights.append(weight.astype(BF16))
                score_grad = jnp.concatenate(score_grads, 0)
                value_part = nn(jnp.concatenate(weights, 0), grad)
                key_part = nn(score_grad, query)
                query_grad[across, at] += transposed(score_grad, keys)
                keep = lane_half((size, TILE), 0)
                pair_grad[rows, at] = jnp.where(keep, key_part[:size], key_part[size:]).astype(BF16)
                pair_grad[rows, value_at] = jnp.where(keep, value_part[:size], value_part[size:]).astype(BF16)
            return unused

        lax.fori_loop(0, HEADS // 4, heads, 0)


def self_back_jobs(side):
    near = pl.multiple_of((1 - side) * 256, 256)
    return [(0, 256, 0, 384), (256, 256, TILE, 384), (OWN, WINDOW, near, 256)]


def pack_body(
    place, vectors, project, output, query, keyval, crossout, up, down, states, source,
    one, three, near, own_source, block, semaphores
):
    me, side = place[0], place[1]
    copies = [
        (project, one.at[:, :1536]),
        (output, one.at[:, 1664:2176]),
        (query, one.at[:, 2176:2688]),
        (keyval, one.at[:, 2688:3712]),
        (crossout, one.at[:, 3712:]),
        (down, three.at[64:]),
    ] + [
        (up.at[:, part * 512 : (part + 1) * 512], three.at[part * BLOCK : (part + 1) * BLOCK, :])
        for part in range(4)
    ] + [
        (states.at[pl.ds(pl.multiple_of((1 - side) * WINDOW, WINDOW), WINDOW), :], near.at[:WINDOW])
    ]
    copies = [pltpu.make_async_copy(*copy, semaphores.at[i]) for i, copy in enumerate(copies)]
    for copy in copies:
        copy.start()
    gap = jnp.zeros((HALF_SOURCE - source.shape[0], MODEL), F32)
    padded = jnp.concatenate([source[...].astype(F32), gap], 0).astype(BF16)
    own_source[...] = padded
    near[WINDOW:, :] = padded
    values = jnp.broadcast_to(vectors[...].astype(F32), (8, 256))
    lanes = lax.broadcasted_iota(jnp.int32, (8, TILE), 1)
    rows = lax.broadcasted_iota(jnp.int32, (8, TILE), 0)
    packed = jnp.zeros((8, TILE), F32)
    spot, wide = (me & 7) * 16, (me & 1) * 64
    for row in range(7):
        moved = pltpu.roll(values, spot + 256 - 16 * row, 1)[:, :TILE]
        inside = jnp.logical_and(lanes >= spot, lanes < spot + 16)
        packed = jnp.where(jnp.logical_and(rows == row, inside), moved, packed)
    moved = pltpu.roll(values, wide + 256 - 112, 1)[:, :TILE]
    inside = jnp.logical_and(lanes >= wide, lanes < wide + 64)
    packed = jnp.where(jnp.logical_and(rows == 7, inside), moved, packed)
    block[...] = jnp.concatenate([packed, jnp.zeros((8, TILE), F32)], 0).astype(BF16)
    last = pltpu.make_async_copy(block, one.at[:, 1536:1664], semaphores.at[len(copies)])
    last.start()
    for copy in copies + [last]:
        copy.wait()


def self_body(place, states, window, *refs):
    pieces, refs = refs[:4], refs[4:]
    queries, pair, lowered, vectors, up_bias, weight, weight_two, packed = refs
    me = place[0]
    load_blocks(me, pieces, slice(1536, 1664), packed)
    load_blocks(me, pieces, slice(0, 1536), weight)
    load_blocks(me, pieces, slice(1664, 4224), weight_two)
    for tile in range(4):
        total = jnp.zeros((8, TILE), F32)
        for i in range(8):
            total = total + packed[(tile * 8 + i) * BLOCK : (tile * 8 + i + 1) * BLOCK, :].astype(F32)[:8]
        vectors[:, tile * TILE : (tile + 1) * TILE] = total
    for tile in range(16):
        total = (
            packed[2 * tile * BLOCK : (2 * tile + 1) * BLOCK, :].astype(F32)
            + packed[(2 * tile + 1) * BLOCK : (2 * tile + 2) * BLOCK, :].astype(F32)
        )
        up_bias[:, tile * TILE : (tile + 1) * TILE] = total[7:8]
    gain, shift = vectors[1:2, :], vectors[2:3, :]
    for i in range(KEYS // TILE):
        rows = slice(i * TILE, (i + 1) * TILE)
        value = states[rows, :] if i < 4 else window[(i - 4) * TILE : (i - 3) * TILE, :]
        lowered[rows, :] = (normed_rows(value.astype(F32))[0] * gain + shift).astype(BF16)
    for i in range(KEYS // 256):
        rows = slice(i * 256, (i + 1) * 256)
        if i < 2:
            queries[rows, :] = (nn(lowered[rows, :], weight[:, :512]) .astype(BF16) * SCALE).astype(BF16)
        pair[rows, :] = nn(lowered[rows, :], weight[:, 512:]).astype(BF16)


def forward_body(
    place, segments, source_segments, states, own_source, other_source, vectors, weight, self_queries, self_pair,
    self_mixed, self_logs, after_self, lowered, queries, pair, mixed, logs, after_cross,
    query_seg, key_row, source_row, source,
):
    self_mix(place, segments, self_queries, self_pair, self_mixed, self_logs, query_seg, key_row)
    cross_lower(
        place, states, own_source, other_source, self_mixed, vectors, after_self, lowered, queries, pair, weight, source
    )
    source_row[...] = source_segments[...].astype(F32)
    attend(queries, pair, mixed, logs, query_seg, source_row, [(pl.ds(0, OWN), [(0, SOURCES)], OWN)])
    for i in range(2):
        rows = slice(i * 256, (i + 1) * 256)
        after_cross[rows, :] = after_self[rows, :] + nn(mixed[rows, :], weight[:, 2048:])


def self_mix(place, segments, queries, pair, mixed, log_rows, query_seg, key_row):
    query_seg[...] = spread(own_segments_of(place[1], segments[...]))
    key_row[...] = key_segments_of(place[1], segments[...])
    attend(queries, pair, mixed, log_rows, query_seg, key_row, self_jobs(place[1]))


def cross_lower(
    place, states, own_source, other_source, self_mixed, vectors, after_self, lowered, queries, pair, weight, source
):
    side = place[1]
    source[:HALF_SOURCE, :] = jnp.where(side == 0, own_source[...], other_source[...])
    source[HALF_SOURCE:, :] = jnp.where(side == 0, other_source[...], own_source[...])
    gain, shift = vectors[3:4, :], vectors[4:5, :]
    pair[...] = nn(source[...], weight[:, 1024:2048]).astype(BF16)
    for i in range(2):
        rows = slice(i * 256, (i + 1) * 256)
        value = states[rows, :].astype(F32) + nn(self_mixed[rows, :], weight[:, :512])
        after_self[rows, :] = value
        lowered[rows, :] = (normed_rows(value)[0] * gain + shift).astype(BF16)
        queries[rows, :] = (nn(lowered[rows, :], weight[:, 512:1024]).astype(BF16) * SCALE).astype(BF16)


CHUNK, UNROLL = 512, 4


def feed_front_body(place, after_cross, vectors, lowered, flipped):
    gain, shift = vectors[5:6, :], vectors[6:7, :]
    for i in range(4):
        rows = slice(i * TILE, (i + 1) * TILE)
        low = (normed_rows(after_cross[rows, :])[0] * gain + shift).astype(BF16)
        lowered[rows, :] = low
    flipped[...] = lowered[...].T


def feed_body(place, lowered, flipped, output_grad, up_bias, *refs):
    pieces, refs = refs[:4], refs[4:]
    (
        total, back, kept, sent, bias_sums, ups, downs, up_grads, down_grads,
    ) = refs
    me = place[0]
    places = block_places(me)

    def chunk_of(z):
        return pl.multiple_of(((me >> 3) ^ z) * CHUNK, CHUNK)

    grad_low = output_grad[...]
    total[...] = jnp.zeros_like(total)
    back[...] = jnp.zeros_like(back)

    def chunk(z):
        at = pl.ds(chunk_of(z), CHUNK)
        mine = me >> 3
        z_row = (mine ^ z) * BLOCK
        up, down, up_grad, down_grad = ups.at[z], downs.at[z], up_grads.at[z], down_grads.at[z]
        swapped_z = (z & 1) * 2 + (z >> 1)
        for piece, row, owner in places:
            owner = (owner & 7) + (mine ^ (row % 2 * 2 + row % 4 // 2)) * FLIP_Z
            up[block_rows(owner), :] = pieces[piece][pl.ds(pl.multiple_of(row * 128 + z_row, BLOCK), BLOCK), :]
            if row % 4 == 0:
                start = pl.multiple_of((row + swapped_z) * 128 + 64, 64)
                down[block_rows(owner & 7, 64), :] = pieces[piece][pl.ds(start, 64), :]
        hidden = nn(lowered[...], up[...]) + up_bias[:, at]
        square = hidden * hidden
        inner = 0.7978845608028654 * hidden * (1.0 + 0.044715 * square)
        curve = jnp.tanh(inner)
        half = 0.5 * (1.0 + curve)
        activated = (hidden * half).astype(BF16)
        slope = half + (0.5 * 0.7978845608028654) * hidden * (1.0 - curve * curve) * (
            1.0 + (3 * 0.044715) * square
        )
        down_grad[...] = transposed(activated, grad_low).astype(BF16)
        for piece, row, owner in places:
            if row % 4 == 0:
                to = pl.multiple_of((piece % 2 * 8 + row + z) * 128 + 64, 64)
                (kept, sent)[piece // 2][pl.ds(to, 64), :] = down_grad[block_rows(owner & 7, 64), :]
        grad_hidden = (against(grad_low, down[...]) * slope).astype(BF16)
        bias_sums[:, at] = column_sum(grad_hidden.astype(F32))
        up_grad[...] = nn(flipped[...], grad_hidden).astype(BF16)
        for piece, row, owner in places:
            to = (piece % 2 * 8 + row) * 128
            (kept, sent)[piece // 2][pl.ds(pl.multiple_of(to + z_row, BLOCK), BLOCK), :] = up_grad[block_rows(owner), :]
        total[...] += nn(activated, down[...])
        back[...] += against(grad_hidden, up[...])

    def chunks(step, unused):
        for z in range(UNROLL):
            chunk(step * UNROLL + z)
        return unused

    lax.fori_loop(0, 4 // UNROLL, chunks, 0)


def feed_last_body(
    place, after_cross, output_grad, vectors, total, back, mixed, weight,
    layer_out, after_grad, sums, mixed_grad, dot_rows, crossout_grad,
):
    gain = vectors[5:6, :]
    gain_sum, shift_sum, bias_sum = (jnp.zeros((1, MODEL), F32) for _ in range(3))
    for i in range(4):
        rows = slice(i * TILE, (i + 1) * TILE)
        value, grad = after_cross[rows, :], output_grad[rows, :].astype(F32)
        layer_out[rows, :] = (value + total[rows, :] + vectors[0:1, :]).astype(BF16)
        normed, inverse = normed_rows(value)
        upstream = back[rows, :]
        after_grad[rows, :] = grad + norm_back_rows(upstream, normed, inverse, gain)
        gain_sum, shift_sum = gain_sum + column_sum(upstream * normed), shift_sum + column_sum(upstream)
        bias_sum = bias_sum + column_sum(grad)
    zero = jnp.zeros((1, MODEL), F32)
    sums[...] = jnp.concatenate([bias_sum, zero, zero, zero, zero, gain_sum, shift_sum, zero], 0)
    grad_low = after_grad[...].astype(BF16)
    mixed_grad[...] = against(grad_low, weight[:, 2048:]).astype(BF16)
    dot_rows[...] = head_dots(mixed_grad[...], mixed[...])
    crossout_grad[...] = transposed(mixed[...], grad_low).astype(BF16)


def cross_back_body(
    place, segments, source_segments, own_source, other_source, queries, pair, log_rows, upstream, dot_rows, weight,
    asked, source_own, source_send, grads, query_grad, pair_grad, source, key_seg, query_row,
):
    side = place[1]
    key_seg[...] = spread(source_segments[...].astype(F32))
    query_row[...] = own_segments_of(side, segments[...])
    source[:HALF_SOURCE, :] = jnp.where(side == 0, own_source[...], other_source[...])
    source[HALF_SOURCE:, :] = jnp.where(side == 0, other_source[...], own_source[...])
    attend_back(
        queries, upstream, pair, log_rows, dot_rows, query_row, key_seg, query_grad, pair_grad,
        [(0, SOURCES, 0, OWN)],
    )
    asked[...] = (query_grad[...] * SCALE).astype(BF16)
    grads[...] = transposed(source[...], pair_grad[...]).astype(BF16)
    back = against(pair_grad[...], weight[:, 1024:2048])
    first, second = back[:HALF_SOURCE], back[HALF_SOURCE:]
    source_own[...] = jnp.where(side == 0, first, second)
    source_send[...] = jnp.where(side == 0, second, first).astype(BF16)


def cross_weight_body(
    place, after_self, lowered, self_mixed, after_grad, asked, vectors, sums, weight, crossout_grad, keyval_grad, *refs
):
    self_grad, upstream, dot_rows, kept, sent, new_sums, grads = refs
    me = place[0]
    store_blocks(me, crossout_grad, (kept, sent), slice(0, 512))
    store_blocks(me, keyval_grad, (kept, sent), slice(512, 1536))
    gain = vectors[3:4, :]
    gain_sum, shift_sum = jnp.zeros((1, MODEL), F32), jnp.zeros((1, MODEL), F32)
    for i in range(2):
        rows = slice(i * 256, (i + 1) * 256)
        normed, inverse = normed_rows(after_self[rows, :])
        up = against(asked[rows, :], weight[:, 512:1024])
        self_grad[rows, :] = after_grad[rows, :] + norm_back_rows(up, normed, inverse, gain)
        gain_sum, shift_sum = gain_sum + column_sum(up * normed), shift_sum + column_sum(up)
    grads[:, :512] = transposed(lowered[...], asked[...]).astype(BF16)
    grad_low = self_grad[...].astype(BF16)
    grads[:, 512:] = transposed(self_mixed[...], grad_low).astype(BF16)
    store_blocks(me, grads, (kept, sent), slice(1536, 2560))
    upstream[...] = against(grad_low, weight[:, :512]).astype(BF16)
    dot_rows[...] = head_dots(upstream[...], self_mixed[...])
    zero = jnp.zeros((1, MODEL), F32)
    new_sums[...] = sums[...] + jnp.concatenate(
        [zero, zero, zero, gain_sum, shift_sum, zero, zero, zero], 0
    )


def self_back_body(
    place, segments, states, window, lowered, queries, pair, log_rows, upstream, dot_rows, weight, sums, bias_sums,
    source_send, own_back, near_back, kept, sent, query_grad, pair_grad, grads, key_seg, query_row,
):
    near_back[WINDOW:, :] = source_send[...]
    key_seg[...] = spread(key_segments_of(place[1], segments[...]))
    query_row[...] = own_segments_of(place[1], segments[...])
    attend_back(
        queries, upstream, pair, log_rows, dot_rows, query_row, key_seg, query_grad, pair_grad,
        self_back_jobs(place[1]),
    )
    asked = (query_grad[...] * SCALE).astype(BF16)
    grads[:, :MODEL] = transposed(lowered[:OWN, :], asked).astype(BF16)
    grads[:, MODEL:1536] = transposed(lowered[...], pair_grad[...]).astype(BF16)
    gain_sum, shift_sum = jnp.zeros((1, MODEL), F32), jnp.zeros((1, MODEL), F32)
    for i in range(3):
        rows = slice(i * 256, (i + 1) * 256)
        part = against(pair_grad[rows, :], weight[:, MODEL:])
        if i < 2:
            part = part + against(asked[rows, :], weight[:, :MODEL])
            own_back[rows, :] = part
            value = states[rows, :]
        else:
            near_back[:WINDOW, :] = part.astype(BF16)
            value = window[...]
        normed = normed_rows(value.astype(F32))[0]
        gain_sum, shift_sum = gain_sum + column_sum(part * normed), shift_sum + column_sum(part)
    zero = jnp.zeros((1, MODEL), F32)
    sums = sums[...] + jnp.concatenate([zero, gain_sum, shift_sum, zero, zero, zero, zero, zero], 0)
    last = lax.broadcasted_iota(jnp.int32, (8, TILE), 0) == 7
    for device in range(32):
        tile, wide = device // 8 * TILE, device // 2 * TILE
        value = jnp.where(last, bias_sums[:, wide : wide + TILE], sums[:, tile : tile + TILE])
        high = value.astype(BF16).astype(F32)
        grads[device * BLOCK : (device + 1) * BLOCK, 1536:] = jnp.concatenate([high, value - high], 0).astype(BF16)
    store_blocks(place[0], grads, (kept, sent), slice(0, 1664))


def target_body(place, back, came, states, self_grad, vectors, out):
    gain = vectors[1:2, :]
    for i in range(4):
        rows = slice(i * TILE, (i + 1) * TILE)
        here = (i < 2) == (place[1] == 1)
        extra = came[(i % 2) * TILE : (i % 2 + 1) * TILE, :].astype(F32)
        upstream = back[rows, :] + jnp.where(here, extra, 0.0)
        normed, inverse = normed_rows(states[rows, :].astype(F32))
        out[rows, :] = self_grad[rows, :] + norm_back_rows(upstream, normed, inverse, gain)


def finish_body(place, *refs):
    feed, cross, last, outs = refs[:2], refs[2:6], refs[6:10], refs[10:]
    project, output, query, keyval, crossout, up, down, *small = outs
    me = place[0]

    def total(parts, begin, end, rows=slice(None)):
        value = parts[0][rows, begin:end].astype(F32)
        for part in parts[1:]:
            value = value + part[rows, begin:end].astype(F32)
        return value

    for part in range(4):
        rows = slice(part * BLOCK, (part + 1) * BLOCK)
        up[:, part * 512 : (part + 1) * 512] = total(feed, 0, MODEL, rows)
    down[...] = total(feed, 0, MODEL, slice(64, 128))
    crossout[...] = total(cross, 0, 512)
    keyval[...] = total(cross, 512, 1536)
    query[...] = total(cross, 1536, 2048)
    output[...] = total(cross, 2048, 2560)
    project[...] = total(last, 0, 1536)
    value = total(last, 1536, 1664)
    value = value[:8] + value[8:]
    narrow = pltpu.roll(value, (TILE - (me & 7) * 16) & 127, 1)
    wide = pltpu.roll(value, (TILE - (me & 1) * 64) & 127, 1)
    for row in range(7):
        small[row][...] = narrow[row : row + 1, :16]
    small[7][...] = wide[7:8, :64]


def shape_of(*shape, dtype=BF16):
    return jax.ShapeDtypeStruct(shape, dtype)


VMEM_SPEC = pl.BlockSpec(memory_space=pltpu.VMEM)
ANY_SPEC = pl.BlockSpec(memory_space=pl.ANY)
HBM_SPEC = pl.BlockSpec(memory_space=pltpu.HBM)
SMEM_SPEC = pl.BlockSpec(memory_space=pltpu.SMEM)


def call(body, name, place, inputs, pieces, outs, scratch, flops, any_outs=(), any_ins=(), vmem=20):
    return pl.pallas_call(
        body,
        name=name,
        out_shape=outs,
        in_specs=[SMEM_SPEC]
        + [HBM_SPEC if i in any_ins else VMEM_SPEC for i in range(len(inputs))]
        + [VMEM_SPEC] * len(pieces),
        out_specs=[ANY_SPEC if i in any_outs else VMEM_SPEC for i in range(len(outs))],
        scratch_shapes=scratch,
        compiler_params=pltpu.CompilerParams(vmem_limit_bytes=vmem * 2**20),
        cost_estimate=pl.CostEstimate(flops=flops, bytes_accessed=4 * 2**20, transcendentals=0),
    )(place, *inputs, *pieces)


def fast_device(
    target_states, source_states, target_segments, source_segments, output_grad, self_project,
    self_output, cross_query, cross_keyval, cross_output, hidden_up, hidden_bias, hidden_down,
    output_bias, first_gain, first_shift, second_gain, second_shift, third_gain, third_shift,
):
    vmem, dma = pltpu.VMEM, pltpu.SemaphoreType.DMA
    side = lax.axis_index("seq")
    place = jnp.stack([lax.axis_index("rows") * 2 + side, side]).astype(jnp.int32)
    states, grad = target_states[0], output_grad[0]
    small = jnp.pad(hidden_bias[None], ((0, 0), (112, 80)))
    for i, vector in enumerate(
        (output_bias, first_gain, first_shift, second_gain, second_shift, third_gain, third_shift)
    ):
        small = small + jnp.pad(vector[None], ((0, 0), (16 * i, 240 - 16 * i)))
    one, three, near, own_source = call(
        pack_body, "pack", place,
        [
            small, self_project, self_output, cross_query, cross_keyval, cross_output, hidden_up, hidden_down, states,
            source_states[0],
        ],
        [],
        [
            shape_of(16, 4224), shape_of(128, MODEL), shape_of(WINDOW + HALF_SOURCE, MODEL),
            shape_of(HALF_SOURCE, MODEL),
        ],
        [vmem((BLOCK, TILE), BF16), dma((12,))], 1000000, any_ins=range(1, 9), vmem=60,
    )
    parts = along_z(one)
    near = exchange(near, FLIP_Y)
    one = join(one, *parts)
    one = tied(one, near)
    came = exchange_side(one, 0)
    three = tied(three, one)
    far = exchange(three, 2 * FLIP_Z)
    came = tied(came, far)
    one = join(one, came)
    one_core = exchange(one, FLIP_CORE)
    other = exchange_side(one, 1)
    three = join(three, tied(far, one))
    three = join(three, exchange(three, FLIP_Z))
    came = exchange_side(three, 0)
    other = tied(other, came)
    window, other_source = near[:WINDOW], near[WINDOW:]
    pieces_one = [one, other, one_core, exchange(other, FLIP_CORE)]
    three = join(three, came)
    three_core = exchange(three, FLIP_CORE)
    three_other = exchange_side(three, 1)
    half = source_states.shape[1]
    gap = jnp.full((1, HALF_SOURCE - half), -1, jnp.int32)
    source_seg = jnp.concatenate([source_segments[:, :half], gap, source_segments[:, half:], gap], 1)

    queries, pair, lowered, vectors, up_bias, weight_one, weight_two = call(
        self_body, "self_lower", place, [states, window], pieces_one,
        [
            shape_of(OWN, MODEL), shape_of(KEYS, 2 * MODEL), shape_of(KEYS, MODEL), shape_of(8, MODEL, dtype=F32),
            shape_of(1, FEED, dtype=F32), shape_of(MODEL, 1536), shape_of(MODEL, 2560),
        ],
        [vmem((MODEL, TILE), BF16)], 1000,
    )
    mixed, logs, after_self, lowered_two, queries_two, pair_two, mixed_two, logs_two, after_cross = call(
        forward_body, "forward", place,
        [
            target_segments, source_seg, states, own_source, other_source, vectors, weight_two, queries, pair,
        ],
        [],
        [
            shape_of(OWN, MODEL), shape_of(HEADS, OWN, dtype=F32), shape_of(OWN, MODEL, dtype=F32), shape_of(OWN, MODEL),
            shape_of(OWN, MODEL), shape_of(SOURCES, 2 * MODEL), shape_of(OWN, MODEL), shape_of(HEADS, OWN, dtype=F32),
            shape_of(OWN, MODEL, dtype=F32),
        ],
        [
            vmem((OWN, TILE), F32), vmem((1, KEYS), F32), vmem((1, SOURCES), F32), vmem((SOURCES, MODEL), BF16),
        ],
        1000,
    )
    three_core, three_other = tied((three_core, three_other), after_cross)
    last_piece = exchange(three_other, FLIP_CORE)
    feed_in = call(
        feed_front_body, "feed_front", place, [tied(after_cross, three_other), vectors], [],
        [shape_of(OWN, MODEL), shape_of(MODEL, OWN)], [], 1000,
    )
    pieces_three = [three, three_other, three_core, tied(last_piece, feed_in)]
    total, back, feed_kept, feed_sent, bias_sums = call(
        feed_body, "feed", place, [*feed_in, grad, up_bias], pieces_three,
        [shape_of(OWN, MODEL, dtype=F32)] * 2 + [shape_of(2048, MODEL)] * 2 + [shape_of(1, FEED, dtype=F32)],
        [
            vmem((4, MODEL, CHUNK), BF16), vmem((4, CHUNK, MODEL), BF16), vmem((4, MODEL, CHUNK), BF16), vmem((4, CHUNK, MODEL), BF16),
        ],
        10000000000,
    )
    feed_came = exchange(feed_sent, FLIP_CORE)
    layer_out, after_grad, sums, upstream_two, dots_two, crossout_grad = call(
        feed_last_body, "feed_last", place, [after_cross, grad, vectors, total, back, mixed_two, weight_two], [],
        [
            shape_of(OWN, MODEL), shape_of(OWN, MODEL, dtype=F32), shape_of(8, MODEL, dtype=F32), shape_of(OWN, MODEL),
            shape_of(HEADS, OWN, dtype=F32), shape_of(MODEL, MODEL),
        ],
        [], 4000000000,
    )
    feed_came = tied(feed_came, after_grad)
    feed_sent, feed_kept = add_halves(feed_kept, feed_came)
    upstream_two = tied(upstream_two, feed_sent)
    feed_came = exchange_side(feed_sent, 1)
    asked, source_own, source_send, keyval_grad = call(
        cross_back_body, "cross_backward", place,
        [
            target_segments, source_seg, own_source, other_source, queries_two, pair_two, logs_two,
            upstream_two, dots_two, weight_two,
        ],
        [],
        [
            shape_of(OWN, MODEL), shape_of(HALF_SOURCE, MODEL, dtype=F32), shape_of(HALF_SOURCE, MODEL),
            shape_of(MODEL, 1024),
        ],
        [
            vmem((OWN, MODEL), F32), vmem((SOURCES, 2 * MODEL), BF16),
            vmem((SOURCES, MODEL), BF16), vmem((SOURCES, TILE), F32), vmem((1, OWN), F32),
        ],
        10000000000,
    )
    self_grad, upstream, dot_rows, cross_kept, cross_sent, sums = call(
        cross_weight_body, "cross_weights", place,
        [after_self, lowered_two, mixed, after_grad, asked, vectors, sums, weight_two, crossout_grad, keyval_grad],
        [],
        [shape_of(OWN, MODEL, dtype=F32), shape_of(OWN, MODEL), shape_of(HEADS, OWN, dtype=F32)]
        + [shape_of(256, 2560)] * 2 + [shape_of(8, MODEL, dtype=F32)],
        [vmem((MODEL, 1024), BF16)], 6000000000,
    )
    cross_came = exchange(cross_sent, FLIP_CORE)
    feed_came = tied(feed_came, upstream)
    feed_sent, feed_kept = add_halves(feed_kept, feed_came)
    feed_came = exchange_side(feed_sent, 0)
    cross_came = tied(cross_came, feed_sent)
    cross_sent, cross_kept = add_halves(cross_kept, cross_came)
    cross_came = exchange_side(cross_sent, 1)
    upstream = tied(upstream, cross_sent)
    own_back, near_back, last_kept, last_sent = call(
        self_back_body, "self_backward", place,
        [
            target_segments, states, window, lowered, queries, pair, logs, upstream, dot_rows, weight_one, sums,
            bias_sums, source_send,
        ],
        [],
        [shape_of(OWN, MODEL, dtype=F32), shape_of(WINDOW + HALF_SOURCE, MODEL)] + [shape_of(256, 1664)] * 2,
        [
            vmem((OWN, MODEL), F32), vmem((KEYS, 2 * MODEL), BF16), vmem((MODEL, 1664), BF16), vmem((KEYS, TILE), F32),
            vmem((1, OWN), F32),
        ],
        16000000000,
    )
    last_came = exchange(last_sent, FLIP_CORE)
    cross_came, feed_came = tied((cross_came, feed_came), own_back)
    feed_kept = feed_kept + feed_came
    feed_kept, feed_sent = (
        join(feed_kept[i * 128 : (i + 1) * 128], feed_kept[(i + 2) * 128 : (i + 3) * 128]) for i in range(2)
    )
    feed_came = exchange(feed_sent, FLIP_Z)
    cross_came = tied(cross_came, feed_sent)
    cross_sent, cross_kept = add_halves(cross_kept, cross_came)
    last_came = tied(last_came, feed_sent)
    last_sent, last_kept = add_halves(last_kept, last_came)
    last_came, cross_came = exchange_side(last_sent, 1), exchange_side(cross_sent, 0)
    feed_came = tied(feed_came, last_sent)
    feed_sent, feed_kept = add_halves(feed_kept, feed_came)
    feed = [feed_kept, exchange(feed_sent, 2 * FLIP_Z)]
    cross_came = tied(cross_came, feed_sent)
    cross_kept = cross_kept + cross_came
    last_came = tied(last_came, cross_kept)
    last_sent, last_kept = add_halves(last_kept, last_came)
    last_came = exchange_side(last_sent, 0)
    feed, near_back = tied((feed, near_back), last_sent)
    cross_kept = tied(cross_kept, feed)
    cross = z_blocks(cross_kept)
    near_came = exchange(near_back, FLIP_Y)
    last_came = tied(last_came, cross[0])
    last = z_blocks(last_kept + last_came)
    came, source_came = near_came[:WINDOW], near_came[WINDOW:]
    grad_source = source_own[:half] + source_came[:half].astype(F32)
    (grad_target,) = call(
        target_body, "target_grad", place, [own_back, came, states, self_grad, vectors], [],
        [shape_of(OWN, MODEL, dtype=F32)], [], 1000000,
    )
    last = tied(last, grad_target, grad_source)
    project, output, query, keyval, crossout, up, down, *small = call(
        finish_body, "finish", place, feed + cross + last, [],
        [
            shape_of(16, 1536, dtype=F32), shape_of(16, 512, dtype=F32), shape_of(16, 512, dtype=F32),
            shape_of(16, 1024, dtype=F32), shape_of(16, 512, dtype=F32), shape_of(16, 2048, dtype=F32),
            shape_of(64, 512, dtype=F32),
        ]
        + [shape_of(1, 16, dtype=F32)] * 7 + [shape_of(1, 64, dtype=F32)],
        [], 1000000,
    )
    *rows, up_sum = [row[0] for row in small]
    return (
        layer_out[None], grad_target[None], grad_source[None], project, output, query, keyval, crossout, up,
        up_sum, down, *rows,
    )


def specs():
    in_specs = (
        P("rows", "seq", None),
        P("rows", "seq", None),
        P("rows", None),
        P("rows", None),
        P("rows", "seq", None),
        P(("rows", "seq"), None),
        P(("rows", "seq"), None),
        P(("rows", "seq"), None),
        P(("rows", "seq"), None),
        P(("rows", "seq"), None),
        P(("rows", "seq"), None),
        P(("rows", "seq")),
        P(("rows", "seq"), None),
        P(("rows", "seq")),
        P(("rows", "seq")),
        P(("rows", "seq")),
        P(("rows", "seq")),
        P(("rows", "seq")),
        P(("rows", "seq")),
        P(("rows", "seq")),
    )
    out_specs = (
        P("rows", "seq", None),
        P("rows", "seq", None),
        P("rows", "seq", None),
        P(("rows", "seq"), None),
        P(("rows", "seq"), None),
        P(("rows", "seq"), None),
        P(("rows", "seq"), None),
        P(("rows", "seq"), None),
        P(("rows", "seq"), None),
        P(("rows", "seq")),
        P(("rows", "seq"), None),
        P(("rows", "seq")),
        P(("rows", "seq")),
        P(("rows", "seq")),
        P(("rows", "seq")),
        P(("rows", "seq")),
        P(("rows", "seq")),
        P(("rows", "seq")),
    )
    return in_specs, out_specs


def solution(mesh):
    in_specs, out_specs = specs()
    fast = mesh.shape["rows"] == 16 and mesh.shape["seq"] == 2
    return jax.shard_map(
        fast_device if fast else general_device,
        mesh=mesh, in_specs=in_specs, out_specs=out_specs, check_vma=False,
    )
```
